32 devices in a mesh: dp: 2 (over core), ctx: 4 (over y, x), expert: 4 (over z).
Axes of the slice: x: 2, y: 2, z: 4, core: 2. Of those that a mesh axis runs over, the one named last changes fastest.
Arguments:
- tokens: bfloat16 [2, 2048, 768], P('dp', ('ctx', 'expert')), may hold values from -6 to 6
- lengths: int32 [2], P('dp'), may hold values from 512 to 2048, as said below
- routes: int32 [2, 2048, 2], P('dp', ('ctx', 'expert')), may hold values from 0 to 15, all different within a row; in each aligned block of 128 rows (0 to 127, 128 to 255, ..., all dimensions but the last counted through in order) at most 22 rows name the same one
- norm1_gain: float32 [768], replicated, may hold values from 0.5 to 1.5
- query_weight: bfloat16 [768, 768], replicated, may hold values from -0.21875 to 0.21875
- key_weight: bfloat16 [768, 768], replicated, may hold values from -0.21875 to 0.21875
- value_weight: bfloat16 [768, 768], replicated, may hold values from -0.21875 to 0.21875
- output_weight: bfloat16 [768, 768], replicated, may hold values from -6 to 6
- norm2_gain: float32 [768], replicated, may hold values from 0.5 to 1.5
- router_weight: bfloat16 [768, 16], replicated, may hold values from -0.21875 to 0.21875
- expert_gate: bfloat16 [16, 768, 2048], P('expert'), may hold values from -0.21875 to 0.21875
- expert_up: bfloat16 [16, 768, 2048], P('expert'), may hold values from -0.21875 to 0.21875
- expert_down: bfloat16 [16, 2048, 768], P('expert'), may hold values from -0.125 to 0.125
- shared_gate: bfloat16 [768, 2048], replicated, may hold values from -0.21875 to 0.21875
- shared_up: bfloat16 [768, 2048], replicated, may hold values from -0.21875 to 0.21875
- shared_down: bfloat16 [2048, 768], replicated, may hold values from -0.125 to 0.125
- cotangent: bfloat16 [2, 2048, 768], P('dp', ('ctx', 'expert')), may hold values from -6 to 6
Outputs:
- output_rows: bfloat16 [2, 2048, 768], P('dp', ('ctx', 'expert'))
- input_grad: bfloat16 [2, 2048, 768], P('dp', ('ctx', 'expert'))
- norm1_gain_grad: float32 [768], P(('dp', 'ctx', 'expert'))
- query_weight_grad: float32 [768, 768], P(('dp', 'ctx', 'expert'))
- key_weight_grad: float32 [768, 768], P(('dp', 'ctx', 'expert'))
- value_weight_grad: float32 [768, 768], P(('dp', 'ctx', 'expert'))
- output_weight_grad: float32 [768, 768], P(('dp', 'ctx', 'expert'))
- norm2_gain_grad: float32 [768], P(('dp', 'ctx', 'expert'))
- router_weight_grad: float32 [768, 16], P(('dp', 'ctx', 'expert'))
- expert_gate_grad: float32 [16, 768, 2048], P('expert', None, ('dp', 'ctx'))
- expert_up_grad: float32 [16, 768, 2048], P('expert', None, ('dp', 'ctx'))
- expert_down_grad: float32 [16, 2048, 768], P('expert', ('dp', 'ctx'))
- shared_gate_grad: float32 [768, 2048], P(('dp', 'ctx', 'expert'))
- shared_up_grad: float32 [768, 2048], P(('dp', 'ctx', 'expert'))
- shared_down_grad: float32 [2048, 768], P(('dp', 'ctx', 'expert'))
The draws below stay inside these ranges and needn't reach their ends.
Inputs may be any that keep to these rules, and one draw needn't show every extreme that they name: `lengths`: one slot, drawn from the seed, is valid over all 2048 places; the others over a prefix of at least 512. `routes`: within the 128 tokens of one device (aligned blocks), no expert is named by more than 22 tokens; a token's two experts differ.
All inputs are finite; a program needn't handle non-finite values.
Results may differ from the reference program's by a relative error of at most 0.025.
Values may be sent and summed in bfloat16 or wider, within the bound.
A program may use at most 256 MiB of HBM per device.

```python
import math
import jax
import jax.numpy as jnp
import numpy as np
from jax import lax

D = 768
HEADS = 12
HEAD_DIM = 64
FF = 2048
SFF = 2048
EXPERTS = 16
TOP = 2
TOK_DEV = 128
SEQ = 2048
SLOTS = 2
CAP = 22


def draw_lengths(key, part):
    key = jax.random.fold_in(key, 17)
    pick_key, span_key = jax.random.split(key)
    full_slot = jax.random.randint(pick_key, (), 0, SLOTS)
    drawn_spans = jax.random.randint(span_key, (SLOTS,), SEQ // 4, SEQ + 1)
    return jnp.where(jnp.arange(SLOTS) == full_slot, SEQ, drawn_spans).astype(jnp.int32)


def block_scale(stream_key, extent, shards, low, top_value):
    gain, own = 1.0, jax.random.fold_in(stream_key, 6)
    for dim, parts in shards:
        draws = jnp.exp(jax.random.uniform(jax.random.fold_in(own, dim), (parts,), jnp.float32, low / len(shards), top_value / len(shards)))
        gain = gain * jnp.repeat(draws, extent[dim] // parts).reshape([-1 if axis == dim else 1 for axis in range(len(extent))])
    return gain


def assign_block(rng, own, number, rows, amount, top, most, lean):
    sequence = jax.random.permutation(rng, amount)
    heavy_load, usual = load_shares(amount, rows * top, most, lean, True), load_shares(amount, rows * top, most, lean, False)
    places = jnp.arange(amount)

    def named(tallies, rotation):
        used = int((tallies > 0).sum())
        fixed = max(1, used // 4)
        passed = fixed + (places - fixed + rotation * (used - fixed)) % max(1, amount - fixed)
        return jnp.zeros((amount,), jnp.int32).at[sequence[jnp.where(places < fixed, places, passed)]].set(jnp.asarray(tallies, jnp.int32))

    tallies = jnp.where(number % 4 == 0, named(heavy_load, number // 4), named(usual, number - number // 4 - 1))
    mixed = jax.random.permutation(jax.random.fold_in(own, 3), amount)
    giver, taker = mixed[0:amount // 2 * 2:2], mixed[1:amount // 2 * 2:2]
    room = jnp.minimum(tallies[giver] - 1, most - tallies[taker]) // 2
    room = jnp.where((giver == sequence[0]) | (taker == sequence[0]) | (tallies[taker] == 0), 0, jnp.maximum(room, 0))
    passed = jax.random.randint(jax.random.fold_in(own, 4), (amount // 2,), 0, 1 << 20) % (room + 1)
    tallies = tallies.at[giver].add(-passed).at[taker].add(passed)
    labels = jnp.searchsorted(jnp.cumsum(tallies), jnp.arange(rows * top), side="right").astype(jnp.int32)
    grid = labels.reshape(top, rows).T
    grid = grid[jax.random.permutation(jax.random.fold_in(own, 1), rows)]
    rotation = jax.random.randint(jax.random.fold_in(own, 2), (rows, 1), 0, top)
    return jnp.take_along_axis(grid, (jnp.arange(top)[None, :] + rotation) % top, axis=1)


def load_shares(number_of, total, most, lean, full):
    weights = [(1 << 20) // math.isqrt(grade ** lean) + 1 for grade in range(1, number_of + 1)]
    largest = most if full else min(most, max(-(-total // number_of), total * weights[0] // sum(weights)))
    least = 1 if total - largest >= number_of - 1 else 0
    given, surplus = [largest] + [least] * (number_of - 1), total - largest - least * (number_of - 1)
    while surplus > 0:
        movable = [i for i in range(1, number_of) if given[i] < largest] or [i for i in range(1, number_of) if given[i] < most]
        mass, remaining = sum([weights[i] for i in movable]), surplus
        for i in movable:
            extra = min(most - given[i], max(1, remaining * weights[i] // mass), surplus)
            given[i] = given[i] + extra
            surplus = surplus - extra
    return np.array(given)


def normal_values(stream_key, extent, spread, limit, cuts=(), kind=jnp.bfloat16):
    values = jax.random.normal(stream_key, extent, jnp.float32) * spread
    if len(cuts) > 0:
        values = block_scale(stream_key, extent, cuts, -0.22, 0.18) * values
    return jnp.clip(values, min=-limit, max=limit).astype(kind)


def setup_inputs(seed: int = 0) -> dict:
    key_list = jax.random.split(jax.random.key(seed), 18)
    tokens = normal_values(key_list[0], (SLOTS, SEQ, D), 1.0, 6.0, ((0, 2), (1, 16)))
    lengths = draw_lengths(jax.random.fold_in(key_list[17], 71), 0)
    routes_keys = jax.random.split(jax.random.fold_in(key_list[2], 1), SLOTS * SEQ // TOK_DEV)
    routes_turns = jax.random.permutation(jax.random.fold_in(key_list[2], 3), SLOTS * SEQ // TOK_DEV)
    routes = jax.vmap(lambda own, number: assign_block(jax.random.fold_in(key_list[2], 2), own, number, TOK_DEV, EXPERTS, TOP, CAP, 1))(routes_keys, routes_turns).reshape((SLOTS, SEQ, TOP))
    norm1_gain = jnp.clip(1.0 + 0.1 * jax.random.normal(key_list[3], (D,), jnp.float32), 0.5, 1.5)
    query_weight = normal_values(key_list[4], (D, D), D ** -0.5, 0.21875)
    key_weight = normal_values(key_list[5], (D, D), D ** -0.5, 0.21875)
    value_weight = normal_values(key_list[6], (D, D), D ** -0.5, 0.21875)
    output_weight = normal_values(key_list[7], (D, D), 1.0, 6.0)
    norm2_gain = jnp.clip(1.0 + 0.1 * jax.random.normal(key_list[8], (D,), jnp.float32), 0.5, 1.5)
    router_weight = normal_values(key_list[9], (D, EXPERTS), D ** -0.5, 0.21875)
    expert_gate = normal_values(key_list[10], (EXPERTS, D, FF), D ** -0.5, 0.21875, ((0, 4),))
    expert_up = normal_values(key_list[11], (EXPERTS, D, FF), D ** -0.5, 0.21875, ((0, 4),))
    expert_down = normal_values(key_list[12], (EXPERTS, FF, D), FF ** -0.5, 0.125, ((0, 4),))
    shared_gate = normal_values(key_list[13], (D, SFF), D ** -0.5, 0.21875)
    shared_up = normal_values(key_list[14], (D, SFF), D ** -0.5, 0.21875)
    shared_down = normal_values(key_list[15], (SFF, D), SFF ** -0.5, 0.125)
    cotangent = normal_values(key_list[16], (SLOTS, SEQ, D), 1.0, 6.0, ((0, 2), (1, 16)))
    return {"tokens": tokens, "lengths": lengths, "routes": routes, "norm1_gain": norm1_gain, "query_weight": query_weight, "key_weight": key_weight, "value_weight": value_weight, "output_weight": output_weight, "norm2_gain": norm2_gain, "router_weight": router_weight, "expert_gate": expert_gate, "expert_up": expert_up, "expert_down": expert_down, "shared_gate": shared_gate, "shared_up": shared_up, "shared_down": shared_down, "cotangent": cotangent}


@jax.custom_vjp
def low(v):
    return lax.optimization_barrier(v.astype(jnp.bfloat16)).astype(jnp.float32)

@jax.custom_vjp
def low_back(v):
    return v

def low_keep(v):
    return (low(v), None)

def low_pass(kept, grad):
    return (grad,)

def back_keep(v):
    return (v, None)

def back_low(kept, grad):
    return (low(grad),)
low.defvjp(low_keep, low_pass)
low_back.defvjp(back_keep, back_low)
highest = lax.Precision.HIGHEST
norm_epsilon = 1e-06
rope_base = 10000.0
score_scale = 0.125
masked_value = -1e+30

def rms_norm(values, gain_vector):
    scale_rows = lax.rsqrt(lax.optimization_barrier(jnp.mean(values * values, axis=-1, keepdims=True)) + norm_epsilon)
    return values * scale_rows * gain_vector

def rotate(values, positions):
    half_dim = values.shape[-1] // 2
    exponent = jnp.arange(half_dim, dtype=jnp.float32) * (2.0 / values.shape[-1])
    inverse_freq = rope_base ** (-exponent)
    angles = positions[:, None] * inverse_freq[None, :]
    cosine = jnp.cos(angles)[:, None, :]
    sine = jnp.sin(angles)[:, None, :]
    first_half = values[..., :half_dim]
    second_half = values[..., half_dim:]
    return jnp.concatenate([first_half * cosine - second_half * sine, second_half * cosine + first_half * sine], axis=-1)

def gated_unit(gate_lin, up_lin):
    return jax.nn.silu(gate_lin) * up_lin

def pair_softmax(chosen):
    shifted = chosen - lax.optimization_barrier(jnp.max(chosen, axis=-1, keepdims=True))
    exponentials = jnp.exp(shifted)
    return exponentials / lax.optimization_barrier(jnp.sum(exponentials, axis=-1, keepdims=True))

def attend(query, key_rows, value_rows, length):
    seq_rows = query.shape[0]
    block_rows = min(512, seq_rows)
    key_pos = jnp.arange(seq_rows, dtype=jnp.int32)
    key_live = key_pos < length

    def query_block(offset):
        block_query = lax.dynamic_slice_in_dim(query, offset.astype(jnp.int32), block_rows, 0)
        scores = jnp.einsum('qhd,khd->hqk', block_query, key_rows, precision=highest)
        scores = low_back(scores * score_scale)
        rows_pos = offset + jnp.arange(block_rows, dtype=jnp.int32)
        allowed = (key_pos[None, :] <= rows_pos[:, None]) & key_live[None, :]
        scores = jnp.where(allowed[None], scores, masked_value)
        shifted = scores - lax.optimization_barrier(jnp.max(scores, axis=-1, keepdims=True))
        exponentials = jnp.exp(shifted)
        weights = low(exponentials / lax.optimization_barrier(jnp.sum(exponentials, axis=-1, keepdims=True)))
        return jnp.einsum('hqk,khd->qhd', weights, value_rows, precision=highest)
    offsets = jnp.arange(seq_rows // block_rows, dtype=jnp.int32) * block_rows
    blocks = lax.map(jax.checkpoint(query_block), offsets)
    return blocks.reshape(seq_rows, query.shape[1], query.shape[2])

def expert_mix(normed, router, expert_gate, expert_up, expert_down, routes, valid_rows):
    model_width = normed.shape[-1]
    logits = low_back(jnp.einsum('std,de->ste', normed, router, precision=highest))
    chosen = jnp.take_along_axis(logits, routes, axis=-1)
    gate_weights = pair_softmax(chosen)
    block_count = SEQ // TOK_DEV
    live_pairs = jnp.broadcast_to(valid_rows[:, :, None] > 0, routes.shape)
    expert_hits = ((routes[..., None] == jnp.arange(EXPERTS, dtype=jnp.int32)) & live_pairs[..., None]).astype(jnp.int32)
    expert_hits = expert_hits.reshape(SLOTS, block_count, TOK_DEV * TOP, EXPERTS)
    places = lax.optimization_barrier(jnp.sum((jnp.cumsum(expert_hits, axis=2) - 1) * expert_hits, axis=-1))
    block_ids = (jnp.arange(SLOTS, dtype=jnp.int32)[:, None] * block_count + jnp.arange(block_count, dtype=jnp.int32)[None, :])[:, :, None]
    rows_total = SLOTS * block_count * CAP
    flat_index = routes.reshape(SLOTS, block_count, TOK_DEV * TOP) * rows_total + block_ids * CAP + places
    flat_index = jnp.where(live_pairs.reshape(flat_index.shape), flat_index, EXPERTS * rows_total).reshape(-1).astype(jnp.int32)
    pair_rows = jnp.broadcast_to(normed[:, :, None, :], routes.shape + (model_width,)).reshape(-1, model_width)
    table = jnp.zeros((EXPERTS * rows_total + 1, model_width), jnp.float32).at[flat_index].add(pair_rows)
    expert_input = low_back(table[:-1].reshape(EXPERTS, rows_total, model_width))
    gate_lin = low_back(jnp.einsum('erd,edf->erf', expert_input, expert_gate, precision=highest))
    up_lin = low_back(jnp.einsum('erd,edf->erf', expert_input, expert_up, precision=highest))
    hidden = low(gated_unit(gate_lin, up_lin))
    expert_output = low(low_back(jnp.einsum('erf,efd->erd', hidden, expert_down, precision=highest)))
    padded_out = jnp.concatenate([expert_output.reshape(-1, model_width), jnp.zeros((1, model_width), jnp.float32)], axis=0)
    per_choice = padded_out[flat_index].reshape(routes.shape + (model_width,))
    return lax.optimization_barrier(jnp.sum(gate_weights[..., None] * per_choice, axis=2))

def reference(tokens, lengths, routes, norm1_gain, query_weight, key_weight, value_weight, output_weight, norm2_gain, router_weight, expert_gate, expert_up, expert_down, shared_gate, shared_up, shared_down, cotangent):
    positions = jnp.arange(SEQ, dtype=jnp.int32)
    valid_rows = (positions[None, :] < lengths[:, None]).astype(jnp.float32)
    angle_pos = positions.astype(jnp.float32)

    def forward_layer(inputs, gain_one, w_query, w_key, w_value, w_output, gain_two, w_router, e_gate, e_up, e_down, s_gate, s_up, s_down):
        normed = low(rms_norm(inputs, gain_one))
        split_shape = (SLOTS, SEQ, HEADS, HEAD_DIM)
        query_lin = low_back(jnp.einsum('std,de->ste', normed, w_query, precision=highest))
        key_lin = low_back(jnp.einsum('std,de->ste', normed, w_key, precision=highest))
        value_lin = low_back(jnp.einsum('std,de->ste', normed, w_value, precision=highest))
        query = low(rotate(query_lin.reshape(split_shape), angle_pos))
        key_all = low(rotate(key_lin.reshape(split_shape), angle_pos))
        value_all = low(value_lin).reshape(split_shape)
        attended_all = jnp.stack([attend(query[slot_index], key_all[slot_index], value_all[slot_index], lengths[slot_index]) for slot_index in range(SLOTS)])
        attended = low(low_back(attended_all.reshape(SLOTS, SEQ, HEADS * HEAD_DIM)))
        attn_out = low_back(jnp.einsum('ste,ed->std', attended, w_output, precision=highest))
        hidden_in = inputs + valid_rows[..., None] * attn_out
        normed_two = low(rms_norm(hidden_in, gain_two))
        mixed = expert_mix(normed_two, w_router, e_gate, e_up, e_down, routes, valid_rows)
        shared_gate_lin = low_back(jnp.einsum('std,df->stf', normed_two, s_gate, precision=highest))
        shared_up_lin = low_back(jnp.einsum('std,df->stf', normed_two, s_up, precision=highest))
        shared_hidden = low(gated_unit(shared_gate_lin, shared_up_lin))
        shared_out = jnp.einsum('stf,fd->std', shared_hidden, s_down, precision=highest)
        return hidden_in + valid_rows[..., None] * (mixed + shared_out)
    result, pullback = jax.vjp(forward_layer, tokens.astype(jnp.float32), norm1_gain.astype(jnp.float32), query_weight.astype(jnp.float32), key_weight.astype(jnp.float32), value_weight.astype(jnp.float32), output_weight.astype(jnp.float32), norm2_gain.astype(jnp.float32), router_weight.astype(jnp.float32), expert_gate.astype(jnp.float32), expert_up.astype(jnp.float32), expert_down.astype(jnp.float32), shared_gate.astype(jnp.float32), shared_up.astype(jnp.float32), shared_down.astype(jnp.float32))
    grads = pullback(cotangent.astype(jnp.float32))
    return (result.astype(jnp.bfloat16), grads[0].astype(jnp.bfloat16), grads[1], grads[2], grads[3], grads[4], grads[5], grads[6], grads[7], grads[8], grads[9], grads[10], grads[11], grads[12], grads[13])
```

```python
import functools

import jax
import jax.numpy as jnp
from jax import lax
from jax.experimental import pallas as pl
from jax.experimental.pallas import tpu as pltpu
from jax.sharding import PartitionSpec as P

HEAD_DIM = 64
EXPERTS = 16
TOP = 2
CAP = 22
PLACES = 24

norm_epsilon = 1e-06
rope_base = 10000.0
score_scale = 0.125
masked_value = -1e30
PLANE = ("dp", "ctx")
SLOT = ("ctx", "expert")
bf16 = jnp.bfloat16
f32 = jnp.float32


def rms_scale(values):
    return lax.rsqrt(jnp.mean(values * values, axis=-1, keepdims=True) + norm_epsilon)


def rms_back(normal, scale, gain, upstream):
    lifted = upstream * gain
    return scale * (lifted - normal * jnp.mean(lifted * normal, axis=-1, keepdims=True))


def rope_tables(positions):
    half = HEAD_DIM // 2
    exponent = jnp.arange(half, dtype=f32) * (2.0 / HEAD_DIM)
    inverse_freq = rope_base ** (-exponent)
    angles = inverse_freq[:, None] * positions[None, :].astype(f32)
    return jnp.cos(angles), jnp.sin(angles)


def head_rows(qkv_ref, first, count):
    return jnp.concatenate(
        [qkv_ref[block, first : first + count, :] for block in range(qkv_ref.shape[0])], axis=1
    )


def live_keys(key_t, length):
    span = key_t.shape[1]
    place = lax.broadcasted_iota(jnp.int32, (8, span), 1)
    row = lax.broadcasted_iota(jnp.int32, (8, span), 0)
    bias = jnp.where((place >= length) & (row == 0), masked_value, 0.0)
    padded = jnp.concatenate(
        [key_t.astype(f32), bias, jnp.zeros((HEAD_DIM - 8, span), f32)], axis=0
    )
    return jnp.transpose(padded).astype(bf16)


def scaled_queries(query_t):
    span = query_t.shape[1]
    row = lax.broadcasted_iota(jnp.int32, (HEAD_DIM, span), 0)
    ones = jnp.where(row == 0, 1.0, 0.0)
    return jnp.concatenate([query_t.astype(f32) * score_scale, ones], axis=0).astype(bf16)


def causal(scores):
    key = lax.broadcasted_iota(jnp.int32, scores.shape, 0)
    query = lax.broadcasted_iota(jnp.int32, scores.shape, 1)
    return jnp.where(key <= query, scores, masked_value)


def attend_kernel(step, length_ref, qkv_ref, out_ref, total_ref, key_ref, query_ref, value_ref):
    span = qkv_ref.shape[0] * qkv_ref.shape[2]
    key_ref[...] = live_keys(head_rows(qkv_ref, HEAD_DIM, HEAD_DIM), length_ref[0])
    query_ref[...] = scaled_queries(head_rows(qkv_ref, 0, HEAD_DIM))
    value_ref[...] = head_rows(qkv_ref, 2 * HEAD_DIM, HEAD_DIM)

    def query_block(q, carry):
        here = pl.ds(pl.multiple_of(q * step, step), step)
        query = query_ref[:, here]

        def absorb(k, state, masked):
            top, total, out = state
            there = pl.ds(pl.multiple_of(k * step, step), step)
            scores = jnp.dot(key_ref[there, :], query, preferred_element_type=f32)
            if masked:
                scores = causal(scores)
            new_top = jnp.maximum(top, jnp.max(scores, axis=0, keepdims=True))
            shrink = jnp.exp(top - new_top)
            weights = jnp.exp(scores - new_top)
            total = total * shrink + jnp.sum(weights, axis=0, keepdims=True)
            out = out * shrink + jnp.dot(
                value_ref[:, there], weights.astype(bf16), preferred_element_type=f32
            )
            return new_top, total, out

        state = (
            jnp.full((1, step), masked_value, f32),
            jnp.zeros((1, step), f32),
            jnp.zeros((HEAD_DIM, step), f32),
        )
        state = absorb(q, state, True)
        top, total, out = lax.fori_loop(0, q, lambda k, s: absorb(k, s, False), state)
        out_ref[:, here] = out / total
        total_ref[:, here] = top + jnp.log(total)
        return carry

    lax.fori_loop(0, span // step, query_block, 0)


def attend(qkv, length):
    blocks, _, rows = qkv.shape
    span = blocks * rows
    step = min(512, span)
    return pl.pallas_call(
        functools.partial(attend_kernel, step),
        out_shape=(
            jax.ShapeDtypeStruct((HEAD_DIM, span), f32),
            jax.ShapeDtypeStruct((1, span), f32),
        ),
        in_specs=[
            pl.BlockSpec(memory_space=pltpu.SMEM),
            pl.BlockSpec(memory_space=pltpu.VMEM),
        ],
        out_specs=(pl.BlockSpec(memory_space=pltpu.VMEM),) * 2,
        scratch_shapes=[
            pltpu.VMEM((span, 2 * HEAD_DIM), bf16),
            pltpu.VMEM((2 * HEAD_DIM, span), bf16),
            pltpu.VMEM((HEAD_DIM, span), bf16),
        ],
        compiler_params=pltpu.CompilerParams(vmem_limit_bytes=48 << 20),
    )(length, qkv)


def unrotate(grad_t, cosine, sine):
    half = HEAD_DIM // 2
    first, second = grad_t[:half], grad_t[half:]
    return jnp.concatenate(
        [first * cosine + second * sine, second * cosine - first * sine], axis=0
    )


def attend_back_kernel(
    step,
    length_ref,
    qkv_ref,
    out_ref,
    total_ref,
    upstream_ref,
    cosine_ref,
    sine_ref,
    grad_ref,
    key_ref,
    query_ref,
    value_ref,
    key_t_ref,
    query_sum,
    key_sum,
    value_sum,
    delta_ref,
    up_ref,
):
    blocks, _, rows = qkv_ref.shape
    span = blocks * rows
    key_t = head_rows(qkv_ref, HEAD_DIM, HEAD_DIM)
    key_ref[...] = live_keys(key_t, length_ref[0])
    key_t_ref[...] = key_t
    query_ref[...] = scaled_queries(head_rows(qkv_ref, 0, HEAD_DIM))
    value_t = head_rows(qkv_ref, 2 * HEAD_DIM, HEAD_DIM)
    value_ref[...] = jnp.transpose(value_t.astype(f32)).astype(bf16)
    upstream = head_rows(upstream_ref, 0, HEAD_DIM)
    up_ref[...] = upstream
    delta_ref[...] = jnp.sum(upstream.astype(f32) * out_ref[...], axis=0, keepdims=True)
    query_sum[...] = jnp.zeros_like(query_sum)

    def key_block(k, carry):
        there = pl.ds(pl.multiple_of(k * step, step), step)
        key, value, key_flat = key_ref[there, :], value_ref[there, :], key_t_ref[:, there]

        def meet(q, sums, masked):
            key_add, value_add = sums
            here = pl.ds(pl.multiple_of(q * step, step), step)
            query, up = query_ref[:, here], up_ref[:, here]
            scores = jnp.dot(key, query, preferred_element_type=f32)
            if masked:
                scores = causal(scores)
            probs = jnp.exp(scores - total_ref[:, here])
            d_probs = jnp.dot(value, up, preferred_element_type=f32)
            d_scores = (probs * (d_probs - delta_ref[:, here])).astype(bf16)
            query_sum[:, here] += jnp.dot(key_flat, d_scores, preferred_element_type=f32)
            contract = (((1,), (1,)), ((), ()))
            key_add = key_add + lax.dot_general(
                query[:HEAD_DIM], d_scores, contract, preferred_element_type=f32
            )
            value_add = value_add + lax.dot_general(
                up, probs.astype(bf16), contract, preferred_element_type=f32
            )
            return key_add, value_add

        zero = jnp.zeros((HEAD_DIM, step), f32)
        sums = meet(k, (zero, zero), True)
        key_add, value_add = lax.fori_loop(
            k + 1, span // step, lambda q, s: meet(q, s, False), sums
        )
        key_sum[:, there] = key_add
        value_sum[:, there] = value_add
        return carry

    lax.fori_loop(0, span // step, key_block, 0)
    cosine, sine = cosine_ref[...], sine_ref[...]
    d_query = unrotate(query_sum[...] * score_scale, cosine, sine).astype(bf16)
    d_key = unrotate(key_sum[...], cosine, sine).astype(bf16)
    d_value = value_sum[...].astype(bf16)
    for block in range(blocks):
        at = slice(block * rows, (block + 1) * rows)
        grad_ref[block, :HEAD_DIM, :] = d_query[:, at]
        grad_ref[block, HEAD_DIM : 2 * HEAD_DIM, :] = d_key[:, at]
        grad_ref[block, 2 * HEAD_DIM :, :] = d_value[:, at]


def attend_back(qkv, length, out, total, upstream, cosine, sine):
    blocks, _, rows = qkv.shape
    span = blocks * rows
    step = min(512, span)
    return pl.pallas_call(
        functools.partial(attend_back_kernel, step),
        out_shape=jax.ShapeDtypeStruct(qkv.shape, bf16),
        in_specs=[pl.BlockSpec(memory_space=pltpu.SMEM)]
        + [pl.BlockSpec(memory_space=pltpu.VMEM)] * 6,
        out_specs=pl.BlockSpec(memory_space=pltpu.VMEM),
        scratch_shapes=[
            pltpu.VMEM((span, 2 * HEAD_DIM), bf16),
            pltpu.VMEM((2 * HEAD_DIM, span), bf16),
            pltpu.VMEM((span, HEAD_DIM), bf16),
            pltpu.VMEM((HEAD_DIM, span), bf16),
            pltpu.VMEM((HEAD_DIM, span), f32),
            pltpu.VMEM((HEAD_DIM, span), f32),
            pltpu.VMEM((HEAD_DIM, span), f32),
            pltpu.VMEM((1, span), f32),
            pltpu.VMEM((HEAD_DIM, span), bf16),
        ],
        compiler_params=pltpu.CompilerParams(vmem_limit_bytes=56 << 20),
    )(length, qkv, out, total, upstream, cosine, sine)


def local(
    tokens,
    lengths,
    routes,
    norm1_gain,
    query_weight,
    key_weight,
    value_weight,
    output_weight,
    norm2_gain,
    router_weight,
    expert_gate,
    expert_up,
    expert_down,
    shared_gate,
    shared_up,
    shared_down,
    cotangent,
):
    dp_size, ctx_size, expert_size = (lax.axis_size(a) for a in ("dp", "ctx", "expert"))
    plane_size, slot_size = dp_size * ctx_size, ctx_size * expert_size
    rows, width = tokens.shape[1:]
    heads = width // HEAD_DIM
    own = EXPERTS // expert_size
    hidden_width = expert_gate.shape[2]
    part = hidden_width // plane_size
    plane = lax.axis_index("dp") * ctx_size + lax.axis_index("ctx")
    first_row = (lax.axis_index("ctx") * expert_size + lax.axis_index("expert")) * rows
    positions = first_row + jnp.arange(rows, dtype=jnp.int32)
    length = lengths[0]
    live_rows = positions < length
    valid = live_rows.astype(f32)[:, None]
    inputs = tokens[0].astype(f32)
    upstream = cotangent[0].astype(f32)
    d_branch = valid * upstream
    d_branch_low = d_branch.astype(bf16)

    route_ids = routes[0]
    expert_range = jnp.arange(EXPERTS, dtype=jnp.int32)
    picked = (route_ids[:, :, None] == expert_range).astype(f32)
    expert_hits = (
        ((route_ids[:, :, None] == expert_range) & live_rows[:, None, None])
        .astype(jnp.int32)
        .reshape(rows * TOP, EXPERTS)
    )
    places = jnp.sum((jnp.cumsum(expert_hits, axis=0) - 1) * expert_hits, axis=-1)
    live_pairs = jnp.broadcast_to(live_rows[:, None], (rows, TOP)).reshape(-1)
    slot_ids = jnp.where(live_pairs, route_ids.reshape(-1) * PLACES + places, -1)
    dispatch = (
        slot_ids[:, None] == jnp.arange(EXPERTS * PLACES, dtype=jnp.int32)[None, :]
    ).reshape(rows, TOP, EXPERTS * PLACES)
    either = jnp.any(dispatch, axis=1).astype(bf16)

    def to_experts(flat):
        return lax.all_to_all(
            flat.reshape((expert_size, -1) + flat.shape[1:]), "expert", 0, 0
        )

    def spread(flat):
        placed = jnp.einsum("ts,td->sd", either, flat, preferred_element_type=f32).astype(bf16)
        mine = to_experts(placed).reshape(-1, width)
        return lax.all_gather(jnp.concatenate([mine, flat], axis=0), PLANE, axis=0)

    up_all = spread(d_branch_low)

    scale_one = rms_scale(inputs)
    normal_one = inputs * scale_one
    normed_low = (normal_one * norm1_gain).astype(bf16)
    normed_all = lax.all_gather(normed_low, SLOT, axis=0, tiled=True)
    cosine, sine = rope_tables(positions)

    def project(weight):
        lin = jnp.dot(normed_low, weight, preferred_element_type=f32)
        return jnp.transpose(lin).reshape(heads, HEAD_DIM, rows)

    def rotated(lin_t):
        half = HEAD_DIM // 2
        first, second = lin_t[:, :half], lin_t[:, half:]
        return jnp.concatenate(
            [first * cosine - second * sine, second * cosine + first * sine], axis=1
        )

    query = rotated(project(query_weight)).astype(bf16)
    key = rotated(project(key_weight)).astype(bf16)
    value = project(value_weight).astype(bf16)

    def to_heads(blocks):
        spare = jnp.zeros((slot_size - heads,) + blocks.shape[1:], blocks.dtype)
        return lax.all_to_all(jnp.concatenate([blocks, spare], axis=0), SLOT, 0, 0)

    def from_heads(blocks):
        return lax.all_to_all(blocks, SLOT, 0, 0)[:heads]

    def by_block(flat_t):
        return jnp.transpose(flat_t.reshape(-1, slot_size, rows), (1, 0, 2))

    qkv = to_heads(jnp.concatenate([query, key, value], axis=1))
    out_t, log_total = attend(qkv, lengths)
    attended = jnp.transpose(
        from_heads(by_block(out_t.astype(bf16))).reshape(width, rows)
    )
    attn_out = jnp.dot(attended, output_weight, preferred_element_type=f32)
    hidden_in = inputs + valid * attn_out

    scale_two = rms_scale(hidden_in)
    normal_two = hidden_in * scale_two
    normed_two_low = (normal_two * norm2_gain).astype(bf16)
    logits = jnp.dot(normed_two_low, router_weight, preferred_element_type=f32)
    chosen = jnp.sum(picked * logits[:, None, :], axis=-1)
    shifted = jnp.exp(chosen - jnp.max(chosen, axis=-1, keepdims=True))
    gate_weights = shifted / jnp.sum(shifted, axis=-1, keepdims=True)

    in_all = spread(normed_two_low)
    gate_rows = jnp.sum(jnp.where(dispatch, gate_weights[:, :, None], 0.0), axis=(0, 1))
    gate_all = lax.all_gather(to_experts(gate_rows).reshape(-1), PLANE, axis=0)
    placed_rows = EXPERTS * PLACES

    def by_expert(both):
        cut = both[:, :placed_rows].reshape((plane_size * expert_size, own, PLACES) + both.shape[2:])
        return jnp.swapaxes(cut, 0, 1).reshape((own, -1) + both.shape[2:])

    def by_source(flat):
        cut = flat.reshape((own, plane_size * expert_size, PLACES) + flat.shape[2:])
        return jnp.swapaxes(cut, 0, 1).reshape((plane_size, placed_rows) + flat.shape[2:])

    def column(weight):
        return lax.dynamic_slice_in_dim(weight, plane * part, part, weight.ndim - 1)

    def row(weight):
        return lax.dynamic_slice_in_dim(weight, plane * part, part, weight.ndim - 2)

    def branch(rows_in, up, gate_w, up_w, down_w, weight):
        def dot(spec, a, b):
            return jnp.einsum(spec, a, b, preferred_element_type=f32)

        gate_lin, up_lin = dot("erd,edf->erf", rows_in, gate_w), dot("erd,edf->erf", rows_in, up_w)
        sigmoid = 1.0 / (1.0 + jnp.exp(-gate_lin))
        silu = gate_lin * sigmoid
        hidden = (silu * up_lin).astype(bf16)
        result = dot("erf,efd->erd", hidden, down_w)
        d_out = (weight * up.astype(f32)).astype(bf16)
        d_hidden = dot("erd,efd->erf", d_out, down_w)
        d_gate = (d_hidden * up_lin * (sigmoid + silu * (1.0 - sigmoid))).astype(bf16)
        d_up = (d_hidden * silu).astype(bf16)
        d_in = dot("erf,edf->erd", d_gate, gate_w) + dot("erf,edf->erd", d_up, up_w)
        grads = (
            dot("erd,erf->edf", rows_in, d_gate),
            dot("erd,erf->edf", rows_in, d_up),
            dot("erf,erd->efd", hidden, d_out),
        )
        return result, d_in, grads

    gate_factor = by_expert(gate_all)[:, :, None]
    up_rows = by_expert(up_all)
    result, d_rows, expert_grads = branch(
        by_expert(in_all), up_rows, column(expert_gate), column(expert_up), row(expert_down),
        gate_factor,
    )
    d_gate_part = by_source(jnp.sum(result * up_rows.astype(f32), axis=-1))
    shared_result, shared_d, shared_grads = branch(
        in_all[:, placed_rows:].reshape(1, -1, width),
        up_all[:, placed_rows:].reshape(1, -1, width),
        column(shared_gate)[None],
        column(shared_up)[None],
        row(shared_down)[None],
        1.0,
    )

    def home(expert_part, shared_part):
        both = jnp.concatenate(
            [by_source(expert_part), shared_part.reshape(plane_size, rows, width)], axis=1
        ).astype(bf16)
        both = lax.psum_scatter(both, "dp", scatter_dimension=0, tiled=True)
        both = lax.psum_scatter(both, "ctx", scatter_dimension=0, tiled=True)[0]
        back = to_experts(both[:placed_rows]).reshape(placed_rows, width)
        spread_rows = jnp.dot(either, back, preferred_element_type=f32)
        return spread_rows + both[placed_rows:].astype(f32)

    d_gate_rows = lax.psum_scatter(d_gate_part, PLANE, scatter_dimension=0, tiled=True)[0]
    d_gate_rows = to_experts(d_gate_rows).reshape(-1)
    d_gates = jnp.sum(jnp.where(dispatch, d_gate_rows, 0.0), axis=-1)
    d_chosen = gate_weights * (
        d_gates - jnp.sum(gate_weights * d_gates, axis=-1, keepdims=True)
    )
    d_logits = jnp.sum(picked * d_chosen[:, :, None], axis=1).astype(bf16)
    d_router = jnp.einsum("td,te->de", normed_two_low, d_logits, preferred_element_type=f32)
    d_normed_two = home(d_rows, shared_d) + jnp.einsum(
        "te,de->td", d_logits, router_weight, preferred_element_type=f32
    )
    output_rows = hidden_in + valid * home(result * gate_factor, shared_result)
    output_rows = output_rows.astype(bf16)[None]
    d_gain_two = jnp.sum(d_normed_two * normal_two, axis=0)
    d_hidden_in = upstream + rms_back(normal_two, scale_two, norm2_gain, d_normed_two)

    d_attn_low = (valid * d_hidden_in).astype(bf16)
    d_output_weight = jnp.einsum("td,te->de", attended, d_attn_low, preferred_element_type=f32)
    d_attended = jnp.einsum("te,de->dt", d_attn_low, output_weight, preferred_element_type=f32)
    d_attended = to_heads(d_attended.astype(bf16).reshape(heads, HEAD_DIM, rows))
    all_cosine, all_sine = rope_tables(jnp.arange(slot_size * rows, dtype=jnp.int32))
    d_qkv = attend_back(qkv, lengths, out_t, log_total, d_attended, all_cosine, all_sine)
    head_grad = jnp.einsum(
        "bet,btd->ed", d_qkv, normed_all.reshape(slot_size, rows, width), preferred_element_type=f32
    )
    d_own = jnp.swapaxes(from_heads(d_qkv).reshape(heads, 3, HEAD_DIM, rows), 0, 1)
    d_own = d_own.reshape(3, width, rows)
    d_normed = jnp.zeros((width, rows), f32)
    for weight, grad in zip((query_weight, key_weight, value_weight), d_own):
        d_normed = d_normed + jnp.dot(weight, grad, preferred_element_type=f32)
    d_normed = jnp.transpose(d_normed)
    d_gain_one = jnp.sum(d_normed * normal_one, axis=0)
    input_grad = d_hidden_in + rms_back(normal_one, scale_one, norm1_gain, d_normed)
    input_grad = input_grad.astype(bf16)[None]

    shard = width // (dp_size * slot_size)
    head_grad = jnp.transpose(head_grad).reshape(-1, 3 * HEAD_DIM)
    head_grad = lax.psum_scatter(head_grad, "dp", scatter_dimension=0, tiled=True)
    head_grad = lax.all_to_all(head_grad.reshape(slot_size, shard, 3 * HEAD_DIM), SLOT, 0, 0)
    head_grad = jnp.transpose(
        head_grad[:heads].reshape(heads, shard, 3, HEAD_DIM), (2, 1, 0, 3)
    ).reshape(3, shard, width)

    def scatter(grad):
        for axis in ("dp", "ctx", "expert"):
            grad = lax.psum_scatter(grad, axis, scatter_dimension=0, tiled=True)
        return grad

    output_grad = scatter(d_output_weight.astype(bf16)).astype(f32)
    small = lax.psum(
        jnp.concatenate([d_router, d_gain_one[:, None], d_gain_two[:, None]], axis=1),
        ("dp", "ctx", "expert"),
    )
    linear = plane * expert_size + lax.axis_index("expert")
    small = lax.dynamic_slice_in_dim(small, linear * shard, shard, 0)

    def shared_columns(grad):
        grad = grad[0].reshape(plane_size, expert_size, shard, part).astype(bf16)
        grad = lax.psum_scatter(grad, "expert", scatter_dimension=1, tiled=True)[:, 0]
        grad = lax.all_to_all(grad, PLANE, 0, 0)
        return jnp.swapaxes(grad, 0, 1).reshape(shard, hidden_width).astype(f32)

    shared_down_grad = lax.psum_scatter(
        shared_grads[2][0].astype(bf16), "expert", scatter_dimension=0, tiled=True
    ).astype(f32)
    return (
        output_rows,
        input_grad,
        small[:, EXPERTS],
        head_grad[0],
        head_grad[1],
        head_grad[2],
        output_grad,
        small[:, EXPERTS + 1],
        small[:, :EXPERTS],
        expert_grads[0],
        expert_grads[1],
        expert_grads[2],
        shared_columns(shared_grads[0]),
        shared_columns(shared_grads[1]),
        shared_down_grad,
    )


def solution(mesh):
    tokens = P("dp", ("ctx", "expert"), None)
    whole = P()
    experts = P("expert", None, None)
    everywhere = ("dp", "ctx", "expert")
    return jax.shard_map(
        local,
        mesh=mesh,
        in_specs=(tokens, P("dp"), tokens)
        + (whole,) * 7
        + (experts,) * 3
        + (whole,) * 3
        + (tokens,),
        out_specs=(tokens, tokens, P(everywhere))
        + (P(everywhere, None),) * 4
        + (P(everywhere), P(everywhere, None))
        + (P("expert", None, PLANE),) * 2
        + (P("expert", PLANE, None),)
        + (P(everywhere, None),) * 3,
        check_vma=False,
    )
```

```python
import functools

import jax
import jax.numpy as jnp
from jax import lax
from jax.experimental import pallas as pl
from jax.experimental.pallas import tpu as pltpu
from jax.sharding import PartitionSpec as P

HEAD_DIM = 64
EXPERTS = 16
TOP = 2
CAP = 22
PLACES = 24

norm_epsilon = 1e-06
rope_base = 10000.0
score_scale = 0.125
masked_value = -1e30
PLANE = ("dp", "ctx")
SLOT = ("ctx", "expert")
bf16 = jnp.bfloat16
f32 = jnp.float32


def rms_scale(values):
    return lax.rsqrt(jnp.mean(values * values, axis=-1, keepdims=True) + norm_epsilon)


def rms_back(normal, scale, gain, upstream):
    lifted = upstream * gain
    return scale * (lifted - normal * jnp.mean(lifted * normal, axis=-1, keepdims=True))


def rope_tables(positions):
    half = HEAD_DIM // 2
    exponent = jnp.arange(half, dtype=f32) * (2.0 / HEAD_DIM)
    inverse_freq = rope_base ** (-exponent)
    angles = inverse_freq[:, None] * positions[None, :].astype(f32)
    return jnp.cos(angles), jnp.sin(angles)


def head_rows(qkv_ref, first, count):
    return jnp.concatenate(
        [qkv_ref[block, first : first + count, :] for block in range(qkv_ref.shape[0])], axis=1
    )


def live_keys(key_t, length):
    span = key_t.shape[1]
    place = lax.broadcasted_iota(jnp.int32, (8, span), 1)
    row = lax.broadcasted_iota(jnp.int32, (8, span), 0)
    bias = jnp.where((place >= length) & (row == 0), masked_value, 0.0)
    padded = jnp.concatenate(
        [key_t.astype(f32), bias, jnp.zeros((HEAD_DIM - 8, span), f32)], axis=0
    )
    return jnp.transpose(padded).astype(bf16)


def scaled_queries(query_t):
    span = query_t.shape[1]
    row = lax.broadcasted_iota(jnp.int32, (HEAD_DIM, span), 0)
    ones = jnp.where(row == 0, 1.0, 0.0)
    return jnp.concatenate([query_t.astype(f32) * score_scale, ones], axis=0).astype(bf16)


def causal(scores):
    key = lax.broadcasted_iota(jnp.int32, scores.shape, 0)
    query = lax.broadcasted_iota(jnp.int32, scores.shape, 1)
    return jnp.where(key <= query, scores, masked_value)


def attend_kernel(step, length_ref, qkv_ref, out_ref, total_ref, key_ref, query_ref, value_ref):
    span = qkv_ref.shape[0] * qkv_ref.shape[2]
    key_ref[...] = live_keys(head_rows(qkv_ref, HEAD_DIM, HEAD_DIM), length_ref[0])
    query_ref[...] = scaled_queries(head_rows(qkv_ref, 0, HEAD_DIM))
    value_ref[...] = head_rows(qkv_ref, 2 * HEAD_DIM, HEAD_DIM)

    def query_block(q, carry):
        here = pl.ds(pl.multiple_of(q * step, step), step)
        query = query_ref[:, here]

        def absorb(k, state, masked):
            top, total, out = state
            there = pl.ds(pl.multiple_of(k * step, step), step)
            scores = jnp.dot(key_ref[there, :], query, preferred_element_type=f32)
            if masked:
                scores = causal(scores)
            new_top = jnp.maximum(top, jnp.max(scores, axis=0, keepdims=True))
            shrink = jnp.exp(top - new_top)
            weights = jnp.exp(scores - new_top)
            total = total * shrink + jnp.sum(weights, axis=0, keepdims=True)
            out = out * shrink + jnp.dot(
                value_ref[:, there], weights.astype(bf16), preferred_element_type=f32
            )
            return new_top, total, out

        state = (
            jnp.full((1, step), masked_value, f32),
            jnp.zeros((1, step), f32),
            jnp.zeros((HEAD_DIM, step), f32),
        )
        state = absorb(q, state, True)
        top, total, out = lax.fori_loop(0, q, lambda k, s: absorb(k, s, False), state)
        out_ref[:, here] = out / total
        total_ref[:, here] = top + jnp.log(total)
        return carry

    lax.fori_loop(0, span // step, query_block, 0)


def attend(qkv, length):
    blocks, _, rows = qkv.shape
    span = blocks * rows
    step = min(512, span)
    return pl.pallas_call(
        functools.partial(attend_kernel, step),
        out_shape=(
            jax.ShapeDtypeStruct((HEAD_DIM, span), f32),
            jax.ShapeDtypeStruct((1, span), f32),
        ),
        in_specs=[
            pl.BlockSpec(memory_space=pltpu.SMEM),
            pl.BlockSpec(memory_space=pltpu.VMEM),
        ],
        out_specs=(pl.BlockSpec(memory_space=pltpu.VMEM),) * 2,
        scratch_shapes=[
            pltpu.VMEM((span, 2 * HEAD_DIM), bf16),
            pltpu.VMEM((2 * HEAD_DIM, span), bf16),
            pltpu.VMEM((HEAD_DIM, span), bf16),
        ],
        compiler_params=pltpu.CompilerParams(vmem_limit_bytes=48 << 20),
    )(length, qkv)


def unrotate(grad_t, cosine, sine):
    half = HEAD_DIM // 2
    first, second = grad_t[:half], grad_t[half:]
    return jnp.concatenate(
        [first * cosine + second * sine, second * cosine - first * sine], axis=0
    )


def attend_back_kernel(
    step,
    length_ref,
    qkv_ref,
    out_ref,
    total_ref,
    upstream_ref,
    cosine_ref,
    sine_ref,
    grad_ref,
    key_ref,
    query_ref,
    value_ref,
    key_t_ref,
    query_sum,
    key_sum,
    value_sum,
    delta_ref,
    up_ref,
):
    blocks, _, rows = qkv_ref.shape
    span = blocks * rows
    key_t = head_rows(qkv_ref, HEAD_DIM, HEAD_DIM)
    key_ref[...] = live_keys(key_t, length_ref[0])
    key_t_ref[...] = key_t
    query_ref[...] = scaled_queries(head_rows(qkv_ref, 0, HEAD_DIM))
    value_t = head_rows(qkv_ref, 2 * HEAD_DIM, HEAD_DIM)
    value_ref[...] = jnp.transpose(value_t.astype(f32)).astype(bf16)
    upstream = head_rows(upstream_ref, 0, HEAD_DIM)
    up_ref[...] = upstream
    delta_ref[...] = jnp.sum(upstream.astype(f32) * out_ref[...], axis=0, keepdims=True)
    query_sum[...] = jnp.zeros_like(query_sum)

    def key_block(k, carry):
        there = pl.ds(pl.multiple_of(k * step, step), step)
        key, value, key_flat = key_ref[there, :], value_ref[there, :], key_t_ref[:, there]

        def meet(q, sums, masked):
            key_add, value_add = sums
            here = pl.ds(pl.multiple_of(q * step, step), step)
            query, up = query_ref[:, here], up_ref[:, here]
            scores = jnp.dot(key, query, preferred_element_type=f32)
            if masked:
                scores = causal(scores)
            probs = jnp.exp(scores - total_ref[:, here])
            d_probs = jnp.dot(value, up, preferred_element_type=f32)
            d_scores = (probs * (d_probs - delta_ref[:, here])).astype(bf16)
            query_sum[:, here] += jnp.dot(key_flat, d_scores, preferred_element_type=f32)
            contract = (((1,), (1,)), ((), ()))
            key_add = key_add + lax.dot_general(
                query[:HEAD_DIM], d_scores, contract, preferred_element_type=f32
            )
            value_add = value_add + lax.dot_general(
                up, probs.astype(bf16), contract, preferred_element_type=f32
            )
            return key_add, value_add

        zero = jnp.zeros((HEAD_DIM, step), f32)
        sums = meet(k, (zero, zero), True)
        key_add, value_add = lax.fori_loop(
            k + 1, span // step, lambda q, s: meet(q, s, False), sums
        )
        key_sum[:, there] = key_add
        value_sum[:, there] = value_add
        return carry

    lax.fori_loop(0, span // step, key_block, 0)
    cosine, sine = cosine_ref[...], sine_ref[...]
    d_query = unrotate(query_sum[...] * score_scale, cosine, sine).astype(bf16)
    d_key = unrotate(key_sum[...], cosine, sine).astype(bf16)
    d_value = value_sum[...].astype(bf16)
    for block in range(blocks):
        at = slice(block * rows, (block + 1) * rows)
        grad_ref[block, :HEAD_DIM, :] = d_query[:, at]
        grad_ref[block, HEAD_DIM : 2 * HEAD_DIM, :] = d_key[:, at]
        grad_ref[block, 2 * HEAD_DIM :, :] = d_value[:, at]


def attend_back(qkv, length, out, total, upstream, cosine, sine):
    blocks, _, rows = qkv.shape
    span = blocks * rows
    step = min(512, span)
    return pl.pallas_call(
        functools.partial(attend_back_kernel, step),
        out_shape=jax.ShapeDtypeStruct(qkv.shape, bf16),
        in_specs=[pl.BlockSpec(memory_space=pltpu.SMEM)]
        + [pl.BlockSpec(memory_space=pltpu.VMEM)] * 6,
        out_specs=pl.BlockSpec(memory_space=pltpu.VMEM),
        scratch_shapes=[
            pltpu.VMEM((span, 2 * HEAD_DIM), bf16),
            pltpu.VMEM((2 * HEAD_DIM, span), bf16),
            pltpu.VMEM((span, HEAD_DIM), bf16),
            pltpu.VMEM((HEAD_DIM, span), bf16),
            pltpu.VMEM((HEAD_DIM, span), f32),
            pltpu.VMEM((HEAD_DIM, span), f32),
            pltpu.VMEM((HEAD_DIM, span), f32),
            pltpu.VMEM((1, span), f32),
            pltpu.VMEM((HEAD_DIM, span), bf16),
        ],
        compiler_params=pltpu.CompilerParams(vmem_limit_bytes=56 << 20),
    )(length, qkv, out, total, upstream, cosine, sine)


MESH = pl.DeviceIdType.MESH
ANY = pl.BlockSpec(memory_space=pl.ANY)
VMEM = pl.BlockSpec(memory_space=pltpu.VMEM)
DMA = pltpu.SemaphoreType.DMA


def head_place(head, heads, ctx_size, expert_size):
    per = expert_size - 1
    if ctx_size <= expert_size and ctx_size * per == heads:
        row = head // per
        step = head % per
        return row, step + jnp.where(step >= row, 1, 0)
    return head // expert_size, head % expert_size


def head_of(ctx, expert, heads, ctx_size, expert_size):
    per = expert_size - 1
    if ctx_size <= expert_size and ctx_size * per == heads:
        head = ctx * per + expert - jnp.where(expert > ctx, 1, 0)
        return jnp.where(expert == ctx, heads, head)
    return ctx * expert_size + expert


def greet(partners):
    barrier = pltpu.get_barrier_semaphore()
    for partner in partners:
        pl.semaphore_signal(barrier, inc=1, device_id=partner, device_id_type=MESH)
    pl.semaphore_wait(barrier, len(partners))


def trade_kernel(heads, inward, in_ref, out_ref, send_sem, recv_sem):
    ctx_size, expert_size = lax.axis_size("ctx"), lax.axis_size("expert")
    count = ctx_size * expert_size
    ctx, expert = lax.axis_index("ctx"), lax.axis_index("expert")
    me = ctx * expert_size + expert
    mine = head_of(ctx, expert, heads, ctx_size, expert_size)
    holds = mine < heads
    greet(
        [
            {"ctx": ((me + i) % count) // expert_size, "expert": ((me + i) % count) % expert_size}
            for i in range(1, count)
        ]
    )

    def copy(source, target, at, by, there):
        return pltpu.make_async_remote_copy(
            src_ref=in_ref.at[source],
            dst_ref=out_ref.at[target],
            send_sem=send_sem.at[at],
            recv_sem=recv_sem.at[by],
            device_id=there,
            device_id_type=MESH,
        )

    if inward:
        def sends():
            for i in range(heads):
                head = (me + i) % heads
                row, column = head_place(head, heads, ctx_size, expert_size)
                yield head != mine, copy(head, me, head, me, {"ctx": row, "expert": column})

        for needed, one in sends():
            pl.when(needed)(one.start)

        @pl.when(holds)
        def _():
            out_ref[me] = in_ref[mine % heads]

        @pl.when(jnp.logical_not(holds))
        def _():
            out_ref[...] = jnp.zeros_like(out_ref)

        for i in range(1, count):
            source = (me + count - i) % count
            pl.when(holds)(copy(0, source, 0, source, {"ctx": ctx, "expert": expert}).wait_recv)
        for needed, one in sends():
            pl.when(needed)(one.wait_send)
    else:
        def sends():
            for i in range(1, count):
                there = (me + i) % count
                yield copy(
                    there,
                    mine % heads,
                    i,
                    mine % heads,
                    {"ctx": there // expert_size, "expert": there % expert_size},
                )

        for one in sends():
            pl.when(holds)(one.start)

        @pl.when(holds)
        def _():
            out_ref[mine % heads] = in_ref[me]

        for i in range(heads):
            head = (me + i) % heads
            pl.when(head != mine)(copy(0, head, 0, head, {"ctx": ctx, "expert": expert}).wait_recv)
        for one in sends():
            pl.when(holds)(one.wait_send)


def trade(blocks, heads, count, inward, number):
    lead = count if inward else heads
    return pl.pallas_call(
        functools.partial(trade_kernel, heads, inward),
        out_shape=jax.ShapeDtypeStruct((lead,) + blocks.shape[1:], blocks.dtype),
        in_specs=[VMEM],
        out_specs=VMEM,
        scratch_shapes=[DMA((count,)), DMA((count,))],
        compiler_params=pltpu.CompilerParams(
            collective_id=number, has_side_effects=True, vmem_limit_bytes=32 << 20
        ),
    )(blocks)


def across(axis, bit):
    index = lax.axis_index(axis)
    return index + bit * (1 - 2 * ((index // bit) % 2))


def flip(index, mask):
    bit = 1
    while bit <= mask:
        if mask & bit:
            index = index + bit * (1 - 2 * ((index // bit) % 2))
        bit *= 2
    return index


def plan(expert_size, ctx_size, chunk, rows):
    bits = [1 << b for b in range(ctx_size.bit_length() - 1)]
    items = []
    for step in range(expert_size):
        items.append((step, None, chunk, bits if step % 2 == 0 else bits[::-1]))
    half = rows // 2
    items.append((None, 0, half, bits))
    items.append((None, half, rows - half, bits[::-1]))
    return items, bits


def spread_kernel(
    rows_ref, flat_ref, gate_ref, out_ref, gates_ref, z_send, z_recv, send, recv, pair_recv, gate_send,
    gate_recv, gate_z_send, gate_z_recv, local_sem,
):
    dp_size, ctx_size, expert_size = (lax.axis_size(a) for a in ("dp", "ctx", "expert"))
    dp, ctx, expert = (lax.axis_index(a) for a in ("dp", "ctx", "expert"))
    chunk, rows = rows_ref.shape[1], flat_ref.shape[0]
    items, bits = plan(expert_size, ctx_size, chunk, rows)
    plane_size = dp_size * ctx_size
    own = dp * ctx_size + ctx

    def z_at(step):
        return (expert + step) % expert_size

    def z_from(step):
        return (expert + expert_size - step) % expert_size

    plane = [(d, c) for d in range(dp_size) for c in range(ctx_size) if (d, c) != (0, 0)]
    greet(
        [{"expert": z_at(step)} for step in range(1, expert_size)]
        + [{"dp": (dp + d) % dp_size, "ctx": flip(ctx, c)} for d, c in plane]
    )

    def region(item):
        step, first, size, _ = item
        if step is None:
            return pl.ds(expert_size * chunk + first, size)
        return pl.ds(pl.multiple_of(z_from(step) * chunk, 16), size)

    def z_copy(step, landing=False):
        place = z_from(step) if landing else expert
        return pltpu.make_async_remote_copy(
            src_ref=rows_ref.at[z_at(step)],
            dst_ref=out_ref.at[own, pl.ds(pl.multiple_of(place * chunk, 16), chunk)],
            send_sem=z_send.at[step],
            recv_sem=z_recv.at[step],
            device_id={"expert": z_at(step)},
            device_id_type=MESH,
        )

    def gate_z(step, landing=False):
        return pltpu.make_async_remote_copy(
            src_ref=gate_ref.at[z_at(step)],
            dst_ref=gates_ref.at[own, z_from(step) if landing else expert],
            send_sem=gate_z_send.at[step],
            recv_sem=gate_z_recv.at[step],
            device_id={"expert": z_at(step)},
            device_id_type=MESH,
        )

    def gate_plane(d, c, block):
        return pltpu.make_async_remote_copy(
            src_ref=gates_ref.at[block],
            dst_ref=gates_ref.at[block],
            send_sem=gate_send.at[d, c],
            recv_sem=gate_recv.at[d, c],
            device_id={"dp": (dp + d) % dp_size, "ctx": flip(ctx, c)},
            device_id_type=MESH,
        )

    for step in range(1, expert_size):
        gate_z(step).start()
        z_copy(step).start()

    def source(number):
        step, first, size, _ = items[number]
        if step is None:
            return flat_ref.at[pl.ds(first, size)]
        if step == 0:
            return rows_ref.at[expert]
        return out_ref.at[own, region(items[number])]

    def passing(number, mask, bit, origin):
        block = dp * ctx_size + flip(ctx, mask)
        here = out_ref.at[block, region(items[number])]
        return pltpu.make_async_remote_copy(
            src_ref=source(number) if origin else here,
            dst_ref=here,
            send_sem=send.at[number, mask, bits.index(bit)],
            recv_sem=recv.at[number, mask ^ bit],
            device_id={"ctx": flip(ctx, bit)},
            device_id_type=MESH,
        )

    def crossing(number, mask, other, origin):
        block = dp * ctx_size + flip(ctx, mask)
        here = out_ref.at[block, region(items[number])]
        return pltpu.make_async_remote_copy(
            src_ref=source(number) if origin else here,
            dst_ref=here,
            send_sem=send.at[number, mask, len(bits) + other - 1],
            recv_sem=pair_recv.at[number, mask, other - 1],
            device_id={"dp": (dp + other) % dp_size},
            device_id_type=MESH,
        )

    def arrived(number, mask):
        block = dp * ctx_size + flip(ctx, mask)
        here = out_ref.at[block, region(items[number])]
        pltpu.make_async_remote_copy(
            src_ref=here, dst_ref=here, send_sem=send.at[0, 0, 0], recv_sem=recv.at[number, mask],
            device_id={"ctx": ctx}, device_id_type=MESH,
        ).wait_recv()

    started = []

    def begin(number):
        for bit in items[number][3]:
            one = passing(number, 0, bit, True)
            one.start()
            started.append(one)
        for other in range(1, dp_size):
            one = crossing(number, 0, other, True)
            one.start()
            started.append(one)

    def forward(number):
        order = items[number][3]
        masks = [0]
        for place, bit in enumerate(order):
            for mask in [m | bit for m in masks]:
                arrived(number, mask)
                for later in order[place + 1 :]:
                    one = passing(number, mask, later, False)
                    one.start()
                    started.append(one)
                for other in range(1, dp_size):
                    one = crossing(number, mask, other, False)
                    one.start()
                    started.append(one)
            masks = masks + [m | bit for m in masks]

    ready = [0, expert_size, expert_size + 1]
    for number in ready:
        begin(number)
    kept = [
        pltpu.make_async_copy(source(number), out_ref.at[own, region(items[number])], local_sem.at[i])
        for i, number in enumerate(ready)
    ]
    for one in kept:
        one.start()
    gates_ref[own, expert] = gate_ref[expert]
    waiting = list(ready)
    for step in range(1, expert_size):
        z_copy(step, True).wait_recv()
        begin(step)
        waiting.append(step)
        forward(waiting.pop(0))
    for step in range(1, expert_size):
        gate_z(step, True).wait_recv()
    for d, c in plane:
        gate_plane(d, c, own).start()
    for number in waiting:
        forward(number)
    for d, c in plane:
        gate_plane(d, c, ((dp + d) % dp_size) * ctx_size + flip(ctx, c)).wait_recv()
        gate_plane(d, c, own).wait_send()
    for number in range(len(items)):
        for mask in range(ctx_size):
            for other in range(1, dp_size):
                block = ((dp + dp_size - other) % dp_size) * ctx_size + flip(ctx, mask)
                here = out_ref.at[block, region(items[number])]
                pltpu.make_async_remote_copy(
                    src_ref=here, dst_ref=here, send_sem=send.at[0, 0, 0],
                    recv_sem=pair_recv.at[number, mask, other - 1], device_id={"dp": dp}, device_id_type=MESH,
                ).wait_recv()
    for one in started:
        one.wait_send()
    for step in range(1, expert_size):
        z_copy(step).wait_send()
        gate_z(step).wait_send()
    for one in kept:
        one.wait()


def spread(rows, flat, gate, sizes, number):
    dp_size, ctx_size, expert_size = sizes
    chunk, width = rows.shape[1:]
    count = expert_size + 2
    links = max(ctx_size.bit_length() - 1 + dp_size - 1, 1)
    block = expert_size * chunk + flat.shape[0]
    return pl.pallas_call(
        spread_kernel,
        out_shape=(
            jax.ShapeDtypeStruct((dp_size * ctx_size, block, width), rows.dtype),
            jax.ShapeDtypeStruct((dp_size * ctx_size,) + gate.shape, gate.dtype),
        ),
        in_specs=[VMEM, VMEM, VMEM],
        out_specs=(ANY, VMEM),
        scratch_shapes=[
            DMA((expert_size,)),
            DMA((expert_size,)),
            DMA((count, ctx_size, links)),
            DMA((count, ctx_size)),
            DMA((count, ctx_size, dp_size)),
            DMA((dp_size, ctx_size)),
            DMA((dp_size, ctx_size)),
            DMA((expert_size,)),
            DMA((expert_size,)),
            DMA((3,)),
        ],
        compiler_params=pltpu.CompilerParams(
            collective_id=number, has_side_effects=True, vmem_limit_bytes=32 << 20
        ),
    )(rows, flat, gate)


def home_kernel(
    depth, part_ref, dot_ref, rows_ref, flat_ref, dots_ref, mine, theirs, dot_in, dot_sum, mine_sem,
    pair_send, pair_recv, send, recv, z_send, z_recv, dot_send, dot_recv, dot_z_send, dot_z_recv,
    *arrivals,
):
    dp_size, ctx_size, expert_size = (lax.axis_size(a) for a in ("dp", "ctx", "expert"))
    dp, ctx, expert = (lax.axis_index(a) for a in ("dp", "ctx", "expert"))
    chunk, rows = rows_ref.shape[1], flat_ref.shape[0]
    items, bits = plan(expert_size, ctx_size, chunk, rows)
    own = dp * ctx_size + ctx
    other = (dp + 1) % dp_size

    def z_at(step):
        return (expert + step) % expert_size

    def z_from(step):
        return (expert + expert_size - step) % expert_size

    plane = [(d, c) for d in range(dp_size) for c in range(ctx_size) if (d, c) != (0, 0)]
    greet(
        [{"expert": z_at(step)} for step in range(1, expert_size)]
        + [{"dp": (dp + d) % dp_size, "ctx": flip(ctx, c)} for d, c in plane]
    )

    def region(number):
        step, start, size, _ = items[number]
        if step is None:
            return pl.ds(expert_size * chunk + start, size)
        return pl.ds(pl.multiple_of(z_at(step) * chunk, 16), size)

    starts = [0]
    for item in items:
        starts.append(starts[-1] + item[2])

    def held(number):
        return pl.ds(starts[number], items[number][2])

    def load(number, mask):
        return pltpu.make_async_copy(
            part_ref.at[dp * ctx_size + flip(ctx, mask), region(number)],
            mine.at[mask, held(number)],
            mine_sem.at[number, mask],
        )

    def cross(number, mask):
        return pltpu.make_async_remote_copy(
            src_ref=part_ref.at[other * ctx_size + flip(ctx, mask), region(number)],
            dst_ref=theirs.at[mask, held(number)],
            send_sem=pair_send.at[number, mask],
            recv_sem=pair_recv.at[number, mask],
            device_id={"dp": other},
            device_id_type=MESH,
        )

    def dot_plane(d, c):
        return pltpu.make_async_remote_copy(
            src_ref=dot_ref.at[((dp + d) % dp_size) * ctx_size + flip(ctx, c)],
            dst_ref=dot_in.at[d, c],
            send_sem=dot_send.at[d, c],
            recv_sem=dot_recv.at[d, c],
            device_id={"dp": (dp + d) % dp_size, "ctx": flip(ctx, c)},
            device_id_type=MESH,
        )

    def dot_z(step, landing=False):
        return pltpu.make_async_remote_copy(
            src_ref=dot_sum.at[z_at(step)],
            dst_ref=dots_ref.at[z_from(step) if landing else expert],
            send_sem=dot_z_send.at[step],
            recv_sem=dot_z_recv.at[step],
            device_id={"expert": z_at(step)},
            device_id_type=MESH,
        )

    order = list(range(1, expert_size)) + [0, expert_size, expert_size + 1]
    for number in order:
        for mask in range(ctx_size):
            cross(number, mask).start()
            load(number, mask).start()
    for d, c in plane:
        dot_plane(d, c).start()

    def stage(number, place):
        order = items[number][3][::-1]
        done = sum(order[:place])
        bit = order[place]
        rest = [m for m in range(ctx_size) if not m & (done | bit)]
        return bit, [(m | bit, m) for m in rest]

    def hop(number, place, index):
        bit, moves = stage(number, place)
        source = moves[index][0]
        return pltpu.make_async_remote_copy(
            src_ref=mine.at[source, held(number)],
            dst_ref=arrivals[place].at[index, held(number)],
            send_sem=send.at[number, source],
            recv_sem=recv.at[number, place, index],
            device_id={"ctx": flip(ctx, bit)},
            device_id_type=MESH,
        )

    def z_copy(number, landing=False):
        return pltpu.make_async_remote_copy(
            src_ref=mine.at[0, held(number)],
            dst_ref=rows_ref.at[z_from(number) if landing else expert],
            send_sem=z_send.at[number],
            recv_sem=z_recv.at[number],
            device_id={"expert": z_at(number)},
            device_id_type=MESH,
        )

    def add(number, mask, buffer, index):
        at = held(number)
        mine[mask, at] = (mine[mask, at].astype(f32) + buffer[index, at].astype(f32)).astype(mine.dtype)

    def pair(number):
        leaving = [source for source, _ in stage(number, 0)[1]]
        for mask in leaving + [m for m in range(ctx_size) if m not in leaving]:
            load(number, mask).wait()
            cross(number, mask).wait_recv()
            add(number, mask, theirs, mask)
            if mask in leaving:
                hop(number, 0, leaving.index(mask)).start()

    def step(number, place):
        _, moves = stage(number, place)
        for index, (_, target) in enumerate(moves):
            hop(number, place, index).wait_recv()
        following = stage(number, place + 1)[1] if place + 1 < depth else []
        leaving = [source for source, _ in following]
        targets = [target for _, target in moves]
        for mask in leaving + [m for m in targets if m not in leaving]:
            add(number, mask, arrivals[place], targets.index(mask))
            if mask in leaving:
                hop(number, place + 1, leaving.index(mask)).start()

    def finish(number):
        kind = items[number][0]
        if kind is None:
            start, size = items[number][1], items[number][2]
            flat_ref[pl.ds(start, size)] = mine[0, held(number)]
        elif kind == 0:
            rows_ref[expert] = mine[0, held(number)]
        else:
            z_copy(number).start()

    for tick in range(len(order) + depth):
        for place in reversed(range(depth + 1)):
            index = tick - place
            if not 0 <= index < len(order):
                continue
            number = order[index]
            if place == 0:
                pair(number)
            else:
                step(number, place - 1)
            if place == depth:
                finish(number)

    total_dots = dot_ref[own]
    for d, c in plane:
        dot_plane(d, c).wait_recv()
        total_dots = total_dots + dot_in[d, c]
    dot_sum[...] = total_dots
    for number in range(1, expert_size):
        dot_z(number).start()
    dots_ref[expert] = dot_sum[expert]

    for number in range(1, expert_size):
        z_copy(number, True).wait_recv()
        dot_z(number, True).wait_recv()
    for number in range(1, expert_size):
        z_copy(number).wait_send()
        dot_z(number).wait_send()
    for d, c in plane:
        dot_plane(d, c).wait_send()
    for number in order:
        for mask in range(ctx_size):
            cross(number, mask).wait_send()
        for place in range(depth):
            for index in range(len(stage(number, place)[1])):
                hop(number, place, index).wait_send()


def bring_home(part, dots, rows, sizes, number):
    dp_size, ctx_size, expert_size = sizes
    block, width = part.shape[1:]
    chunk = (block - rows) // expert_size
    count = expert_size + 2
    depth = ctx_size.bit_length() - 1
    buffer = (ctx_size, block, width)
    return pl.pallas_call(
        functools.partial(home_kernel, depth),
        out_shape=(
            jax.ShapeDtypeStruct((expert_size, chunk, width), part.dtype),
            jax.ShapeDtypeStruct((rows, width), part.dtype),
            jax.ShapeDtypeStruct(dots.shape[1:], dots.dtype),
        ),
        in_specs=[ANY, VMEM],
        out_specs=(VMEM, VMEM, VMEM),
        scratch_shapes=[
            pltpu.VMEM(buffer, part.dtype),
            pltpu.VMEM(buffer, part.dtype),
            pltpu.VMEM((dp_size, ctx_size) + dots.shape[1:], dots.dtype),
            pltpu.VMEM(dots.shape[1:], dots.dtype),
            DMA((count, ctx_size)),
            DMA((count, ctx_size)),
            DMA((count, ctx_size)),
            DMA((count, ctx_size)),
            DMA((count, depth, max(ctx_size // 2, 1))),
            DMA((count,)),
            DMA((count,)),
            DMA((dp_size, ctx_size)),
            DMA((dp_size, ctx_size)),
            DMA((expert_size,)),
            DMA((expert_size,)),
        ]
        + [pltpu.VMEM((ctx_size >> (place + 1),) + buffer[1:], part.dtype) for place in range(depth)],
        compiler_params=pltpu.CompilerParams(
            collective_id=number, has_side_effects=True, vmem_limit_bytes=56 << 20
        ),
    )(part, dots)


def local(
    tokens,
    lengths,
    routes,
    norm1_gain,
    query_weight,
    key_weight,
    value_weight,
    output_weight,
    norm2_gain,
    router_weight,
    expert_gate,
    expert_up,
    expert_down,
    shared_gate,
    shared_up,
    shared_down,
    cotangent,
):
    dp_size, ctx_size, expert_size = (lax.axis_size(a) for a in ("dp", "ctx", "expert"))
    plane_size, slot_size = dp_size * ctx_size, ctx_size * expert_size
    rows, width = tokens.shape[1:]
    heads = width // HEAD_DIM
    own = EXPERTS // expert_size
    hidden_width = expert_gate.shape[2]
    part = hidden_width // plane_size
    plane = lax.axis_index("dp") * ctx_size + lax.axis_index("ctx")
    first_row = (lax.axis_index("ctx") * expert_size + lax.axis_index("expert")) * rows
    positions = first_row + jnp.arange(rows, dtype=jnp.int32)
    length = lengths[0]
    live_rows = positions < length
    valid = live_rows.astype(f32)[:, None]
    inputs = tokens[0].astype(f32)
    upstream = cotangent[0].astype(f32)
    d_branch = valid * upstream
    d_branch_low = d_branch.astype(bf16)

    route_ids = routes[0]
    expert_range = jnp.arange(EXPERTS, dtype=jnp.int32)
    picked = (route_ids[:, :, None] == expert_range).astype(f32)
    expert_hits = (
        ((route_ids[:, :, None] == expert_range) & live_rows[:, None, None])
        .astype(jnp.int32)
        .reshape(rows * TOP, EXPERTS)
    )
    places = jnp.sum((jnp.cumsum(expert_hits, axis=0) - 1) * expert_hits, axis=-1)
    live_pairs = jnp.broadcast_to(live_rows[:, None], (rows, TOP)).reshape(-1)
    slot_ids = jnp.where(live_pairs, route_ids.reshape(-1) * PLACES + places, -1)
    dispatch = (
        slot_ids[:, None] == jnp.arange(EXPERTS * PLACES, dtype=jnp.int32)[None, :]
    ).reshape(rows, TOP, EXPERTS * PLACES)
    either = jnp.any(dispatch, axis=1).astype(bf16)

    sizes = (dp_size, ctx_size, expert_size)

    def place_rows(flat):
        placed = jnp.einsum("ts,td->sd", either, flat, preferred_element_type=f32).astype(bf16)
        return placed.reshape(expert_size, -1, width)

    def to_experts(blocks):
        here = lax.axis_index("expert")
        taken = [lax.dynamic_index_in_dim(blocks, here, 0, False)]
        for step in range(1, expert_size):
            sent = lax.dynamic_index_in_dim(blocks, (here + step) % expert_size, 0, False)
            ring = [(i, (i + step) % expert_size) for i in range(expert_size)]
            taken.append(lax.ppermute(sent, "expert", ring))
        return jnp.take(jnp.stack(taken), (here - jnp.arange(expert_size)) % expert_size, axis=0)

    up_mine = to_experts(place_rows(d_branch_low)).reshape(-1, width)
    up_all = lax.all_gather(jnp.concatenate([up_mine, d_branch_low], axis=0), PLANE, axis=0)

    scale_one = rms_scale(inputs)
    normal_one = inputs * scale_one
    normed_low = (normal_one * norm1_gain).astype(bf16)
    cosine, sine = rope_tables(positions)

    def project(weight):
        lin = jnp.dot(normed_low, weight, preferred_element_type=f32)
        return jnp.transpose(lin).reshape(heads, HEAD_DIM, rows)

    def rotated(lin_t):
        half = HEAD_DIM // 2
        first, second = lin_t[:, :half], lin_t[:, half:]
        return jnp.concatenate(
            [first * cosine - second * sine, second * cosine + first * sine], axis=1
        )

    query = rotated(project(query_weight)).astype(bf16)
    key = rotated(project(key_weight)).astype(bf16)
    value = project(value_weight).astype(bf16)

    def to_heads(blocks, number):
        return trade(blocks, heads, slot_size, True, number)

    def from_heads(blocks, number):
        return trade(blocks, heads, slot_size, False, number)

    def by_block(flat_t):
        return jnp.transpose(flat_t.reshape(-1, slot_size, rows), (1, 0, 2))

    qkv = to_heads(jnp.concatenate([query, key, value], axis=1), 1)
    normed_all = lax.all_gather(normed_low, SLOT, axis=0, tiled=True)
    out_t, log_total = attend(qkv, lengths)
    attended = jnp.transpose(
        from_heads(by_block(out_t.astype(bf16)), 2).reshape(width, rows)
    )
    attn_out = jnp.dot(attended, output_weight, preferred_element_type=f32)
    hidden_in = inputs + valid * attn_out

    scale_two = rms_scale(hidden_in)
    normal_two = hidden_in * scale_two
    normed_two_low = (normal_two * norm2_gain).astype(bf16)
    logits = jnp.dot(normed_two_low, router_weight, preferred_element_type=f32)
    chosen = jnp.sum(picked * logits[:, None, :], axis=-1)
    shifted = jnp.exp(chosen - jnp.max(chosen, axis=-1, keepdims=True))
    gate_weights = shifted / jnp.sum(shifted, axis=-1, keepdims=True)

    gate_rows = jnp.sum(jnp.where(dispatch, gate_weights[:, :, None], 0.0), axis=(0, 1))
    placed_rows = EXPERTS * PLACES

    def tiled(row):
        row = row.reshape(row.shape[:-1] + (expert_size, 1, -1))
        return jnp.pad(row, [(0, 0)] * (row.ndim - 2) + [(0, 7), (0, 128 - row.shape[-1])])

    def flat_row(tile):
        return tile[..., 0, : own * PLACES].reshape(tile.shape[:-3] + (placed_rows,))

    in_all, gate_all = spread(place_rows(normed_two_low), normed_two_low, tiled(gate_rows), sizes, 3)
    gate_all = flat_row(gate_all)

    def by_expert(both):
        cut = both[:, :placed_rows].reshape((plane_size * expert_size, own, PLACES) + both.shape[2:])
        return jnp.swapaxes(cut, 0, 1).reshape((own, -1) + both.shape[2:])

    def by_source(flat):
        cut = flat.reshape((own, plane_size * expert_size, PLACES) + flat.shape[2:])
        return jnp.swapaxes(cut, 0, 1).reshape((plane_size, placed_rows) + flat.shape[2:])

    def column(weight):
        return lax.dynamic_slice_in_dim(weight, plane * part, part, weight.ndim - 1)

    def row(weight):
        return lax.dynamic_slice_in_dim(weight, plane * part, part, weight.ndim - 2)

    def branch(rows_in, up, gate_w, up_w, down_w, weight):
        def dot(spec, a, b):
            return jnp.einsum(spec, a, b, preferred_element_type=f32)

        gate_lin, up_lin = dot("erd,edf->erf", rows_in, gate_w), dot("erd,edf->erf", rows_in, up_w)
        sigmoid = 1.0 / (1.0 + jnp.exp(-gate_lin))
        silu = gate_lin * sigmoid
        hidden = (silu * up_lin).astype(bf16)
        result = dot("erf,efd->erd", hidden, down_w)
        d_out = (weight * up.astype(f32)).astype(bf16)
        d_hidden = dot("erd,efd->erf", d_out, down_w)
        d_gate = (d_hidden * up_lin * (sigmoid + silu * (1.0 - sigmoid))).astype(bf16)
        d_up = (d_hidden * silu).astype(bf16)
        d_in = dot("erf,edf->erd", d_gate, gate_w) + dot("erf,edf->erd", d_up, up_w)
        grads = (
            dot("erd,erf->edf", rows_in, d_gate),
            dot("erd,erf->edf", rows_in, d_up),
            dot("erf,erd->efd", hidden, d_out),
        )
        return result, d_in, grads

    gate_factor = by_expert(gate_all)[:, :, None]
    up_rows = by_expert(up_all)
    result, d_rows, expert_grads = branch(
        by_expert(in_all), up_rows, column(expert_gate), column(expert_up), row(expert_down),
        gate_factor,
    )
    d_gate_part = by_source(jnp.sum(result * up_rows.astype(f32), axis=-1))
    shared_result, shared_d, shared_grads = branch(
        in_all[:, placed_rows:].reshape(1, -1, width),
        up_all[:, placed_rows:].reshape(1, -1, width),
        column(shared_gate)[None],
        column(shared_up)[None],
        row(shared_down)[None],
        1.0,
    )

    def joined(expert_part, shared_part):
        return jnp.concatenate(
            [by_source(expert_part), shared_part.reshape(plane_size, rows, width)], axis=1
        ).astype(bf16)

    def collect(back, flat):
        spread_rows = jnp.dot(either, back.reshape(placed_rows, width), preferred_element_type=f32)
        return spread_rows + flat.astype(f32)

    back, flat, d_gate_rows = bring_home(joined(d_rows, shared_d), tiled(d_gate_part), rows, sizes, 4)
    d_gate_rows = flat_row(d_gate_rows)
    out_back, out_flat, _ = bring_home(
        joined(result * gate_factor, shared_result), tiled(d_gate_part), rows, sizes, 5
    )
    d_gates = jnp.sum(jnp.where(dispatch, d_gate_rows, 0.0), axis=-1)
    d_chosen = gate_weights * (
        d_gates - jnp.sum(gate_weights * d_gates, axis=-1, keepdims=True)
    )
    d_logits = jnp.sum(picked * d_chosen[:, :, None], axis=1).astype(bf16)
    d_router = jnp.einsum("td,te->de", normed_two_low, d_logits, preferred_element_type=f32)
    d_normed_two = collect(back, flat) + jnp.einsum(
        "te,de->td", d_logits, router_weight, preferred_element_type=f32
    )
    output_rows = hidden_in + valid * collect(out_back, out_flat)
    output_rows = output_rows.astype(bf16)[None]
    d_gain_two = jnp.sum(d_normed_two * normal_two, axis=0)
    d_hidden_in = upstream + rms_back(normal_two, scale_two, norm2_gain, d_normed_two)

    d_attn_low = (valid * d_hidden_in).astype(bf16)
    d_output_weight = jnp.einsum("td,te->de", attended, d_attn_low, preferred_element_type=f32)
    d_attended = jnp.einsum("te,de->dt", d_attn_low, output_weight, preferred_element_type=f32)
    d_attended = to_heads(d_attended.astype(bf16).reshape(heads, HEAD_DIM, rows), 6)
    all_cosine, all_sine = rope_tables(jnp.arange(slot_size * rows, dtype=jnp.int32))
    d_qkv = attend_back(qkv, lengths, out_t, log_total, d_attended, all_cosine, all_sine)
    d_mine = from_heads(d_qkv, 7)
    head_grad = jnp.einsum(
        "bet,btd->ed", d_qkv, normed_all.reshape(slot_size, rows, width), preferred_element_type=f32
    )
    d_own = jnp.swapaxes(d_mine.reshape(heads, 3, HEAD_DIM, rows), 0, 1)
    d_own = d_own.reshape(3, width, rows)
    d_normed = jnp.zeros((width, rows), f32)
    for weight, grad in zip((query_weight, key_weight, value_weight), d_own):
        d_normed = d_normed + jnp.dot(weight, grad, preferred_element_type=f32)
    d_normed = jnp.transpose(d_normed)
    d_gain_one = jnp.sum(d_normed * normal_one, axis=0)
    input_grad = d_hidden_in + rms_back(normal_one, scale_one, norm1_gain, d_normed)
    input_grad = input_grad.astype(bf16)[None]

    shard = width // (dp_size * slot_size)
    head_grad = jnp.transpose(head_grad).reshape(-1, 3 * HEAD_DIM)
    head_grad = lax.psum_scatter(head_grad, "dp", scatter_dimension=0, tiled=True)
    head_grad = from_heads(head_grad.reshape(slot_size, shard, 3 * HEAD_DIM), 8)
    head_grad = jnp.transpose(
        head_grad.reshape(heads, shard, 3, HEAD_DIM), (2, 1, 0, 3)
    ).reshape(3, shard, width)

    def scatter(grad):
        for axis in ("dp", "ctx", "expert"):
            grad = lax.psum_scatter(grad, axis, scatter_dimension=0, tiled=True)
        return grad

    output_grad = scatter(d_output_weight.astype(bf16)).astype(f32)
    small = lax.psum(
        jnp.concatenate([d_router, d_gain_one[:, None], d_gain_two[:, None]], axis=1),
        ("dp", "ctx", "expert"),
    )
    linear = plane * expert_size + lax.axis_index("expert")
    small = lax.dynamic_slice_in_dim(small, linear * shard, shard, 0)

    def shared_columns(grad):
        grad = grad[0].reshape(plane_size, expert_size, shard, part).astype(bf16)
        grad = lax.psum_scatter(grad, "expert", scatter_dimension=1, tiled=True)[:, 0]
        grad = lax.all_to_all(grad, PLANE, 0, 0)
        return jnp.swapaxes(grad, 0, 1).reshape(shard, hidden_width).astype(f32)

    shared_down_grad = lax.psum_scatter(
        shared_grads[2][0].astype(bf16), "expert", scatter_dimension=0, tiled=True
    ).astype(f32)
    return (
        output_rows,
        input_grad,
        small[:, EXPERTS],
        head_grad[0],
        head_grad[1],
        head_grad[2],
        output_grad,
        small[:, EXPERTS + 1],
        small[:, :EXPERTS],
        expert_grads[0],
        expert_grads[1],
        expert_grads[2],
        shared_columns(shared_grads[0]),
        shared_columns(shared_grads[1]),
        shared_down_grad,
    )


def solution(mesh):
    tokens = P("dp", ("ctx", "expert"), None)
    whole = P()
    experts = P("expert", None, None)
    everywhere = ("dp", "ctx", "expert")
    return jax.shard_map(
        local,
        mesh=mesh,
        in_specs=(tokens, P("dp"), tokens)
        + (whole,) * 7
        + (experts,) * 3
        + (whole,) * 3
        + (tokens,),
        out_specs=(tokens, tokens, P(everywhere))
        + (P(everywhere, None),) * 4
        + (P(everywhere), P(everywhere, None))
        + (P("expert", None, PLANE),) * 2
        + (P("expert", PLANE, None),)
        + (P(everywhere, None),) * 3,
        check_vma=False,
    )
```

```python
import functools

import jax
import jax.numpy as jnp
from jax import lax
from jax.experimental import pallas as pl
from jax.experimental.pallas import tpu as pltpu
from jax.sharding import PartitionSpec as P

HEAD_DIM = 64
EXPERTS = 16
TOP = 2
CAP = 22
PLACES = 24

norm_epsilon = 1e-06
rope_base = 10000.0
score_scale = 0.125
masked_value = -1e30
PLANE = ("dp", "ctx")
SLOT = ("ctx", "expert")
AHEAD = 2
bf16 = jnp.bfloat16
f32 = jnp.float32


def rms_scale(values):
    return lax.rsqrt(jnp.mean(values * values, axis=-1, keepdims=True) + norm_epsilon)


def rms_back(normal, scale, gain, upstream):
    lifted = upstream * gain
    return scale * (lifted - normal * jnp.mean(lifted * normal, axis=-1, keepdims=True))


def rope_tables(positions):
    half = HEAD_DIM // 2
    exponent = jnp.arange(half, dtype=f32) * (2.0 / HEAD_DIM)
    inverse_freq = rope_base ** (-exponent)
    angles = inverse_freq[:, None] * positions[None, :].astype(f32)
    return jnp.cos(angles), jnp.sin(angles)


def head_rows(qkv_ref, first, count):
    return jnp.concatenate(
        [qkv_ref[block, first : first + count, :] for block in range(qkv_ref.shape[0])], axis=1
    )


def live_keys(key_t, length):
    span = key_t.shape[1]
    place = lax.broadcasted_iota(jnp.int32, (8, span), 1)
    row = lax.broadcasted_iota(jnp.int32, (8, span), 0)
    bias = jnp.where((place >= length) & (row == 0), masked_value, 0.0)
    padded = jnp.concatenate(
        [key_t.astype(f32), bias, jnp.zeros((HEAD_DIM - 8, span), f32)], axis=0
    )
    return jnp.transpose(padded).astype(bf16)


def scaled_queries(query_t):
    span = query_t.shape[1]
    row = lax.broadcasted_iota(jnp.int32, (HEAD_DIM, span), 0)
    ones = jnp.where(row == 0, 1.0, 0.0)
    return jnp.concatenate([query_t.astype(f32) * score_scale, ones], axis=0).astype(bf16)


def causal(scores):
    key = lax.broadcasted_iota(jnp.int32, scores.shape, 0)
    query = lax.broadcasted_iota(jnp.int32, scores.shape, 1)
    return jnp.where(key <= query, scores, masked_value)


def attend_kernel(step, length_ref, qkv_ref, out_ref, total_ref, key_ref, query_ref, value_ref):
    span = qkv_ref.shape[0] * qkv_ref.shape[2]
    key_ref[...] = live_keys(head_rows(qkv_ref, HEAD_DIM, HEAD_DIM), length_ref[0])
    query_ref[...] = scaled_queries(head_rows(qkv_ref, 0, HEAD_DIM))
    value_ref[...] = head_rows(qkv_ref, 2 * HEAD_DIM, HEAD_DIM)

    def query_block(q, carry):
        here = pl.ds(pl.multiple_of(q * step, step), step)
        query = query_ref[:, here]

        def absorb(k, state, masked):
            top, total, out = state
            there = pl.ds(pl.multiple_of(k * step, step), step)
            scores = jnp.dot(key_ref[there, :], query, preferred_element_type=f32)
            if masked:
                scores = causal(scores)
            new_top = jnp.maximum(top, jnp.max(scores, axis=0, keepdims=True))
            shrink = jnp.exp(top - new_top)
            weights = jnp.exp(scores - new_top)
            total = total * shrink + jnp.sum(weights, axis=0, keepdims=True)
            out = out * shrink + jnp.dot(
                value_ref[:, there], weights.astype(bf16), preferred_element_type=f32
            )
            return new_top, total, out

        state = (
            jnp.full((1, step), masked_value, f32),
            jnp.zeros((1, step), f32),
            jnp.zeros((HEAD_DIM, step), f32),
        )
        state = absorb(q, state, True)
        top, total, out = lax.fori_loop(0, q, lambda k, s: absorb(k, s, False), state)
        out_ref[:, here] = out / total
        total_ref[:, here] = top + jnp.log(total)
        return carry

    lax.fori_loop(0, span // step, query_block, 0)


def attend(qkv, length):
    blocks, _, rows = qkv.shape
    span = blocks * rows
    step = min(512, span)
    return pl.pallas_call(
        functools.partial(attend_kernel, step),
        out_shape=(
            jax.ShapeDtypeStruct((HEAD_DIM, span), f32),
            jax.ShapeDtypeStruct((1, span), f32),
        ),
        in_specs=[
            pl.BlockSpec(memory_space=pltpu.SMEM),
            pl.BlockSpec(memory_space=pltpu.VMEM),
        ],
        out_specs=(pl.BlockSpec(memory_space=pltpu.VMEM),) * 2,
        scratch_shapes=[
            pltpu.VMEM((span, 2 * HEAD_DIM), bf16),
            pltpu.VMEM((2 * HEAD_DIM, span), bf16),
            pltpu.VMEM((HEAD_DIM, span), bf16),
        ],
        compiler_params=pltpu.CompilerParams(vmem_limit_bytes=48 << 20),
    )(length, qkv)


def unrotate(grad_t, cosine, sine):
    half = HEAD_DIM // 2
    first, second = grad_t[:half], grad_t[half:]
    return jnp.concatenate(
        [first * cosine + second * sine, second * cosine - first * sine], axis=0
    )


def attend_back_kernel(
    step,
    length_ref,
    qkv_ref,
    out_ref,
    total_ref,
    upstream_ref,
    cosine_ref,
    sine_ref,
    grad_ref,
    key_ref,
    query_ref,
    value_ref,
    key_t_ref,
    query_sum,
    key_sum,
    value_sum,
    delta_ref,
    up_ref,
):
    blocks, _, rows = qkv_ref.shape
    span = blocks * rows
    key_t = head_rows(qkv_ref, HEAD_DIM, HEAD_DIM)
    key_ref[...] = live_keys(key_t, length_ref[0])
    key_t_ref[...] = key_t
    query_ref[...] = scaled_queries(head_rows(qkv_ref, 0, HEAD_DIM))
    value_t = head_rows(qkv_ref, 2 * HEAD_DIM, HEAD_DIM)
    value_ref[...] = jnp.transpose(value_t.astype(f32)).astype(bf16)
    upstream = head_rows(upstream_ref, 0, HEAD_DIM)
    up_ref[...] = upstream
    delta_ref[...] = jnp.sum(upstream.astype(f32) * out_ref[...], axis=0, keepdims=True)
    query_sum[...] = jnp.zeros_like(query_sum)

    def key_block(k, carry):
        there = pl.ds(pl.multiple_of(k * step, step), step)
        key, value, key_flat = key_ref[there, :], value_ref[there, :], key_t_ref[:, there]

        def meet(q, sums, masked):
            key_add, value_add = sums
            here = pl.ds(pl.multiple_of(q * step, step), step)
            query, up = query_ref[:, here], up_ref[:, here]
            scores = jnp.dot(key, query, preferred_element_type=f32)
            if masked:
                scores = causal(scores)
            probs = jnp.exp(scores - total_ref[:, here])
            d_probs = jnp.dot(value, up, preferred_element_type=f32)
            d_scores = (probs * (d_probs - delta_ref[:, here])).astype(bf16)
            query_sum[:, here] += jnp.dot(key_flat, d_scores, preferred_element_type=f32)
            contract = (((1,), (1,)), ((), ()))
            key_add = key_add + lax.dot_general(
                query[:HEAD_DIM], d_scores, contract, preferred_element_type=f32
            )
            value_add = value_add + lax.dot_general(
                up, probs.astype(bf16), contract, preferred_element_type=f32
            )
            return key_add, value_add

        zero = jnp.zeros((HEAD_DIM, step), f32)
        sums = meet(k, (zero, zero), True)
        key_add, value_add = lax.fori_loop(
            k + 1, span // step, lambda q, s: meet(q, s, False), sums
        )
        key_sum[:, there] = key_add
        value_sum[:, there] = value_add
        return carry

    lax.fori_loop(0, span // step, key_block, 0)
    cosine, sine = cosine_ref[...], sine_ref[...]
    d_query = unrotate(query_sum[...] * score_scale, cosine, sine).astype(bf16)
    d_key = unrotate(key_sum[...], cosine, sine).astype(bf16)
    d_value = value_sum[...].astype(bf16)
    for block in range(blocks):
        at = slice(block * rows, (block + 1) * rows)
        grad_ref[block, :HEAD_DIM, :] = d_query[:, at]
        grad_ref[block, HEAD_DIM : 2 * HEAD_DIM, :] = d_key[:, at]
        grad_ref[block, 2 * HEAD_DIM :, :] = d_value[:, at]


def attend_back(qkv, length, out, total, upstream, cosine, sine):
    blocks, _, rows = qkv.shape
    span = blocks * rows
    step = min(512, span)
    return pl.pallas_call(
        functools.partial(attend_back_kernel, step),
        out_shape=jax.ShapeDtypeStruct(qkv.shape, bf16),
        in_specs=[pl.BlockSpec(memory_space=pltpu.SMEM)]
        + [pl.BlockSpec(memory_space=pltpu.VMEM)] * 6,
        out_specs=pl.BlockSpec(memory_space=pltpu.VMEM),
        scratch_shapes=[
            pltpu.VMEM((span, 2 * HEAD_DIM), bf16),
            pltpu.VMEM((2 * HEAD_DIM, span), bf16),
            pltpu.VMEM((span, HEAD_DIM), bf16),
            pltpu.VMEM((HEAD_DIM, span), bf16),
            pltpu.VMEM((HEAD_DIM, span), f32),
            pltpu.VMEM((HEAD_DIM, span), f32),
            pltpu.VMEM((HEAD_DIM, span), f32),
            pltpu.VMEM((1, span), f32),
            pltpu.VMEM((HEAD_DIM, span), bf16),
        ],
        compiler_params=pltpu.CompilerParams(vmem_limit_bytes=56 << 20),
    )(length, qkv, out, total, upstream, cosine, sine)


MESH = pl.DeviceIdType.MESH
ANY = pl.BlockSpec(memory_space=pl.ANY)
VMEM = pl.BlockSpec(memory_space=pltpu.VMEM)
DMA = pltpu.SemaphoreType.DMA


def head_place(head, heads, ctx_size, expert_size):
    per = expert_size - 1
    if ctx_size <= expert_size and ctx_size * per == heads:
        row = head // per
        step = head % per
        return row, step + jnp.where(step >= row, 1, 0)
    return head // expert_size, head % expert_size


def head_of(ctx, expert, heads, ctx_size, expert_size):
    per = expert_size - 1
    if ctx_size <= expert_size and ctx_size * per == heads:
        head = ctx * per + expert - jnp.where(expert > ctx, 1, 0)
        return jnp.where(expert == ctx, heads, head)
    return ctx * expert_size + expert


def greet(partners):
    barrier = pltpu.get_barrier_semaphore()
    for partner in partners:
        pl.semaphore_signal(barrier, inc=1, device_id=partner, device_id_type=MESH)
    pl.semaphore_wait(barrier, len(partners))


def trade_kernel(heads, inward, in_ref, out_ref, send_sem, recv_sem):
    ctx_size, expert_size = lax.axis_size("ctx"), lax.axis_size("expert")
    count = ctx_size * expert_size
    ctx, expert = lax.axis_index("ctx"), lax.axis_index("expert")
    me = ctx * expert_size + expert
    mine = head_of(ctx, expert, heads, ctx_size, expert_size)
    holds = mine < heads
    greet(
        [
            {"ctx": ((me + i) % count) // expert_size, "expert": ((me + i) % count) % expert_size}
            for i in range(1, count)
        ]
    )

    def copy(source, target, at, by, there):
        return pltpu.make_async_remote_copy(
            src_ref=in_ref.at[source],
            dst_ref=out_ref.at[target],
            send_sem=send_sem.at[at],
            recv_sem=recv_sem.at[by],
            device_id=there,
            device_id_type=MESH,
        )

    if inward:
        def sends():
            for i in range(heads):
                head = (me + i) % heads
                row, column = head_place(head, heads, ctx_size, expert_size)
                yield head != mine, copy(head, me, head, me, {"ctx": row, "expert": column})

        for needed, one in sends():
            pl.when(needed)(one.start)

        @pl.when(holds)
        def _():
            out_ref[me] = in_ref[mine % heads]

        @pl.when(jnp.logical_not(holds))
        def _():
            out_ref[...] = jnp.zeros_like(out_ref)

        for i in range(1, count):
            source = (me + count - i) % count
            pl.when(holds)(copy(0, source, 0, source, {"ctx": ctx, "expert": expert}).wait_recv)
        for needed, one in sends():
            pl.when(needed)(one.wait_send)
    else:
        def sends():
            for i in range(1, count):
                there = (me + i) % count
                yield copy(
                    there,
                    mine % heads,
                    i,
                    mine % heads,
                    {"ctx": there // expert_size, "expert": there % expert_size},
                )

        for one in sends():
            pl.when(holds)(one.start)

        @pl.when(holds)
        def _():
            out_ref[mine % heads] = in_ref[me]

        for i in range(heads):
            head = (me + i) % heads
            pl.when(head != mine)(copy(0, head, 0, head, {"ctx": ctx, "expert": expert}).wait_recv)
        for one in sends():
            pl.when(holds)(one.wait_send)


def trade(blocks, heads, count, inward, number):
    lead = count if inward else heads
    return pl.pallas_call(
        functools.partial(trade_kernel, heads, inward),
        out_shape=jax.ShapeDtypeStruct((lead,) + blocks.shape[1:], blocks.dtype),
        in_specs=[VMEM],
        out_specs=VMEM,
        scratch_shapes=[DMA((count,)), DMA((count,))],
        compiler_params=pltpu.CompilerParams(
            collective_id=number, has_side_effects=True, vmem_limit_bytes=32 << 20
        ),
    )(blocks)


def across(axis, bit):
    index = lax.axis_index(axis)
    return index + bit * (1 - 2 * ((index // bit) % 2))


def flip(index, mask):
    bit = 1
    while bit <= mask:
        if mask & bit:
            index = index + bit * (1 - 2 * ((index // bit) % 2))
        bit *= 2
    return index


def plan(expert_size, ctx_size, chunk, rows):
    bits = [1 << b for b in range(ctx_size.bit_length() - 1)]
    items = []
    for step in range(expert_size):
        items.append((step, None, chunk, bits if step % 2 == 0 else bits[::-1]))
    half = rows // 2
    items.append((None, 0, half, bits))
    items.append((None, half, rows - half, bits[::-1]))
    return items, bits


def spread_kernel(
    rows_ref, flat_ref, gate_ref, out_ref, flats_ref, gates_ref, z_send, z_recv, send, recv, pair_recv, gate_send,
    gate_recv, gate_z_send, gate_z_recv, local_sem,
):
    dp_size, ctx_size, expert_size = (lax.axis_size(a) for a in ("dp", "ctx", "expert"))
    dp, ctx, expert = (lax.axis_index(a) for a in ("dp", "ctx", "expert"))
    chunk, rows = rows_ref.shape[1], flat_ref.shape[0]
    items, bits = plan(expert_size, ctx_size, chunk, rows)
    own = dp * ctx_size + ctx

    def z_at(step):
        return (expert + step) % expert_size

    def z_from(step):
        return (expert + expert_size - step) % expert_size

    plane = [(d, c) for d in range(dp_size) for c in range(ctx_size) if (d, c) != (0, 0)]
    greet(
        [{"expert": z_at(step)} for step in range(1, expert_size)]
        + [{"dp": (dp + d) % dp_size, "ctx": flip(ctx, c)} for d, c in plane]
    )

    def landed(number, block):
        step, first, size, _ = items[number]
        if step is None:
            return flats_ref.at[block, pl.ds(first, size)]
        return out_ref.at[block, z_from(step)]

    def z_copy(step, landing=False):
        place = z_from(step) if landing else expert
        return pltpu.make_async_remote_copy(
            src_ref=rows_ref.at[z_at(step)],
            dst_ref=out_ref.at[own, place],
            send_sem=z_send.at[step],
            recv_sem=z_recv.at[step],
            device_id={"expert": z_at(step)},
            device_id_type=MESH,
        )

    def gate_z(step, landing=False):
        return pltpu.make_async_remote_copy(
            src_ref=gate_ref.at[z_at(step)],
            dst_ref=gates_ref.at[own, z_from(step) if landing else expert],
            send_sem=gate_z_send.at[step],
            recv_sem=gate_z_recv.at[step],
            device_id={"expert": z_at(step)},
            device_id_type=MESH,
        )

    def gate_plane(d, c, block):
        return pltpu.make_async_remote_copy(
            src_ref=gates_ref.at[block],
            dst_ref=gates_ref.at[block],
            send_sem=gate_send.at[d, c],
            recv_sem=gate_recv.at[d, c],
            device_id={"dp": (dp + d) % dp_size, "ctx": flip(ctx, c)},
            device_id_type=MESH,
        )

    for step in range(1, expert_size):
        gate_z(step).start()
        z_copy(step).start()

    def source(number):
        step, first, size, _ = items[number]
        if step is None:
            return flat_ref.at[pl.ds(first, size)]
        if step == 0:
            return rows_ref.at[expert]
        return landed(number, own)

    def passing(number, mask, bit, origin):
        block = dp * ctx_size + flip(ctx, mask)
        here = landed(number, block)
        return pltpu.make_async_remote_copy(
            src_ref=source(number) if origin else here,
            dst_ref=here,
            send_sem=send.at[number, mask, bits.index(bit)],
            recv_sem=recv.at[number, mask ^ bit],
            device_id={"ctx": flip(ctx, bit)},
            device_id_type=MESH,
        )

    def crossing(number, mask, other, origin):
        block = dp * ctx_size + flip(ctx, mask)
        here = landed(number, block)
        return pltpu.make_async_remote_copy(
            src_ref=source(number) if origin else here,
            dst_ref=here,
            send_sem=send.at[number, mask, len(bits) + other - 1],
            recv_sem=pair_recv.at[number, mask, other - 1],
            device_id={"dp": (dp + other) % dp_size},
            device_id_type=MESH,
        )

    def arrived(number, mask):
        block = dp * ctx_size + flip(ctx, mask)
        here = landed(number, block)
        pltpu.make_async_remote_copy(
            src_ref=here, dst_ref=here, send_sem=send.at[0, 0, 0], recv_sem=recv.at[number, mask],
            device_id={"ctx": ctx}, device_id_type=MESH,
        ).wait_recv()

    started = []

    def begin(number):
        for bit in items[number][3]:
            one = passing(number, 0, bit, True)
            one.start()
            started.append(one)
        for other in range(1, dp_size):
            one = crossing(number, 0, other, True)
            one.start()
            started.append(one)

    def forward(number, place):
        order = items[number][3]
        masks = [0]
        for bit in order[:place]:
            masks = masks + [m | bit for m in masks]
        for mask in [m | order[place] for m in masks]:
            arrived(number, mask)
            for later in order[place + 1 :]:
                one = passing(number, mask, later, False)
                one.start()
                started.append(one)
            for other in range(1, dp_size):
                one = crossing(number, mask, other, False)
                one.start()
                started.append(one)

    ready = [0, expert_size, expert_size + 1]
    kept = [
        pltpu.make_async_copy(source(number), landed(number, own), local_sem.at[i])
        for i, number in enumerate(ready)
    ]
    order = ready + list(range(1, expert_size))
    depth = len(bits)
    for tick in range(len(order) + AHEAD + depth):
        for place in range(depth + 1):
            index = tick if place == 0 else tick - AHEAD - place + 1
            if not 0 <= index < len(order):
                continue
            number = order[index]
            if place:
                forward(number, place - 1)
                continue
            if number not in ready:
                z_copy(number, True).wait_recv()
            begin(number)
            if index == len(ready) - 1:
                for one in kept:
                    one.start()
                gates_ref[own, expert] = gate_ref[expert]
            if index == len(order) - 1:
                for step in range(1, expert_size):
                    gate_z(step, True).wait_recv()
                for d, c in plane:
                    gate_plane(d, c, own).start()
    for d, c in plane:
        gate_plane(d, c, ((dp + d) % dp_size) * ctx_size + flip(ctx, c)).wait_recv()
        gate_plane(d, c, own).wait_send()
    for number in range(len(items)):
        for mask in range(ctx_size):
            for other in range(1, dp_size):
                block = ((dp + dp_size - other) % dp_size) * ctx_size + flip(ctx, mask)
                here = landed(number, block)
                pltpu.make_async_remote_copy(
                    src_ref=here, dst_ref=here, send_sem=send.at[0, 0, 0],
                    recv_sem=pair_recv.at[number, mask, other - 1], device_id={"dp": dp}, device_id_type=MESH,
                ).wait_recv()
    for one in started:
        one.wait_send()
    for step in range(1, expert_size):
        z_copy(step).wait_send()
        gate_z(step).wait_send()
    for one in kept:
        one.wait()


def spread(rows, flat, gate, sizes, number):
    dp_size, ctx_size, expert_size = sizes
    chunk, width = rows.shape[1:]
    count = expert_size + 2
    links = max(ctx_size.bit_length() - 1 + dp_size - 1, 1)
    plane_size = dp_size * ctx_size
    return pl.pallas_call(
        functools.partial(spread_kernel),
        out_shape=(
            jax.ShapeDtypeStruct((plane_size,) + rows.shape, rows.dtype),
            jax.ShapeDtypeStruct((plane_size,) + flat.shape, flat.dtype),
            jax.ShapeDtypeStruct((plane_size,) + gate.shape, gate.dtype),
        ),
        in_specs=[VMEM, VMEM, VMEM],
        out_specs=(ANY, ANY, VMEM),
        scratch_shapes=[
            DMA((expert_size,)),
            DMA((expert_size,)),
            DMA((count, ctx_size, links)),
            DMA((count, ctx_size)),
            DMA((count, ctx_size, dp_size)),
            DMA((dp_size, ctx_size)),
            DMA((dp_size, ctx_size)),
            DMA((expert_size,)),
            DMA((expert_size,)),
            DMA((3,)),
        ],
        compiler_params=pltpu.CompilerParams(
            collective_id=number, has_side_effects=True, vmem_limit_bytes=32 << 20
        ),
    )(rows, flat, gate)


def pieces(kinds, expert_size, ctx_size):
    bits = [1 << b for b in range(ctx_size.bit_length() - 1)]
    moving, staying = [], []
    for array, (by_expert, rows) in enumerate(kinds):
        if by_expert:
            for step in range(expert_size):
                order = bits if (step + array) % 2 == 0 else bits[::-1]
                (moving if step else staying).append((array, step, 0, rows, order))
        else:
            half = rows // 2
            staying.append((array, None, 0, half, bits))
            staying.append((array, None, half, rows - half, bits[::-1]))
    return moving + staying, bits


def home_kernel(kinds, has_dots, has_shared, depth, *refs):
    rest = iter(refs)

    def take(count):
        return [next(rest) for _ in range(count)]

    parts = take(len(kinds))
    dot_ref = next(rest) if has_dots else None
    grads = take(3) if has_shared else []
    outs = take(len(kinds))
    dots_ref = next(rest) if has_dots else None
    grads_out = take(3) if has_shared else []
    mine, theirs, mine_sem, pair_send, pair_recv, send, recv, z_send, z_recv = take(9)
    arrivals = take(depth)

    dp_size, ctx_size, expert_size = (lax.axis_size(a) for a in ("dp", "ctx", "expert"))
    dp, ctx, expert = (lax.axis_index(a) for a in ("dp", "ctx", "expert"))
    items, _ = pieces(kinds, expert_size, ctx_size)
    own = dp * ctx_size + ctx
    other = (dp + 1) % dp_size

    def z_at(step):
        return (expert + step) % expert_size

    def z_from(step):
        return (expert + expert_size - step) % expert_size

    def plane_from(d, c):
        return ((dp + dp_size - d) % dp_size) * ctx_size + flip(ctx, c)

    def plane_at(d, c):
        return ((dp + d) % dp_size) * ctx_size + flip(ctx, c)

    plane = [(d, c) for d in range(dp_size) for c in range(ctx_size) if (d, c) != (0, 0)]
    partners = {(d, c): {"dp": (dp + d) % dp_size, "ctx": flip(ctx, c)} for d, c in plane}
    greet([{"expert": z_at(step)} for step in range(1, expert_size)] + list(partners.values()))

    starts = [0]
    for item in items:
        starts.append(starts[-1] + item[3])

    def held(number):
        return pl.ds(starts[number], items[number][3])

    def piece(number, block):
        array, step, first, size, _ = items[number]
        if step is None:
            return parts[array].at[block, pl.ds(first, size)]
        return parts[array].at[block, z_at(step)]

    def load(number, mask):
        return pltpu.make_async_copy(
            piece(number, dp * ctx_size + flip(ctx, mask)),
            mine.at[mask, held(number)],
            mine_sem.at[number, mask],
        )

    def cross(number, mask):
        return pltpu.make_async_remote_copy(
            src_ref=piece(number, other * ctx_size + flip(ctx, mask)),
            dst_ref=theirs.at[mask, held(number)],
            send_sem=pair_send.at[number, mask],
            recv_sem=pair_recv.at[number, mask],
            device_id={"dp": other},
            device_id_type=MESH,
        )

    for number in range(len(items)):
        for mask in range(ctx_size):
            cross(number, mask).start()
            load(number, mask).start()

    if has_dots:
        dot_in, dot_sum, dot_send, dot_recv, dot_z_send, dot_z_recv = take(6)

        def dot_plane(d, c):
            return pltpu.make_async_remote_copy(
                src_ref=dot_ref.at[plane_at(d, c)],
                dst_ref=dot_in.at[d, c],
                send_sem=dot_send.at[d, c],
                recv_sem=dot_recv.at[d, c],
                device_id=partners[d, c],
                device_id_type=MESH,
            )

        def dot_z(step, landing=False):
            return pltpu.make_async_remote_copy(
                src_ref=dot_sum.at[z_at(step)],
                dst_ref=dots_ref.at[z_from(step) if landing else expert],
                send_sem=dot_z_send.at[step],
                recv_sem=dot_z_recv.at[step],
                device_id={"expert": z_at(step)},
                device_id_type=MESH,
            )

        for d, c in plane:
            dot_plane(d, c).start()

    if has_shared:
        grad_in, column_sum = take(3), take(2)
        grad_send, grad_recv, column_send, column_recv, grad_sem = take(5)
        part = grads[0].shape[2]

        def grad_z(kind, step):
            return pltpu.make_async_remote_copy(
                src_ref=grads[kind].at[z_at(step)],
                dst_ref=grad_in[kind].at[step],
                send_sem=grad_send.at[kind, step],
                recv_sem=grad_recv.at[kind, step],
                device_id={"expert": z_at(step)},
                device_id_type=MESH,
            )

        def grad_own(kind):
            return pltpu.make_async_copy(
                grads[kind].at[expert], grad_in[kind].at[0], grad_sem.at[kind]
            )

        def column(kind, d, c, landing=False):
            at = plane_from(d, c) if landing else own
            return pltpu.make_async_remote_copy(
                src_ref=column_sum[kind].at[plane_at(d, c)],
                dst_ref=grads_out[kind].at[:, pl.ds(pl.multiple_of(at * part, 128), part)],
                send_sem=column_send.at[kind, d, c],
                recv_sem=column_recv.at[kind, d, c],
                device_id=partners[d, c],
                device_id_type=MESH,
            )

        for kind in range(3):
            grad_own(kind).start()
            for step in range(1, expert_size):
                grad_z(kind, step).start()

        def sum_grads():
            for kind in range(3):
                grad_own(kind).wait()
                total = grad_in[kind][0].astype(f32)
                for step in range(1, expert_size):
                    grad_z(kind, step).wait_recv()
                    total = total + grad_in[kind][step].astype(f32)
                if kind == 2:
                    grads_out[2][...] = total
                    continue
                shard = grads_out[kind].shape[0]
                for block in range(dp_size * ctx_size):
                    column_sum[kind][block] = total[block * shard : (block + 1) * shard]
                for d, c in plane:
                    column(kind, d, c).start()
                here = pl.ds(pl.multiple_of(own * part, 128), part)
                grads_out[kind][:, here] = column_sum[kind][own]

    def stage(number, place):
        order = items[number][4][::-1]
        done = sum(order[:place])
        bit = order[place]
        kept = [m for m in range(ctx_size) if not m & (done | bit)]
        return bit, [(m | bit, m) for m in kept]

    def hop(number, place, index):
        bit, moves = stage(number, place)
        return pltpu.make_async_remote_copy(
            src_ref=mine.at[moves[index][0], held(number)],
            dst_ref=arrivals[place].at[index, held(number)],
            send_sem=send.at[number, moves[index][0]],
            recv_sem=recv.at[number, place, index],
            device_id={"ctx": flip(ctx, bit)},
            device_id_type=MESH,
        )

    def z_copy(number, landing=False):
        array, step = items[number][:2]
        return pltpu.make_async_remote_copy(
            src_ref=mine.at[0, held(number)],
            dst_ref=outs[array].at[z_from(step) if landing else expert],
            send_sem=z_send.at[number],
            recv_sem=z_recv.at[number],
            device_id={"expert": z_at(step)},
            device_id_type=MESH,
        )

    def add(number, mask, buffer, index):
        at = held(number)
        mine[mask, at] = (mine[mask, at].astype(f32) + buffer[index, at].astype(f32)).astype(mine.dtype)

    def pair(number):
        leaving = [source for source, _ in stage(number, 0)[1]]
        for mask in leaving + [m for m in range(ctx_size) if m not in leaving]:
            load(number, mask).wait()
            cross(number, mask).wait_recv()
            add(number, mask, theirs, mask)
            if mask in leaving:
                hop(number, 0, leaving.index(mask)).start()

    def step(number, place):
        targets = [target for _, target in stage(number, place)[1]]
        leaving = []
        if place + 1 < depth:
            leaving = [source for source, _ in stage(number, place + 1)[1]]
        for index in range(len(targets)):
            hop(number, place, index).wait_recv()
        for mask in leaving + [m for m in targets if m not in leaving]:
            add(number, mask, arrivals[place], targets.index(mask))
            if mask in leaving:
                hop(number, place + 1, leaving.index(mask)).start()

    def finish(number):
        array, step_z, first, size, _ = items[number]
        if step_z is None:
            outs[array][pl.ds(first, size)] = mine[0, held(number)]
        elif step_z == 0:
            outs[array][expert] = mine[0, held(number)]
        else:
            z_copy(number).start()

    for tick in range(len(items) + AHEAD + depth):
        for place in range(depth + 1):
            number = tick if place == 0 else tick - AHEAD - place + 1
            if not 0 <= number < len(items):
                continue
            if place == 0:
                pair(number)
            else:
                step(number, place - 1)
            if place == depth:
                finish(number)

    if has_dots:
        total = dot_ref[own]
        for d, c in plane:
            dot_plane(d, c).wait_recv()
            total = total + dot_in[d, c]
        dot_sum[...] = total
        for step_z in range(1, expert_size):
            dot_z(step_z).start()
        dots_ref[expert] = dot_sum[expert]
    if has_shared:
        sum_grads()

    moving = [n for n in range(len(items)) if items[n][1]]
    for number in moving:
        z_copy(number, True).wait_recv()
    if has_dots:
        for step_z in range(1, expert_size):
            dot_z(step_z, True).wait_recv()
            dot_z(step_z).wait_send()
        for d, c in plane:
            dot_plane(d, c).wait_send()
    if has_shared:
        for kind in range(3):
            for step_z in range(1, expert_size):
                grad_z(kind, step_z).wait_send()
            if kind < 2:
                for d, c in plane:
                    column(kind, d, c, True).wait_recv()
                    column(kind, d, c).wait_send()
    for number in moving:
        z_copy(number).wait_send()
    for number in range(len(items)):
        for mask in range(ctx_size):
            cross(number, mask).wait_send()
        for place in range(depth):
            for index in range(len(stage(number, place)[1])):
                hop(number, place, index).wait_send()


def bring_home(parts, sizes, number, dots=None, grads=None):
    dp_size, ctx_size, expert_size = sizes
    assert dp_size == 2
    width, dtype = parts[0].shape[-1], parts[0].dtype
    kinds = tuple((part.ndim == 4, part.shape[-2]) for part in parts)
    items, bits = pieces(kinds, expert_size, ctx_size)
    count, depth = len(items), len(bits)
    buffer = (ctx_size, sum(item[3] for item in items), width)
    out_shape = [jax.ShapeDtypeStruct(part.shape[1:], dtype) for part in parts]
    operands, in_specs = list(parts), [ANY] * len(parts)
    scratch = [
        pltpu.VMEM(buffer, dtype),
        pltpu.VMEM(buffer, dtype),
        DMA((count, ctx_size)),
        DMA((count, ctx_size)),
        DMA((count, ctx_size)),
        DMA((count, ctx_size)),
        DMA((count, depth, max(ctx_size // 2, 1))),
        DMA((count,)),
        DMA((count,)),
    ]
    scratch += [pltpu.VMEM((ctx_size >> (place + 1),) + buffer[1:], dtype) for place in range(depth)]
    if dots is not None:
        operands.append(dots)
        in_specs.append(VMEM)
        out_shape.append(jax.ShapeDtypeStruct(dots.shape[1:], dots.dtype))
        scratch += [
            pltpu.VMEM((dp_size, ctx_size) + dots.shape[1:], dots.dtype),
            pltpu.VMEM(dots.shape[1:], dots.dtype),
            DMA((dp_size, ctx_size)),
            DMA((dp_size, ctx_size)),
            DMA((expert_size,)),
            DMA((expert_size,)),
        ]
    if grads is not None:
        operands += list(grads)
        in_specs += [ANY] * 3
        plane_size, part = dp_size * ctx_size, grads[0].shape[2]
        shard = grads[0].shape[1] // plane_size
        columns = jax.ShapeDtypeStruct((shard, plane_size * part), f32)
        out_shape += [columns, columns, jax.ShapeDtypeStruct(grads[2].shape[1:], f32)]
        scratch += [pltpu.VMEM(grad.shape, grad.dtype) for grad in grads]
        scratch += [pltpu.VMEM((plane_size, shard, part), f32)] * 2
        scratch += [
            DMA((3, expert_size)),
            DMA((3, expert_size)),
            DMA((2, dp_size, ctx_size)),
            DMA((2, dp_size, ctx_size)),
            DMA((3,)),
        ]
    return pl.pallas_call(
        functools.partial(home_kernel, kinds, dots is not None, grads is not None, depth),
        out_shape=out_shape,
        in_specs=in_specs,
        out_specs=[VMEM] * len(out_shape),
        scratch_shapes=scratch,
        compiler_params=pltpu.CompilerParams(
            collective_id=number, has_side_effects=True, vmem_limit_bytes=58 << 20
        ),
    )(*operands)


NT = (((1,), (1,)), ((), ()))
TN = (((0,), (0,)), ((), ()))


def contract(a, b, dims=(((1,), (0,)), ((), ()))):
    return lax.dot_general(a, b, dims, preferred_element_type=f32)


def branch(rows, d_out, gate_w, up_w, down_w):
    gate_lin, up_lin = contract(rows, gate_w), contract(rows, up_w)
    sigmoid = 1.0 / (1.0 + jnp.exp(-gate_lin))
    silu = gate_lin * sigmoid
    hidden = (silu * up_lin).astype(bf16)
    d_hidden = contract(d_out, down_w, NT)
    d_gate = (d_hidden * up_lin * (sigmoid + silu * (1.0 - sigmoid))).astype(bf16)
    d_up = (d_hidden * silu).astype(bf16)
    result = contract(hidden, down_w)
    d_rows = contract(d_gate, gate_w, NT) + contract(d_up, up_w, NT)
    d_lin = contract(rows, jnp.concatenate([d_gate, d_up], axis=1), TN)
    d_down = contract(hidden, d_out, TN)
    return result, d_rows, d_lin, d_down


def experts_kernel(
    plane_ref, rows_ref, up_ref, scale_ref, gate_w, up_w, down_w, result_ref, d_rows_ref, dots_ref, gate_grad,
    up_grad, down_grad, rows_f32, up_f32,
):
    planes, expert_size = rows_ref.shape[:2]
    sources = planes * expert_size
    group, width, part = gate_w.shape
    rows_in = rows_ref.at[:, :, 0]

    @pl.when(pl.program_id(1) == 0)
    def _():
        for grad in (gate_grad, up_grad, down_grad):
            grad[...] = jnp.zeros_like(grad)

    def unpack(source, carry):
        there = pl.ds(pl.multiple_of(source * PLACES, 8), PLACES)
        at = source // expert_size, source % expert_size
        rows, up = rows_in[at].astype(f32), up_ref.at[:, :, 0][at].astype(f32)
        for i in range(group):
            rows_f32[i, there] = rows[i * PLACES : (i + 1) * PLACES]
            up_f32[i, there] = up[i * PLACES : (i + 1) * PLACES]
        return carry

    lax.fori_loop(0, sources, unpack, 0)
    for i in range(group):
        rows, up = rows_f32[i].astype(bf16), up_f32[i]
        scale = scale_ref[i][:, :, None]
        by_source = (sources, PLACES, width)
        d_out = (up.reshape(by_source) * scale).reshape(up.shape).astype(bf16)
        result, d_rows, d_lin, d_down = branch(rows, d_out, gate_w[i], up_w[i], down_w[i])
        gate_grad[i] += d_lin[:, :part]
        up_grad[i] += d_lin[:, part:]
        down_grad[i] += d_down
        dots_ref[i] = jnp.sum((result * up).reshape(by_source), axis=-1)
        up_f32[i] = (result.reshape(by_source) * scale).reshape(up.shape)
        rows_f32[i] = d_rows

    def pack(source, carry):
        there = pl.ds(pl.multiple_of(source * PLACES, 8), PLACES)
        at = source // expert_size, source % expert_size
        result_ref.at[:, :, 0][at] = jnp.concatenate([up_f32[i, there] for i in range(group)]).astype(bf16)
        d_rows_ref.at[:, :, 0][at] = jnp.concatenate([rows_f32[i, there] for i in range(group)]).astype(bf16)
        return carry

    lax.fori_loop(0, sources, pack, 0)


def experts(plane, rows, up, scale, gate_w, up_w, down_w):
    plane_size, expert_size, chunk, width = rows.shape
    own, sources = scale.shape[:2]
    part = gate_w.shape[2] // plane_size
    group = 2
    planes = max(16 // expert_size, 1)
    steps = plane_size // planes
    paired = (plane_size, expert_size, own // group, group * PLACES, width)
    rows_spec = pl.BlockSpec((planes, expert_size, 1) + paired[3:], lambda g, c, p: (c, 0, g, 0, 0))
    dots_spec = pl.BlockSpec((group, sources // steps, PLACES), lambda g, c, p: (g, c, 0))
    column = lambda g, c, p: (g, 0, p[0])
    whole = lambda g, c, p: (g, 0, 0)
    result, d_rows, dots, *grads = pl.pallas_call(
        experts_kernel,
        grid_spec=pltpu.PrefetchScalarGridSpec(
            num_scalar_prefetch=1,
            grid=(own // group, steps),
            in_specs=[
                rows_spec,
                rows_spec,
                dots_spec,
                pl.BlockSpec((group, width, part), column),
                pl.BlockSpec((group, width, part), column),
                pl.BlockSpec((group, part, width), lambda g, c, p: (g, p[0], 0)),
            ],
            out_specs=[
                rows_spec,
                rows_spec,
                dots_spec,
                pl.BlockSpec((group, width, part), whole),
                pl.BlockSpec((group, width, part), whole),
                pl.BlockSpec((group, part, width), whole),
            ],
            scratch_shapes=[
                pltpu.VMEM((group, sources // steps * PLACES, width), f32),
                pltpu.VMEM((group, sources // steps * PLACES, width), f32),
            ],
        ),
        out_shape=[
            jax.ShapeDtypeStruct(paired, bf16),
            jax.ShapeDtypeStruct(paired, bf16),
            jax.ShapeDtypeStruct(scale.shape, f32),
            jax.ShapeDtypeStruct((own, width, part), f32),
            jax.ShapeDtypeStruct((own, width, part), f32),
            jax.ShapeDtypeStruct((own, part, width), f32),
        ],
        compiler_params=pltpu.CompilerParams(vmem_limit_bytes=62 << 20),
    )(plane, rows.reshape(paired), up.reshape(paired), scale, gate_w, up_w, down_w)
    return result.reshape(rows.shape), d_rows.reshape(rows.shape), dots, grads


def shared_kernel(
    plane_size, plane_ref, rows_ref, up_ref, gate_w, up_w, down_w, result_ref, d_rows_ref, gate_grad, up_grad,
    down_grad, lin_sum, down_sum,
):
    planes, rows, width = rows_ref.shape
    expert_size, column, part = gate_grad.shape
    shard = column // plane_size
    flat = (planes * rows, width)
    result, d_rows, d_lin, d_down = branch(
        rows_ref[...].reshape(flat), up_ref[...].reshape(flat), gate_w[...], up_w[...], down_w[...]
    )
    result_ref[...] = result.reshape(rows_ref.shape).astype(bf16)
    d_rows_ref[...] = d_rows.reshape(rows_ref.shape).astype(bf16)

    @pl.when(pl.program_id(0) == 0)
    def _():
        lin_sum[...] = jnp.zeros_like(lin_sum)
        down_sum[...] = jnp.zeros_like(down_sum)

    lin_sum[...] += d_lin
    down_sum[...] += d_down

    @pl.when(pl.program_id(0) == pl.num_programs(0) - 1)
    def _():
        for z in range(expert_size):
            firsts = [(p * expert_size + z) * shard for p in range(plane_size)]
            mine = jnp.concatenate([lin_sum[first : first + shard] for first in firsts]).astype(bf16)
            gate_grad[z] = mine[:, :part]
            up_grad[z] = mine[:, part:]
        down_grad[...] = down_sum[...].astype(bf16).reshape(down_grad.shape)


def shared(plane, rows, up, gate_w, up_w, down_w, expert_size):
    plane_size, count, width = rows.shape
    hidden_width = gate_w.shape[1]
    part = hidden_width // plane_size
    planes = 4
    flat = pl.BlockSpec((planes, count, width), lambda c, p: (c, 0, 0))
    columns = (expert_size, width // expert_size, part)
    down = (expert_size, part // expert_size, width)
    return pl.pallas_call(
        functools.partial(shared_kernel, plane_size),
        grid_spec=pltpu.PrefetchScalarGridSpec(
            num_scalar_prefetch=1,
            grid=(plane_size // planes,),
            in_specs=[
                flat,
                flat,
                pl.BlockSpec((width, part), lambda c, p: (0, p[0])),
                pl.BlockSpec((width, part), lambda c, p: (0, p[0])),
                pl.BlockSpec((part, width), lambda c, p: (p[0], 0)),
            ],
            out_specs=[
                flat,
                flat,
                pl.BlockSpec(columns, lambda c, p: (0, 0, 0)),
                pl.BlockSpec(columns, lambda c, p: (0, 0, 0)),
                pl.BlockSpec(down, lambda c, p: (0, 0, 0)),
            ],
            scratch_shapes=[pltpu.VMEM((width, 2 * part), f32), pltpu.VMEM((part, width), f32)],
        ),
        out_shape=[
            jax.ShapeDtypeStruct(rows.shape, bf16),
            jax.ShapeDtypeStruct(rows.shape, bf16),
            jax.ShapeDtypeStruct(columns, bf16),
            jax.ShapeDtypeStruct(columns, bf16),
            jax.ShapeDtypeStruct(down, bf16),
        ],
        compiler_params=pltpu.CompilerParams(vmem_limit_bytes=58 << 20),
    )(plane, rows, up, gate_w, up_w, down_w)


def local(
    tokens,
    lengths,
    routes,
    norm1_gain,
    query_weight,
    key_weight,
    value_weight,
    output_weight,
    norm2_gain,
    router_weight,
    expert_gate,
    expert_up,
    expert_down,
    shared_gate,
    shared_up,
    shared_down,
    cotangent,
):
    dp_size, ctx_size, expert_size = (lax.axis_size(a) for a in ("dp", "ctx", "expert"))
    plane_size, slot_size = dp_size * ctx_size, ctx_size * expert_size
    rows, width = tokens.shape[1:]
    heads = width // HEAD_DIM
    own = EXPERTS // expert_size
    plane = lax.axis_index("dp") * ctx_size + lax.axis_index("ctx")
    first_row = (lax.axis_index("ctx") * expert_size + lax.axis_index("expert")) * rows
    positions = first_row + jnp.arange(rows, dtype=jnp.int32)
    length = lengths[0]
    live_rows = positions < length
    valid = live_rows.astype(f32)[:, None]
    inputs = tokens[0].astype(f32)
    upstream = cotangent[0].astype(f32)
    d_branch = valid * upstream
    d_branch_low = d_branch.astype(bf16)

    route_ids = routes[0]
    expert_range = jnp.arange(EXPERTS, dtype=jnp.int32)
    picked = (route_ids[:, :, None] == expert_range).astype(f32)
    expert_hits = (
        ((route_ids[:, :, None] == expert_range) & live_rows[:, None, None])
        .astype(jnp.int32)
        .reshape(rows * TOP, EXPERTS)
    )
    places = jnp.sum((jnp.cumsum(expert_hits, axis=0) - 1) * expert_hits, axis=-1)
    live_pairs = jnp.broadcast_to(live_rows[:, None], (rows, TOP)).reshape(-1)
    slot_ids = jnp.where(live_pairs, route_ids.reshape(-1) * PLACES + places, -1)
    dispatch = (
        slot_ids[:, None] == jnp.arange(EXPERTS * PLACES, dtype=jnp.int32)[None, :]
    ).reshape(rows, TOP, EXPERTS * PLACES)
    either = jnp.any(dispatch, axis=1).astype(bf16)

    sizes = (dp_size, ctx_size, expert_size)

    def place_rows(flat):
        placed = jnp.einsum("ts,td->sd", either, flat, preferred_element_type=f32).astype(bf16)
        return placed.reshape(expert_size, -1, width)

    def to_experts(blocks):
        here = lax.axis_index("expert")
        taken = [lax.dynamic_index_in_dim(blocks, here, 0, False)]
        for step in range(1, expert_size):
            sent = lax.dynamic_index_in_dim(blocks, (here + step) % expert_size, 0, False)
            ring = [(i, (i + step) % expert_size) for i in range(expert_size)]
            taken.append(lax.ppermute(sent, "expert", ring))
        return jnp.take(jnp.stack(taken), (here - jnp.arange(expert_size)) % expert_size, axis=0)

    up_rows = lax.all_gather(to_experts(place_rows(d_branch_low)), PLANE, axis=0)
    up_flat = lax.all_gather(d_branch_low, PLANE, axis=0)

    scale_one = rms_scale(inputs)
    normal_one = inputs * scale_one
    normed_low = (normal_one * norm1_gain).astype(bf16)
    cosine, sine = rope_tables(positions)

    def project(weight):
        lin = jnp.dot(normed_low, weight, preferred_element_type=f32)
        return jnp.transpose(lin).reshape(heads, HEAD_DIM, rows)

    def rotated(lin_t):
        half = HEAD_DIM // 2
        first, second = lin_t[:, :half], lin_t[:, half:]
        return jnp.concatenate(
            [first * cosine - second * sine, second * cosine + first * sine], axis=1
        )

    query = rotated(project(query_weight)).astype(bf16)
    key = rotated(project(key_weight)).astype(bf16)
    value = project(value_weight).astype(bf16)

    def to_heads(blocks, number):
        return trade(blocks, heads, slot_size, True, number)

    def from_heads(blocks, number):
        return trade(blocks, heads, slot_size, False, number)

    def by_block(flat_t):
        return jnp.transpose(flat_t.reshape(-1, slot_size, rows), (1, 0, 2))

    qkv = to_heads(jnp.concatenate([query, key, value], axis=1), 1)
    normed_all = lax.all_gather(normed_low, SLOT, axis=0, tiled=True)
    out_t, log_total = attend(qkv, lengths)
    attended = jnp.transpose(
        from_heads(by_block(out_t.astype(bf16)), 2).reshape(width, rows)
    )
    attn_out = jnp.dot(attended, output_weight, preferred_element_type=f32)
    hidden_in = inputs + valid * attn_out

    scale_two = rms_scale(hidden_in)
    normal_two = hidden_in * scale_two
    normed_two_low = (normal_two * norm2_gain).astype(bf16)
    logits = jnp.dot(normed_two_low, router_weight, preferred_element_type=f32)
    chosen = jnp.sum(picked * logits[:, None, :], axis=-1)
    shifted = jnp.exp(chosen - jnp.max(chosen, axis=-1, keepdims=True))
    gate_weights = shifted / jnp.sum(shifted, axis=-1, keepdims=True)

    gate_rows = jnp.sum(jnp.where(dispatch, gate_weights[:, :, None], 0.0), axis=(0, 1))
    placed_rows = EXPERTS * PLACES

    def tiled(row):
        row = row.reshape(row.shape[:-1] + (expert_size, 1, -1))
        return jnp.pad(row, [(0, 0)] * (row.ndim - 2) + [(0, 7), (0, 128 - row.shape[-1])])

    def flat_row(tile):
        return tile[..., 0, : own * PLACES].reshape(tile.shape[:-3] + (placed_rows,))

    in_rows, in_flat, gate_all = spread(
        place_rows(normed_two_low), normed_two_low, tiled(gate_rows), sizes, 3
    )
    sources = plane_size * expert_size
    scale = jnp.swapaxes(flat_row(gate_all).reshape(sources, own, PLACES), 0, 1)
    plane_at = plane.astype(jnp.int32)[None]
    shared_result, shared_d, *shared_grads = shared(
        plane_at, in_flat, up_flat, shared_gate, shared_up, shared_down, expert_size
    )
    result, d_rows, dots, expert_grads = experts(
        plane_at, in_rows, up_rows, scale, expert_gate, expert_up, expert_down
    )
    dots = tiled(jnp.swapaxes(dots, 0, 1).reshape(plane_size, placed_rows))

    def collect(back, flat):
        spread_rows = jnp.dot(either, back.reshape(placed_rows, width), preferred_element_type=f32)
        return spread_rows + flat.astype(f32)

    back, flat, d_gate_rows = bring_home([d_rows, shared_d], sizes, 4, dots=dots)
    d_gate_rows = flat_row(d_gate_rows)
    d_gates = jnp.sum(jnp.where(dispatch, d_gate_rows, 0.0), axis=-1)
    d_chosen = gate_weights * (
        d_gates - jnp.sum(gate_weights * d_gates, axis=-1, keepdims=True)
    )
    d_logits = jnp.sum(picked * d_chosen[:, :, None], axis=1).astype(bf16)
    d_router = jnp.einsum("td,te->de", normed_two_low, d_logits, preferred_element_type=f32)
    d_normed_two = collect(back, flat) + jnp.einsum(
        "te,de->td", d_logits, router_weight, preferred_element_type=f32
    )
    d_gain_two = jnp.sum(d_normed_two * normal_two, axis=0)
    d_hidden_in = upstream + rms_back(normal_two, scale_two, norm2_gain, d_normed_two)

    d_attn_low = (valid * d_hidden_in).astype(bf16)
    d_output_weight = jnp.einsum("td,te->de", attended, d_attn_low, preferred_element_type=f32)
    d_attended = jnp.einsum("te,de->dt", d_attn_low, output_weight, preferred_element_type=f32)
    d_attended = to_heads(d_attended.astype(bf16).reshape(heads, HEAD_DIM, rows), 6)
    all_cosine, all_sine = rope_tables(jnp.arange(slot_size * rows, dtype=jnp.int32))
    d_qkv = attend_back(qkv, lengths, out_t, log_total, d_attended, all_cosine, all_sine)
    d_mine = from_heads(d_qkv, 7)

    shard = width // (dp_size * slot_size)
    devices = (plane_size, expert_size)
    small = jnp.concatenate(
        [
            d_router.reshape(devices + (1, shard * EXPERTS)),
            d_gain_two.reshape(devices + (1, shard)),
            jnp.zeros(devices + (1, width - shard * (EXPERTS + 1)), f32),
        ],
        axis=-1,
    )
    extra = jnp.concatenate([d_output_weight.reshape(devices + (shard, width)), small], axis=2)
    extra = jnp.pad(extra, [(0, 0), (0, 0), (0, -(shard + 1) % 16), (0, 0)]).astype(bf16)
    out_back, out_flat, extra, shared_gate_grad, shared_up_grad, shared_down_grad = bring_home(
        [result, shared_result, extra], sizes, 5, grads=shared_grads
    )
    extra = jnp.sum(extra.astype(f32), axis=0)
    output_rows = hidden_in + valid * collect(out_back, out_flat)
    output_rows = output_rows.astype(bf16)[None]

    head_grad = jnp.einsum(
        "bet,btd->ed", d_qkv, normed_all.reshape(slot_size, rows, width), preferred_element_type=f32
    )
    d_own = jnp.swapaxes(d_mine.reshape(heads, 3, HEAD_DIM, rows), 0, 1)
    d_own = d_own.reshape(3, width, rows)
    d_normed = jnp.zeros((width, rows), f32)
    for weight, grad in zip((query_weight, key_weight, value_weight), d_own):
        d_normed = d_normed + jnp.dot(weight, grad, preferred_element_type=f32)
    d_normed = jnp.transpose(d_normed)
    d_gain_one = jnp.sum(d_normed * normal_one, axis=0)
    input_grad = d_hidden_in + rms_back(normal_one, scale_one, norm1_gain, d_normed)
    input_grad = input_grad.astype(bf16)[None]

    head_grad = jnp.transpose(head_grad).reshape(-1, 3 * HEAD_DIM)
    head_grad = lax.psum_scatter(head_grad, "dp", scatter_dimension=0, tiled=True)
    head_grad = from_heads(head_grad.reshape(slot_size, shard, 3 * HEAD_DIM), 8)
    head_grad = jnp.transpose(
        head_grad.reshape(heads, shard, 3, HEAD_DIM), (2, 1, 0, 3)
    ).reshape(3, shard, width)
    linear = plane * expert_size + lax.axis_index("expert")
    d_gain_one = lax.psum(d_gain_one, ("dp", "ctx", "expert"))
    d_gain_one = lax.dynamic_slice_in_dim(d_gain_one, linear * shard, shard, 0)
    return (
        output_rows,
        input_grad,
        d_gain_one,
        head_grad[0],
        head_grad[1],
        head_grad[2],
        extra[:shard],
        extra[shard, shard * EXPERTS : shard * (EXPERTS + 1)],
        extra[shard, : shard * EXPERTS].reshape(shard, EXPERTS),
        *expert_grads,
        shared_gate_grad,
        shared_up_grad,
        shared_down_grad,
    )


def solution(mesh):
    tokens = P("dp", ("ctx", "expert"), None)
    whole = P()
    experts = P("expert", None, None)
    everywhere = ("dp", "ctx", "expert")
    return jax.shard_map(
        local,
        mesh=mesh,
        in_specs=(tokens, P("dp"), tokens)
        + (whole,) * 7
        + (experts,) * 3
        + (whole,) * 3
        + (tokens,),
        out_specs=(tokens, tokens, P(everywhere))
        + (P(everywhere, None),) * 4
        + (P(everywhere), P(everywhere, None))
        + (P("expert", None, PLANE),) * 2
        + (P("expert", PLANE, None),)
        + (P(everywhere, None),) * 3,
        check_vma=False,
    )
```

```python
import functools

import jax
import jax.numpy as jnp
from jax import lax
from jax.experimental import pallas as pl
from jax.experimental.pallas import tpu as pltpu
from jax.sharding import PartitionSpec as P

HEAD_DIM = 64
EXPERTS = 16
TOP = 2
CAP = 22
PLACES = 24

norm_epsilon = 1e-06
rope_base = 10000.0
score_scale = 0.125
masked_value = -1e30
PLANE = ("dp", "ctx")
SLOT = ("ctx", "expert")
AHEAD = 2
bf16 = jnp.bfloat16
f32 = jnp.float32


def rms_scale(values):
    return lax.rsqrt(jnp.mean(values * values, axis=-1, keepdims=True) + norm_epsilon)


def rms_back(normal, scale, gain, upstream):
    lifted = upstream * gain
    return scale * (lifted - normal * jnp.mean(lifted * normal, axis=-1, keepdims=True))


def rope_tables(positions):
    half = HEAD_DIM // 2
    exponent = jnp.arange(half, dtype=f32) * (2.0 / HEAD_DIM)
    inverse_freq = rope_base ** (-exponent)
    angles = inverse_freq[:, None] * positions[None, :].astype(f32)
    return jnp.cos(angles), jnp.sin(angles)


def head_rows(qkv_ref, first, count):
    return jnp.concatenate(
        [qkv_ref[block, first : first + count, :] for block in range(qkv_ref.shape[0])], axis=1
    )


def live_keys(key_t, length):
    span = key_t.shape[1]
    place = lax.broadcasted_iota(jnp.int32, (8, span), 1)
    row = lax.broadcasted_iota(jnp.int32, (8, span), 0)
    bias = jnp.where((place >= length) & (row == 0), masked_value, 0.0)
    padded = jnp.concatenate(
        [key_t.astype(f32), bias, jnp.zeros((HEAD_DIM - 8, span), f32)], axis=0
    )
    return jnp.transpose(padded).astype(bf16)


def scaled_queries(query_t):
    span = query_t.shape[1]
    row = lax.broadcasted_iota(jnp.int32, (HEAD_DIM, span), 0)
    ones = jnp.where(row == 0, 1.0, 0.0)
    return jnp.concatenate([query_t.astype(f32) * score_scale, ones], axis=0).astype(bf16)


def causal(scores):
    key = lax.broadcasted_iota(jnp.int32, scores.shape, 0)
    query = lax.broadcasted_iota(jnp.int32, scores.shape, 1)
    return jnp.where(key <= query, scores, masked_value)


MESH = pl.DeviceIdType.MESH
ANY = pl.BlockSpec(memory_space=pl.ANY)
VMEM = pl.BlockSpec(memory_space=pltpu.VMEM)
SMEM = pl.BlockSpec(memory_space=pltpu.SMEM)
DMA = pltpu.SemaphoreType.DMA


def head_place(head, heads, ctx_size, expert_size):
    per = expert_size - 1
    if ctx_size <= expert_size and ctx_size * per == heads:
        row = head // per
        step = head % per
        return row, step + jnp.where(step >= row, 1, 0)
    return head // expert_size, head % expert_size


def head_of(ctx, expert, heads, ctx_size, expert_size):
    per = expert_size - 1
    if ctx_size <= expert_size and ctx_size * per == heads:
        head = ctx * per + expert - jnp.where(expert > ctx, 1, 0)
        return jnp.where(expert == ctx, heads, head)
    return ctx * expert_size + expert


def sizes_of():
    return tuple(lax.axis_size(a) for a in ("dp", "ctx", "expert"))


def greet(partners):
    barrier = pltpu.get_barrier_semaphore()
    for partner in partners:
        pl.semaphore_signal(barrier, inc=1, device_id=partner, device_id_type=MESH)
    pl.semaphore_wait(barrier, len(partners))


GROUP = 2


def flip(index, mask):
    bit = 1
    while bit <= mask:
        if mask & bit:
            index = index + bit * (1 - 2 * ((index // bit) % 2))
        bit *= 2
    return index


def bits_of(ctx_size):
    return [1 << b for b in range(ctx_size.bit_length() - 1)]


def group_bit(group, ctx_size):
    bits = bits_of(ctx_size)
    return bits[group % len(bits)]


def subsets(order):
    masks = [0]
    for bit in order:
        masks = masks + [m | bit for m in masks]
    return masks


class Piece:
    def __init__(self, array, kind, group, step, first, size, order):
        self.array, self.kind, self.group, self.step = array, kind, group, step
        self.first, self.size, self.order = first, size, order
        self.masks = subsets(order)


def pieces(kinds, expert_size, ctx_size):
    bits = bits_of(ctx_size)
    moving, staying = [], []
    for array, (kind, groups, rows) in enumerate(kinds):
        if kind == "flat":
            half = rows // 2
            staying.append(Piece(array, kind, None, None, 0, half, bits))
            staying.append(Piece(array, kind, None, None, half, rows - half, bits[::-1]))
            continue
        for step in range(expert_size):
            for group in range(groups or 1):
                if kind == "group":
                    order = [group_bit(group, ctx_size)]
                else:
                    order = bits if (step + array) % 2 == 0 else bits[::-1]
                (moving if step else staying).append(Piece(array, kind, group, step, 0, rows, order))
    return moving, staying


def plane_partners():
    dp_size, ctx_size, expert_size = sizes_of()
    dp, ctx, expert = (lax.axis_index(a) for a in ("dp", "ctx", "expert"))
    plane = [(d, c) for d in range(dp_size) for c in range(ctx_size) if (d, c) != (0, 0)]
    return [{"expert": (expert + step) % expert_size} for step in range(1, expert_size)] + [
        {"dp": (dp + d) % dp_size, "ctx": flip(ctx, c)} for d, c in plane
    ]


def spread_kernel(kinds, has_gate, *refs):
    greet(plane_partners())
    for _ in spread_steps(kinds, has_gate, refs):
        pass


def spread_steps(kinds, has_gate, refs):
    rest = iter(refs)

    def take(count):
        return [next(rest) for _ in range(count)]

    ins = take(len(kinds))
    gate_ref = next(rest) if has_gate else None
    outs = take(len(kinds))
    gates_ref = next(rest) if has_gate else None
    z_send, z_recv, send, recv, pair_recv, local_sem = take(6)
    if has_gate:
        gate_send, gate_recv, gate_z_send, gate_z_recv = take(4)
    dp_size, ctx_size, expert_size = (lax.axis_size(a) for a in ("dp", "ctx", "expert"))
    dp, ctx, expert = (lax.axis_index(a) for a in ("dp", "ctx", "expert"))
    moving, staying = pieces(kinds, expert_size, ctx_size)
    order = staying + moving
    own = dp * ctx_size + ctx
    other = (dp + 1) % dp_size

    def z_at(step):
        return (expert + step) % expert_size

    def z_from(step):
        return (expert + expert_size - step) % expert_size

    plane = [(d, c) for d in range(dp_size) for c in range(ctx_size) if (d, c) != (0, 0)]

    def landed(piece, core, mask, at=0):
        if piece.step is None:
            block = (dp if core == 0 else other) * ctx_size + flip(ctx, mask)
            return outs[piece.array].at[block, pl.ds(piece.first, piece.size)]
        return outs[piece.array].at[piece.group, core * 2 + (1 if mask ^ at else 0), z_from(piece.step)]

    def z_copy(piece, landing=False):
        place = z_from(piece.step) if landing else expert
        return pltpu.make_async_remote_copy(
            src_ref=ins[piece.array].at[z_at(piece.step), piece.group],
            dst_ref=outs[piece.array].at[piece.group, 0, place],
            send_sem=z_send.at[number[id(piece)]],
            recv_sem=z_recv.at[number[id(piece)]],
            device_id={"expert": z_at(piece.step)},
            device_id_type=MESH,
        )

    def gate_z(step, landing=False):
        return pltpu.make_async_remote_copy(
            src_ref=gate_ref.at[z_at(step)],
            dst_ref=gates_ref.at[own, z_from(step) if landing else expert],
            send_sem=gate_z_send.at[step],
            recv_sem=gate_z_recv.at[step],
            device_id={"expert": z_at(step)},
            device_id_type=MESH,
        )

    def gate_plane(d, c, block):
        return pltpu.make_async_remote_copy(
            src_ref=gates_ref.at[block],
            dst_ref=gates_ref.at[block],
            send_sem=gate_send.at[d, c],
            recv_sem=gate_recv.at[d, c],
            device_id={"dp": (dp + d) % dp_size, "ctx": flip(ctx, c)},
            device_id_type=MESH,
        )

    number = {id(piece): i for i, piece in enumerate(order)}
    def z_starts():
        if has_gate:
            for step in range(1, expert_size):
                gate_z(step).start()
        for piece in moving:
            z_copy(piece).start()

    def source(piece):
        if piece.step is None:
            return ins[piece.array].at[pl.ds(piece.first, piece.size)]
        if piece.step == 0:
            return ins[piece.array].at[expert, piece.group]
        return landed(piece, 0, 0)

    bits = bits_of(ctx_size)

    def passing(piece, mask, bit):
        return pltpu.make_async_remote_copy(
            src_ref=landed(piece, 0, mask) if mask else source(piece),
            dst_ref=landed(piece, 0, mask, bit),
            send_sem=send.at[number[id(piece)], mask, bits.index(bit)],
            recv_sem=recv.at[number[id(piece)], mask ^ bit],
            device_id={"ctx": flip(ctx, bit)},
            device_id_type=MESH,
        )

    def arrived(piece, mask):
        here = landed(piece, 0, mask)
        return pltpu.make_async_remote_copy(
            src_ref=here, dst_ref=here, send_sem=send.at[0, 0, 0],
            recv_sem=recv.at[number[id(piece)], mask], device_id={"ctx": ctx}, device_id_type=MESH,
        )

    def crossing(piece, mask, landing=False):
        if piece.step is None:
            there = landed(piece, 1 if landing else 0, mask)
        else:
            there = landed(piece, 1, mask)
        return pltpu.make_async_remote_copy(
            src_ref=landed(piece, 0, mask) if mask else source(piece),
            dst_ref=there,
            send_sem=send.at[number[id(piece)], mask, len(bits)],
            recv_sem=pair_recv.at[number[id(piece)], mask],
            device_id={"dp": other},
            device_id_type=MESH,
        )

    started = []

    def begin(one):
        one.start()
        started.append(one)

    def first(piece):
        for bit in piece.order:
            begin(passing(piece, 0, bit))
        begin(crossing(piece, 0))

    def forward(piece, place):
        bit = piece.order[place]
        for mask in [m | bit for m in subsets(piece.order[:place])]:
            arrived(piece, mask).wait_recv()
            for later in piece.order[place + 1 :]:
                begin(passing(piece, mask, later))
            begin(crossing(piece, mask))

    kept = [
        pltpu.make_async_copy(source(piece), landed(piece, 0, 0), local_sem.at[i])
        for i, piece in enumerate(staying)
    ]
    depth = len(bits)
    if has_gate:
        z_starts()
    for tick in range(len(order) + AHEAD + depth):
        for place in range(depth + 1):
            index = tick if place == 0 else tick - AHEAD - place + 1
            if not 0 <= index < len(order):
                continue
            piece = order[index]
            if place:
                if place <= len(piece.order):
                    forward(piece, place - 1)
                continue
            if piece.step:
                z_copy(piece, True).wait_recv()
            first(piece)
            if index == len(staying) - 1:
                for one in kept:
                    one.start()
                if has_gate:
                    gates_ref[own, expert] = gate_ref[expert]
                else:
                    yield
                    z_starts()
            if has_gate and index == len(order) - 1:
                for step in range(1, expert_size):
                    gate_z(step, True).wait_recv()
                for d, c in plane:
                    gate_plane(d, c, own).start()
        if tick >= len(staying) - 1:
            yield
    if has_gate:
        for d, c in plane:
            gate_plane(d, c, ((dp + d) % dp_size) * ctx_size + flip(ctx, c)).wait_recv()
            gate_plane(d, c, own).wait_send()
    for piece in order:
        for mask in piece.masks:
            crossing(piece, mask, True).wait_recv()
    for one in started:
        one.wait_send()
    for piece in moving:
        z_copy(piece).wait_send()
    if has_gate:
        for step in range(1, expert_size):
            gate_z(step).wait_send()
    for one in kept:
        one.wait()


def spread_plan(arrays, gate, sizes):
    dp_size, ctx_size, expert_size = sizes
    assert dp_size == 2
    plane_size = dp_size * ctx_size
    kinds, out_shape = [], []
    for array in arrays:
        if array.ndim == 4:
            kinds.append(("group", array.shape[1], array.shape[2]))
            shape = (array.shape[1], 4, expert_size) + array.shape[2:]
        else:
            kinds.append(("flat", None, array.shape[0]))
            shape = (plane_size,) + array.shape
        out_shape.append(jax.ShapeDtypeStruct(shape, array.dtype))
    moving, staying = pieces(kinds, expert_size, ctx_size)
    count = len(moving + staying)
    scratch = [
        DMA((count,)),
        DMA((count,)),
        DMA((count, ctx_size, len(bits_of(ctx_size)) + 1)),
        DMA((count, ctx_size)),
        DMA((count, ctx_size)),
        DMA((len(staying),)),
    ]
    if gate is not None:
        out_shape.append(jax.ShapeDtypeStruct((plane_size,) + gate.shape, gate.dtype))
        scratch += [DMA((dp_size, ctx_size))] * 2 + [DMA((expert_size,))] * 2
    return tuple(kinds), out_shape, scratch


def spread(arrays, gate, sizes, number):
    kinds, out_shape, scratch = spread_plan(arrays, gate, sizes)
    return pl.pallas_call(
        functools.partial(spread_kernel, kinds, True),
        out_shape=out_shape,
        in_specs=[VMEM] * (len(arrays) + 1),
        out_specs=[ANY] * len(arrays) + [VMEM],
        scratch_shapes=scratch,
        compiler_params=pltpu.CompilerParams(
            collective_id=number, has_side_effects=True, vmem_limit_bytes=32 << 20
        ),
    )(*arrays, gate)


def stage(piece, place):
    order = piece.order[::-1]
    done, bit = sum(order[:place]), order[place]
    kept = [m for m in piece.masks if not m & (done | bit)]
    return bit, [(m | bit, m) for m in kept]


def buffer_places(order):
    held, arriving, here, there = {}, {}, 0, 0
    for piece in order:
        for mask in piece.masks:
            held[id(piece), mask] = here
            here += piece.size
        for place in range(len(piece.order)):
            for index in range(len(stage(piece, place)[1])):
                arriving[id(piece), place, index] = there
                there += piece.size
    held["rows"], arriving["rows"] = here, there
    return held, arriving


def home_kernel(kinds, has_dots, has_shared, masks, ins, outs, *refs):
    ins += len(masks)
    outs += len(masks)
    refs = list(refs)
    carried, carried_out = refs[ins - len(masks) : ins], refs[ins + outs - len(masks) : ins + outs]
    carry = []
    if masks:
        carry = carry_copies(masks, carried, carried_out, *refs[-2:])
        del refs[-2:], refs[ins + outs - len(masks) : ins + outs], refs[ins - len(masks) : ins]
    greet(plane_partners())
    steps = home_steps(kinds, has_dots, has_shared, refs)
    next(steps)
    for one in carry:
        one.start()
    for _ in steps:
        pass
    for one in carry:
        one.wait()


def home_steps(kinds, has_dots, has_shared, refs):
    rest = iter(refs)

    def take(count):
        return [next(rest) for _ in range(count)]

    parts = take(len(kinds))
    dot_ref = next(rest) if has_dots else None
    grads = take(3) if has_shared else []
    outs = take(len(kinds))
    dots_ref = next(rest) if has_dots else None
    grads_out = take(3) if has_shared else []
    mine, theirs, arrivals, mine_sem, pair_send, pair_recv, send, recv, z_send, z_recv = take(10)

    dp_size, ctx_size, expert_size = (lax.axis_size(a) for a in ("dp", "ctx", "expert"))
    dp, ctx, expert = (lax.axis_index(a) for a in ("dp", "ctx", "expert"))
    moving, staying = pieces(kinds, expert_size, ctx_size)
    order = moving + staying
    number = {id(piece): i for i, piece in enumerate(order)}
    own = dp * ctx_size + ctx
    other = (dp + 1) % dp_size

    def z_at(step):
        return (expert + step) % expert_size

    def z_from(step):
        return (expert + expert_size - step) % expert_size

    def plane_from(d, c):
        return ((dp + dp_size - d) % dp_size) * ctx_size + flip(ctx, c)

    def plane_at(d, c):
        return ((dp + d) % dp_size) * ctx_size + flip(ctx, c)

    plane = [(d, c) for d in range(dp_size) for c in range(ctx_size) if (d, c) != (0, 0)]
    partners = {(d, c): {"dp": (dp + d) % dp_size, "ctx": flip(ctx, c)} for d, c in plane}
    held, arriving = buffer_places(order)

    def whole(piece, core, mask):
        if piece.kind == "group":
            return parts[piece.array].at[piece.group, core * 2 + (1 if mask else 0), z_at(piece.step)]
        block = (dp if core == 0 else other) * ctx_size + flip(ctx, mask)
        if piece.kind == "flat":
            return parts[piece.array].at[block, pl.ds(piece.first, piece.size)]
        return parts[piece.array].at[block, z_at(piece.step)]

    def at(piece, mask):
        return pl.ds(held[id(piece), mask], piece.size)

    def load(piece, mask):
        return pltpu.make_async_copy(
            whole(piece, 0, mask), mine.at[at(piece, mask)], mine_sem.at[number[id(piece)], mask]
        )

    def cross(piece, mask):
        return pltpu.make_async_remote_copy(
            src_ref=whole(piece, 1, mask),
            dst_ref=theirs.at[at(piece, mask)],
            send_sem=pair_send.at[number[id(piece)], mask],
            recv_sem=pair_recv.at[number[id(piece)], mask],
            device_id={"dp": other},
            device_id_type=MESH,
        )

    for piece in order:
        for mask in piece.masks:
            cross(piece, mask).start()
            load(piece, mask).start()

    if has_dots:
        dot_in, dot_sum, dot_send, dot_recv, dot_z_send, dot_z_recv = take(6)

        def dot_plane(d, c):
            return pltpu.make_async_remote_copy(
                src_ref=dot_ref.at[plane_at(d, c)],
                dst_ref=dot_in.at[d, c],
                send_sem=dot_send.at[d, c],
                recv_sem=dot_recv.at[d, c],
                device_id=partners[d, c],
                device_id_type=MESH,
            )

        def dot_z(step, landing=False):
            return pltpu.make_async_remote_copy(
                src_ref=dot_sum.at[z_at(step)],
                dst_ref=dots_ref.at[z_from(step) if landing else expert],
                send_sem=dot_z_send.at[step],
                recv_sem=dot_z_recv.at[step],
                device_id={"expert": z_at(step)},
                device_id_type=MESH,
            )

        for d, c in plane:
            dot_plane(d, c).start()

    if has_shared:
        grad_in, column_sum = take(3), take(2)
        grad_send, grad_recv, column_send, column_recv, grad_sem = take(5)
        part = grads[0].shape[2]

        def grad_z(kind, step):
            return pltpu.make_async_remote_copy(
                src_ref=grads[kind].at[z_at(step)],
                dst_ref=grad_in[kind].at[step],
                send_sem=grad_send.at[kind, step],
                recv_sem=grad_recv.at[kind, step],
                device_id={"expert": z_at(step)},
                device_id_type=MESH,
            )

        def grad_own(kind):
            return pltpu.make_async_copy(
                grads[kind].at[expert], grad_in[kind].at[0], grad_sem.at[kind]
            )

        def column(kind, d, c, landing=False):
            at = plane_from(d, c) if landing else own
            return pltpu.make_async_remote_copy(
                src_ref=column_sum[kind].at[plane_at(d, c)],
                dst_ref=grads_out[kind].at[:, pl.ds(pl.multiple_of(at * part, 128), part)],
                send_sem=column_send.at[kind, d, c],
                recv_sem=column_recv.at[kind, d, c],
                device_id=partners[d, c],
                device_id_type=MESH,
            )

        for kind in range(3):
            grad_own(kind).start()
            for step in range(1, expert_size):
                grad_z(kind, step).start()

        def sum_grads():
            for kind in range(3):
                grad_own(kind).wait()
                total = grad_in[kind][0].astype(f32)
                for step in range(1, expert_size):
                    grad_z(kind, step).wait_recv()
                    total = total + grad_in[kind][step].astype(f32)
                if kind == 2:
                    grads_out[2][...] = total
                    continue
                shard = grads_out[kind].shape[0]
                for block in range(dp_size * ctx_size):
                    column_sum[kind][block] = total[block * shard : (block + 1) * shard]
                for d, c in plane:
                    column(kind, d, c).start()
                here = pl.ds(pl.multiple_of(own * part, 128), part)
                grads_out[kind][:, here] = column_sum[kind][own]

    def hop(piece, place, index):
        bit, moves = stage(piece, place)
        return pltpu.make_async_remote_copy(
            src_ref=mine.at[at(piece, moves[index][0])],
            dst_ref=arrivals.at[pl.ds(arriving[id(piece), place, index], piece.size)],
            send_sem=send.at[number[id(piece)], moves[index][0]],
            recv_sem=recv.at[number[id(piece)], place, index],
            device_id={"ctx": flip(ctx, bit)},
            device_id_type=MESH,
        )

    def z_copy(piece, landing=False):
        place = z_from(piece.step) if landing else expert
        out = outs[piece.array]
        return pltpu.make_async_remote_copy(
            src_ref=mine.at[at(piece, 0)],
            dst_ref=out.at[place, piece.group] if piece.kind == "group" else out.at[place],
            send_sem=z_send.at[number[id(piece)]],
            recv_sem=z_recv.at[number[id(piece)]],
            device_id={"expert": z_at(piece.step)},
            device_id_type=MESH,
        )

    def add(here, buffer, there):
        mine[here] = (mine[here].astype(f32) + buffer[there].astype(f32)).astype(mine.dtype)

    def pair(piece):
        leaving = [source for source, _ in stage(piece, 0)[1]]
        for mask in leaving + [m for m in piece.masks if m not in leaving]:
            load(piece, mask).wait()
            cross(piece, mask).wait_recv()
            add(at(piece, mask), theirs, at(piece, mask))
            if mask in leaving:
                hop(piece, 0, leaving.index(mask)).start()

    def step(piece, place):
        targets = [target for _, target in stage(piece, place)[1]]
        leaving = []
        if place + 1 < len(piece.order):
            leaving = [source for source, _ in stage(piece, place + 1)[1]]
        for index in range(len(targets)):
            hop(piece, place, index).wait_recv()
        for mask in leaving + [m for m in targets if m not in leaving]:
            there = pl.ds(arriving[id(piece), place, targets.index(mask)], piece.size)
            add(at(piece, mask), arrivals, there)
            if mask in leaving:
                hop(piece, place + 1, leaving.index(mask)).start()

    def finish(piece):
        result, out = mine.at[at(piece, 0)], outs[piece.array]
        if piece.kind == "flat":
            out[pl.ds(piece.first, piece.size)] = result[...]
        elif piece.step:
            z_copy(piece).start()
        elif piece.kind == "group":
            out[expert, piece.group] = result[...]
        else:
            out[expert] = result[...]

    depth = max(len(piece.order) for piece in order)
    for tick in range(len(order) + AHEAD + depth):
        for place in range(depth + 1):
            index = tick if place == 0 else tick - AHEAD - place + 1
            if not 0 <= index < len(order) or place > len(order[index].order):
                continue
            if place == 0:
                pair(order[index])
            else:
                step(order[index], place - 1)
            if place == len(order[index].order):
                finish(order[index])
        yield

    if has_dots:
        total = dot_ref[own]
        for d, c in plane:
            dot_plane(d, c).wait_recv()
            total = total + dot_in[d, c]
        dot_sum[...] = total
        for step_z in range(1, expert_size):
            dot_z(step_z).start()
        dots_ref[expert] = dot_sum[expert]
    if has_shared:
        sum_grads()

    for piece in moving:
        z_copy(piece, True).wait_recv()
    if has_dots:
        for step_z in range(1, expert_size):
            dot_z(step_z, True).wait_recv()
            dot_z(step_z).wait_send()
        for d, c in plane:
            dot_plane(d, c).wait_send()
    if has_shared:
        for kind in range(3):
            for step_z in range(1, expert_size):
                grad_z(kind, step_z).wait_send()
            if kind < 2:
                for d, c in plane:
                    column(kind, d, c, True).wait_recv()
                    column(kind, d, c).wait_send()
    for piece in moving:
        z_copy(piece).wait_send()
    for piece in order:
        for mask in piece.masks:
            cross(piece, mask).wait_send()
        for place in range(len(piece.order)):
            for index in range(len(stage(piece, place)[1])):
                hop(piece, place, index).wait_send()


def home_plan(parts, sizes, dots=None, grads=None):
    dp_size, ctx_size, expert_size = sizes
    assert dp_size == 2
    width, dtype = parts[0].shape[-1], parts[0].dtype
    kinds, out_shape = [], []
    for part in parts:
        if part.ndim == 5:
            kinds.append(("group", part.shape[0], part.shape[3]))
            shape = (expert_size, part.shape[0]) + part.shape[3:]
        else:
            kinds.append(("plane" if part.ndim == 4 else "flat", None, part.shape[-2]))
            shape = part.shape[1:]
        out_shape.append(jax.ShapeDtypeStruct(shape, dtype))
    moving, staying = pieces(kinds, expert_size, ctx_size)
    held, arriving = buffer_places(moving + staying)
    count, depth = len(moving + staying), len(bits_of(ctx_size))
    operands, in_specs = list(parts), [ANY] * len(parts)
    scratch = [
        pltpu.VMEM((held["rows"], width), dtype),
        pltpu.VMEM((held["rows"], width), dtype),
        pltpu.VMEM((arriving["rows"], width), dtype),
        DMA((count, ctx_size)),
        DMA((count, ctx_size)),
        DMA((count, ctx_size)),
        DMA((count, ctx_size)),
        DMA((count, depth, max(ctx_size // 2, 1))),
        DMA((count,)),
        DMA((count,)),
    ]
    if dots is not None:
        operands.append(dots)
        in_specs.append(VMEM)
        out_shape.append(jax.ShapeDtypeStruct(dots.shape[1:], dots.dtype))
        scratch += [
            pltpu.VMEM((dp_size, ctx_size) + dots.shape[1:], dots.dtype),
            pltpu.VMEM(dots.shape[1:], dots.dtype),
            DMA((dp_size, ctx_size)),
            DMA((dp_size, ctx_size)),
            DMA((expert_size,)),
            DMA((expert_size,)),
        ]
    if grads is not None:
        operands += list(grads)
        in_specs += [ANY] * 3
        plane_size, part = dp_size * ctx_size, grads[0].shape[2]
        shard = grads[0].shape[1] // plane_size
        columns = jax.ShapeDtypeStruct((shard, plane_size * part), f32)
        out_shape += [columns, columns, jax.ShapeDtypeStruct(grads[2].shape[1:], f32)]
        scratch += [pltpu.VMEM(grad.shape, grad.dtype) for grad in grads]
        scratch += [pltpu.VMEM((plane_size, shard, part), f32)] * 2
        scratch += [
            DMA((3, expert_size)),
            DMA((3, expert_size)),
            DMA((2, dp_size, ctx_size)),
            DMA((2, dp_size, ctx_size)),
            DMA((3,)),
        ]
    return tuple(kinds), operands, in_specs, out_shape, scratch


def bring_home(parts, sizes, number, dots=None, grads=None, carried=(), masks=()):
    kinds, operands, in_specs, out_shape, scratch = home_plan(parts, sizes, dots, grads)
    ins, outs = len(operands), len(out_shape)
    carry_shapes = [jax.ShapeDtypeStruct(array.shape, array.dtype) for array in carried]
    carry_sems = [DMA((len(masks), len(masks[0])))] * 2 if masks else []
    got = pl.pallas_call(
        functools.partial(home_kernel, kinds, dots is not None, grads is not None, masks, ins, outs),
        out_shape=out_shape + carry_shapes,
        in_specs=in_specs + [ANY] * len(carried),
        out_specs=[VMEM] * outs + [ANY] * len(carried),
        scratch_shapes=scratch + carry_sems,
        compiler_params=pltpu.CompilerParams(
            collective_id=number, has_side_effects=True, vmem_limit_bytes=58 << 20
        ),
    )(*operands, *carried)
    return got


NT = (((1,), (1,)), ((), ()))
TN = (((0,), (0,)), ((), ()))


def contract(a, b, dims=(((1,), (0,)), ((), ()))):
    return lax.dot_general(a, b, dims, preferred_element_type=f32)


def branch(rows, d_out, gate_w, up_w, down_w):
    gate_lin, up_lin = contract(rows, gate_w), contract(rows, up_w)
    sigmoid = 1.0 / (1.0 + jnp.exp(-gate_lin))
    silu = gate_lin * sigmoid
    hidden = (silu * up_lin).astype(bf16)
    d_hidden = contract(d_out, down_w, NT)
    d_gate = (d_hidden * up_lin * (sigmoid + silu * (1.0 - sigmoid))).astype(bf16)
    d_up = (d_hidden * silu).astype(bf16)
    result = contract(hidden, down_w)
    d_rows = contract(d_gate, gate_w, NT) + contract(d_up, up_w, NT)
    d_lin = contract(rows, jnp.concatenate([d_gate, d_up], axis=1), TN)
    d_down = contract(hidden, d_out, TN)
    return result, d_rows, d_lin, d_down


def experts_kernel(slices, table_ref, rows_ref, up_ref, scale_ref, *refs):
    rest = iter(refs)

    def take(count):
        return [next(rest) for _ in range(count)]

    gate_ws, up_ws, down_ws = take(slices), take(slices), take(slices)
    result_ref, d_rows_ref, dots_ref = take(3)
    gate_grads, up_grads, down_grads = take(slices), take(slices), take(slices)
    rows_f32, up_f32 = take(2)
    sums = list(rest)
    blocks, expert_size = rows_ref.shape[1:3]
    sources = blocks * expert_size
    width, part = gate_ws[0].shape[1:]
    last_chunk = pl.program_id(1) == pl.num_programs(1) - 1

    def unpack(source, carry):
        there = pl.ds(pl.multiple_of(source * PLACES, 8), PLACES)
        at = 0, source // expert_size, source % expert_size
        rows, up = rows_ref[at].astype(f32), up_ref[at].astype(f32)
        for i in range(GROUP):
            rows_f32[i, there] = rows[i * PLACES : (i + 1) * PLACES]
            up_f32[i, there] = up[i * PLACES : (i + 1) * PLACES]
        return carry

    lax.fori_loop(0, sources, unpack, 0)
    for i in range(GROUP):
        rows, up = rows_f32[i].astype(bf16), up_f32[i]
        scale = scale_ref[0, i][:, :, None]
        by_source = (sources, PLACES, width)
        d_out = (up.reshape(by_source) * scale).reshape(up.shape).astype(bf16)
        result, d_rows, d_lin, d_down = branch(
            rows,
            d_out,
            jnp.concatenate([w[i] for w in gate_ws], axis=1),
            jnp.concatenate([w[i] for w in up_ws], axis=1),
            jnp.concatenate([w[i] for w in down_ws], axis=0),
        )
        if sums:

            @pl.when(pl.program_id(1) == 0)
            def _(i=i):
                for total in sums:
                    total[i] = jnp.zeros(total.shape[1:], f32)

            sums[0][i] += d_lin
            sums[1][i] += d_down
            d_lin, d_down = sums[0].at[i], sums[1].at[i]

        def write(i=i, d_lin=d_lin, d_down=d_down):
            for k in range(slices):
                gate_grads[k][i] = d_lin[:, k * part : (k + 1) * part].astype(bf16)
                up_grads[k][i] = d_lin[:, (slices + k) * part : (slices + k + 1) * part].astype(bf16)
                down_grads[k][i] = d_down[k * part : (k + 1) * part, :].astype(bf16)

        if sums:
            pl.when(last_chunk)(write)
        else:
            write()
        dots_ref[0, i] = jnp.sum((result * up).reshape(by_source), axis=-1)
        up_f32[i] = (result.reshape(by_source) * scale).reshape(up.shape)
        rows_f32[i] = d_rows

    def pack(source, carry):
        there = pl.ds(pl.multiple_of(source * PLACES, 8), PLACES)
        at = 0, source // expert_size, source % expert_size
        result_ref[at] = jnp.concatenate([up_f32[i, there] for i in range(GROUP)]).astype(bf16)
        d_rows_ref[at] = jnp.concatenate([rows_f32[i, there] for i in range(GROUP)]).astype(bf16)
        return carry

    lax.fori_loop(0, sources, pack, 0)


def experts(table, rows, up, scale, gate_w, up_w, down_w, part):
    groups, blocks, expert_size, size, width = rows.shape
    slices = table.shape[0] // groups
    chunk = max(16 // expert_size, 1)
    steps = blocks // chunk
    sources = chunk * expert_size
    rows_spec = pl.BlockSpec((1, chunk, expert_size, size, width), lambda g, c, t: (g, c, 0, 0, 0))
    dots_spec = pl.BlockSpec((1, GROUP, sources, PLACES), lambda g, c, t: (g, 0, c, 0))
    column = lambda k: lambda g, c, t: (g, 0, t[g * slices + k])
    row = lambda k: lambda g, c, t: (g, t[g * slices + k], 0)
    whole = lambda g, c, t: (g, 0, 0)
    columns = [pl.BlockSpec((GROUP, width, part), column(k)) for k in range(slices)]
    lin = jax.ShapeDtypeStruct((groups * GROUP, width, part), bf16)
    down = jax.ShapeDtypeStruct((groups * GROUP, part, width), bf16)
    accumulators = [
        pltpu.VMEM((GROUP, width, 2 * slices * part), f32),
        pltpu.VMEM((GROUP, slices * part, width), f32),
    ]
    out = pl.pallas_call(
        functools.partial(experts_kernel, slices),
        grid_spec=pltpu.PrefetchScalarGridSpec(
            num_scalar_prefetch=1,
            grid=(groups, steps),
            in_specs=[rows_spec, rows_spec, dots_spec]
            + columns * 2
            + [pl.BlockSpec((GROUP, part, width), row(k)) for k in range(slices)],
            out_specs=[rows_spec, rows_spec, dots_spec]
            + [pl.BlockSpec((GROUP, width, part), whole)] * (2 * slices)
            + [pl.BlockSpec((GROUP, part, width), whole)] * slices,
            scratch_shapes=[pltpu.VMEM((GROUP, sources * PLACES, width), f32)] * 2
            + (accumulators if steps > 1 else []),
        ),
        out_shape=[
            jax.ShapeDtypeStruct(rows.shape, bf16),
            jax.ShapeDtypeStruct(rows.shape, bf16),
            jax.ShapeDtypeStruct(scale.shape, f32),
        ]
        + [lin] * (2 * slices)
        + [down] * slices,
        compiler_params=pltpu.CompilerParams(vmem_limit_bytes=62 << 20),
    )(table, rows, up, scale, *[gate_w] * slices, *[up_w] * slices, *[down_w] * slices)
    result, d_rows, dots = out[:3]
    return result, d_rows, dots, [out[3 + kind * slices : 3 + (kind + 1) * slices] for kind in range(3)]


def shared_kernel(
    plane_size, plane_ref, rows_ref, up_ref, gate_w, up_w, down_w, result_ref, d_rows_ref, gate_grad, up_grad,
    down_grad, lin_sum, down_sum,
):
    planes, rows, width = rows_ref.shape
    expert_size, column, part = gate_grad.shape
    shard = column // plane_size
    flat = (planes * rows, width)
    result, d_rows, d_lin, d_down = branch(
        rows_ref[...].reshape(flat), up_ref[...].reshape(flat), gate_w[...], up_w[...], down_w[...]
    )
    result_ref[...] = result.reshape(rows_ref.shape).astype(bf16)
    d_rows_ref[...] = d_rows.reshape(rows_ref.shape).astype(bf16)

    @pl.when(pl.program_id(0) == 0)
    def _():
        lin_sum[...] = jnp.zeros_like(lin_sum)
        down_sum[...] = jnp.zeros_like(down_sum)

    lin_sum[...] += d_lin
    down_sum[...] += d_down

    @pl.when(pl.program_id(0) == pl.num_programs(0) - 1)
    def _():
        for z in range(expert_size):
            firsts = [(p * expert_size + z) * shard for p in range(plane_size)]
            mine = jnp.concatenate([lin_sum[first : first + shard] for first in firsts]).astype(bf16)
            gate_grad[z] = mine[:, :part]
            up_grad[z] = mine[:, part:]
        down_grad[...] = down_sum[...].astype(bf16).reshape(down_grad.shape)


def shared(plane, rows, up, gate_w, up_w, down_w, expert_size):
    plane_size, count, width = rows.shape
    hidden_width = gate_w.shape[1]
    part = hidden_width // plane_size
    planes = 4
    flat = pl.BlockSpec((planes, count, width), lambda c, p: (c, 0, 0))
    columns = (expert_size, width // expert_size, part)
    down = (expert_size, part // expert_size, width)
    return pl.pallas_call(
        functools.partial(shared_kernel, plane_size),
        grid_spec=pltpu.PrefetchScalarGridSpec(
            num_scalar_prefetch=1,
            grid=(plane_size // planes,),
            in_specs=[
                flat,
                flat,
                pl.BlockSpec((width, part), lambda c, p: (0, p[0])),
                pl.BlockSpec((width, part), lambda c, p: (0, p[0])),
                pl.BlockSpec((part, width), lambda c, p: (p[0], 0)),
            ],
            out_specs=[
                flat,
                flat,
                pl.BlockSpec(columns, lambda c, p: (0, 0, 0)),
                pl.BlockSpec(columns, lambda c, p: (0, 0, 0)),
                pl.BlockSpec(down, lambda c, p: (0, 0, 0)),
            ],
            scratch_shapes=[pltpu.VMEM((width, 2 * part), f32), pltpu.VMEM((part, width), f32)],
        ),
        out_shape=[
            jax.ShapeDtypeStruct(rows.shape, bf16),
            jax.ShapeDtypeStruct(rows.shape, bf16),
            jax.ShapeDtypeStruct(columns, bf16),
            jax.ShapeDtypeStruct(columns, bf16),
            jax.ShapeDtypeStruct(down, bf16),
        ],
        compiler_params=pltpu.CompilerParams(vmem_limit_bytes=58 << 20),
    )(plane, rows, up, gate_w, up_w, down_w)


def carry_copies(masks, sources, targets, send_sem, recv_sem):
    ctx = lax.axis_index("ctx")
    return [
        pltpu.make_async_remote_copy(
            src_ref=sources[array].at[pl.ds(g * GROUP, GROUP)],
            dst_ref=targets[array].at[pl.ds(g * GROUP, GROUP)],
            send_sem=send_sem.at[array, g],
            recv_sem=recv_sem.at[array, g],
            device_id={"ctx": flip(ctx, mask)},
            device_id_type=MESH,
        )
        for array, by_group in enumerate(masks)
        for g, mask in enumerate(by_group)
    ]


class Slot:
    def __init__(self, heads):
        _, self.ctx_size, self.expert_size = sizes_of()
        self.heads, self.count = heads, self.ctx_size * self.expert_size
        ctx, expert = lax.axis_index("ctx"), lax.axis_index("expert")
        self.me = ctx * self.expert_size + expert
        head = head_of(ctx, expert, heads, self.ctx_size, self.expert_size)
        self.holds = head < heads
        self.head = head % heads

    def device(self, place):
        return {"ctx": place // self.expert_size, "expert": place % self.expert_size}

    def partners(self):
        dp, ctx = lax.axis_index("dp"), lax.axis_index("ctx")
        dp_size = lax.axis_size("dp")
        return [self.device((self.me + i) % self.count) for i in range(1, self.count)] + [
            {"dp": (dp + d) % dp_size, "ctx": flip(ctx, c)} for d in range(1, dp_size) for c in range(self.ctx_size)
        ]

    def copy(self, source, target, send, recv, there):
        return pltpu.make_async_remote_copy(
            src_ref=source, dst_ref=target, send_sem=send, recv_sem=recv, device_id=there, device_id_type=MESH
        )

    def inward(self, blocks, landing, send, recv):
        for i in range(self.heads):
            head = (self.me + i) % self.heads
            row, column = head_place(head, self.heads, self.ctx_size, self.expert_size)
            one = self.copy(
                blocks.at[head], landing.at[self.me], send.at[head], recv.at[self.me],
                {"ctx": row, "expert": column},
            )
            yield jnp.logical_not(self.holds & (head == self.head)), one

    def inward_landed(self, landing, send, recv):
        for i in range(1, self.count):
            source = (self.me + self.count - i) % self.count
            here = landing.at[source]
            yield self.copy(here, here, send.at[0], recv.at[source], self.device(self.me))

    def outward(self, blocks, landing, send, recv, place):
        return self.copy(
            blocks.at[place], landing.at[self.head], send.at[place], recv.at[self.head], self.device(place)
        )

    def outward_landed(self, landing, send, recv):
        for head in range(self.heads):
            here = landing.at[head]
            one = self.copy(here, here, send.at[0], recv.at[head], self.device(self.me))
            yield jnp.logical_not(self.holds & (head == self.head)), one


def attend_kernel(step, heads, kinds, length_ref, blocks_ref, *refs):
    rest = iter(refs)

    def take(count):
        return [next(rest) for _ in range(count)]

    side_ins = take(len(kinds))
    qkv_ref, out_ref, total_ref, landed_ref = take(4)
    side_outs = take(len(kinds))
    key_ref, query_ref, value_ref, sent_ref = take(4)
    in_send, in_recv, out_send, out_recv = take(4)
    side = spread_steps(kinds, False, side_ins + side_outs + list(rest))

    slot = Slot(heads)
    rows = blocks_ref.shape[2]
    span = slot.count * rows
    greet(slot.partners())
    for needed, one in slot.inward(blocks_ref, qkv_ref, in_send, in_recv):
        pl.when(needed)(one.start)
    next(side)

    @pl.when(slot.holds)
    def _():
        qkv_ref[slot.me] = blocks_ref[slot.head]
        for one in slot.inward_landed(qkv_ref, in_send, in_recv):
            one.wait_recv()

    next(side)

    @pl.when(slot.holds)
    def _():
        key_ref[...] = live_keys(head_rows(qkv_ref, HEAD_DIM, HEAD_DIM), length_ref[0])
        query_ref[...] = scaled_queries(head_rows(qkv_ref, 0, HEAD_DIM))
        value_ref[...] = head_rows(qkv_ref, 2 * HEAD_DIM, HEAD_DIM)

    def query_block(q):
        here = pl.ds(q * step, step)
        query = query_ref[:, here]

        def absorb(k, state, masked):
            top, total, out = state
            there = pl.ds(k * step if masked else pl.multiple_of(k * step, step), step)
            scores = jnp.dot(key_ref[there, :], query, preferred_element_type=f32)
            if masked:
                scores = causal(scores)
            new_top = jnp.maximum(top, jnp.max(scores, axis=0, keepdims=True))
            shrink = jnp.exp(top - new_top)
            weights = jnp.exp(scores - new_top)
            total = total * shrink + jnp.sum(weights, axis=0, keepdims=True)
            out = out * shrink + jnp.dot(
                value_ref[:, there], weights.astype(bf16), preferred_element_type=f32
            )
            return new_top, total, out

        state = (
            jnp.full((1, step), masked_value, f32),
            jnp.zeros((1, step), f32),
            jnp.zeros((HEAD_DIM, step), f32),
        )
        state = absorb(q, state, True)
        if q:
            state = lax.fori_loop(0, q, lambda k, s: absorb(k, s, False), state)
        top, total, out = state
        out = out / total
        out_ref[:, here] = out
        total_ref[:, here] = top + jnp.log(total)
        for i in range(step // rows):
            place = q * (step // rows) + i
            sent_ref[place] = out[:, i * rows : (i + 1) * rows].astype(bf16)
            one = slot.outward(sent_ref, landed_ref, out_send, out_recv, place)
            pl.when(slot.me != place)(one.start)

    for q in range(span // step):
        pl.when(slot.holds)(functools.partial(query_block, q))
        next(side, None)

    @pl.when(slot.holds)
    def _():
        landed_ref[slot.head] = sent_ref[slot.me]

    for needed, one in slot.outward_landed(landed_ref, out_send, out_recv):
        pl.when(needed)(one.wait_recv)
    for _ in side:
        pass
    for needed, one in slot.inward(blocks_ref, qkv_ref, in_send, in_recv):
        pl.when(needed)(one.wait_send)
    for place in range(slot.count):
        one = slot.outward(sent_ref, landed_ref, out_send, out_recv, place)
        pl.when(slot.holds & (slot.me != place))(one.wait_send)


def attend(blocks, length, arrays, sizes, number):
    heads, _, rows = blocks.shape
    count = sizes[1] * sizes[2]
    span = count * rows
    step = min(512, span)
    kinds, side_shapes, side_scratch = spread_plan(arrays, None, sizes)
    out = pl.pallas_call(
        functools.partial(attend_kernel, step, heads, kinds),
        out_shape=[
            jax.ShapeDtypeStruct((count,) + blocks.shape[1:], bf16),
            jax.ShapeDtypeStruct((HEAD_DIM, span), f32),
            jax.ShapeDtypeStruct((1, span), f32),
            jax.ShapeDtypeStruct((heads, HEAD_DIM, rows), bf16),
        ]
        + side_shapes,
        in_specs=[SMEM] + [VMEM] * (1 + len(arrays)),
        out_specs=[VMEM] * 4 + [ANY] * len(arrays),
        scratch_shapes=[
            pltpu.VMEM((span, 2 * HEAD_DIM), bf16),
            pltpu.VMEM((2 * HEAD_DIM, span), bf16),
            pltpu.VMEM((HEAD_DIM, span), bf16),
            pltpu.VMEM((count, HEAD_DIM, rows), bf16),
        ]
        + [DMA((count,))] * 4
        + side_scratch,
        compiler_params=pltpu.CompilerParams(
            collective_id=number, has_side_effects=True, vmem_limit_bytes=56 << 20
        ),
    )(length, blocks, *arrays)
    return out[:4], out[4:]


def unrotate(grad_t, cosine, sine):
    half = HEAD_DIM // 2
    first, second = grad_t[:half], grad_t[half:]
    return jnp.concatenate(
        [first * cosine + second * sine, second * cosine - first * sine], axis=0
    )


def attend_back_kernel(
    step, heads, kinds, masks, length_ref, qkv_ref, out_ref, total_ref, cosine_ref, sine_ref, blocks_ref, *refs
):
    rest = iter(refs)

    def take(count):
        return [next(rest) for _ in range(count)]

    side_ins, carried = take(len(kinds)), take(len(masks))
    landed_ref = next(rest)
    side_outs, carried_out = take(len(kinds)), take(len(masks))
    upstream_ref, key_ref, query_ref, value_ref, key_t_ref, key_sum, value_sum, delta_ref, up_ref, sent_ref = take(10)
    in_send, in_recv, out_send, out_recv = take(4)
    carry = carry_copies(masks, carried, carried_out, *take(2)) if masks else []
    side = home_steps(kinds, False, False, side_ins + side_outs + list(rest))

    slot = Slot(heads)
    rows = blocks_ref.shape[2]
    span = slot.count * rows
    greet(slot.partners())
    for needed, one in slot.inward(blocks_ref, upstream_ref, in_send, in_recv):
        pl.when(needed)(one.start)

    @pl.when(slot.holds)
    def _():
        key_t = head_rows(qkv_ref, HEAD_DIM, HEAD_DIM)
        key_ref[...] = live_keys(key_t, length_ref[0])
        key_t_ref[...] = key_t
        query_ref[...] = scaled_queries(head_rows(qkv_ref, 0, HEAD_DIM))
        value_t = head_rows(qkv_ref, 2 * HEAD_DIM, HEAD_DIM)
        value_ref[...] = jnp.transpose(value_t.astype(f32)).astype(bf16)
        key_sum[...] = jnp.zeros_like(key_sum)
        value_sum[...] = jnp.zeros_like(value_sum)
        upstream_ref[slot.me] = blocks_ref[slot.head]
        for one in slot.inward_landed(upstream_ref, in_send, in_recv):
            one.wait_recv()
        upstream = head_rows(upstream_ref, 0, HEAD_DIM)
        up_ref[...] = upstream
        delta_ref[...] = jnp.sum(upstream.astype(f32) * out_ref[...], axis=0, keepdims=True)

    next(side)
    for one in carry:
        one.start()

    def query_block(q):
        here = pl.ds(q * step, step)
        query, up = query_ref[:, here], up_ref[:, here]
        total, delta = total_ref[:, here], delta_ref[:, here]

        def meet(k, query_sum, masked):
            there = pl.ds(k * step if masked else pl.multiple_of(k * step, step), step)
            scores = jnp.dot(key_ref[there, :], query, preferred_element_type=f32)
            if masked:
                scores = causal(scores)
            probs = jnp.exp(scores - total)
            d_probs = jnp.dot(value_ref[there, :], up, preferred_element_type=f32)
            d_scores = (probs * (d_probs - delta)).astype(bf16)
            key_sum[:, there] += contract(query[:HEAD_DIM], d_scores, NT)
            value_sum[:, there] += contract(up, probs.astype(bf16), NT)
            return query_sum + contract(key_t_ref[:, there], d_scores)

        query_sum = meet(q, jnp.zeros((HEAD_DIM, step), f32), True)
        if q:
            query_sum = lax.fori_loop(0, q, lambda k, s: meet(k, s, False), query_sum)
        cosine, sine = cosine_ref[:, here], sine_ref[:, here]
        grad = jnp.concatenate(
            [
                unrotate(query_sum * score_scale, cosine, sine),
                unrotate(key_sum[:, here], cosine, sine),
                value_sum[:, here],
            ],
            axis=0,
        ).astype(bf16)
        for i in range(step // rows):
            place = q * (step // rows) + i
            sent_ref[place] = grad[:, i * rows : (i + 1) * rows]
            one = slot.outward(sent_ref, landed_ref, out_send, out_recv, place)
            pl.when(slot.me != place)(one.start)

    for q in reversed(range(span // step)):
        pl.when(slot.holds)(functools.partial(query_block, q))
        next(side, None)

    @pl.when(slot.holds)
    def _():
        landed_ref[slot.head] = sent_ref[slot.me]

    for _ in side:
        pass
    for needed, one in slot.outward_landed(landed_ref, out_send, out_recv):
        pl.when(needed)(one.wait_recv)
    for one in carry:
        one.wait()
    for needed, one in slot.inward(blocks_ref, upstream_ref, in_send, in_recv):
        pl.when(needed)(one.wait_send)
    for place in range(slot.count):
        one = slot.outward(sent_ref, landed_ref, out_send, out_recv, place)
        pl.when(slot.holds & (slot.me != place))(one.wait_send)


def attend_back(qkv, length, out, total, blocks, tables, parts, carried, masks, sizes, number):
    heads, _, rows = blocks.shape
    count = qkv.shape[0]
    span = count * rows
    step = min(512, span)
    kinds, operands, side_specs, side_shapes, side_scratch = home_plan(parts, sizes)
    carry_shapes = [jax.ShapeDtypeStruct(array.shape, array.dtype) for array in carried]
    carry_sems = [DMA((len(masks), len(masks[0])))] * 2 if masks else []
    got = pl.pallas_call(
        functools.partial(attend_back_kernel, step, heads, kinds, masks),
        out_shape=[jax.ShapeDtypeStruct((heads,) + qkv.shape[1:], bf16)] + side_shapes + carry_shapes,
        in_specs=[SMEM] + [VMEM] * 6 + side_specs + [ANY] * len(carried),
        out_specs=[VMEM] * (1 + len(side_shapes)) + [ANY] * len(carried),
        scratch_shapes=[
            pltpu.VMEM(blocks.shape[:0] + (count,) + blocks.shape[1:], bf16),
            pltpu.VMEM((span, 2 * HEAD_DIM), bf16),
            pltpu.VMEM((2 * HEAD_DIM, span), bf16),
            pltpu.VMEM((span, HEAD_DIM), bf16),
            pltpu.VMEM((HEAD_DIM, span), bf16),
            pltpu.VMEM((HEAD_DIM, span), f32),
            pltpu.VMEM((HEAD_DIM, span), f32),
            pltpu.VMEM((1, span), f32),
            pltpu.VMEM((HEAD_DIM, span), bf16),
            pltpu.VMEM(qkv.shape, bf16),
        ]
        + [DMA((count,))] * 4
        + carry_sems
        + side_scratch,
        compiler_params=pltpu.CompilerParams(
            collective_id=number, has_side_effects=True, vmem_limit_bytes=58 << 20
        ),
    )(length, qkv, out, total, *tables, blocks, *operands, *carried)
    return got[0], got[1 : 1 + len(side_shapes)], got[1 + len(side_shapes) :]


EXACT = lax.Precision.HIGHEST


def expert_of_place(count, stride, own):
    expert = lax.broadcasted_iota(jnp.int32, (EXPERTS, count), 0)
    column = lax.broadcasted_iota(jnp.int32, (EXPERTS, count), 1)
    place = column - ((expert // own) * stride + (expert % own) * PLACES)
    inside = (place >= 0) & (place < PLACES)
    at = jnp.sum(jnp.where(inside, place, 0), axis=0, keepdims=True)
    return inside.astype(f32), at.astype(f32)


def spots(hits, earlier, count, stride, own):
    expert_at, place_at = expert_of_place(count, stride, own)
    low = expert_at.astype(bf16)
    hit = contract(hits.astype(bf16), low)
    before = contract(earlier.astype(bf16), low)
    return jnp.where((hit > 0.5) & (before == place_at), 1.0, 0.0)


def first_place(rows):
    return (lax.axis_index("ctx") * lax.axis_size("expert") + lax.axis_index("expert")) * rows


def live(length_ref, first_ref, shape):
    return first_ref[0] + lax.broadcasted_iota(jnp.int32, shape, 0) < length_ref[0]


def routing_kernel(length_ref, first_ref, routes_ref, cotangent_ref, branch_ref, rows_ref, hits_ref, earlier_ref):
    rows = routes_ref.shape[0]
    own = EXPERTS // rows_ref.shape[0]
    alive = live(length_ref, first_ref, (rows, 1))
    expert = lax.broadcasted_iota(jnp.int32, (rows, EXPERTS), 1)
    routes = routes_ref[...]
    named = (routes[:, 0:1] == expert) | (routes[:, 1:2] == expert)
    hits = jnp.where(named, 1.0, 0.0) * jnp.where(alive, 1.0, 0.0)
    token = lax.broadcasted_iota(jnp.int32, (rows, rows), 0)
    other = lax.broadcasted_iota(jnp.int32, (rows, rows), 1)
    earlier = contract(jnp.where(other < token, 1.0, 0.0).astype(bf16), hits.astype(bf16))
    hits_ref[...] = hits
    earlier_ref[...] = earlier
    branch = jnp.where(alive, cotangent_ref[...].astype(f32), 0.0).astype(bf16)
    branch_ref[...] = branch
    spread_out = spots(hits, earlier, EXPERTS * PLACES, own * PLACES, own)
    placed = contract(jnp.transpose(spread_out).astype(bf16), branch)
    rows_ref[...] = placed.astype(bf16).reshape(rows_ref.shape)


def routing(length, first, routes, cotangent, expert_size):
    rows, width = cotangent.shape
    return pl.pallas_call(
        routing_kernel,
        out_shape=(
            jax.ShapeDtypeStruct((rows, width), bf16),
            jax.ShapeDtypeStruct((expert_size, EXPERTS // expert_size * PLACES, width), bf16),
            jax.ShapeDtypeStruct((rows, EXPERTS), f32),
            jax.ShapeDtypeStruct((rows, EXPERTS), f32),
        ),
        in_specs=[SMEM, SMEM, VMEM, VMEM],
        out_specs=(VMEM,) * 4,
    )(length, first, routes, cotangent)


def project_kernel(tokens_ref, gain_ref, query_ref, key_ref, value_ref, cosine_ref, sine_ref, normed_ref, qkv_ref):
    inputs = tokens_ref[...].astype(f32)
    normed = (inputs * rms_scale(inputs) * gain_ref[...]).astype(bf16)
    normed_ref[...] = normed
    heads, _, rows = qkv_ref.shape
    half = HEAD_DIM // 2
    cosine, sine = cosine_ref[...], sine_ref[...]
    for kind, weight in enumerate((query_ref, key_ref, value_ref)):
        lin = jnp.transpose(contract(normed, weight[...]))
        for head in range(heads):
            mine = lin[head * HEAD_DIM : (head + 1) * HEAD_DIM]
            if kind < 2:
                first, second = mine[:half], mine[half:]
                mine = jnp.concatenate(
                    [first * cosine - second * sine, second * cosine + first * sine], axis=0
                )
            qkv_ref[head, kind * HEAD_DIM : (kind + 1) * HEAD_DIM, :] = mine.astype(bf16)


def project(tokens, gain, weights, tables):
    rows, width = tokens.shape
    return pl.pallas_call(
        project_kernel,
        out_shape=(
            jax.ShapeDtypeStruct((rows, width), bf16),
            jax.ShapeDtypeStruct((width // HEAD_DIM, 3 * HEAD_DIM, rows), bf16),
        ),
        in_specs=[VMEM] * 7,
        out_specs=(VMEM,) * 2,
        compiler_params=pltpu.CompilerParams(vmem_limit_bytes=32 << 20),
    )(tokens, gain, *weights, *tables)


def middle_kernel(
    length_ref, first_ref, tokens_ref, attended_ref, output_ref, gain_ref, router_ref, hits_ref, earlier_ref,
    hidden_ref, normed_ref, rows_ref, scale_ref, gates_ref, flat_ref,
):
    rows, width = tokens_ref.shape
    expert_size = rows_ref.shape[0]
    own = EXPERTS // expert_size
    attended = jnp.transpose(attended_ref[...].reshape(width, rows).astype(f32)).astype(bf16)
    flat_ref[...] = attended
    alive = live(length_ref, first_ref, (rows, 1))
    attn_out = contract(attended, output_ref[...])
    hidden = tokens_ref[...].astype(f32) + jnp.where(alive, attn_out, 0.0)
    hidden_ref[...] = hidden
    normed = (hidden * rms_scale(hidden) * gain_ref[...]).astype(bf16)
    normed_ref[...] = normed
    hits, earlier = hits_ref[...], earlier_ref[...]
    logits = contract(normed, router_ref[...])
    top = jnp.max(jnp.where(hits > 0.5, logits, masked_value), axis=1, keepdims=True)
    powers = jnp.where(hits > 0.5, jnp.exp(logits - top), 0.0)
    total = jnp.sum(powers, axis=1, keepdims=True)
    gates = powers / jnp.where(total > 0.0, total, 1.0)
    gates_ref[...] = gates
    spread_out = spots(hits, earlier, EXPERTS * PLACES, own * PLACES, own)
    placed = contract(jnp.transpose(spread_out).astype(bf16), normed)
    rows_ref[...] = placed.astype(bf16).reshape(rows_ref.shape)
    lanes = expert_size * 128
    expert_at, _ = expert_of_place(lanes, 128, own)
    by_place = jnp.dot(gates, expert_at, preferred_element_type=f32, precision=EXACT)
    at_place = spots(hits, earlier, lanes, 128, own) * by_place
    row = jnp.sum(at_place, axis=0, keepdims=True)
    for z in range(expert_size):
        scale_ref[z] = jnp.broadcast_to(row[:, z * 128 : (z + 1) * 128], (8, 128))


def middle(length, first, tokens, attended, output_weight, gain, router, hits, earlier, expert_size):
    rows, width = tokens.shape
    return pl.pallas_call(
        middle_kernel,
        out_shape=(
            jax.ShapeDtypeStruct((rows, width), f32),
            jax.ShapeDtypeStruct((rows, width), bf16),
            jax.ShapeDtypeStruct((expert_size, EXPERTS // expert_size * PLACES, width), bf16),
            jax.ShapeDtypeStruct((expert_size, 8, 128), f32),
            jax.ShapeDtypeStruct((rows, EXPERTS), f32),
            jax.ShapeDtypeStruct((rows, width), bf16),
        ),
        in_specs=[SMEM, SMEM] + [VMEM] * 7,
        out_specs=(VMEM,) * 6,
        compiler_params=pltpu.CompilerParams(vmem_limit_bytes=32 << 20),
    )(length, first, tokens, attended, output_weight, gain, router, hits, earlier)


def turn_kernel(
    length_ref, first_ref, back_ref, flat_ref, dots_ref, hits_ref, earlier_ref, gates_ref, normed_ref, hidden_ref,
    cotangent_ref, gain_ref, router_ref, output_ref, d_hidden_ref, d_attended_ref, d_attn_ref, router_grad, gain_grad,
):
    rows, width = normed_ref.shape
    expert_size = back_ref.shape[0]
    own = EXPERTS // expert_size
    alive = live(length_ref, first_ref, (rows, 1))
    hits, earlier, gates = hits_ref[...], earlier_ref[...], gates_ref[...]
    lanes = expert_size * 128
    expert_at, _ = expert_of_place(lanes, 128, own)
    row = jnp.concatenate([dots_ref[z, 0:1, :] for z in range(expert_size)], axis=1)
    at_place = jnp.where(spots(hits, earlier, lanes, 128, own) > 0.5, row, 0.0)
    d_gates = lax.dot_general(at_place, expert_at, NT, preferred_element_type=f32, precision=EXACT)
    mean = jnp.sum(gates * d_gates, axis=1, keepdims=True)
    d_logits = (gates * (d_gates - mean)).astype(bf16)
    normed = normed_ref[...]
    router_grad[...] = contract(normed, d_logits, TN)
    spread_out = spots(hits, earlier, EXPERTS * PLACES, own * PLACES, own).astype(bf16)
    placed = back_ref[...].reshape(EXPERTS * PLACES, width)
    d_normed = contract(spread_out, placed) + flat_ref[...].astype(f32)
    d_normed = d_normed + contract(d_logits, router_ref[...], NT)
    hidden = hidden_ref[...]
    scale = rms_scale(hidden)
    normal = hidden * scale
    gain_grad[...] = jnp.sum(d_normed * normal, axis=0, keepdims=True)
    d_hidden = cotangent_ref[...].astype(f32) + rms_back(normal, scale, gain_ref[...], d_normed)
    d_hidden_ref[...] = d_hidden
    d_attn = jnp.where(alive, d_hidden, 0.0).astype(bf16)
    d_attn_ref[...] = d_attn
    d_attended = jnp.transpose(contract(d_attn, output_ref[...], NT))
    d_attended_ref[...] = d_attended.astype(bf16).reshape(d_attended_ref.shape)


def turn(length, first, back, flat, dots, hits, earlier, gates, normed, hidden, cotangent, gain, router, output_weight):
    rows, width = normed.shape
    return pl.pallas_call(
        turn_kernel,
        out_shape=(
            jax.ShapeDtypeStruct((rows, width), f32),
            jax.ShapeDtypeStruct((width // HEAD_DIM, HEAD_DIM, rows), bf16),
            jax.ShapeDtypeStruct((rows, width), bf16),
            jax.ShapeDtypeStruct((width, EXPERTS), f32),
            jax.ShapeDtypeStruct((1, width), f32),
        ),
        in_specs=[SMEM, SMEM] + [VMEM] * 12,
        out_specs=(VMEM,) * 5,
        compiler_params=pltpu.CompilerParams(vmem_limit_bytes=32 << 20),
    )(length, first, back, flat, dots, hits, earlier, gates, normed, hidden, cotangent, gain, router, output_weight)


def join_kernel(
    length_ref, first_ref, back_ref, flat_ref, hits_ref, earlier_ref, hidden_ref, out_ref,
):
    rows, width = hidden_ref.shape
    own = EXPERTS // back_ref.shape[0]
    spread_out = spots(hits_ref[...], earlier_ref[...], EXPERTS * PLACES, own * PLACES, own).astype(bf16)
    mixed = contract(spread_out, back_ref[...].reshape(EXPERTS * PLACES, width)) + flat_ref[...].astype(f32)
    alive = live(length_ref, first_ref, (rows, 1))
    out_ref[...] = (hidden_ref[...] + jnp.where(alive, mixed, 0.0)).astype(bf16)


def join(length, first, back, flat, hits, earlier, hidden):
    return pl.pallas_call(
        join_kernel,
        out_shape=jax.ShapeDtypeStruct(hidden.shape, bf16),
        in_specs=[SMEM, SMEM] + [VMEM] * 5,
        out_specs=VMEM,
        compiler_params=pltpu.CompilerParams(vmem_limit_bytes=32 << 20),
    )(length, first, back, flat, hits, earlier, hidden)


def last_kernel(
    shard, grads_ref, query_ref, key_ref, value_ref, normed_ref, tokens_ref, gain_ref, d_hidden_ref, attended_ref,
    d_attn_ref, input_grad, gain_grad, sums_ref,
):
    rows, width = normed_ref.shape
    heads = grads_ref.shape[0]
    lins = []
    d_normed = jnp.zeros((width, rows), f32)
    for kind, weight in enumerate((query_ref, key_ref, value_ref)):
        at = slice(kind * HEAD_DIM, (kind + 1) * HEAD_DIM)
        lin = jnp.concatenate([grads_ref[head, at, :] for head in range(heads)], axis=0)
        lins.append(lin)
        d_normed = d_normed + contract(weight[...], lin)
    d_normed = jnp.transpose(d_normed)
    inputs = tokens_ref[...].astype(f32)
    scale = rms_scale(inputs)
    normal = inputs * scale
    gain_grad[...] = jnp.sum(d_normed * normal, axis=0, keepdims=True)
    d_inputs = d_hidden_ref[...] + rms_back(normal, scale, gain_ref[...], d_normed)
    input_grad[...] = d_inputs.astype(bf16)
    normed_t = jnp.transpose(normed_ref[...].astype(f32)).astype(bf16)
    attended_t = jnp.transpose(attended_ref[...].astype(f32)).astype(bf16)
    grads = [contract(normed_t, lin, NT) for lin in lins] + [contract(attended_t, d_attn_ref[...])]
    plane_size, expert_size, count, _ = sums_ref.shape
    for p in range(plane_size):
        for z in range(expert_size):
            first = (p * expert_size + z) * shard
            parts = [grad[first : first + shard] for grad in grads]
            if count > 4 * shard:
                parts.append(jnp.zeros((count - 4 * shard, width), f32))
            sums_ref[p, z] = jnp.concatenate(parts, axis=0).astype(bf16)


def last(grads, weights, normed, tokens, gain, d_hidden, attended, d_attn, sizes):
    rows, width = normed.shape
    dp_size, ctx_size, expert_size = sizes
    shard = width // (dp_size * ctx_size * expert_size)
    count = -(-4 * shard // 16) * 16
    return pl.pallas_call(
        functools.partial(last_kernel, shard),
        out_shape=(
            jax.ShapeDtypeStruct((rows, width), bf16),
            jax.ShapeDtypeStruct((1, width), f32),
            jax.ShapeDtypeStruct((dp_size * ctx_size, expert_size, count, width), bf16),
        ),
        in_specs=[VMEM] * 10,
        out_specs=(VMEM,) * 3,
        compiler_params=pltpu.CompilerParams(vmem_limit_bytes=48 << 20),
    )(grads, *weights, normed, tokens, gain, d_hidden, attended, d_attn)


def local(
    tokens,
    lengths,
    routes,
    norm1_gain,
    query_weight,
    key_weight,
    value_weight,
    output_weight,
    norm2_gain,
    router_weight,
    expert_gate,
    expert_up,
    expert_down,
    shared_gate,
    shared_up,
    shared_down,
    cotangent,
):
    sizes = dp_size, ctx_size, expert_size = sizes_of()
    plane_size, slot_size = dp_size * ctx_size, ctx_size * expert_size
    rows, width = tokens.shape[1:]
    heads, own, shard = width // HEAD_DIM, EXPERTS // expert_size, width // (dp_size * slot_size)
    plane = (lax.axis_index("dp") * ctx_size + lax.axis_index("ctx")).astype(jnp.int32)[None]
    first = first_place(rows).astype(jnp.int32)[None]
    tokens, routes, cotangent = tokens[0], routes[0], cotangent[0]
    gain_one, gain_two = norm1_gain[None], norm2_gain[None]
    weights = (query_weight, key_weight, value_weight)

    branch_rows, up_placed, hits, earlier = routing(lengths, first, routes, cotangent, expert_size)

    groups = own // GROUP
    other_core = (lax.axis_index("dp") + 1) % dp_size
    ctx = lax.axis_index("ctx")
    bits = bits_of(ctx_size)
    group_bits = [group_bit(g, ctx_size) for g in range(groups)]
    slice_masks = [subsets([bit for bit in bits if bit != mine]) for mine in group_bits]

    def grouped(placed):
        return placed.reshape(expert_size, groups, GROUP * PLACES, width)

    places = jnp.arange(rows, dtype=jnp.int32)
    normed, qkv = project(tokens, gain_one, weights, rope_tables(first[0] + places))
    (qkv, out_t, log_total, attended), (up_rows, up_flat) = attend(
        qkv, lengths, [grouped(up_placed), branch_rows], sizes, 1
    )
    hidden, normed_two, in_placed, scale, gates, attended = middle(
        lengths, first, tokens, attended, output_weight, gain_two, router_weight, hits, earlier, expert_size
    )

    in_rows, in_flat, scale = spread([grouped(in_placed), normed_two], scale, sizes, 3)
    sources = 4 * expert_size
    here = lax.axis_index("dp")
    blocks = jnp.stack(
        [
            jnp.stack([core * ctx_size + flip(ctx, mask) for core in (here, other_core) for mask in (0, bit)])
            for bit in group_bits
        ]
    )
    scale = jnp.take(scale[:, :, 0, : own * PLACES], blocks.reshape(-1), axis=0)
    scale = scale.reshape(groups, sources, groups, GROUP, PLACES)
    scale = jnp.stack([jnp.swapaxes(scale[g, :, g], 0, 1) for g in range(groups)])
    table = jnp.concatenate(
        [
            jnp.stack([here * ctx_size + flip(ctx, mask) for mask in masks])
            for masks in slice_masks
        ]
    ).astype(jnp.int32)
    shared_result, shared_d, *shared_grads = shared(
        plane, in_flat, up_flat, shared_gate, shared_up, shared_down, expert_size
    )
    part = shared_gate.shape[1] // plane_size
    result, d_rows, dots, slice_grads = experts(
        table, in_rows, up_rows, scale, expert_gate, expert_up, expert_down, part
    )
    dots = jnp.swapaxes(dots, 1, 2).reshape(groups, 4, expert_size, GROUP * PLACES)
    dots = jnp.stack(
        [
            jnp.pad(dots[g], [(0, 0), (0, 0), (g * GROUP * PLACES, (groups - 1 - g) * GROUP * PLACES)])
            for g in range(groups)
        ]
    )
    owner = blocks[:, :, None] == jnp.arange(plane_size)
    dots = jnp.sum(jnp.where(owner[..., None, None], dots[:, :, None], 0.0), axis=(0, 1))
    dots = jnp.pad(dots[:, :, None], [(0, 0), (0, 0), (0, 7), (0, 128 - own * PLACES)])
    back, flat, dots = bring_home([d_rows, shared_d], sizes, 4, dots=dots)

    d_hidden, d_attended, d_attn, router_grad, gain_two_grad = turn(
        lengths, first, back, flat, dots, hits, earlier, gates, normed_two, hidden, cotangent, gain_two,
        router_weight, output_weight,
    )

    all_tables = rope_tables(jnp.arange(slot_size * rows, dtype=jnp.int32))
    others = [
        (array, tuple(masks[k] for masks in slice_masks))
        for slices in slice_grads
        for k, array in enumerate(slices)
        if k
    ]
    early, late = others[: len(others) // 3], others[len(others) // 3 :]
    d_qkv, (out_back, out_flat), early_in = attend_back(
        qkv, lengths, out_t, log_total, d_attended, all_tables, [result, shared_result],
        [array for array, _ in early], tuple(masks for _, masks in early), sizes, 6,
    )
    output_rows = join(lengths, first, out_back, out_flat, hits, earlier, hidden)

    input_grad, gain_one_grad, sums = last(
        d_qkv, weights, normed, tokens, gain_one, d_hidden, attended, d_attn, sizes
    )
    devices = (plane_size, expert_size)
    small = jnp.concatenate(
        [
            router_grad.reshape(devices + (shard * EXPERTS,)),
            gain_one_grad.reshape(devices + (shard,)),
            gain_two_grad.reshape(devices + (shard,)),
        ],
        axis=-1,
    )
    small = jnp.pad(small, [(0, 0), (0, 0), (0, 1024 - small.shape[-1])])
    sums, small, shared_gate_grad, shared_up_grad, shared_down_grad, *late_in = bring_home(
        [sums], sizes, 8, dots=small.reshape(devices + (8, 128)), grads=shared_grads,
        carried=[array for array, _ in late], masks=tuple(masks for _, masks in late),
    )
    arrived = list(early_in) + list(late_in)
    count = len(arrived) // 3
    expert_grads = [
        sum((array.astype(f32) for array in arrived[kind * count : (kind + 1) * count]), slices[0].astype(f32))
        for kind, slices in enumerate(slice_grads)
    ]
    sums = jnp.sum(sums.astype(f32), axis=0)
    small = jnp.sum(small, axis=0).reshape(1024)
    routed = shard * EXPERTS
    return (
        output_rows[None],
        input_grad[None],
        small[routed : routed + shard],
        *(sums[kind * shard : (kind + 1) * shard] for kind in range(4)),
        small[routed + shard : routed + 2 * shard],
        small[:routed].reshape(shard, EXPERTS),
        *expert_grads,
        shared_gate_grad,
        shared_up_grad,
        shared_down_grad,
    )


def solution(mesh):
    tokens = P("dp", ("ctx", "expert"), None)
    whole = P()
    experts = P("expert", None, None)
    everywhere = ("dp", "ctx", "expert")
    return jax.shard_map(
        local,
        mesh=mesh,
        in_specs=(tokens, P("dp"), tokens)
        + (whole,) * 7
        + (experts,) * 3
        + (whole,) * 3
        + (tokens,),
        out_specs=(tokens, tokens, P(everywhere))
        + (P(everywhere, None),) * 4
        + (P(everywhere), P(everywhere, None))
        + (P("expert", None, PLANE),) * 2
        + (P("expert", PLANE, None),)
        + (P(everywhere, None),) * 3,
        check_vma=False,
    )
```

```python
import functools

import jax
import jax.numpy as jnp
from jax import lax
from jax.experimental import pallas as pl
from jax.experimental.pallas import tpu as pltpu
from jax.sharding import PartitionSpec as P

HEAD_DIM = 64
EXPERTS = 16
TOP = 2
CAP = 22
PLACES = 24

norm_epsilon = 1e-06
rope_base = 10000.0
score_scale = 0.125
masked_value = -1e30
PLANE = ("dp", "ctx")
SLOT = ("ctx", "expert")
AHEAD = 2
bf16 = jnp.bfloat16
f32 = jnp.float32


def rms_scale(values):
    return lax.rsqrt(jnp.mean(values * values, axis=-1, keepdims=True) + norm_epsilon)


def rms_back(normal, scale, gain, upstream):
    lifted = upstream * gain
    return scale * (lifted - normal * jnp.mean(lifted * normal, axis=-1, keepdims=True))


def rope_tables(positions):
    half = HEAD_DIM // 2
    exponent = jnp.arange(half, dtype=f32) * (2.0 / HEAD_DIM)
    inverse_freq = rope_base ** (-exponent)
    angles = inverse_freq[:, None] * positions[None, :].astype(f32)
    return jnp.cos(angles), jnp.sin(angles)


def head_rows(qkv_ref, first, count):
    return jnp.concatenate(
        [qkv_ref[block, first : first + count, :] for block in range(qkv_ref.shape[0])], axis=1
    )


def live_keys(key_t, length):
    span = key_t.shape[1]
    place = lax.broadcasted_iota(jnp.int32, (8, span), 1)
    row = lax.broadcasted_iota(jnp.int32, (8, span), 0)
    bias = jnp.where((place >= length) & (row == 0), masked_value, 0.0)
    padded = jnp.concatenate(
        [key_t.astype(f32), bias, jnp.zeros((HEAD_DIM - 8, span), f32)], axis=0
    )
    return jnp.transpose(padded).astype(bf16)


def scaled_queries(query_t):
    span = query_t.shape[1]
    row = lax.broadcasted_iota(jnp.int32, (HEAD_DIM, span), 0)
    ones = jnp.where(row == 0, 1.0, 0.0)
    return jnp.concatenate([query_t.astype(f32) * score_scale, ones], axis=0).astype(bf16)


def causal(scores):
    key = lax.broadcasted_iota(jnp.int32, scores.shape, 0)
    query = lax.broadcasted_iota(jnp.int32, scores.shape, 1)
    return jnp.where(key <= query, scores, masked_value)


MESH = pl.DeviceIdType.MESH
ANY = pl.BlockSpec(memory_space=pl.ANY)
VMEM = pl.BlockSpec(memory_space=pltpu.VMEM)
SMEM = pl.BlockSpec(memory_space=pltpu.SMEM)
DMA = pltpu.SemaphoreType.DMA


def head_place(head, heads, ctx_size, expert_size):
    per = expert_size - 1
    if ctx_size <= expert_size and ctx_size * per == heads:
        row = head // per
        step = head % per
        return row, step + jnp.where(step >= row, 1, 0)
    return head // expert_size, head % expert_size


def head_of(ctx, expert, heads, ctx_size, expert_size):
    per = expert_size - 1
    if ctx_size <= expert_size and ctx_size * per == heads:
        head = ctx * per + expert - jnp.where(expert > ctx, 1, 0)
        return jnp.where(expert == ctx, heads, head)
    return ctx * expert_size + expert


def sizes_of():
    return tuple(lax.axis_size(a) for a in ("dp", "ctx", "expert"))


def greet(partners):
    barrier = pltpu.get_barrier_semaphore()
    for partner in partners:
        pl.semaphore_signal(barrier, inc=1, device_id=partner, device_id_type=MESH)
    pl.semaphore_wait(barrier, len(partners))


GROUP = 2


def flip(index, mask):
    bit = 1
    while bit <= mask:
        if mask & bit:
            index = index + bit * (1 - 2 * ((index // bit) % 2))
        bit *= 2
    return index


def bits_of(ctx_size):
    return [1 << b for b in range(ctx_size.bit_length() - 1)]


def group_bit(group, ctx_size):
    bits = bits_of(ctx_size)
    return bits[group % len(bits)]


def subsets(order):
    masks = [0]
    for bit in order:
        masks = masks + [m | bit for m in masks]
    return masks


class Piece:
    def __init__(self, array, kind, group, step, first, size, order):
        self.array, self.kind, self.group, self.step = array, kind, group, step
        self.first, self.size, self.order = first, size, order
        self.masks = subsets(order)


def pieces(kinds, expert_size, ctx_size):
    bits = bits_of(ctx_size)
    moving, staying = [], []
    for array, (kind, groups, rows) in enumerate(kinds):
        if kind == "flat":
            half = rows // 2
            staying.append(Piece(array, kind, None, None, 0, half, bits))
            staying.append(Piece(array, kind, None, None, half, rows - half, bits[::-1]))
            continue
        for step in range(expert_size):
            for group in range(groups or 1):
                if kind == "group":
                    order = [group_bit(group, ctx_size)]
                else:
                    order = bits if (step + array) % 2 == 0 else bits[::-1]
                (moving if step else staying).append(Piece(array, kind, group, step, 0, rows, order))
    return moving, staying


class Spread:
    def __init__(self, kinds, has_gate, refs):
        rest = iter(refs)

        def take(count):
            return [next(rest) for _ in range(count)]

        self.has_gate = has_gate
        self.ins = take(len(kinds))
        self.gate = next(rest) if has_gate else None
        self.outs = take(len(kinds))
        self.gates = next(rest) if has_gate else None
        self.z_send, self.z_recv, self.send, self.recv, self.pair_recv, self.local_sem = take(6)
        if has_gate:
            self.gate_send, self.gate_recv, self.gate_z_send, self.gate_z_recv = take(4)
        self.dp_size, self.ctx_size, self.expert_size = sizes_of()
        self.dp, self.ctx, self.expert = (lax.axis_index(a) for a in ("dp", "ctx", "expert"))
        self.moving, self.staying = pieces(kinds, self.expert_size, self.ctx_size)
        self.all = self.staying + self.moving
        self.number = {id(piece): i for i, piece in enumerate(self.all)}
        self.own = self.dp * self.ctx_size + self.ctx
        self.other = (self.dp + 1) % self.dp_size
        self.bits = bits_of(self.ctx_size)
        self.started = []
        self.plane = [(d, c) for d in range(self.dp_size) for c in range(self.ctx_size) if (d, c) != (0, 0)]

    def z_at(self, step):
        return (self.expert + step) % self.expert_size

    def z_from(self, step):
        return (self.expert + self.expert_size - step) % self.expert_size

    def block(self, core, mask):
        return (self.dp if core == 0 else self.other) * self.ctx_size + flip(self.ctx, mask)

    def landed(self, piece, core, mask, at=0):
        out = self.outs[piece.array]
        if piece.step is None:
            return out.at[self.block(core, mask), pl.ds(piece.first, piece.size)]
        return out.at[piece.group, core * 2 + (1 if mask ^ at else 0), self.z_from(piece.step)]

    def source(self, piece):
        if piece.step is None:
            return self.ins[piece.array].at[pl.ds(piece.first, piece.size)]
        if piece.step == 0:
            return self.ins[piece.array].at[self.expert, piece.group]
        return self.landed(piece, 0, 0)

    def remote(self, source, target, send, recv, there):
        return pltpu.make_async_remote_copy(
            src_ref=source, dst_ref=target, send_sem=send, recv_sem=recv, device_id=there, device_id_type=MESH
        )

    def z_copy(self, piece, landing=False):
        place = self.z_from(piece.step) if landing else self.expert
        at = self.number[id(piece)]
        return self.remote(
            self.ins[piece.array].at[self.z_at(piece.step), piece.group],
            self.outs[piece.array].at[piece.group, 0, place],
            self.z_send.at[at],
            self.z_recv.at[at],
            {"expert": self.z_at(piece.step)},
        )

    def gate_z(self, step, landing=False):
        return self.remote(
            self.gate.at[self.z_at(step)],
            self.gates.at[self.own, self.z_from(step) if landing else self.expert],
            self.gate_z_send.at[step],
            self.gate_z_recv.at[step],
            {"expert": self.z_at(step)},
        )

    def gate_plane(self, d, c, block):
        return self.remote(
            self.gates.at[block],
            self.gates.at[block],
            self.gate_send.at[d, c],
            self.gate_recv.at[d, c],
            {"dp": (self.dp + d) % self.dp_size, "ctx": flip(self.ctx, c)},
        )

    def passing(self, piece, mask, bit):
        at = self.number[id(piece)]
        return self.remote(
            self.landed(piece, 0, mask) if mask else self.source(piece),
            self.landed(piece, 0, mask, bit),
            self.send.at[at, mask, self.bits.index(bit)],
            self.recv.at[at, mask ^ bit],
            {"ctx": flip(self.ctx, bit)},
        )

    def arrived(self, piece, mask):
        here = self.landed(piece, 0, mask)
        recv = self.recv.at[self.number[id(piece)], mask]
        return self.remote(here, here, self.send.at[0, 0, 0], recv, {"ctx": self.ctx})

    def crossing(self, piece, mask, landing=False):
        at = self.number[id(piece)]
        core = 0 if piece.step is None and not landing else 1
        return self.remote(
            self.landed(piece, 0, mask) if mask else self.source(piece),
            self.landed(piece, core, mask),
            self.send.at[at, mask, len(self.bits)],
            self.pair_recv.at[at, mask],
            {"dp": self.other},
        )

    def kept(self):
        return [
            pltpu.make_async_copy(self.source(piece), self.landed(piece, 0, 0), self.local_sem.at[i])
            for i, piece in enumerate(self.staying)
        ]

    def begin(self, one):
        one.start()
        self.started.append(one)

    def z_start(self):
        if self.has_gate:
            for step in range(1, self.expert_size):
                self.gate_z(step).start()
        for piece in self.moving:
            self.z_copy(piece).start()

    def first(self, some):
        for piece in some:
            if piece.step:
                self.z_copy(piece, True).wait_recv()
            for bit in piece.order:
                self.begin(self.passing(piece, 0, bit))
            self.begin(self.crossing(piece, 0))

    def keep(self):
        for one in self.kept():
            one.start()
        if self.has_gate:
            self.gates[self.own, self.expert] = self.gate[self.expert]

    def forward(self, piece, place):
        if place >= len(piece.order):
            return
        bit = piece.order[place]
        for mask in [m | bit for m in subsets(piece.order[:place])]:
            self.arrived(piece, mask).wait_recv()
            for later in piece.order[place + 1 :]:
                self.begin(self.passing(piece, mask, later))
            self.begin(self.crossing(piece, mask))

    def forward_all(self, some):
        for place in range(len(self.bits)):
            for piece in some:
                self.forward(piece, place)

    def gates_on(self):
        for step in range(1, self.expert_size):
            self.gate_z(step, True).wait_recv()
        for d, c in self.plane:
            self.gate_plane(d, c, self.own).start()

    def gates_landed(self):
        for d, c in self.plane:
            block = ((self.dp + d) % self.dp_size) * self.ctx_size + flip(self.ctx, c)
            self.gate_plane(d, c, block).wait_recv()

    def paired(self, some):
        for piece in some:
            for mask in piece.masks:
                self.crossing(piece, mask, True).wait_recv()

    def sent(self):
        for one in self.started:
            one.wait_send()
        for piece in self.moving:
            self.z_copy(piece).wait_send()
        if self.has_gate:
            for step in range(1, self.expert_size):
                self.gate_z(step).wait_send()
            for d, c in self.plane:
                self.gate_plane(d, c, self.own).wait_send()


def plane_partners():
    dp_size, ctx_size, expert_size = sizes_of()
    dp, ctx, expert = (lax.axis_index(a) for a in ("dp", "ctx", "expert"))
    plane = [(d, c) for d in range(dp_size) for c in range(ctx_size) if (d, c) != (0, 0)]
    return [{"expert": (expert + step) % expert_size} for step in range(1, expert_size)] + [
        {"dp": (dp + d) % dp_size, "ctx": flip(ctx, c)} for d, c in plane
    ]


def spread_plan(arrays, gate, sizes):
    dp_size, ctx_size, expert_size = sizes
    assert dp_size == 2
    plane_size = dp_size * ctx_size
    kinds, out_shape = [], []
    for array in arrays:
        if array.ndim == 4:
            kinds.append(("group", array.shape[1], array.shape[2]))
            shape = (array.shape[1], 4, expert_size) + array.shape[2:]
        else:
            kinds.append(("flat", None, array.shape[0]))
            shape = (plane_size,) + array.shape
        out_shape.append(jax.ShapeDtypeStruct(shape, array.dtype))
    moving, staying = pieces(kinds, expert_size, ctx_size)
    count = len(moving + staying)
    scratch = [
        DMA((count,)),
        DMA((count,)),
        DMA((count, ctx_size, len(bits_of(ctx_size)) + 1)),
        DMA((count, ctx_size)),
        DMA((count, ctx_size)),
        DMA((len(staying),)),
    ]
    if gate is not None:
        out_shape.append(jax.ShapeDtypeStruct((plane_size,) + gate.shape, gate.dtype))
        scratch += [DMA((dp_size, ctx_size))] * 2 + [DMA((expert_size,))] * 2
    return tuple(kinds), out_shape, scratch


def stage(piece, place):
    order = piece.order[::-1]
    done, bit = sum(order[:place]), order[place]
    kept = [m for m in piece.masks if not m & (done | bit)]
    return bit, [(m | bit, m) for m in kept]


def buffer_places(order):
    held, arriving, here, there = {}, {}, 0, 0
    for piece in order:
        for mask in piece.masks:
            held[id(piece), mask] = here
            here += piece.size
        for place in range(len(piece.order)):
            for index in range(len(stage(piece, place)[1])):
                arriving[id(piece), place, index] = there
                there += piece.size
    held["rows"], arriving["rows"] = here, there
    return held, arriving


class Home:
    def __init__(self, kinds, has_dots, parts, dot, outs, dots_out, scratch):
        rest = iter(scratch)

        def take(count):
            return [next(rest) for _ in range(count)]

        self.parts, self.dot, self.outs, self.dots_out, self.has_dots = parts, dot, outs, dots_out, has_dots
        self.mine, self.theirs, self.arrivals = take(3)
        self.mine_sem, self.pair_send, self.pair_recv, self.send, self.recv, self.z_send, self.z_recv = take(7)
        if has_dots:
            self.dot_in, self.dot_sum, self.dot_send, self.dot_recv, self.dot_z_send, self.dot_z_recv = take(6)
        self.dp_size, self.ctx_size, self.expert_size = sizes_of()
        self.dp, self.ctx, self.expert = (lax.axis_index(a) for a in ("dp", "ctx", "expert"))
        self.moving, self.staying = pieces(kinds, self.expert_size, self.ctx_size)
        self.all = self.moving + self.staying
        self.number = {id(piece): i for i, piece in enumerate(self.all)}
        self.held, self.arriving = buffer_places(self.all)
        self.own = self.dp * self.ctx_size + self.ctx
        self.other = (self.dp + 1) % self.dp_size
        self.plane = [(d, c) for d in range(self.dp_size) for c in range(self.ctx_size) if (d, c) != (0, 0)]

    def z_at(self, step):
        return (self.expert + step) % self.expert_size

    def z_from(self, step):
        return (self.expert + self.expert_size - step) % self.expert_size

    def plane_at(self, d, c):
        return ((self.dp + d) % self.dp_size) * self.ctx_size + flip(self.ctx, c)

    def partner(self, d, c):
        return {"dp": (self.dp + d) % self.dp_size, "ctx": flip(self.ctx, c)}

    def remote(self, source, target, send, recv, there):
        return pltpu.make_async_remote_copy(
            src_ref=source, dst_ref=target, send_sem=send, recv_sem=recv, device_id=there, device_id_type=MESH
        )

    def whole(self, piece, core, mask):
        part = self.parts[piece.array]
        if piece.kind == "group":
            return part.at[piece.group, core * 2 + (1 if mask else 0), self.z_at(piece.step)]
        block = (self.dp if core == 0 else self.other) * self.ctx_size + flip(self.ctx, mask)
        if piece.kind == "flat":
            return part.at[block, pl.ds(piece.first, piece.size)]
        return part.at[block, self.z_at(piece.step)]

    def at(self, piece, mask):
        return pl.ds(self.held[id(piece), mask], piece.size)

    def load(self, piece, mask):
        return pltpu.make_async_copy(
            self.whole(piece, 0, mask), self.mine.at[self.at(piece, mask)], self.mine_sem.at[self.number[id(piece)], mask]
        )

    def cross(self, piece, mask):
        number = self.number[id(piece)]
        return self.remote(
            self.whole(piece, 1, mask),
            self.theirs.at[self.at(piece, mask)],
            self.pair_send.at[number, mask],
            self.pair_recv.at[number, mask],
            {"dp": self.other},
        )

    def hop(self, piece, place, index):
        bit, moves = stage(piece, place)
        number = self.number[id(piece)]
        return self.remote(
            self.mine.at[self.at(piece, moves[index][0])],
            self.arrivals.at[pl.ds(self.arriving[id(piece), place, index], piece.size)],
            self.send.at[number, moves[index][0]],
            self.recv.at[number, place, index],
            {"ctx": flip(self.ctx, bit)},
        )

    def z_copy(self, piece, landing=False):
        place = self.z_from(piece.step) if landing else self.expert
        out, number = self.outs[piece.array], self.number[id(piece)]
        return self.remote(
            self.mine.at[self.at(piece, 0)],
            out.at[place, piece.group] if piece.kind == "group" else out.at[place],
            self.z_send.at[number],
            self.z_recv.at[number],
            {"expert": self.z_at(piece.step)},
        )

    def start(self, some):
        for piece in some:
            for mask in piece.masks:
                self.cross(piece, mask).start()
                self.load(piece, mask).start()

    def add(self, here, buffer, there):
        total = self.mine[here].astype(f32) + buffer[there].astype(f32)
        self.mine[here] = total.astype(self.mine.dtype)

    def pair(self, piece):
        leaving = [source for source, _ in stage(piece, 0)[1]]
        for mask in leaving + [m for m in piece.masks if m not in leaving]:
            self.load(piece, mask).wait()
            self.cross(piece, mask).wait_recv()
            self.add(self.at(piece, mask), self.theirs, self.at(piece, mask))
            if mask in leaving:
                self.hop(piece, 0, leaving.index(mask)).start()

    def step(self, piece, place):
        targets = [target for _, target in stage(piece, place)[1]]
        leaving = []
        if place + 1 < len(piece.order):
            leaving = [source for source, _ in stage(piece, place + 1)[1]]
        for index in range(len(targets)):
            self.hop(piece, place, index).wait_recv()
        for mask in leaving + [m for m in targets if m not in leaving]:
            there = pl.ds(self.arriving[id(piece), place, targets.index(mask)], piece.size)
            self.add(self.at(piece, mask), self.arrivals, there)
            if mask in leaving:
                self.hop(piece, place + 1, leaving.index(mask)).start()
        if place + 1 == len(piece.order):
            self.finish(piece)

    def finish(self, piece):
        result, out = self.mine.at[self.at(piece, 0)], self.outs[piece.array]
        if piece.kind == "flat":
            out[pl.ds(piece.first, piece.size)] = result[...]
        elif piece.step:
            self.z_copy(piece).start()
        elif piece.kind == "group":
            out[self.expert, piece.group] = result[...]
        else:
            out[self.expert] = result[...]

    def ticks(self, some):
        depth = max(len(piece.order) for piece in some)
        for tick in range(len(some) + AHEAD + depth):
            for place in range(depth + 1):
                index = tick if place == 0 else tick - AHEAD - place + 1
                if not 0 <= index < len(some) or place > len(some[index].order):
                    continue
                if place == 0:
                    self.pair(some[index])
                else:
                    self.step(some[index], place - 1)
            yield

    def dot_plane(self, d, c):
        return self.remote(
            self.dot.at[self.plane_at(d, c)],
            self.dot_in.at[d, c],
            self.dot_send.at[d, c],
            self.dot_recv.at[d, c],
            self.partner(d, c),
        )

    def dot_z(self, step, landing=False):
        return self.remote(
            self.dot_sum.at[self.z_at(step)],
            self.dots_out.at[self.z_from(step) if landing else self.expert],
            self.dot_z_send.at[step],
            self.dot_z_recv.at[step],
            {"expert": self.z_at(step)},
        )

    def dots_start(self):
        for d, c in self.plane:
            self.dot_plane(d, c).start()

    def dots_on(self):
        total = self.dot[self.own]
        for d, c in self.plane:
            self.dot_plane(d, c).wait_recv()
            total = total + self.dot_in[d, c]
        self.dot_sum[...] = total
        for step in range(1, self.expert_size):
            self.dot_z(step).start()
        self.dots_out[self.expert] = self.dot_sum[self.expert]

    def done(self):
        for piece in self.moving:
            self.z_copy(piece, True).wait_recv()
        if self.has_dots:
            for step in range(1, self.expert_size):
                self.dot_z(step, True).wait_recv()
                self.dot_z(step).wait_send()
            for d, c in self.plane:
                self.dot_plane(d, c).wait_send()
        for piece in self.moving:
            self.z_copy(piece).wait_send()
        for piece in self.all:
            for mask in piece.masks:
                self.cross(piece, mask).wait_send()
            for place in range(len(piece.order)):
                for index in range(len(stage(piece, place)[1])):
                    self.hop(piece, place, index).wait_send()


def home_plan(shapes, sizes, dots=None):
    dp_size, ctx_size, expert_size = sizes
    assert dp_size == 2
    width = shapes[0][-1]
    kinds, out_shape = [], []
    for given in shapes:
        if len(given) == 5:
            kinds.append(("group", given[0], given[3]))
            shape = (expert_size, given[0]) + given[3:]
        else:
            kinds.append(("plane" if len(given) == 4 else "flat", None, given[-2]))
            shape = given[1:]
        out_shape.append(jax.ShapeDtypeStruct(shape, bf16))
    moving, staying = pieces(kinds, expert_size, ctx_size)
    held, arriving = buffer_places(moving + staying)
    count, depth = len(moving + staying), len(bits_of(ctx_size))
    scratch = [
        pltpu.VMEM((held["rows"], width), bf16),
        pltpu.VMEM((held["rows"], width), bf16),
        pltpu.VMEM((arriving["rows"], width), bf16),
        DMA((count, ctx_size)),
        DMA((count, ctx_size)),
        DMA((count, ctx_size)),
        DMA((count, ctx_size)),
        DMA((count, depth, max(ctx_size // 2, 1))),
        DMA((count,)),
        DMA((count,)),
    ]
    if dots is not None:
        out_shape.append(jax.ShapeDtypeStruct(dots[1:], f32))
        scratch += [
            pltpu.VMEM((dp_size, ctx_size) + dots[1:], f32),
            pltpu.VMEM(dots[1:], f32),
            DMA((dp_size, ctx_size)),
            DMA((dp_size, ctx_size)),
            DMA((expert_size,)),
            DMA((expert_size,)),
        ]
    return tuple(kinds), out_shape, scratch


class Shared:
    def __init__(self, grads, outs, scratch):
        self.grads, self.outs = grads, outs
        self.landing, self.columns = scratch[:3], scratch[3:5]
        self.send, self.recv, self.column_send, self.column_recv, self.own_sem = scratch[5:]
        self.dp_size, self.ctx_size, self.expert_size = sizes_of()
        self.dp, self.ctx, self.expert = (lax.axis_index(a) for a in ("dp", "ctx", "expert"))
        self.own = self.dp * self.ctx_size + self.ctx
        self.plane = [(d, c) for d in range(self.dp_size) for c in range(self.ctx_size) if (d, c) != (0, 0)]
        self.part = grads[0].shape[2]

    def z_copy(self, kind, step):
        there = (self.expert + step) % self.expert_size
        return pltpu.make_async_remote_copy(
            src_ref=self.grads[kind].at[there],
            dst_ref=self.landing[kind].at[step],
            send_sem=self.send.at[kind, step],
            recv_sem=self.recv.at[kind, step],
            device_id={"expert": there},
            device_id_type=MESH,
        )

    def kept(self, kind):
        return pltpu.make_async_copy(
            self.grads[kind].at[self.expert], self.landing[kind].at[0], self.own_sem.at[kind]
        )

    def column(self, kind, d, c, landing=False):
        there = ((self.dp + d) % self.dp_size) * self.ctx_size + flip(self.ctx, c)
        source = ((self.dp + self.dp_size - d) % self.dp_size) * self.ctx_size + flip(self.ctx, c)
        at = source if landing else self.own
        return pltpu.make_async_remote_copy(
            src_ref=self.columns[kind].at[there],
            dst_ref=self.outs[kind].at[:, pl.ds(pl.multiple_of(at * self.part, 128), self.part)],
            send_sem=self.column_send.at[kind, d, c],
            recv_sem=self.column_recv.at[kind, d, c],
            device_id={"dp": (self.dp + d) % self.dp_size, "ctx": flip(self.ctx, c)},
            device_id_type=MESH,
        )

    def start(self):
        for kind in range(3):
            self.kept(kind).start()
            for step in range(1, self.expert_size):
                self.z_copy(kind, step).start()

    def sum(self):
        for kind in range(3):
            self.kept(kind).wait()
            total = self.landing[kind][0].astype(f32)
            for step in range(1, self.expert_size):
                self.z_copy(kind, step).wait_recv()
                total = total + self.landing[kind][step].astype(f32)
            if kind == 2:
                self.outs[2][...] = total
                continue
            shard = self.outs[kind].shape[0]
            for block in range(self.dp_size * self.ctx_size):
                self.columns[kind][block] = total[block * shard : (block + 1) * shard]
            for d, c in self.plane:
                self.column(kind, d, c).start()
            here = pl.ds(pl.multiple_of(self.own * self.part, 128), self.part)
            self.outs[kind][:, here] = self.columns[kind][self.own]

    def done(self):
        for kind in range(3):
            for step in range(1, self.expert_size):
                self.z_copy(kind, step).wait_send()
            if kind < 2:
                for d, c in self.plane:
                    self.column(kind, d, c, True).wait_recv()
                    self.column(kind, d, c).wait_send()


def shared_plan(width, part, sizes):
    dp_size, ctx_size, expert_size = sizes
    plane_size = dp_size * ctx_size
    shard = width // (plane_size * expert_size)
    given = [(expert_size, plane_size * shard, part)] * 2 + [(expert_size, part // expert_size, width)]
    columns = jax.ShapeDtypeStruct((shard, plane_size * part), f32)
    out_shape = [columns, columns, jax.ShapeDtypeStruct(given[2][1:], f32)]
    scratch = [pltpu.VMEM(shape, bf16) for shape in given]
    scratch += [pltpu.VMEM((plane_size, shard, part), f32)] * 2
    scratch += [
        DMA((3, expert_size)),
        DMA((3, expert_size)),
        DMA((2, dp_size, ctx_size)),
        DMA((2, dp_size, ctx_size)),
        DMA((3,)),
    ]
    return given, out_shape, scratch


def carry_copies(masks, sources, targets, send_sem, recv_sem):
    ctx = lax.axis_index("ctx")
    return [
        pltpu.make_async_remote_copy(
            src_ref=sources[array].at[pl.ds(g * GROUP, GROUP)],
            dst_ref=targets[array].at[pl.ds(g * GROUP, GROUP)],
            send_sem=send_sem.at[array, g],
            recv_sem=recv_sem.at[array, g],
            device_id={"ctx": flip(ctx, mask)},
            device_id_type=MESH,
        )
        for array, by_group in enumerate(masks)
        for g, mask in enumerate(by_group)
    ]


def home_kernel(kinds, masks, *refs):
    rest = iter(refs)

    def take(count):
        return [next(rest) for _ in range(count)]

    parts, dot, carried = take(len(kinds)), next(rest), take(len(masks))
    outs, dots_out, carried_out = take(len(kinds)), next(rest), take(len(masks))
    carry = carry_copies(masks, carried, carried_out, *take(2)) if masks else []
    home = Home(kinds, True, parts, dot, outs, dots_out, list(rest))
    greet(plane_partners())
    home.start(home.all)
    home.dots_start()
    steps = home.ticks(home.all)
    next(steps)
    for one in carry:
        one.start()
    for _ in steps:
        pass
    home.dots_on()
    home.done()
    for one in carry:
        one.wait()


def bring_home(parts, sizes, number, dots, carried=(), masks=()):
    kinds, out_shape, scratch = home_plan([part.shape for part in parts], sizes, dots.shape)
    carry_shapes = [jax.ShapeDtypeStruct(array.shape, array.dtype) for array in carried]
    carry_sems = [DMA((len(masks), len(masks[0])))] * 2 if masks else []
    return pl.pallas_call(
        functools.partial(home_kernel, kinds, masks),
        out_shape=out_shape + carry_shapes,
        in_specs=[ANY] * len(parts) + [VMEM] + [ANY] * len(carried),
        out_specs=[VMEM] * len(out_shape) + [ANY] * len(carried),
        scratch_shapes=carry_sems + scratch,
        compiler_params=pltpu.CompilerParams(
            collective_id=number, has_side_effects=True, vmem_limit_bytes=58 << 20
        ),
    )(*parts, dots, *carried)


NT = (((1,), (1,)), ((), ()))
TN = (((0,), (0,)), ((), ()))


def contract(a, b, dims=(((1,), (0,)), ((), ()))):
    return lax.dot_general(a, b, dims, preferred_element_type=f32)


def branch(rows, d_out, gate_w, up_w, down_w):
    gate_lin, up_lin = contract(rows, gate_w), contract(rows, up_w)
    sigmoid = 1.0 / (1.0 + jnp.exp(-gate_lin))
    silu = gate_lin * sigmoid
    hidden = (silu * up_lin).astype(bf16)
    d_hidden = contract(d_out, down_w, NT)
    d_gate = (d_hidden * up_lin * (sigmoid + silu * (1.0 - sigmoid))).astype(bf16)
    d_up = (d_hidden * silu).astype(bf16)
    result = contract(hidden, down_w)
    d_rows = contract(d_gate, gate_w, NT) + contract(d_up, up_w, NT)
    d_lin = contract(rows, jnp.concatenate([d_gate, d_up], axis=1), TN)
    d_down = contract(hidden, d_out, TN)
    return result, d_rows, d_lin, d_down


def moe_kernel(spread_kinds, home_kinds, slices, *refs):
    rest = iter(refs)

    def take(count):
        return [next(rest) for _ in range(count)]

    placed, normed, gate = take(3)
    up_rows_in, up_flat_in = take(2)
    weights_in, shared_in = take(3), take(3)
    result_out, shared_out = take(2)
    back, flat, dots_out = take(3)
    grads_out = take(3 * slices)
    shared_grads_out = take(3)
    in_rows, in_flat, gates = take(3)
    up_rows, up_flat = take(2)
    weights, shared_w = take(3), take(3)
    d_rows, shared_d, result, shared_result = take(4)
    lin_out, down_out, rows_f32, up_f32, dot = take(5)
    lin_sum, down_sum = take(2)
    shared_parts = take(3)
    load_sem, store_sem = take(2)
    spread = Spread(spread_kinds, True, [placed, normed, gate, in_rows, in_flat, gates] + take(10))
    shared_sums = Shared(shared_parts, shared_grads_out, take(10))
    home = Home(home_kinds, True, [d_rows, shared_d], dot, [back, flat], dots_out, list(rest))

    dp_size, ctx_size, expert_size = sizes_of()
    ctx, own_block = lax.axis_index("ctx"), spread.own
    groups, blocks, _, size, width = in_rows.shape
    plane_size, rows, _ = in_flat.shape
    part = weights[0].shape[-1]
    sources = blocks * expert_size
    bits = bits_of(ctx_size)

    def column(mask):
        return pl.ds(pl.multiple_of(spread.block(0, mask) * part, 128), part)

    def loads(g):
        masks = subsets([bit for bit in bits if bit != group_bit(g, ctx_size)])
        experts = pl.ds(g * GROUP, GROUP)
        copies = [(up_rows_in.at[g], up_rows.at[g])]
        for k, mask in enumerate(masks):
            copies += [
                (weights_in[0].at[experts, :, column(mask)], weights[0].at[g, k]),
                (weights_in[1].at[experts, :, column(mask)], weights[1].at[g, k]),
                (weights_in[2].at[experts, column(mask)], weights[2].at[g, k]),
            ]
        return [pltpu.make_async_copy(s, t, load_sem.at[g, i]) for i, (s, t) in enumerate(copies)]

    shared_loads = [
        pltpu.make_async_copy(s, t, load_sem.at[groups, i])
        for i, (s, t) in enumerate(
            [
                (shared_in[0].at[:, column(0)], shared_w[0]),
                (shared_in[1].at[:, column(0)], shared_w[1]),
                (shared_in[2].at[column(0)], shared_w[2]),
                (up_flat_in, up_flat),
            ]
        )
    ]
    for one in shared_loads:
        one.start()
    for g in range(groups):
        for one in loads(g):
            one.start()
    greet(plane_partners())
    spread.z_start()
    spread.first(spread.staying)
    spread.keep()
    dot[...] = jnp.zeros_like(dot)
    spread.forward_all(spread.staying)
    spread.paired(spread.staying)
    for one in spread.kept() + shared_loads:
        one.wait()

    def shared_part(first, count):
        here = pl.ds(first, count)
        shape = (count * rows, width)
        some = branch(
            in_flat[here].reshape(shape), up_flat[here].reshape(shape), shared_w[0][...], shared_w[1][...],
            shared_w[2][...],
        )
        shared_result[here] = some[0].reshape((count, rows, width)).astype(bf16)
        shared_d[here] = some[1].reshape((count, rows, width)).astype(bf16)
        if first == 0:
            lin_sum[...] = some[2]
            down_sum[...] = some[3]
        else:
            lin_sum[...] += some[2]
            down_sum[...] += some[3]

    chunk = 4
    shared_part(0, chunk)
    spread.first(spread.moving)
    spread.gates_on()
    for first in range(chunk, plane_size, chunk):
        shared_part(first, chunk)
    shard = shared_parts[0].shape[1] // plane_size
    for z in range(expert_size):
        firsts = [(p * expert_size + z) * shard for p in range(plane_size)]
        mine = jnp.concatenate([lin_sum[first : first + shard] for first in firsts]).astype(bf16)
        shared_parts[0][z] = mine[:, :part]
        shared_parts[1][z] = mine[:, part:]
    shared_parts[2][...] = down_sum[...].astype(bf16).reshape(shared_parts[2].shape)
    stores = [pltpu.make_async_copy(shared_result, shared_out, store_sem.at[groups, 0])]
    stores[0].start()
    home.start(home.staying[-2:])
    shared_sums.start()

    spread.forward_all(spread.moving)
    spread.gates_landed()
    spread.paired(spread.moving)

    def expert(g, i):
        bit = group_bit(g, ctx_size)
        lane = (g * GROUP + i) * PLACES
        owners = [spread.block(core, mask) for core in (0, 1) for mask in (0, bit)]
        scale = jnp.concatenate(
            [gates[owner, z, 0:1, lane : lane + PLACES] for owner in owners for z in range(expert_size)]
        )[:, :, None]
        by_source = (sources, PLACES, width)
        up = up_f32[i]
        d_out = (up.reshape(by_source) * scale).reshape(up.shape).astype(bf16)
        some, d_some, d_lin, d_down = branch(
            rows_f32[i].astype(bf16),
            d_out,
            jnp.concatenate([weights[0][g, k, i] for k in range(slices)], axis=1),
            jnp.concatenate([weights[1][g, k, i] for k in range(slices)], axis=1),
            jnp.concatenate([weights[2][g, k, i] for k in range(slices)], axis=0),
        )
        for k in range(slices):
            lin_out[0, k, i] = d_lin[:, k * part : (k + 1) * part].astype(bf16)
            lin_out[1, k, i] = d_lin[:, (slices + k) * part : (slices + k + 1) * part].astype(bf16)
            down_out[k, i] = d_down[k * part : (k + 1) * part, :].astype(bf16)
        sums = jnp.sum((some * up).reshape(by_source), axis=-1)
        up_f32[i] = (some.reshape(by_source) * scale).reshape(up.shape)
        rows_f32[i] = d_some
        for at, owner in enumerate(owners):
            for z in range(expert_size):
                line = sums[at * expert_size + z : at * expert_size + z + 1]
                pieces_of = [line]
                if lane:
                    pieces_of.insert(0, jnp.zeros((1, lane), f32))
                if lane + PLACES < 128:
                    pieces_of.append(jnp.zeros((1, 128 - lane - PLACES), f32))
                dot[owner, z, 0:1, :] += jnp.concatenate(pieces_of, axis=1)

    def unpack(g):
        def one(source, carry):
            there = pl.ds(pl.multiple_of(source * PLACES, 8), PLACES)
            at = g, source // expert_size, source % expert_size
            some, up = in_rows[at].astype(f32), up_rows[at].astype(f32)
            for i in range(GROUP):
                rows_f32[i, there] = some[i * PLACES : (i + 1) * PLACES]
                up_f32[i, there] = up[i * PLACES : (i + 1) * PLACES]
            return carry

        lax.fori_loop(0, sources, one, 0)

    def pack(g):
        def one(source, carry):
            there = pl.ds(pl.multiple_of(source * PLACES, 8), PLACES)
            at = g, source // expert_size, source % expert_size
            result[at] = jnp.concatenate([up_f32[i, there] for i in range(GROUP)]).astype(bf16)
            d_rows[at] = jnp.concatenate([rows_f32[i, there] for i in range(GROUP)]).astype(bf16)
            return carry

        lax.fori_loop(0, sources, one, 0)

    def stores_of(g):
        experts = pl.ds(g * GROUP, GROUP)
        copies = [(result.at[g], result_out.at[g])]
        for k in range(slices):
            copies += [
                (lin_out.at[0, k], grads_out[k].at[experts]),
                (lin_out.at[1, k], grads_out[slices + k].at[experts]),
                (down_out.at[k], grads_out[2 * slices + k].at[experts]),
            ]
        return [pltpu.make_async_copy(s, t, store_sem.at[g, i]) for i, (s, t) in enumerate(copies)]

    flats = home.staying[-2:]

    def of_group(g):
        return [piece for piece in home.moving + home.staying if piece.group == g]

    depth = len(bits)
    waiting = [functools.partial(home.pair, piece) for piece in flats]
    for place in range(depth):
        waiting += [functools.partial(home.step, piece, place) for piece in flats]
    for g in range(groups):
        for one in loads(g):
            one.wait()
        unpack(g)
        for i in range(GROUP):
            if g and i == 0:
                for one in stores_of(g - 1):
                    one.wait()
            expert(g, i)
            for stage_of in waiting[: -(-len(waiting) // (GROUP - i))]:
                stage_of()
            del waiting[: -(-len(waiting) // (GROUP - i))]
        pack(g)
        home.start(of_group(g))
        for one in stores_of(g):
            one.start()
        waiting = [functools.partial(home.pair, piece) for piece in of_group(g)]
        waiting += [functools.partial(home.step, piece, 0) for piece in of_group(g)]
    home.dots_start()
    for stage_of in waiting:
        stage_of()
    home.dots_on()
    shared_sums.sum()
    home.done()
    shared_sums.done()
    spread.sent()
    for one in stores + stores_of(groups - 1):
        one.wait()


def moe(placed, normed, gate, up_rows, up_flat, weights, shared_weights, sizes, number):
    dp_size, ctx_size, expert_size = sizes
    plane_size = dp_size * ctx_size
    groups, size, width = placed.shape[1:]
    rows = normed.shape[0]
    part = shared_weights[0].shape[1] // plane_size
    slices = max(ctx_size // 2, 1)
    own = groups * GROUP
    sources = 4 * expert_size
    spread_kinds, landing, spread_scratch = spread_plan([placed, normed], gate, sizes)
    dots = (plane_size,) + gate.shape
    home_kinds, home_out, home_scratch = home_plan([up_rows.shape, up_flat.shape], sizes, dots)
    shared_given, shared_out, shared_scratch = shared_plan(width, part, sizes)
    lin = jax.ShapeDtypeStruct((own, width, part), bf16)
    down = jax.ShapeDtypeStruct((own, part, width), bf16)
    columns = pltpu.VMEM((groups, slices, GROUP, width, part), bf16)
    out = pl.pallas_call(
        functools.partial(moe_kernel, spread_kinds, home_kinds, slices),
        out_shape=[
            jax.ShapeDtypeStruct(up_rows.shape, bf16),
            jax.ShapeDtypeStruct(up_flat.shape, bf16),
        ]
        + home_out
        + [lin] * (2 * slices)
        + [down] * slices
        + shared_out,
        in_specs=[VMEM] * 3 + [ANY] * 8,
        out_specs=[ANY] * 2 + [VMEM] * 3 + [ANY] * (3 * slices) + [VMEM] * 3,
        scratch_shapes=[pltpu.VMEM(shape.shape, shape.dtype) for shape in landing]
        + [pltpu.VMEM(up_rows.shape, bf16), pltpu.VMEM(up_flat.shape, bf16)]
        + [columns, columns, pltpu.VMEM((groups, slices, GROUP, part, width), bf16)]
        + [pltpu.VMEM((width, part), bf16)] * 2
        + [pltpu.VMEM((part, width), bf16)]
        + [pltpu.VMEM(up_rows.shape, bf16), pltpu.VMEM(up_flat.shape, bf16)] * 2
        + [
            pltpu.VMEM((2, slices, GROUP, width, part), bf16),
            pltpu.VMEM((slices, GROUP, part, width), bf16),
            pltpu.VMEM((GROUP, sources * PLACES, width), f32),
            pltpu.VMEM((GROUP, sources * PLACES, width), f32),
            pltpu.VMEM(dots, f32),
            pltpu.VMEM((width, 2 * part), f32),
            pltpu.VMEM((part, width), f32),
        ]
        + [pltpu.VMEM(shape, bf16) for shape in shared_given]
        + [DMA((groups + 1, max(1 + 3 * slices, 4)))] * 2
        + spread_scratch
        + shared_scratch
        + home_scratch,
        compiler_params=pltpu.CompilerParams(
            collective_id=number, has_side_effects=True, vmem_limit_bytes=63 << 20
        ),
    )(placed, normed, gate, up_rows, up_flat, *weights, *shared_weights)
    result, shared_result, back, flat, dots = out[:5]
    grads = out[5 : 5 + 3 * slices]
    grads = [grads[kind * slices : (kind + 1) * slices] for kind in range(3)]
    return result, shared_result, back, flat, dots, grads, out[5 + 3 * slices :]


class Slot:
    def __init__(self, heads):
        _, self.ctx_size, self.expert_size = sizes_of()
        self.heads, self.count = heads, self.ctx_size * self.expert_size
        ctx, expert = lax.axis_index("ctx"), lax.axis_index("expert")
        self.me = ctx * self.expert_size + expert
        head = head_of(ctx, expert, heads, self.ctx_size, self.expert_size)
        self.holds = head < heads
        self.head = head % heads

    def device(self, place):
        return {"ctx": place // self.expert_size, "expert": place % self.expert_size}

    def partners(self):
        dp, ctx = lax.axis_index("dp"), lax.axis_index("ctx")
        dp_size = lax.axis_size("dp")
        return [self.device((self.me + i) % self.count) for i in range(1, self.count)] + [
            {"dp": (dp + d) % dp_size, "ctx": flip(ctx, c)} for d in range(1, dp_size) for c in range(self.ctx_size)
        ]

    def copy(self, source, target, send, recv, there):
        return pltpu.make_async_remote_copy(
            src_ref=source, dst_ref=target, send_sem=send, recv_sem=recv, device_id=there, device_id_type=MESH
        )

    def inward(self, blocks, landing, send, recv):
        for i in range(self.heads):
            head = (self.me + i) % self.heads
            row, column = head_place(head, self.heads, self.ctx_size, self.expert_size)
            one = self.copy(
                blocks.at[head], landing.at[self.me], send.at[head], recv.at[self.me],
                {"ctx": row, "expert": column},
            )
            yield jnp.logical_not(self.holds & (head == self.head)), one

    def inward_landed(self, landing, send, recv):
        for i in range(1, self.count):
            source = (self.me + self.count - i) % self.count
            here = landing.at[source]
            yield self.copy(here, here, send.at[0], recv.at[source], self.device(self.me))

    def outward(self, blocks, landing, send, recv, place):
        return self.copy(
            blocks.at[place], landing.at[self.head], send.at[place], recv.at[self.head], self.device(place)
        )

    def outward_landed(self, landing, send, recv):
        for head in range(self.heads):
            here = landing.at[head]
            one = self.copy(here, here, send.at[0], recv.at[head], self.device(self.me))
            yield jnp.logical_not(self.holds & (head == self.head)), one


def attend_kernel(step, heads, kinds, length_ref, blocks_ref, *refs):
    rest = iter(refs)

    def take(count):
        return [next(rest) for _ in range(count)]

    side_ins = take(len(kinds))
    qkv_ref, out_ref, total_ref, landed_ref = take(4)
    side_outs = take(len(kinds))
    key_ref, query_ref, value_ref, sent_ref = take(4)
    in_send, in_recv, out_send, out_recv = take(4)
    side = Spread(kinds, False, side_ins + side_outs + list(rest))

    slot = Slot(heads)
    rows = blocks_ref.shape[2]
    span = slot.count * rows
    greet(slot.partners())
    for needed, one in slot.inward(blocks_ref, qkv_ref, in_send, in_recv):
        pl.when(needed)(one.start)
    side.first(side.staying)
    side.keep()

    @pl.when(slot.holds)
    def _():
        qkv_ref[slot.me] = blocks_ref[slot.head]
        for one in slot.inward_landed(qkv_ref, in_send, in_recv):
            one.wait_recv()

    side.z_start()

    @pl.when(slot.holds)
    def _():
        key_ref[...] = live_keys(head_rows(qkv_ref, HEAD_DIM, HEAD_DIM), length_ref[0])
        query_ref[...] = scaled_queries(head_rows(qkv_ref, 0, HEAD_DIM))
        value_ref[...] = head_rows(qkv_ref, 2 * HEAD_DIM, HEAD_DIM)

    def query_block(q):
        here = pl.ds(q * step, step)
        query = query_ref[:, here]

        def absorb(k, state, masked):
            top, total, out = state
            there = pl.ds(k * step if masked else pl.multiple_of(k * step, step), step)
            scores = jnp.dot(key_ref[there, :], query, preferred_element_type=f32)
            if masked:
                scores = causal(scores)
            new_top = jnp.maximum(top, jnp.max(scores, axis=0, keepdims=True))
            shrink = jnp.exp(top - new_top)
            weights = jnp.exp(scores - new_top)
            total = total * shrink + jnp.sum(weights, axis=0, keepdims=True)
            out = out * shrink + jnp.dot(
                value_ref[:, there], weights.astype(bf16), preferred_element_type=f32
            )
            return new_top, total, out

        state = (
            jnp.full((1, step), masked_value, f32),
            jnp.zeros((1, step), f32),
            jnp.zeros((HEAD_DIM, step), f32),
        )
        state = absorb(q, state, True)
        if q:
            state = lax.fori_loop(0, q, lambda k, s: absorb(k, s, False), state)
        top, total, out = state
        out = out / total
        out_ref[:, here] = out
        total_ref[:, here] = top + jnp.log(total)
        for i in range(step // rows):
            place = q * (step // rows) + i
            sent_ref[place] = out[:, i * rows : (i + 1) * rows].astype(bf16)
            one = slot.outward(sent_ref, landed_ref, out_send, out_recv, place)
            pl.when(slot.me != place)(one.start)

    for q in range(span // step):
        pl.when(slot.holds)(functools.partial(query_block, q))

    @pl.when(slot.holds)
    def _():
        landed_ref[slot.head] = sent_ref[slot.me]

    side.forward_all(side.staying)
    side.first(side.moving)
    side.forward_all(side.moving)
    for needed, one in slot.outward_landed(landed_ref, out_send, out_recv):
        pl.when(needed)(one.wait_recv)
    side.paired(side.all)
    side.sent()
    for one in side.kept():
        one.wait()
    for needed, one in slot.inward(blocks_ref, qkv_ref, in_send, in_recv):
        pl.when(needed)(one.wait_send)
    for place in range(slot.count):
        one = slot.outward(sent_ref, landed_ref, out_send, out_recv, place)
        pl.when(slot.holds & (slot.me != place))(one.wait_send)


def attend(blocks, length, arrays, sizes, number):
    heads, _, rows = blocks.shape
    count = sizes[1] * sizes[2]
    span = count * rows
    step = min(512, span)
    kinds, side_shapes, side_scratch = spread_plan(arrays, None, sizes)
    out = pl.pallas_call(
        functools.partial(attend_kernel, step, heads, kinds),
        out_shape=[
            jax.ShapeDtypeStruct((count,) + blocks.shape[1:], bf16),
            jax.ShapeDtypeStruct((HEAD_DIM, span), f32),
            jax.ShapeDtypeStruct((1, span), f32),
            jax.ShapeDtypeStruct((heads, HEAD_DIM, rows), bf16),
        ]
        + side_shapes,
        in_specs=[SMEM] + [VMEM] * (1 + len(arrays)),
        out_specs=[VMEM] * 4 + [ANY] * len(arrays),
        scratch_shapes=[
            pltpu.VMEM((span, 2 * HEAD_DIM), bf16),
            pltpu.VMEM((2 * HEAD_DIM, span), bf16),
            pltpu.VMEM((HEAD_DIM, span), bf16),
            pltpu.VMEM((count, HEAD_DIM, rows), bf16),
        ]
        + [DMA((count,))] * 4
        + side_scratch,
        compiler_params=pltpu.CompilerParams(
            collective_id=number, has_side_effects=True, vmem_limit_bytes=56 << 20
        ),
    )(length, blocks, *arrays)
    return out[:4], out[4:]


def unrotate(grad_t, cosine, sine):
    half = HEAD_DIM // 2
    first, second = grad_t[:half], grad_t[half:]
    return jnp.concatenate(
        [first * cosine + second * sine, second * cosine - first * sine], axis=0
    )


def attend_back_kernel(
    step, heads, kinds, masks, length_ref, qkv_ref, out_ref, total_ref, cosine_ref, sine_ref, blocks_ref, *refs
):
    rest = iter(refs)

    def take(count):
        return [next(rest) for _ in range(count)]

    side_ins, carried = take(len(kinds)), take(len(masks))
    landed_ref = next(rest)
    side_outs, carried_out = take(len(kinds)), take(len(masks))
    upstream_ref, key_ref, query_ref, value_ref, key_t_ref, key_sum, value_sum, delta_ref, up_ref, sent_ref = take(10)
    in_send, in_recv, out_send, out_recv = take(4)
    carry = carry_copies(masks, carried, carried_out, *take(2)) if masks else []
    side = Home(kinds, False, side_ins, None, side_outs, None, list(rest))

    slot = Slot(heads)
    rows = blocks_ref.shape[2]
    span = slot.count * rows
    greet(slot.partners())
    for needed, one in slot.inward(blocks_ref, upstream_ref, in_send, in_recv):
        pl.when(needed)(one.start)
    side.start(side.all)
    for piece in side.moving:
        side.pair(piece)

    @pl.when(slot.holds)
    def _():
        key_t = head_rows(qkv_ref, HEAD_DIM, HEAD_DIM)
        key_ref[...] = live_keys(key_t, length_ref[0])
        key_t_ref[...] = key_t
        query_ref[...] = scaled_queries(head_rows(qkv_ref, 0, HEAD_DIM))
        value_t = head_rows(qkv_ref, 2 * HEAD_DIM, HEAD_DIM)
        value_ref[...] = jnp.transpose(value_t.astype(f32)).astype(bf16)
        key_sum[...] = jnp.zeros_like(key_sum)
        value_sum[...] = jnp.zeros_like(value_sum)
        upstream_ref[slot.me] = blocks_ref[slot.head]
        for one in slot.inward_landed(upstream_ref, in_send, in_recv):
            one.wait_recv()
        upstream = head_rows(upstream_ref, 0, HEAD_DIM)
        up_ref[...] = upstream
        delta_ref[...] = jnp.sum(upstream.astype(f32) * out_ref[...], axis=0, keepdims=True)

    for piece in side.moving:
        side.step(piece, 0)
    for piece in side.staying:
        side.pair(piece)
    for one in carry:
        one.start()

    def query_block(q):
        here = pl.ds(q * step, step)
        query, up = query_ref[:, here], up_ref[:, here]
        total, delta = total_ref[:, here], delta_ref[:, here]

        def meet(k, query_sum, masked):
            there = pl.ds(k * step if masked else pl.multiple_of(k * step, step), step)
            scores = jnp.dot(key_ref[there, :], query, preferred_element_type=f32)
            if masked:
                scores = causal(scores)
            probs = jnp.exp(scores - total)
            d_probs = jnp.dot(value_ref[there, :], up, preferred_element_type=f32)
            d_scores = (probs * (d_probs - delta)).astype(bf16)
            key_sum[:, there] += contract(query[:HEAD_DIM], d_scores, NT)
            value_sum[:, there] += contract(up, probs.astype(bf16), NT)
            return query_sum + contract(key_t_ref[:, there], d_scores)

        query_sum = meet(q, jnp.zeros((HEAD_DIM, step), f32), True)
        if q:
            query_sum = lax.fori_loop(0, q, lambda k, s: meet(k, s, False), query_sum)
        cosine, sine = cosine_ref[:, here], sine_ref[:, here]
        grad = jnp.concatenate(
            [
                unrotate(query_sum * score_scale, cosine, sine),
                unrotate(key_sum[:, here], cosine, sine),
                value_sum[:, here],
            ],
            axis=0,
        ).astype(bf16)
        for i in range(step // rows):
            place = q * (step // rows) + i
            sent_ref[place] = grad[:, i * rows : (i + 1) * rows]
            one = slot.outward(sent_ref, landed_ref, out_send, out_recv, place)
            pl.when(slot.me != place)(one.start)

    for q in reversed(range(span // step)):
        pl.when(slot.holds)(functools.partial(query_block, q))

    @pl.when(slot.holds)
    def _():
        landed_ref[slot.head] = sent_ref[slot.me]

    for place in range(len(bits_of(lax.axis_size("ctx")))):
        for piece in side.staying:
            if place < len(piece.order):
                side.step(piece, place)
    side.done()
    for needed, one in slot.outward_landed(landed_ref, out_send, out_recv):
        pl.when(needed)(one.wait_recv)
    for one in carry:
        one.wait()
    for needed, one in slot.inward(blocks_ref, upstream_ref, in_send, in_recv):
        pl.when(needed)(one.wait_send)
    for place in range(slot.count):
        one = slot.outward(sent_ref, landed_ref, out_send, out_recv, place)
        pl.when(slot.holds & (slot.me != place))(one.wait_send)


def attend_back(qkv, length, out, total, blocks, tables, parts, carried, masks, sizes, number):
    heads, _, rows = blocks.shape
    count = qkv.shape[0]
    span = count * rows
    step = min(512, span)
    kinds, side_shapes, side_scratch = home_plan([part.shape for part in parts], sizes)
    carry_shapes = [jax.ShapeDtypeStruct(array.shape, array.dtype) for array in carried]
    carry_sems = [DMA((len(masks), len(masks[0])))] * 2 if masks else []
    got = pl.pallas_call(
        functools.partial(attend_back_kernel, step, heads, kinds, masks),
        out_shape=[jax.ShapeDtypeStruct((heads,) + qkv.shape[1:], bf16)] + side_shapes + carry_shapes,
        in_specs=[SMEM] + [VMEM] * 6 + [ANY] * (len(parts) + len(carried)),
        out_specs=[VMEM] * (1 + len(side_shapes)) + [ANY] * len(carried),
        scratch_shapes=[
            pltpu.VMEM((count,) + blocks.shape[1:], bf16),
            pltpu.VMEM((span, 2 * HEAD_DIM), bf16),
            pltpu.VMEM((2 * HEAD_DIM, span), bf16),
            pltpu.VMEM((span, HEAD_DIM), bf16),
            pltpu.VMEM((HEAD_DIM, span), bf16),
            pltpu.VMEM((HEAD_DIM, span), f32),
            pltpu.VMEM((HEAD_DIM, span), f32),
            pltpu.VMEM((1, span), f32),
            pltpu.VMEM((HEAD_DIM, span), bf16),
            pltpu.VMEM(qkv.shape, bf16),
        ]
        + [DMA((count,))] * 4
        + carry_sems
        + side_scratch,
        compiler_params=pltpu.CompilerParams(
            collective_id=number, has_side_effects=True, vmem_limit_bytes=58 << 20
        ),
    )(length, qkv, out, total, *tables, blocks, *parts, *carried)
    return got[0], got[1 : 1 + len(side_shapes)], got[1 + len(side_shapes) :]


EXACT = lax.Precision.HIGHEST


def expert_of_place(count, stride, own):
    expert = lax.broadcasted_iota(jnp.int32, (EXPERTS, count), 0)
    column = lax.broadcasted_iota(jnp.int32, (EXPERTS, count), 1)
    place = column - ((expert // own) * stride + (expert % own) * PLACES)
    inside = (place >= 0) & (place < PLACES)
    at = jnp.sum(jnp.where(inside, place, 0), axis=0, keepdims=True)
    return inside.astype(f32), at.astype(f32)


def spots(hits, earlier, count, stride, own):
    expert_at, place_at = expert_of_place(count, stride, own)
    low = expert_at.astype(bf16)
    hit = contract(hits.astype(bf16), low)
    before = contract(earlier.astype(bf16), low)
    return jnp.where((hit > 0.5) & (before == place_at), 1.0, 0.0)


def first_place(rows):
    return (lax.axis_index("ctx") * lax.axis_size("expert") + lax.axis_index("expert")) * rows


def live(length_ref, first_ref, shape):
    return first_ref[0] + lax.broadcasted_iota(jnp.int32, shape, 0) < length_ref[0]


def routing_kernel(length_ref, first_ref, routes_ref, cotangent_ref, branch_ref, rows_ref, hits_ref, earlier_ref):
    rows = routes_ref.shape[0]
    own = EXPERTS // rows_ref.shape[0]
    alive = live(length_ref, first_ref, (rows, 1))
    expert = lax.broadcasted_iota(jnp.int32, (rows, EXPERTS), 1)
    routes = routes_ref[...]
    named = (routes[:, 0:1] == expert) | (routes[:, 1:2] == expert)
    hits = jnp.where(named, 1.0, 0.0) * jnp.where(alive, 1.0, 0.0)
    token = lax.broadcasted_iota(jnp.int32, (rows, rows), 0)
    other = lax.broadcasted_iota(jnp.int32, (rows, rows), 1)
    earlier = contract(jnp.where(other < token, 1.0, 0.0).astype(bf16), hits.astype(bf16))
    hits_ref[...] = hits
    earlier_ref[...] = earlier
    branch = jnp.where(alive, cotangent_ref[...].astype(f32), 0.0).astype(bf16)
    branch_ref[...] = branch
    spread_out = spots(hits, earlier, EXPERTS * PLACES, own * PLACES, own)
    placed = contract(jnp.transpose(spread_out).astype(bf16), branch)
    rows_ref[...] = placed.astype(bf16).reshape(rows_ref.shape)


def routing(length, first, routes, cotangent, expert_size):
    rows, width = cotangent.shape
    return pl.pallas_call(
        routing_kernel,
        out_shape=(
            jax.ShapeDtypeStruct((rows, width), bf16),
            jax.ShapeDtypeStruct((expert_size, EXPERTS // expert_size * PLACES, width), bf16),
            jax.ShapeDtypeStruct((rows, EXPERTS), f32),
            jax.ShapeDtypeStruct((rows, EXPERTS), f32),
        ),
        in_specs=[SMEM, SMEM, VMEM, VMEM],
        out_specs=(VMEM,) * 4,
    )(length, first, routes, cotangent)


def project_kernel(tokens_ref, gain_ref, query_ref, key_ref, value_ref, cosine_ref, sine_ref, normed_ref, qkv_ref):
    inputs = tokens_ref[...].astype(f32)
    normed = (inputs * rms_scale(inputs) * gain_ref[...]).astype(bf16)
    normed_ref[...] = normed
    heads, _, rows = qkv_ref.shape
    half = HEAD_DIM // 2
    cosine, sine = cosine_ref[...], sine_ref[...]
    for kind, weight in enumerate((query_ref, key_ref, value_ref)):
        lin = jnp.transpose(contract(normed, weight[...]))
        for head in range(heads):
            mine = lin[head * HEAD_DIM : (head + 1) * HEAD_DIM]
            if kind < 2:
                first, second = mine[:half], mine[half:]
                mine = jnp.concatenate(
                    [first * cosine - second * sine, second * cosine + first * sine], axis=0
                )
            qkv_ref[head, kind * HEAD_DIM : (kind + 1) * HEAD_DIM, :] = mine.astype(bf16)


def project(tokens, gain, weights, tables):
    rows, width = tokens.shape
    return pl.pallas_call(
        project_kernel,
        out_shape=(
            jax.ShapeDtypeStruct((rows, width), bf16),
            jax.ShapeDtypeStruct((width // HEAD_DIM, 3 * HEAD_DIM, rows), bf16),
        ),
        in_specs=[VMEM] * 7,
        out_specs=(VMEM,) * 2,
        compiler_params=pltpu.CompilerParams(vmem_limit_bytes=32 << 20),
    )(tokens, gain, *weights, *tables)


def middle_kernel(
    length_ref, first_ref, tokens_ref, attended_ref, output_ref, gain_ref, router_ref, hits_ref, earlier_ref,
    hidden_ref, normed_ref, rows_ref, scale_ref, gates_ref, flat_ref,
):
    rows, width = tokens_ref.shape
    expert_size = rows_ref.shape[0]
    own = EXPERTS // expert_size
    attended = jnp.transpose(attended_ref[...].reshape(width, rows).astype(f32)).astype(bf16)
    flat_ref[...] = attended
    alive = live(length_ref, first_ref, (rows, 1))
    attn_out = contract(attended, output_ref[...])
    hidden = tokens_ref[...].astype(f32) + jnp.where(alive, attn_out, 0.0)
    hidden_ref[...] = hidden
    normed = (hidden * rms_scale(hidden) * gain_ref[...]).astype(bf16)
    normed_ref[...] = normed
    hits, earlier = hits_ref[...], earlier_ref[...]
    logits = contract(normed, router_ref[...])
    top = jnp.max(jnp.where(hits > 0.5, logits, masked_value), axis=1, keepdims=True)
    powers = jnp.where(hits > 0.5, jnp.exp(logits - top), 0.0)
    total = jnp.sum(powers, axis=1, keepdims=True)
    gates = powers / jnp.where(total > 0.0, total, 1.0)
    gates_ref[...] = gates
    spread_out = spots(hits, earlier, EXPERTS * PLACES, own * PLACES, own)
    placed = contract(jnp.transpose(spread_out).astype(bf16), normed)
    rows_ref[...] = placed.astype(bf16).reshape(rows_ref.shape)
    lanes = expert_size * 128
    expert_at, _ = expert_of_place(lanes, 128, own)
    by_place = jnp.dot(gates, expert_at, preferred_element_type=f32, precision=EXACT)
    at_place = spots(hits, earlier, lanes, 128, own) * by_place
    row = jnp.sum(at_place, axis=0, keepdims=True)
    for z in range(expert_size):
        scale_ref[z] = jnp.broadcast_to(row[:, z * 128 : (z + 1) * 128], (8, 128))


def middle(length, first, tokens, attended, output_weight, gain, router, hits, earlier, expert_size):
    rows, width = tokens.shape
    return pl.pallas_call(
        middle_kernel,
        out_shape=(
            jax.ShapeDtypeStruct((rows, width), f32),
            jax.ShapeDtypeStruct((rows, width), bf16),
            jax.ShapeDtypeStruct((expert_size, EXPERTS // expert_size * PLACES, width), bf16),
            jax.ShapeDtypeStruct((expert_size, 8, 128), f32),
            jax.ShapeDtypeStruct((rows, EXPERTS), f32),
            jax.ShapeDtypeStruct((rows, width), bf16),
        ),
        in_specs=[SMEM, SMEM] + [VMEM] * 7,
        out_specs=(VMEM,) * 6,
        compiler_params=pltpu.CompilerParams(vmem_limit_bytes=32 << 20),
    )(length, first, tokens, attended, output_weight, gain, router, hits, earlier)


def turn_kernel(
    length_ref, first_ref, back_ref, flat_ref, dots_ref, hits_ref, earlier_ref, gates_ref, normed_ref, hidden_ref,
    cotangent_ref, gain_ref, router_ref, output_ref, d_hidden_ref, d_attended_ref, d_attn_ref, router_grad, gain_grad,
):
    rows, width = normed_ref.shape
    expert_size = back_ref.shape[0]
    own = EXPERTS // expert_size
    alive = live(length_ref, first_ref, (rows, 1))
    hits, earlier, gates = hits_ref[...], earlier_ref[...], gates_ref[...]
    lanes = expert_size * 128
    expert_at, _ = expert_of_place(lanes, 128, own)
    row = jnp.concatenate([dots_ref[z, 0:1, :] for z in range(expert_size)], axis=1)
    at_place = jnp.where(spots(hits, earlier, lanes, 128, own) > 0.5, row, 0.0)
    d_gates = lax.dot_general(at_place, expert_at, NT, preferred_element_type=f32, precision=EXACT)
    mean = jnp.sum(gates * d_gates, axis=1, keepdims=True)
    d_logits = (gates * (d_gates - mean)).astype(bf16)
    normed = normed_ref[...]
    router_grad[...] = contract(normed, d_logits, TN)
    spread_out = spots(hits, earlier, EXPERTS * PLACES, own * PLACES, own).astype(bf16)
    placed = back_ref[...].reshape(EXPERTS * PLACES, width)
    d_normed = contract(spread_out, placed) + flat_ref[...].astype(f32)
    d_normed = d_normed + contract(d_logits, router_ref[...], NT)
    hidden = hidden_ref[...]
    scale = rms_scale(hidden)
    normal = hidden * scale
    gain_grad[...] = jnp.sum(d_normed * normal, axis=0, keepdims=True)
    d_hidden = cotangent_ref[...].astype(f32) + rms_back(normal, scale, gain_ref[...], d_normed)
    d_hidden_ref[...] = d_hidden
    d_attn = jnp.where(alive, d_hidden, 0.0).astype(bf16)
    d_attn_ref[...] = d_attn
    d_attended = jnp.transpose(contract(d_attn, output_ref[...], NT))
    d_attended_ref[...] = d_attended.astype(bf16).reshape(d_attended_ref.shape)


def turn(length, first, back, flat, dots, hits, earlier, gates, normed, hidden, cotangent, gain, router, output_weight):
    rows, width = normed.shape
    return pl.pallas_call(
        turn_kernel,
        out_shape=(
            jax.ShapeDtypeStruct((rows, width), f32),
            jax.ShapeDtypeStruct((width // HEAD_DIM, HEAD_DIM, rows), bf16),
            jax.ShapeDtypeStruct((rows, width), bf16),
            jax.ShapeDtypeStruct((width, EXPERTS), f32),
            jax.ShapeDtypeStruct((1, width), f32),
        ),
        in_specs=[SMEM, SMEM] + [VMEM] * 12,
        out_specs=(VMEM,) * 5,
        compiler_params=pltpu.CompilerParams(vmem_limit_bytes=32 << 20),
    )(length, first, back, flat, dots, hits, earlier, gates, normed, hidden, cotangent, gain, router, output_weight)


def join_kernel(
    length_ref, first_ref, back_ref, flat_ref, hits_ref, earlier_ref, hidden_ref, out_ref,
):
    rows, width = hidden_ref.shape
    own = EXPERTS // back_ref.shape[0]
    spread_out = spots(hits_ref[...], earlier_ref[...], EXPERTS * PLACES, own * PLACES, own).astype(bf16)
    mixed = contract(spread_out, back_ref[...].reshape(EXPERTS * PLACES, width)) + flat_ref[...].astype(f32)
    alive = live(length_ref, first_ref, (rows, 1))
    out_ref[...] = (hidden_ref[...] + jnp.where(alive, mixed, 0.0)).astype(bf16)


def join(length, first, back, flat, hits, earlier, hidden):
    return pl.pallas_call(
        join_kernel,
        out_shape=jax.ShapeDtypeStruct(hidden.shape, bf16),
        in_specs=[SMEM, SMEM] + [VMEM] * 5,
        out_specs=VMEM,
        compiler_params=pltpu.CompilerParams(vmem_limit_bytes=32 << 20),
    )(length, first, back, flat, hits, earlier, hidden)


def last_kernel(
    shard, grads_ref, query_ref, key_ref, value_ref, normed_ref, tokens_ref, gain_ref, d_hidden_ref, attended_ref,
    d_attn_ref, input_grad, gain_grad, sums_ref,
):
    rows, width = normed_ref.shape
    heads = grads_ref.shape[0]
    lins = []
    d_normed = jnp.zeros((width, rows), f32)
    for kind, weight in enumerate((query_ref, key_ref, value_ref)):
        at = slice(kind * HEAD_DIM, (kind + 1) * HEAD_DIM)
        lin = jnp.concatenate([grads_ref[head, at, :] for head in range(heads)], axis=0)
        lins.append(lin)
        d_normed = d_normed + contract(weight[...], lin)
    d_normed = jnp.transpose(d_normed)
    inputs = tokens_ref[...].astype(f32)
    scale = rms_scale(inputs)
    normal = inputs * scale
    gain_grad[...] = jnp.sum(d_normed * normal, axis=0, keepdims=True)
    d_inputs = d_hidden_ref[...] + rms_back(normal, scale, gain_ref[...], d_normed)
    input_grad[...] = d_inputs.astype(bf16)
    normed_t = jnp.transpose(normed_ref[...].astype(f32)).astype(bf16)
    attended_t = jnp.transpose(attended_ref[...].astype(f32)).astype(bf16)
    grads = [contract(normed_t, lin, NT) for lin in lins] + [contract(attended_t, d_attn_ref[...])]
    plane_size, expert_size, count, _ = sums_ref.shape
    for p in range(plane_size):
        for z in range(expert_size):
            first = (p * expert_size + z) * shard
            parts = [grad[first : first + shard] for grad in grads]
            if count > 4 * shard:
                parts.append(jnp.zeros((count - 4 * shard, width), f32))
            sums_ref[p, z] = jnp.concatenate(parts, axis=0).astype(bf16)


def last(grads, weights, normed, tokens, gain, d_hidden, attended, d_attn, sizes):
    rows, width = normed.shape
    dp_size, ctx_size, expert_size = sizes
    shard = width // (dp_size * ctx_size * expert_size)
    count = -(-4 * shard // 16) * 16
    return pl.pallas_call(
        functools.partial(last_kernel, shard),
        out_shape=(
            jax.ShapeDtypeStruct((rows, width), bf16),
            jax.ShapeDtypeStruct((1, width), f32),
            jax.ShapeDtypeStruct((dp_size * ctx_size, expert_size, count, width), bf16),
        ),
        in_specs=[VMEM] * 10,
        out_specs=(VMEM,) * 3,
        compiler_params=pltpu.CompilerParams(vmem_limit_bytes=48 << 20),
    )(grads, *weights, normed, tokens, gain, d_hidden, attended, d_attn)


def local(
    tokens,
    lengths,
    routes,
    norm1_gain,
    query_weight,
    key_weight,
    value_weight,
    output_weight,
    norm2_gain,
    router_weight,
    expert_gate,
    expert_up,
    expert_down,
    shared_gate,
    shared_up,
    shared_down,
    cotangent,
):
    sizes = dp_size, ctx_size, expert_size = sizes_of()
    plane_size, slot_size = dp_size * ctx_size, ctx_size * expert_size
    rows, width = tokens.shape[1:]
    heads, own, shard = width // HEAD_DIM, EXPERTS // expert_size, width // (dp_size * slot_size)
    first = first_place(rows).astype(jnp.int32)[None]
    tokens, routes, cotangent = tokens[0], routes[0], cotangent[0]
    gain_one, gain_two = norm1_gain[None], norm2_gain[None]
    weights = (query_weight, key_weight, value_weight)

    branch_rows, up_placed, hits, earlier = routing(lengths, first, routes, cotangent, expert_size)

    groups = own // GROUP
    bits = bits_of(ctx_size)
    group_bits = [group_bit(g, ctx_size) for g in range(groups)]
    slice_masks = [subsets([bit for bit in bits if bit != mine]) for mine in group_bits]

    def grouped(placed):
        return placed.reshape(expert_size, groups, GROUP * PLACES, width)

    places = jnp.arange(rows, dtype=jnp.int32)
    normed, qkv = project(tokens, gain_one, weights, rope_tables(first[0] + places))
    (qkv, out_t, log_total, attended), (up_rows, up_flat) = attend(
        qkv, lengths, [grouped(up_placed), branch_rows], sizes, 1
    )
    hidden, normed_two, in_placed, scale, gates, attended = middle(
        lengths, first, tokens, attended, output_weight, gain_two, router_weight, hits, earlier, expert_size
    )

    result, shared_result, back, flat, dots, slice_grads, shared_grads = moe(
        grouped(in_placed), normed_two, scale, up_rows, up_flat, (expert_gate, expert_up, expert_down),
        (shared_gate, shared_up, shared_down), sizes, 3,
    )
    d_hidden, d_attended, d_attn, router_grad, gain_two_grad = turn(
        lengths, first, back, flat, dots, hits, earlier, gates, normed_two, hidden, cotangent, gain_two,
        router_weight, output_weight,
    )

    all_tables = rope_tables(jnp.arange(slot_size * rows, dtype=jnp.int32))
    others = [
        (array, tuple(masks[k] for masks in slice_masks))
        for slices in slice_grads
        for k, array in enumerate(slices)
        if k
    ]
    early, late = others[: len(others) // 3], others[len(others) // 3 :]
    d_qkv, (out_back, out_flat), early_in = attend_back(
        qkv, lengths, out_t, log_total, d_attended, all_tables, [result, shared_result],
        [array for array, _ in early], tuple(masks for _, masks in early), sizes, 6,
    )
    output_rows = join(lengths, first, out_back, out_flat, hits, earlier, hidden)

    input_grad, gain_one_grad, sums = last(
        d_qkv, weights, normed, tokens, gain_one, d_hidden, attended, d_attn, sizes
    )
    devices = (plane_size, expert_size)
    small = jnp.concatenate(
        [
            router_grad.reshape(devices + (shard * EXPERTS,)),
            gain_one_grad.reshape(devices + (shard,)),
            gain_two_grad.reshape(devices + (shard,)),
        ],
        axis=-1,
    )
    small = jnp.pad(small, [(0, 0), (0, 0), (0, 1024 - small.shape[-1])])
    sums, small, *late_in = bring_home(
        [sums], sizes, 8, small.reshape(devices + (8, 128)),
        carried=[array for array, _ in late], masks=tuple(masks for _, masks in late),
    )
    arrived = list(early_in) + list(late_in)
    count = len(arrived) // 3
    expert_grads = [
        sum((array.astype(f32) for array in arrived[kind * count : (kind + 1) * count]), slices[0].astype(f32))
        for kind, slices in enumerate(slice_grads)
    ]
    sums = jnp.sum(sums.astype(f32), axis=0)
    small = jnp.sum(small, axis=0).reshape(1024)
    routed = shard * EXPERTS
    return (
        output_rows[None],
        input_grad[None],
        small[routed : routed + shard],
        *(sums[kind * shard : (kind + 1) * shard] for kind in range(4)),
        small[routed + shard : routed + 2 * shard],
        small[:routed].reshape(shard, EXPERTS),
        *expert_grads,
        *shared_grads,
    )


def solution(mesh):
    tokens = P("dp", ("ctx", "expert"), None)
    whole = P()
    experts = P("expert", None, None)
    everywhere = ("dp", "ctx", "expert")
    return jax.shard_map(
        local,
        mesh=mesh,
        in_specs=(tokens, P("dp"), tokens)
        + (whole,) * 7
        + (experts,) * 3
        + (whole,) * 3
        + (tokens,),
        out_specs=(tokens, tokens, P(everywhere))
        + (P(everywhere, None),) * 4
        + (P(everywhere), P(everywhere, None))
        + (P("expert", None, PLANE),) * 2
        + (P("expert", PLANE, None),)
        + (P(everywhere, None),) * 3,
        check_vma=False,
    )
```

```python
import functools

import jax
import jax.numpy as jnp
from jax import lax
from jax.experimental import pallas as pl
from jax.experimental.pallas import tpu as pltpu
from jax.sharding import PartitionSpec as P

HEAD_DIM = 64
EXPERTS = 16
TOP = 2
CAP = 22
PLACES = 24

norm_epsilon = 1e-06
rope_base = 10000.0
score_scale = 0.125
masked_value = -1e30
PLANE = ("dp", "ctx")
SLOT = ("ctx", "expert")
bf16 = jnp.bfloat16
f32 = jnp.float32


def rms_scale(values):
    return lax.rsqrt(jnp.mean(values * values, axis=-1, keepdims=True) + norm_epsilon)


def rms_back(normal, scale, gain, upstream):
    lifted = upstream * gain
    return scale * (lifted - normal * jnp.mean(lifted * normal, axis=-1, keepdims=True))


def rope_tables(positions):
    half = HEAD_DIM // 2
    exponent = jnp.arange(half, dtype=f32) * (2.0 / HEAD_DIM)
    inverse_freq = rope_base ** (-exponent)
    angles = inverse_freq[:, None] * positions[None, :].astype(f32)
    return jnp.cos(angles), jnp.sin(angles)


def head_rows(qkv_ref, first, count):
    return jnp.concatenate(
        [qkv_ref[block, first : first + count, :] for block in range(qkv_ref.shape[0])], axis=1
    )


def live_keys(key_t, length):
    span = key_t.shape[1]
    place = lax.broadcasted_iota(jnp.int32, (8, span), 1)
    row = lax.broadcasted_iota(jnp.int32, (8, span), 0)
    bias = jnp.where((place >= length) & (row == 0), masked_value, 0.0)
    padded = jnp.concatenate(
        [key_t.astype(f32), bias, jnp.zeros((HEAD_DIM - 8, span), f32)], axis=0
    )
    return jnp.transpose(padded).astype(bf16)


def scaled_queries(query_t):
    span = query_t.shape[1]
    row = lax.broadcasted_iota(jnp.int32, (HEAD_DIM, span), 0)
    ones = jnp.where(row == 0, 1.0, 0.0)
    return jnp.concatenate([query_t.astype(f32) * score_scale, ones], axis=0).astype(bf16)


def causal(scores):
    key = lax.broadcasted_iota(jnp.int32, scores.shape, 0)
    query = lax.broadcasted_iota(jnp.int32, scores.shape, 1)
    return jnp.where(key <= query, scores, masked_value)


MESH = pl.DeviceIdType.MESH
ANY = pl.BlockSpec(memory_space=pl.ANY)
VMEM = pl.BlockSpec(memory_space=pltpu.VMEM)
SMEM = pl.BlockSpec(memory_space=pltpu.SMEM)
DMA = pltpu.SemaphoreType.DMA


def head_place(head, heads, ctx_size, expert_size):
    per = expert_size - 1
    if ctx_size <= expert_size and ctx_size * per == heads:
        row = head // per
        step = head % per
        return row, step + jnp.where(step >= row, 1, 0)
    return head // expert_size, head % expert_size


def head_of(ctx, expert, heads, ctx_size, expert_size):
    per = expert_size - 1
    if ctx_size <= expert_size and ctx_size * per == heads:
        head = ctx * per + expert - jnp.where(expert > ctx, 1, 0)
        return jnp.where(expert == ctx, heads, head)
    return ctx * expert_size + expert


def sizes_of():
    return tuple(lax.axis_size(a) for a in ("dp", "ctx", "expert"))


def greet(partners, meanwhile=lambda: None):
    barrier = pltpu.get_barrier_semaphore()
    for partner in partners:
        pl.semaphore_signal(barrier, inc=1, device_id=partner, device_id_type=MESH)
    meanwhile()
    pl.semaphore_wait(barrier, len(partners))


def fetch(sources, targets, sems):
    return [
        pltpu.make_async_copy(source, target, sems.at[i]) for i, (source, target) in enumerate(zip(sources, targets))
    ]


GROUP = 2


def flip(index, mask):
    bit = 1
    while bit <= mask:
        if mask & bit:
            index = index + bit * (1 - 2 * ((index // bit) % 2))
        bit *= 2
    return index


def bits_of(ctx_size):
    return [1 << b for b in range(ctx_size.bit_length() - 1)]


def group_bit(group, ctx_size):
    bits = bits_of(ctx_size)
    return bits[group % len(bits)]


def subsets(order):
    masks = [0]
    for bit in order:
        masks = masks + [m | bit for m in masks]
    return masks


class Piece:
    def __init__(self, array, kind, group, step, first, size, order):
        self.array, self.kind, self.group, self.step = array, kind, group, step
        self.first, self.size, self.order = first, size, order
        self.masks = subsets(order)


def pieces(kinds, expert_size, ctx_size):
    bits = bits_of(ctx_size)
    moving, staying = [], []
    for array, (kind, groups, rows) in enumerate(kinds):
        if kind == "flat":
            half = rows // 2
            staying.append(Piece(array, kind, None, None, 0, half, bits))
            staying.append(Piece(array, kind, None, None, half, rows - half, bits[::-1]))
            continue
        for group in range(groups or 1):
            for step in range(expert_size):
                if kind == "group":
                    order = [group_bit(group, ctx_size)]
                else:
                    order = bits if (step + array) % 2 == 0 else bits[::-1]
                (moving if step else staying).append(Piece(array, kind, group, step, 0, rows, order))
    return moving, staying


class Spread:
    def __init__(self, kinds, has_gate, refs, near=False):
        self.near = near
        rest = iter(refs)

        def take(count):
            return [next(rest) for _ in range(count)]

        self.has_gate = has_gate
        self.ins = take(len(kinds))
        self.gate = next(rest) if has_gate else None
        self.outs = take(len(kinds))
        self.gates = next(rest) if has_gate else None
        self.z_send, self.z_recv, self.send, self.recv, self.pair_recv, self.local_sem = take(6)
        if has_gate:
            self.gate_send, self.gate_recv, self.gate_z_send, self.gate_z_recv = take(4)
        self.dp_size, self.ctx_size, self.expert_size = sizes_of()
        self.dp, self.ctx, self.expert = (lax.axis_index(a) for a in ("dp", "ctx", "expert"))
        self.moving, self.staying = pieces(kinds, self.expert_size, self.ctx_size)
        self.all = self.staying + self.moving
        self.number = {id(piece): i for i, piece in enumerate(self.all)}
        self.own = self.dp * self.ctx_size + self.ctx
        self.other = (self.dp + 1) % self.dp_size
        self.bits = bits_of(self.ctx_size)
        self.started = []
        self.plane = [(d, c) for d in range(self.dp_size) for c in range(self.ctx_size) if (d, c) != (0, 0)]

    def z_at(self, step):
        return (self.expert + step) % self.expert_size

    def z_from(self, step):
        return (self.expert + self.expert_size - step) % self.expert_size

    def block(self, core, mask):
        return (self.dp if core == 0 else self.other) * self.ctx_size + flip(self.ctx, mask)

    def landed(self, piece, core, mask, at=0):
        out = self.outs[piece.array]
        if piece.step is None:
            return out.at[self.block(core, mask), pl.ds(piece.first, piece.size)]
        return out.at[piece.group, core * 2 + (1 if mask ^ at else 0), self.z_from(piece.step)]

    def source(self, piece):
        if piece.step is None:
            return self.ins[piece.array].at[pl.ds(piece.first, piece.size)]
        if piece.step == 0:
            return self.ins[piece.array].at[self.expert, piece.group]
        return self.landed(piece, 0, 0)

    def remote(self, source, target, send, recv, there):
        return pltpu.make_async_remote_copy(
            src_ref=source, dst_ref=target, send_sem=send, recv_sem=recv, device_id=there, device_id_type=MESH
        )

    def z_copy(self, piece, landing=False):
        place = self.z_from(piece.step) if landing else self.expert
        at = self.number[id(piece)]
        return self.remote(
            self.ins[piece.array].at[self.z_at(piece.step), piece.group],
            self.outs[piece.array].at[piece.group, 0, place],
            self.z_send.at[at],
            self.z_recv.at[at],
            {"expert": self.z_at(piece.step)},
        )

    def gate_z(self, step, landing=False):
        return self.remote(
            self.gate.at[self.z_at(step)],
            self.gates.at[self.own, self.z_from(step) if landing else self.expert],
            self.gate_z_send.at[step],
            self.gate_z_recv.at[step],
            {"expert": self.z_at(step)},
        )

    def gate_plane(self, d, c, block):
        return self.remote(
            self.gates.at[block],
            self.gates.at[block],
            self.gate_send.at[d, c],
            self.gate_recv.at[d, c],
            {"dp": (self.dp + d) % self.dp_size, "ctx": flip(self.ctx, c)},
        )

    def passing(self, piece, mask, bit):
        at = self.number[id(piece)]
        return self.remote(
            self.landed(piece, 0, mask) if mask else self.source(piece),
            self.landed(piece, 0, mask, bit),
            self.send.at[at, mask, self.bits.index(bit)],
            self.recv.at[at, mask ^ bit],
            {"ctx": flip(self.ctx, bit)},
        )

    def arrived(self, piece, mask):
        here = self.landed(piece, 0, mask)
        recv = self.recv.at[self.number[id(piece)], mask]
        return self.remote(here, here, self.send.at[0, 0, 0], recv, {"ctx": self.ctx})

    def crossing(self, piece, mask, landing=False):
        at = self.number[id(piece)]
        core = 0 if piece.step is None and not landing else 1
        return self.remote(
            self.landed(piece, 0, mask) if mask else self.source(piece),
            self.landed(piece, core, mask),
            self.send.at[at, mask, len(self.bits)],
            self.pair_recv.at[at, mask],
            {"dp": self.other},
        )

    def kept(self):
        if self.near:
            return []
        return [
            pltpu.make_async_copy(self.source(piece), self.landed(piece, 0, 0), self.local_sem.at[i])
            for i, piece in enumerate(self.staying)
        ]

    def begin(self, one):
        one.start()
        self.started.append(one)

    def z_start(self):
        if self.has_gate:
            for step in range(1, self.expert_size):
                self.gate_z(step).start()
        for piece in self.moving:
            self.z_copy(piece).start()

    def first(self, some):
        for piece in some:
            if piece.step:
                self.z_copy(piece, True).wait_recv()
            for bit in piece.order:
                self.begin(self.passing(piece, 0, bit))
            self.begin(self.crossing(piece, 0))

    def keep(self):
        for one in self.kept():
            one.start()
        if self.near:
            for piece in self.staying:
                target = self.landed(piece, 0, 0)
                target[...] = self.source(piece)[...]
        if self.has_gate:
            self.gates[self.own, self.expert] = self.gate[self.expert]

    def forward(self, piece, place):
        if place >= len(piece.order):
            return
        bit = piece.order[place]
        for mask in [m | bit for m in subsets(piece.order[:place])]:
            self.arrived(piece, mask).wait_recv()
            for later in piece.order[place + 1 :]:
                self.begin(self.passing(piece, mask, later))
            self.begin(self.crossing(piece, mask))

    def forward_all(self, some):
        for place in range(len(self.bits)):
            for piece in some:
                self.forward(piece, place)

    def gates_on(self):
        for step in range(1, self.expert_size):
            self.gate_z(step, True).wait_recv()
        for d, c in self.plane:
            self.gate_plane(d, c, self.own).start()

    def gates_landed(self):
        for d, c in self.plane:
            block = ((self.dp + d) % self.dp_size) * self.ctx_size + flip(self.ctx, c)
            self.gate_plane(d, c, block).wait_recv()

    def paired(self, some):
        for piece in some:
            for mask in piece.masks:
                self.crossing(piece, mask, True).wait_recv()

    def sent(self):
        for one in self.started:
            one.wait_send()
        for piece in self.moving:
            self.z_copy(piece).wait_send()
        if self.has_gate:
            for step in range(1, self.expert_size):
                self.gate_z(step).wait_send()
            for d, c in self.plane:
                self.gate_plane(d, c, self.own).wait_send()


def plane_partners():
    dp_size, ctx_size, expert_size = sizes_of()
    dp, ctx, expert = (lax.axis_index(a) for a in ("dp", "ctx", "expert"))
    plane = [(d, c) for d in range(dp_size) for c in range(ctx_size) if (d, c) != (0, 0)]
    return [{"expert": (expert + step) % expert_size} for step in range(1, expert_size)] + [
        {"dp": (dp + d) % dp_size, "ctx": flip(ctx, c)} for d, c in plane
    ]


def spread_plan(arrays, gate, sizes):
    dp_size, ctx_size, expert_size = sizes
    assert dp_size == 2
    plane_size = dp_size * ctx_size
    kinds, out_shape = [], []
    for array in arrays:
        if array.ndim == 4:
            kinds.append(("group", array.shape[1], array.shape[2]))
            shape = (array.shape[1], 4, expert_size) + array.shape[2:]
        else:
            kinds.append(("flat", None, array.shape[0]))
            shape = (plane_size,) + array.shape
        out_shape.append(jax.ShapeDtypeStruct(shape, array.dtype))
    moving, staying = pieces(kinds, expert_size, ctx_size)
    count = len(moving + staying)
    scratch = [
        DMA((count,)),
        DMA((count,)),
        DMA((count, ctx_size, len(bits_of(ctx_size)) + 1)),
        DMA((count, ctx_size)),
        DMA((count, ctx_size)),
        DMA((len(staying),)),
    ]
    if gate is not None:
        out_shape.append(jax.ShapeDtypeStruct((plane_size,) + gate.shape, gate.dtype))
        scratch += [DMA((dp_size, ctx_size))] * 2 + [DMA((expert_size,))] * 2
    return tuple(kinds), out_shape, scratch


def stage(piece, place):
    order = piece.order[::-1]
    done, bit = sum(order[:place]), order[place]
    kept = [m for m in piece.masks if not m & (done | bit)]
    return bit, [(m | bit, m) for m in kept]


def buffer_places(order):
    held, arriving, here, there = {}, {}, 0, 0
    for piece in order:
        for mask in piece.masks:
            held[id(piece), mask] = here
            here += piece.size
        for place in range(len(piece.order)):
            for index in range(len(stage(piece, place)[1])):
                arriving[id(piece), place, index] = there
                there += piece.size
    held["rows"], arriving["rows"] = here, there
    return held, arriving


class Home:
    def __init__(self, kinds, has_dots, parts, dot, outs, dots_out, scratch, near=False):
        self.near = near
        rest = iter(scratch)

        def take(count):
            return [next(rest) for _ in range(count)]

        self.parts, self.dot, self.outs, self.dots_out, self.has_dots = parts, dot, outs, dots_out, has_dots
        self.mine, self.theirs, self.arrivals = take(3)
        self.mine_sem, self.pair_send, self.pair_recv, self.send, self.recv, self.z_send, self.z_recv = take(7)
        if has_dots:
            self.dot_in, self.dot_sum, self.dot_send, self.dot_recv, self.dot_z_send, self.dot_z_recv = take(6)
        self.dp_size, self.ctx_size, self.expert_size = sizes_of()
        self.dp, self.ctx, self.expert = (lax.axis_index(a) for a in ("dp", "ctx", "expert"))
        self.moving, self.staying = pieces(kinds, self.expert_size, self.ctx_size)
        self.all = self.moving + self.staying
        self.number = {id(piece): i for i, piece in enumerate(self.all)}
        self.held, self.arriving = buffer_places(self.all)
        self.own = self.dp * self.ctx_size + self.ctx
        self.other = (self.dp + 1) % self.dp_size
        self.plane = [(d, c) for d in range(self.dp_size) for c in range(self.ctx_size) if (d, c) != (0, 0)]

    def z_at(self, step):
        return (self.expert + step) % self.expert_size

    def z_from(self, step):
        return (self.expert + self.expert_size - step) % self.expert_size

    def plane_at(self, d, c):
        return ((self.dp + d) % self.dp_size) * self.ctx_size + flip(self.ctx, c)

    def partner(self, d, c):
        return {"dp": (self.dp + d) % self.dp_size, "ctx": flip(self.ctx, c)}

    def remote(self, source, target, send, recv, there):
        return pltpu.make_async_remote_copy(
            src_ref=source, dst_ref=target, send_sem=send, recv_sem=recv, device_id=there, device_id_type=MESH
        )

    def whole(self, piece, core, mask):
        part = self.parts[piece.array]
        if piece.kind == "group":
            return part.at[piece.group, core * 2 + (1 if mask else 0), self.z_at(piece.step)]
        block = (self.dp if core == 0 else self.other) * self.ctx_size + flip(self.ctx, mask)
        if piece.kind == "flat":
            return part.at[block, pl.ds(piece.first, piece.size)]
        return part.at[block, self.z_at(piece.step)]

    def at(self, piece, mask):
        return pl.ds(self.held[id(piece), mask], piece.size)

    def load(self, piece, mask):
        return pltpu.make_async_copy(
            self.whole(piece, 0, mask), self.mine.at[self.at(piece, mask)], self.mine_sem.at[self.number[id(piece)], mask]
        )

    def cross(self, piece, mask):
        number = self.number[id(piece)]
        return self.remote(
            self.whole(piece, 1, mask),
            self.theirs.at[self.at(piece, mask)],
            self.pair_send.at[number, mask],
            self.pair_recv.at[number, mask],
            {"dp": self.other},
        )

    def hop(self, piece, place, index):
        bit, moves = stage(piece, place)
        number = self.number[id(piece)]
        return self.remote(
            self.mine.at[self.at(piece, moves[index][0])],
            self.arrivals.at[pl.ds(self.arriving[id(piece), place, index], piece.size)],
            self.send.at[number, moves[index][0]],
            self.recv.at[number, place, index],
            {"ctx": flip(self.ctx, bit)},
        )

    def z_copy(self, piece, landing=False):
        place = self.z_from(piece.step) if landing else self.expert
        out, number = self.outs[piece.array], self.number[id(piece)]
        return self.remote(
            self.mine.at[self.at(piece, 0)],
            out.at[place, piece.group] if piece.kind == "group" else out.at[place],
            self.z_send.at[number],
            self.z_recv.at[number],
            {"expert": self.z_at(piece.step)},
        )

    def start(self, some):
        for piece in some:
            for mask in piece.masks:
                self.cross(piece, mask).start()
                if not self.near:
                    self.load(piece, mask).start()

    def add(self, here, buffer, there):
        total = self.mine[here].astype(f32) + buffer[there].astype(f32)
        self.mine[here] = total.astype(self.mine.dtype)

    def pair(self, piece):
        leaving = [source for source, _ in stage(piece, 0)[1]]
        for mask in leaving + [m for m in piece.masks if m not in leaving]:
            here = self.at(piece, mask)
            if not self.near:
                self.load(piece, mask).wait()
            self.cross(piece, mask).wait_recv()
            if self.near:
                total = self.whole(piece, 0, mask)[...].astype(f32) + self.theirs[here].astype(f32)
                self.mine[here] = total.astype(self.mine.dtype)
            else:
                self.add(here, self.theirs, here)
            if mask in leaving:
                self.hop(piece, 0, leaving.index(mask)).start()

    def step(self, piece, place):
        targets = [target for _, target in stage(piece, place)[1]]
        leaving = []
        if place + 1 < len(piece.order):
            leaving = [source for source, _ in stage(piece, place + 1)[1]]
        for index in range(len(targets)):
            self.hop(piece, place, index).wait_recv()
        for mask in leaving + [m for m in targets if m not in leaving]:
            there = pl.ds(self.arriving[id(piece), place, targets.index(mask)], piece.size)
            self.add(self.at(piece, mask), self.arrivals, there)
            if mask in leaving:
                self.hop(piece, place + 1, leaving.index(mask)).start()
        if place + 1 == len(piece.order):
            self.finish(piece)

    def finish(self, piece):
        result, out = self.mine.at[self.at(piece, 0)], self.outs[piece.array]
        if piece.kind == "flat":
            out[pl.ds(piece.first, piece.size)] = result[...]
        elif piece.step:
            self.z_copy(piece).start()
        elif piece.kind == "group":
            out[self.expert, piece.group] = result[...]
        else:
            out[self.expert] = result[...]

    def ticks(self, some, ahead):
        depth = max(len(piece.order) for piece in some)
        for tick in range(len(some) + ahead + depth):
            for place in range(depth + 1):
                index = tick if place == 0 else tick - ahead - place + 1
                if not 0 <= index < len(some) or place > len(some[index].order):
                    continue
                if place == 0:
                    self.pair(some[index])
                else:
                    self.step(some[index], place - 1)
            yield

    def dot_plane(self, d, c):
        return self.remote(
            self.dot.at[self.plane_at(d, c)],
            self.dot_in.at[d, c],
            self.dot_send.at[d, c],
            self.dot_recv.at[d, c],
            self.partner(d, c),
        )

    def dot_z(self, step, landing=False):
        return self.remote(
            self.dot_sum.at[self.z_at(step)],
            self.dots_out.at[self.z_from(step) if landing else self.expert],
            self.dot_z_send.at[step],
            self.dot_z_recv.at[step],
            {"expert": self.z_at(step)},
        )

    def dots_start(self):
        for d, c in self.plane:
            self.dot_plane(d, c).start()

    def dots_on(self):
        total = self.dot[self.own]
        for d, c in self.plane:
            self.dot_plane(d, c).wait_recv()
            total = total + self.dot_in[d, c]
        self.dot_sum[...] = total
        for step in range(1, self.expert_size):
            self.dot_z(step).start()
        self.dots_out[self.expert] = self.dot_sum[self.expert]

    def done(self):
        for piece in self.moving:
            self.z_copy(piece, True).wait_recv()
        if self.has_dots:
            for step in range(1, self.expert_size):
                self.dot_z(step, True).wait_recv()
                self.dot_z(step).wait_send()
            for d, c in self.plane:
                self.dot_plane(d, c).wait_send()
        for piece in self.moving:
            self.z_copy(piece).wait_send()
        for piece in self.all:
            for mask in piece.masks:
                self.cross(piece, mask).wait_send()
            for place in range(len(piece.order)):
                for index in range(len(stage(piece, place)[1])):
                    self.hop(piece, place, index).wait_send()


def home_plan(shapes, sizes, dots=None):
    dp_size, ctx_size, expert_size = sizes
    assert dp_size == 2
    width = shapes[0][-1]
    kinds, out_shape = [], []
    for given in shapes:
        if len(given) == 5:
            kinds.append(("group", given[0], given[3]))
            shape = (expert_size, given[0]) + given[3:]
        else:
            kinds.append(("plane" if len(given) == 4 else "flat", None, given[-2]))
            shape = given[1:]
        out_shape.append(jax.ShapeDtypeStruct(shape, bf16))
    moving, staying = pieces(kinds, expert_size, ctx_size)
    held, arriving = buffer_places(moving + staying)
    count, depth = len(moving + staying), len(bits_of(ctx_size))
    scratch = [
        pltpu.VMEM((held["rows"], width), bf16),
        pltpu.VMEM((held["rows"], width), bf16),
        pltpu.VMEM((arriving["rows"], width), bf16),
        DMA((count, ctx_size)),
        DMA((count, ctx_size)),
        DMA((count, ctx_size)),
        DMA((count, ctx_size)),
        DMA((count, depth, max(ctx_size // 2, 1))),
        DMA((count,)),
        DMA((count,)),
    ]
    if dots is not None:
        out_shape.append(jax.ShapeDtypeStruct(dots[1:], f32))
        scratch += [
            pltpu.VMEM((dp_size, ctx_size) + dots[1:], f32),
            pltpu.VMEM(dots[1:], f32),
            DMA((dp_size, ctx_size)),
            DMA((dp_size, ctx_size)),
            DMA((expert_size,)),
            DMA((expert_size,)),
        ]
    return tuple(kinds), out_shape, scratch


class Shared:
    def __init__(self, grads, outs, scratch):
        self.grads, self.outs = grads, outs
        self.landing, self.columns = scratch[:3], scratch[3:5]
        self.send, self.recv, self.column_send, self.column_recv = scratch[5:]
        self.dp_size, self.ctx_size, self.expert_size = sizes_of()
        self.dp, self.ctx, self.expert = (lax.axis_index(a) for a in ("dp", "ctx", "expert"))
        self.own = self.dp * self.ctx_size + self.ctx
        self.plane = [(d, c) for d in range(self.dp_size) for c in range(self.ctx_size) if (d, c) != (0, 0)]
        self.part = grads[0].shape[2]

    def z_copy(self, kind, step):
        there = (self.expert + step) % self.expert_size
        return pltpu.make_async_remote_copy(
            src_ref=self.grads[kind].at[there],
            dst_ref=self.landing[kind].at[step],
            send_sem=self.send.at[kind, step],
            recv_sem=self.recv.at[kind, step],
            device_id={"expert": there},
            device_id_type=MESH,
        )

    def column(self, kind, d, c, landing=False):
        there = ((self.dp + d) % self.dp_size) * self.ctx_size + flip(self.ctx, c)
        source = ((self.dp + self.dp_size - d) % self.dp_size) * self.ctx_size + flip(self.ctx, c)
        at = source if landing else self.own
        return pltpu.make_async_remote_copy(
            src_ref=self.columns[kind].at[there],
            dst_ref=self.outs[kind].at[:, pl.ds(pl.multiple_of(at * self.part, 128), self.part)],
            send_sem=self.column_send.at[kind, d, c],
            recv_sem=self.column_recv.at[kind, d, c],
            device_id={"dp": (self.dp + d) % self.dp_size, "ctx": flip(self.ctx, c)},
            device_id_type=MESH,
        )

    def start(self):
        for kind in range(3):
            for step in range(1, self.expert_size):
                self.z_copy(kind, step).start()

    def sum(self):
        for kind in range(3):
            total = self.grads[kind][self.expert].astype(f32)
            for step in range(1, self.expert_size):
                self.z_copy(kind, step).wait_recv()
                total = total + self.landing[kind][step].astype(f32)
            if kind == 2:
                self.outs[2][...] = total
                continue
            shard = self.outs[kind].shape[0]
            for block in range(self.dp_size * self.ctx_size):
                self.columns[kind][block] = total[block * shard : (block + 1) * shard]
            for d, c in self.plane:
                self.column(kind, d, c).start()
            here = pl.ds(pl.multiple_of(self.own * self.part, 128), self.part)
            self.outs[kind][:, here] = self.columns[kind][self.own]

    def done(self):
        for kind in range(3):
            for step in range(1, self.expert_size):
                self.z_copy(kind, step).wait_send()
            if kind < 2:
                for d, c in self.plane:
                    self.column(kind, d, c, True).wait_recv()
                    self.column(kind, d, c).wait_send()


def shared_plan(width, part, sizes):
    dp_size, ctx_size, expert_size = sizes
    plane_size = dp_size * ctx_size
    shard = width // (plane_size * expert_size)
    given = [(expert_size, plane_size * shard, part)] * 2 + [(expert_size, part // expert_size, width)]
    columns = jax.ShapeDtypeStruct((shard, plane_size * part), f32)
    out_shape = [columns, columns, jax.ShapeDtypeStruct(given[2][1:], f32)]
    scratch = [pltpu.VMEM(shape, bf16) for shape in given]
    scratch += [pltpu.VMEM((plane_size, shard, part), f32)] * 2
    scratch += [
        DMA((3, expert_size)),
        DMA((3, expert_size)),
        DMA((2, dp_size, ctx_size)),
        DMA((2, dp_size, ctx_size)),
    ]
    return given, out_shape, scratch


class Carry:
    CHUNKS = 8

    def __init__(self, masks, sources, targets, sems):
        self.masks, self.sources, self.targets, self.sems = masks, sources, targets, sems
        self.ctx = lax.axis_index("ctx")
        groups = len(masks[0]) if masks else 0
        self.queues = [
            [
                (array, g, e, chunk)
                for array in range(len(masks))
                for e in range(GROUP)
                for chunk in range(self.CHUNKS)
            ]
            for g in range(groups)
        ]

    def copy(self, array, g, e, rows):
        return pltpu.make_async_remote_copy(
            src_ref=self.sources[array][g].at[e, rows],
            dst_ref=self.targets[array].at[g * GROUP + e, rows],
            send_sem=self.sems[0].at[array, g],
            recv_sem=self.sems[1].at[array, g],
            device_id={"ctx": flip(self.ctx, self.masks[array][g])},
            device_id_type=MESH,
        )

    def push(self, count, groups=None):
        for g in range(len(self.queues)) if groups is None else groups:
            for array, _, e, chunk in self.queues[g][:count]:
                rows = self.sources[array][g].shape[1] // self.CHUNKS
                self.copy(array, g, e, pl.ds(chunk * rows, rows)).start()
            del self.queues[g][:count]

    def done(self):
        for array, by_group in enumerate(self.masks):
            for g in range(len(by_group)):
                whole = pltpu.make_async_remote_copy(
                    src_ref=self.sources[array][g],
                    dst_ref=self.targets[array].at[pl.ds(g * GROUP, GROUP)],
                    send_sem=self.sems[0].at[array, g],
                    recv_sem=self.sems[1].at[array, g],
                    device_id={"ctx": flip(self.ctx, by_group[g])},
                    device_id_type=MESH,
                )
                whole.wait_recv()
                whole.wait_send()


def by_group(arrays, groups):
    return [[array.at[pl.ds(g * GROUP, GROUP)] for g in range(groups)] for array in arrays]


def sums_kernel(kinds, masks, *refs):
    rest = iter(refs)

    def take(count):
        return [next(rest) for _ in range(count)]

    part, dot, carried = next(rest), next(rest), take(len(masks))
    landed, dots_landed, carried_out = next(rest), next(rest), take(len(masks))
    sems = take(2) if masks else []
    carry = Carry(masks, by_group(carried, len(masks[0]) if masks else 0), carried_out, sems)
    home = Home(kinds, True, [part], dot, [landed], dots_landed, list(rest))
    greet(plane_partners())
    home.start(home.all)
    home.dots_start()
    for tick, _ in enumerate(home.ticks(home.all, 2)):
        if tick >= 2:
            carry.push(1)
    home.dots_on()
    carry.push(len(masks) * GROUP * carry.CHUNKS)
    home.done()
    carry.done()


def bring_sums(part, dots, carried, masks, sizes, number):
    kinds, out_shape, scratch = home_plan([part.shape], sizes, dots.shape)
    return pl.pallas_call(
        functools.partial(sums_kernel, kinds, masks),
        out_shape=out_shape + [jax.ShapeDtypeStruct(array.shape, array.dtype) for array in carried],
        in_specs=[ANY, VMEM] + [ANY] * len(carried),
        out_specs=[VMEM] * 2 + [ANY] * len(carried),
        scratch_shapes=([DMA((len(masks), len(masks[0])))] * 2 if masks else []) + scratch,
        compiler_params=pltpu.CompilerParams(
            collective_id=number, has_side_effects=True, vmem_limit_bytes=58 << 20
        ),
    )(part, dots, *carried)


def finish_kernel(slices, kept, *refs):
    rest = iter(refs)

    def take(count):
        return [next(rest) for _ in range(count)]

    slices_in, landed, dots_landed, through = take(3 * slices), next(rest), next(rest), take(kept)
    grads, sums, dots, outs = take(3), take(4), next(rest), take(kept)
    for kind, grad in enumerate(grads):
        total = slices_in[kind][...].astype(f32)
        for k in range(1, slices):
            total = total + slices_in[k * 3 + kind][...].astype(f32)
        grad[...] = total

    @pl.when(pl.program_id(0) == 0)
    def _():
        for source, target in zip(through, outs):
            target[...] = source[...]
        expert_size, shard = landed.shape[0], sums[0].shape[0]
        whole, small = landed[0].astype(f32), dots_landed[0]
        for z in range(1, expert_size):
            whole = whole + landed[z].astype(f32)
            small = small + dots_landed[z]
        for i, out in enumerate(sums):
            out[...] = whole[i * shard : (i + 1) * shard]
        dots[...] = small


def finish(slices_in, landed, dots_landed, through, shard):
    width = landed.shape[-1]
    slices = len(slices_in) // 3
    own = slices_in[0].shape[0]

    def each(array):
        return pl.BlockSpec((1,) + array.shape[1:], lambda e: (e, 0, 0))

    def whole(array):
        return pl.BlockSpec(array.shape, lambda e: (0,) * len(array.shape))

    sums = [jax.ShapeDtypeStruct((shard, width), f32)] * 4 + [jax.ShapeDtypeStruct(dots_landed.shape[1:], f32)]
    kept = [jax.ShapeDtypeStruct(array.shape, array.dtype) for array in through]
    return pl.pallas_call(
        functools.partial(finish_kernel, slices, len(through)),
        grid=(own,),
        out_shape=[jax.ShapeDtypeStruct(array.shape, f32) for array in slices_in[:3]] + sums + kept,
        in_specs=[each(array) for array in slices_in]
        + [whole(array) for array in [landed, dots_landed] + list(through)],
        out_specs=[each(array) for array in slices_in[:3]] + [whole(array) for array in sums + kept],
        compiler_params=pltpu.CompilerParams(vmem_limit_bytes=48 << 20),
    )(*slices_in, landed, dots_landed, *through)


NT = (((1,), (1,)), ((), ()))
TN = (((0,), (0,)), ((), ()))


def contract(a, b, dims=(((1,), (0,)), ((), ()))):
    return lax.dot_general(a, b, dims, preferred_element_type=f32)


EXACT = lax.Precision.HIGHEST


def expert_of_place(count, stride, own):
    expert = lax.broadcasted_iota(jnp.int32, (EXPERTS, count), 0)
    column = lax.broadcasted_iota(jnp.int32, (EXPERTS, count), 1)
    place = column - ((expert // own) * stride + (expert % own) * PLACES)
    inside = (place >= 0) & (place < PLACES)
    at = jnp.sum(jnp.where(inside, place, 0), axis=0, keepdims=True)
    return inside.astype(f32), at.astype(f32)


def spots(hits, earlier, count, stride, own):
    expert_at, place_at = expert_of_place(count, stride, own)
    low = expert_at.astype(bf16)
    hit = contract(hits.astype(bf16), low)
    before = contract(earlier.astype(bf16), low)
    return jnp.where((hit > 0.5) & (before == place_at), 1.0, 0.0)


def row_spots(hits, earlier, expert_size):
    own = EXPERTS // expert_size
    return spots(hits, earlier, EXPERTS * PLACES, own * PLACES, own)


def first_place(rows):
    return (lax.axis_index("ctx") * lax.axis_size("expert") + lax.axis_index("expert")) * rows


def live(length_ref, rows):
    return first_place(rows) + lax.broadcasted_iota(jnp.int32, (rows, 1), 0) < length_ref[0]


def route(routes, alive):
    rows = routes.shape[1]
    expert = lax.broadcasted_iota(jnp.int32, (EXPERTS, rows), 0)
    named = (routes[0:1] == expert) | (routes[1:2] == expert)
    hits = jnp.transpose(jnp.where(named, 1.0, 0.0)) * jnp.where(alive, 1.0, 0.0)
    token = lax.broadcasted_iota(jnp.int32, (rows, rows), 0)
    other = lax.broadcasted_iota(jnp.int32, (rows, rows), 1)
    earlier = contract(jnp.where(other < token, 1.0, 0.0).astype(bf16), hits.astype(bf16))
    return hits, earlier


def place_rows(hits, earlier, flat, placed_ref):
    spread_out = jnp.transpose(row_spots(hits, earlier, placed_ref.shape[0])).astype(bf16)
    placed_ref[...] = contract(spread_out, flat).astype(bf16).reshape(placed_ref.shape)


def project(normed, weights, cosine, sine, qkv_ref):
    heads = qkv_ref.shape[0]
    half = HEAD_DIM // 2
    for kind, weight in enumerate(weights):
        lin = jnp.transpose(contract(normed, weight[...]))
        for head in range(heads):
            mine = lin[head * HEAD_DIM : (head + 1) * HEAD_DIM]
            if kind < 2:
                first, second = mine[:half], mine[half:]
                mine = jnp.concatenate(
                    [first * cosine - second * sine, second * cosine + first * sine], axis=0
                )
            qkv_ref[head, kind * HEAD_DIM : (kind + 1) * HEAD_DIM, :] = mine.astype(bf16)


def router_gates(normed, router, hits):
    logits = contract(normed, router, NT)
    top = jnp.max(jnp.where(hits > 0.5, logits, masked_value), axis=1, keepdims=True)
    powers = jnp.where(hits > 0.5, jnp.exp(logits - top), 0.0)
    total = jnp.sum(powers, axis=1, keepdims=True)
    return powers / jnp.where(total > 0.0, total, 1.0)


def gate_tiles(gates, hits, earlier, scale_ref):
    expert_size = scale_ref.shape[0]
    own, lanes = EXPERTS // expert_size, expert_size * 128
    expert_at, _ = expert_of_place(lanes, 128, own)
    by_place = jnp.dot(gates, expert_at, preferred_element_type=f32, precision=EXACT)
    row = jnp.sum(spots(hits, earlier, lanes, 128, own) * by_place, axis=0, keepdims=True)
    for z in range(expert_size):
        scale_ref[z] = jnp.broadcast_to(row[:, z * 128 : (z + 1) * 128], (8, 128))


def gates_back(dots_ref, gates, hits, earlier):
    expert_size = dots_ref.shape[0]
    own, lanes = EXPERTS // expert_size, expert_size * 128
    expert_at, _ = expert_of_place(lanes, 128, own)
    row = jnp.concatenate([dots_ref[z, 0:1, :] for z in range(expert_size)], axis=1)
    at_place = jnp.where(spots(hits, earlier, lanes, 128, own) > 0.5, row, 0.0)
    d_gates = lax.dot_general(at_place, expert_at, NT, preferred_element_type=f32, precision=EXACT)
    mean = jnp.sum(gates * d_gates, axis=1, keepdims=True)
    return (gates * (d_gates - mean)).astype(bf16)


def collect(hits, earlier, back_ref, flat_ref):
    width = flat_ref.shape[1]
    spread_out = row_spots(hits, earlier, back_ref.shape[0]).astype(bf16)
    placed = back_ref[...].reshape(EXPERTS * PLACES, width)
    return contract(spread_out, placed) + flat_ref[...].astype(f32)


def weight_sums(shard, grads, sums_ref):
    plane_size, expert_size, count, width = sums_ref.shape
    for p in range(plane_size):
        for z in range(expert_size):
            first = (p * expert_size + z) * shard
            parts = [grad[first : first + shard] for grad in grads]
            if count > len(grads) * shard:
                parts.append(jnp.zeros((count - len(grads) * shard, width), f32))
            sums_ref[p, z] = jnp.concatenate(parts, axis=0).astype(bf16)


def branch(rows, d_out, gate_w, up_w, down_w):
    gate_lin, up_lin = contract(rows, gate_w), contract(rows, up_w)
    sigmoid = 1.0 / (1.0 + jnp.exp(-gate_lin))
    silu = gate_lin * sigmoid
    hidden = (silu * up_lin).astype(bf16)
    d_hidden = contract(d_out, down_w, NT)
    d_gate = (d_hidden * up_lin * (sigmoid + silu * (1.0 - sigmoid))).astype(bf16)
    d_up = (d_hidden * silu).astype(bf16)
    result = contract(hidden, down_w)
    d_rows = contract(d_gate, gate_w, NT) + contract(d_up, up_w, NT)
    d_lin = contract(rows, jnp.concatenate([d_gate, d_up], axis=1), TN)
    d_down = contract(hidden, d_out, TN)
    return result, d_rows, d_lin, d_down


def moe_kernel(spread_kinds, home_kinds, slices, length_ref, *refs):
    rest = iter(refs)

    def take(count):
        return [next(rest) for _ in range(count)]

    tokens, attended_in, gain, router, hits_ref, earlier_ref, cotangent = take(7)
    output_in = next(rest)
    up_rows_in, up_flat_in = take(2)
    weights_in, shared_in = take(3), take(3)
    hidden, attended_out, d_hidden_out, d_attended_out, d_attn_out, router_grad, gain_grad = take(7)
    shared_grads_out = take(3)
    result_out, shared_out = take(2)
    grads_out = take(3 * slices)
    placed, normed, gate, output_w, output_sem = take(5)
    back, flat, dots_out = take(3)
    in_rows, in_flat, gates = take(3)
    up_rows, up_flat = take(2)
    weights, shared_w = take(3), take(3)
    result, shared_result = take(2)
    d_rows, shared_d = up_rows, up_flat
    lin_out, down_out, rows_f32, up_f32, dot, gates_own = take(6)
    lin_sum, down_sum = take(2)
    shared_parts = take(3)
    load_sem, store_sem = take(2)
    spread = Spread(spread_kinds, True, [placed, normed, gate, in_rows, in_flat, gates] + take(10), True)
    shared_sums = Shared(shared_parts, shared_grads_out, take(9))
    home = Home(home_kinds, True, [d_rows, shared_d], dot, [back, flat], dots_out, list(rest), True)

    dp_size, ctx_size, expert_size = sizes_of()
    ctx, own_block = lax.axis_index("ctx"), spread.own
    groups, blocks, _, size, width = in_rows.shape
    plane_size, rows, _ = in_flat.shape
    part = weights[0].shape[-1]
    sources = blocks * expert_size
    bits = bits_of(ctx_size)

    def column(mask):
        return pl.ds(pl.multiple_of(spread.block(0, mask) * part, 128), part)

    def loads(g):
        masks = subsets([bit for bit in bits if bit != group_bit(g, ctx_size)])
        experts = pl.ds(g * GROUP, GROUP)
        copies = [(up_rows_in.at[g], up_rows.at[g])]
        for k, mask in enumerate(masks):
            copies += [
                (weights_in[0].at[experts, :, column(mask)], weights[0].at[g, k]),
                (weights_in[1].at[experts, :, column(mask)], weights[1].at[g, k]),
                (weights_in[2].at[experts, column(mask)], weights[2].at[g, k]),
            ]
        return [pltpu.make_async_copy(s, t, load_sem.at[g, i]) for i, (s, t) in enumerate(copies)]

    shared_loads = [
        pltpu.make_async_copy(s, t, load_sem.at[groups, i])
        for i, (s, t) in enumerate(
            [
                (shared_in[0].at[:, column(0)], shared_w[0]),
                (shared_in[1].at[:, column(0)], shared_w[1]),
                (shared_in[2].at[column(0)], shared_w[2]),
                (up_flat_in, up_flat),
            ]
        )
    ]
    (output_load,) = fetch([output_in], [output_w], output_sem)
    output_load.start()
    for one in shared_loads:
        one.start()
    for g in range(groups):
        for one in loads(g):
            one.start()
    alive = live(length_ref, rows)
    hits, earlier = hits_ref[...], earlier_ref[...]

    def prepare():
        attended = jnp.transpose(attended_in[...].reshape(width, rows).astype(f32)).astype(bf16)
        attended_out[...] = attended
        output_load.wait()
        attn_out = contract(attended, output_w[...])
        into = tokens[...].astype(f32) + jnp.where(alive, attn_out, 0.0)
        hidden[...] = into
        normed[...] = (into * rms_scale(into) * gain[...][None]).astype(bf16)
        gates_own[...] = router_gates(normed[...], router[...], hits)
        place_rows(hits, earlier, normed[...], placed)
        gate_tiles(gates_own[...], hits, earlier, gate)

    greet(plane_partners(), prepare)
    spread.z_start()
    spread.first(spread.staying)
    spread.keep()
    dot[...] = jnp.zeros_like(dot)
    def arriving(g):
        return [piece for piece in spread.moving if piece.group == g]

    spread.forward_all(spread.staying)
    spread.first(arriving(0))
    spread.gates_on()
    spread.paired(spread.staying)
    for one in spread.kept() + shared_loads:
        one.wait()

    def shared_part(first, count):
        here = pl.ds(first, count)
        shape = (count * rows, width)
        some = branch(
            in_flat[here].reshape(shape), up_flat[here].reshape(shape), shared_w[0][...], shared_w[1][...],
            shared_w[2][...],
        )
        shared_result[here] = some[0].reshape((count, rows, width)).astype(bf16)
        shared_d[here] = some[1].reshape((count, rows, width)).astype(bf16)
        if first == 0:
            lin_sum[...] = some[2]
            down_sum[...] = some[3]
        else:
            lin_sum[...] += some[2]
            down_sum[...] += some[3]

    chunk = 4
    flats = home.staying[-2:]
    flat_store = pltpu.make_async_copy(shared_result, shared_out, store_sem.at[groups, 0])
    shared_part(0, chunk)
    spread.forward_all(arriving(0))
    for g in range(1, groups):
        spread.first(arriving(g))
    spread.gates_landed()
    spread.paired(arriving(0))

    def shared_rest():
        for first in range(chunk, plane_size, chunk):
            shared_part(first, chunk)
        home.start(flats)
        shard = shared_parts[0].shape[1] // plane_size
        for z in range(expert_size):
            firsts = [(p * expert_size + z) * shard for p in range(plane_size)]
            mine = jnp.concatenate([lin_sum[first : first + shard] for first in firsts]).astype(bf16)
            shared_parts[0][z] = mine[:, :part]
            shared_parts[1][z] = mine[:, part:]
        shared_parts[2][...] = down_sum[...].astype(bf16).reshape(shared_parts[2].shape)
        flat_store.start()
        shared_sums.start()

    def expert(g, i):
        bit = group_bit(g, ctx_size)
        lane = (g * GROUP + i) * PLACES
        owners = [spread.block(core, mask) for core in (0, 1) for mask in (0, bit)]
        scale = jnp.concatenate(
            [gates[owner, z, 0:1, lane : lane + PLACES] for owner in owners for z in range(expert_size)]
        )[:, :, None]
        by_source = (sources, PLACES, width)
        up = up_f32[i]
        d_out = (up.reshape(by_source) * scale).reshape(up.shape).astype(bf16)
        some, d_some, d_lin, d_down = branch(
            rows_f32[i].astype(bf16),
            d_out,
            jnp.concatenate([weights[0][g, k, i] for k in range(slices)], axis=1),
            jnp.concatenate([weights[1][g, k, i] for k in range(slices)], axis=1),
            jnp.concatenate([weights[2][g, k, i] for k in range(slices)], axis=0),
        )
        for k in range(slices):
            lin_out[g, 0, k, i] = d_lin[:, k * part : (k + 1) * part].astype(bf16)
            lin_out[g, 1, k, i] = d_lin[:, (slices + k) * part : (slices + k + 1) * part].astype(bf16)
            down_out[g, k, i] = d_down[k * part : (k + 1) * part, :].astype(bf16)
        sums = jnp.sum((some * up).reshape(by_source), axis=-1)
        up_f32[i] = (some.reshape(by_source) * scale).reshape(up.shape)
        rows_f32[i] = d_some
        for at, owner in enumerate(owners):
            for z in range(expert_size):
                line = sums[at * expert_size + z : at * expert_size + z + 1]
                pieces_of = [line]
                if lane:
                    pieces_of.insert(0, jnp.zeros((1, lane), f32))
                if lane + PLACES < 128:
                    pieces_of.append(jnp.zeros((1, 128 - lane - PLACES), f32))
                dot[owner, z, 0:1, :] += jnp.concatenate(pieces_of, axis=1)

    def unpack(g):
        def one(source, carry):
            there = pl.ds(pl.multiple_of(source * PLACES, 8), PLACES)
            at = g, source // expert_size, source % expert_size
            some, up = in_rows[at].astype(f32), up_rows[at].astype(f32)
            for i in range(GROUP):
                rows_f32[i, there] = some[i * PLACES : (i + 1) * PLACES]
                up_f32[i, there] = up[i * PLACES : (i + 1) * PLACES]
            return carry

        lax.fori_loop(0, sources, one, 0)

    def pack(g):
        def one(source, carry):
            there = pl.ds(pl.multiple_of(source * PLACES, 8), PLACES)
            at = g, source // expert_size, source % expert_size
            result[at] = jnp.concatenate([up_f32[i, there] for i in range(GROUP)]).astype(bf16)
            d_rows[at] = jnp.concatenate([rows_f32[i, there] for i in range(GROUP)]).astype(bf16)
            return carry

        lax.fori_loop(0, sources, one, 0)

    def stores_of(g):
        experts = pl.ds(g * GROUP, GROUP)
        copies = [(result.at[g], result_out.at[g])]
        for k in range(slices):
            copies += [
                (lin_out.at[g, 0, k], grads_out[k].at[experts]),
                (lin_out.at[g, 1, k], grads_out[slices + k].at[experts]),
                (down_out.at[g, k], grads_out[2 * slices + k].at[experts]),
            ]
        return [pltpu.make_async_copy(s, t, store_sem.at[g, i]) for i, (s, t) in enumerate(copies)]

    def of_group(g):
        return [piece for piece in home.moving + home.staying if piece.group == g]

    depth = len(bits)
    waiting = []

    def move_on(count):
        for stage_of in waiting[:count]:
            stage_of()
        del waiting[:count]

    for g in range(groups):
        for one in loads(g):
            one.wait()
        if g:
            spread.paired(arriving(g))
        unpack(g)
        for i in range(GROUP):
            expert(g, i)
            if g == 0 and i == 0:
                for later in range(1, groups):
                    spread.forward_all(arriving(later))
            move_on(-(-len(waiting) // (GROUP - i)))
        if g == groups - 1:
            home.dots_start()
        pack(g)
        home.start(of_group(g))
        for one in stores_of(g):
            one.start()
        if g == 0:
            shared_rest()
        waiting += [functools.partial(home.pair, piece) for piece in of_group(g)]
        if g == 0:
            waiting += [functools.partial(home.pair, piece) for piece in flats]
        waiting += [functools.partial(home.step, piece, 0) for piece in of_group(g)]
        if g == 0:
            for place in range(depth):
                waiting += [functools.partial(home.step, piece, place) for piece in flats]
    move_on(len(waiting) // 2)
    home.dots_on()
    move_on(len(waiting))
    shared_sums.sum()
    home.done()

    d_logits = gates_back(dots_out, gates_own[...], hits, earlier)
    router_grad[...] = contract(normed[...], d_logits, TN)
    d_normed = collect(hits, earlier, back, flat) + contract(d_logits, router[...])
    into = hidden[...]
    scale = rms_scale(into)
    normal = into * scale
    gain_grad[...] = jnp.sum(d_normed * normal, axis=0, keepdims=True)
    d_hidden = cotangent[...].astype(f32) + rms_back(normal, scale, gain[...][None], d_normed)
    d_hidden_out[...] = d_hidden
    d_attn = jnp.where(alive, d_hidden, 0.0).astype(bf16)
    d_attn_out[...] = d_attn
    d_attended = jnp.transpose(contract(d_attn, output_w[...], NT))
    d_attended_out[...] = d_attended.astype(bf16).reshape(d_attended_out.shape)

    shared_sums.done()
    spread.sent()
    for g in range(groups):
        for one in stores_of(g):
            one.wait()
    flat_store.wait()


def moe(length, tokens, attended, gain, router, routing, cotangent, output_weight, up_rows, up_flat, weights,
        shared_weights, sizes, number):
    dp_size, ctx_size, expert_size = sizes
    plane_size = dp_size * ctx_size
    rows, width = tokens.shape
    part = shared_weights[0].shape[1] // plane_size
    slices = max(ctx_size // 2, 1)
    own = EXPERTS // expert_size
    groups = own // GROUP
    sources = 4 * expert_size
    placed = jax.ShapeDtypeStruct((expert_size, groups, GROUP * PLACES, width), bf16)
    flat = jax.ShapeDtypeStruct((rows, width), bf16)
    hidden = jax.ShapeDtypeStruct((rows, width), f32)
    gate = jax.ShapeDtypeStruct((expert_size, 8, 128), f32)
    spread_kinds, landing, spread_scratch = spread_plan([placed, flat], gate, sizes)
    dots = (plane_size,) + gate.shape
    home_kinds, home_out, home_scratch = home_plan([up_rows.shape, up_flat.shape], sizes, dots)
    shared_given, shared_out, shared_scratch = shared_plan(width, part, sizes)
    lin = jax.ShapeDtypeStruct((own, width, part), bf16)
    down = jax.ShapeDtypeStruct((own, part, width), bf16)
    columns = pltpu.VMEM((groups, slices, GROUP, width, part), bf16)

    def buffers(shapes):
        return [pltpu.VMEM(shape.shape, shape.dtype) for shape in shapes]

    out = pl.pallas_call(
        functools.partial(moe_kernel, spread_kinds, home_kinds, slices),
        out_shape=[
            hidden,
            flat,
            hidden,
            jax.ShapeDtypeStruct(attended.shape, bf16),
            flat,
            jax.ShapeDtypeStruct(router.shape[::-1], f32),
            jax.ShapeDtypeStruct((1, width), f32),
        ]
        + shared_out
        + [jax.ShapeDtypeStruct(up_rows.shape, bf16), jax.ShapeDtypeStruct(up_flat.shape, bf16)]
        + [lin] * (2 * slices)
        + [down] * slices,
        in_specs=[SMEM] + [VMEM] * 7 + [ANY] * 9,
        out_specs=[VMEM] * 10 + [ANY] * (2 + 3 * slices),
        scratch_shapes=buffers([placed, flat, gate])
        + [pltpu.VMEM(output_weight.shape, bf16), DMA((1,))]
        + buffers(home_out)
        + buffers(landing)
        + [pltpu.VMEM(up_rows.shape, bf16), pltpu.VMEM(up_flat.shape, bf16)]
        + [columns, columns, pltpu.VMEM((groups, slices, GROUP, part, width), bf16)]
        + [pltpu.VMEM((width, part), bf16)] * 2
        + [pltpu.VMEM((part, width), bf16)]
        + [pltpu.VMEM(up_rows.shape, bf16), pltpu.VMEM(up_flat.shape, bf16)]
        + [
            pltpu.VMEM((groups, 2, slices, GROUP, width, part), bf16),
            pltpu.VMEM((groups, slices, GROUP, part, width), bf16),
            pltpu.VMEM((GROUP, sources * PLACES, width), f32),
            pltpu.VMEM((GROUP, sources * PLACES, width), f32),
            pltpu.VMEM(dots, f32),
            pltpu.VMEM((rows, EXPERTS), f32),
            pltpu.VMEM((width, 2 * part), f32),
            pltpu.VMEM((part, width), f32),
        ]
        + [pltpu.VMEM(shape, bf16) for shape in shared_given]
        + [DMA((groups + 1, max(1 + 3 * slices, 4)))] * 2
        + spread_scratch
        + shared_scratch
        + home_scratch,
        compiler_params=pltpu.CompilerParams(
            collective_id=number, has_side_effects=True, vmem_limit_bytes=63 << 20
        ),
    )(length, tokens, attended, gain, router, *routing, cotangent, output_weight, up_rows, up_flat, *weights,
      *shared_weights)
    grads = out[12 : 12 + 3 * slices]
    grads = [grads[kind * slices : (kind + 1) * slices] for kind in range(3)]
    return out[:7], out[7:10], out[10:12], grads


class Slot:
    def __init__(self, heads):
        _, self.ctx_size, self.expert_size = sizes_of()
        self.heads, self.count = heads, self.ctx_size * self.expert_size
        ctx, expert = lax.axis_index("ctx"), lax.axis_index("expert")
        self.me = ctx * self.expert_size + expert
        head = head_of(ctx, expert, heads, self.ctx_size, self.expert_size)
        self.holds = head < heads
        self.head = head % heads

    def device(self, place):
        return {"ctx": place // self.expert_size, "expert": place % self.expert_size}

    def partners(self):
        dp, ctx = lax.axis_index("dp"), lax.axis_index("ctx")
        dp_size = lax.axis_size("dp")
        return [self.device((self.me + i) % self.count) for i in range(1, self.count)] + [
            {"dp": (dp + d) % dp_size, "ctx": flip(ctx, c)} for d in range(1, dp_size) for c in range(self.ctx_size)
        ]

    def copy(self, source, target, send, recv, there):
        return pltpu.make_async_remote_copy(
            src_ref=source, dst_ref=target, send_sem=send, recv_sem=recv, device_id=there, device_id_type=MESH
        )

    def inward(self, blocks, landing, send, recv):
        for i in range(self.heads):
            head = (self.me + i) % self.heads
            row, column = head_place(head, self.heads, self.ctx_size, self.expert_size)
            one = self.copy(
                blocks.at[head], landing.at[self.me], send.at[head], recv.at[self.me],
                {"ctx": row, "expert": column},
            )
            yield jnp.logical_not(self.holds & (head == self.head)), one

    def inward_landed(self, landing, send, recv):
        for i in range(1, self.count):
            source = (self.me + self.count - i) % self.count
            here = landing.at[source]
            yield self.copy(here, here, send.at[0], recv.at[source], self.device(self.me))

    def outward(self, blocks, landing, send, recv, place):
        return self.copy(
            blocks.at[place], landing.at[self.head], send.at[place], recv.at[self.head], self.device(place)
        )

    def outward_landed(self, landing, send, recv):
        for head in range(self.heads):
            here = landing.at[head]
            one = self.copy(here, here, send.at[0], recv.at[head], self.device(self.me))
            yield jnp.logical_not(self.holds & (head == self.head)), one


def attend_kernel(
    step, heads, kinds, length_ref, routes_ref, cotangent_ref, tokens_ref, gain_ref, cosine_ref, sine_ref, *refs
):
    rest = iter(refs)

    def take(count):
        return [next(rest) for _ in range(count)]

    weights_in = take(3)
    qkv_ref, out_ref, total_ref, landed_ref, normed_ref, hits_ref, earlier_ref = take(7)
    side_outs = take(len(kinds))
    weights, blocks_ref, placed_ref, branch_ref = take(3), *take(3)
    key_ref, query_ref, value_ref, sent_ref = take(4)
    in_send, in_recv, out_send, out_recv, weight_sem = take(5)
    side = Spread(kinds, False, [placed_ref, branch_ref] + side_outs + list(rest))

    slot = Slot(heads)
    rows, width = tokens_ref.shape
    span = slot.count * rows
    loads = fetch(weights_in, weights, weight_sem)
    for one in loads:
        one.start()

    def prepare():
        alive = live(length_ref, rows)
        hits, earlier = route(routes_ref[...], alive)
        hits_ref[...] = hits
        earlier_ref[...] = earlier
        branch = jnp.where(alive, cotangent_ref[...].astype(f32), 0.0).astype(bf16)
        branch_ref[...] = branch
        place_rows(hits, earlier, branch, placed_ref)

    greet(slot.partners(), prepare)
    side.z_start()
    inputs = tokens_ref[...].astype(f32)
    normed_ref[...] = (inputs * rms_scale(inputs) * gain_ref[...][None]).astype(bf16)
    for one in loads:
        one.wait()
    here = pl.ds(pl.multiple_of(slot.me * rows, 128), rows)
    project(normed_ref[...], weights, cosine_ref[:, here], sine_ref[:, here], blocks_ref)
    for needed, one in slot.inward(blocks_ref, qkv_ref, in_send, in_recv):
        pl.when(needed)(one.start)
    side.first(side.staying)
    side.keep()
    side.forward_all(side.staying)

    @pl.when(slot.holds)
    def _():
        qkv_ref[slot.me] = blocks_ref[slot.head]
        for one in slot.inward_landed(qkv_ref, in_send, in_recv):
            one.wait_recv()
        key_ref[...] = live_keys(head_rows(qkv_ref, HEAD_DIM, HEAD_DIM), length_ref[0])
        query_ref[...] = scaled_queries(head_rows(qkv_ref, 0, HEAD_DIM))
        value_ref[...] = head_rows(qkv_ref, 2 * HEAD_DIM, HEAD_DIM)

    def query_block(q):
        here = pl.ds(q * step, step)
        query = query_ref[:, here]

        def absorb(k, state, masked):
            top, total, out = state
            there = pl.ds(k * step if masked else pl.multiple_of(k * step, step), step)
            scores = jnp.dot(key_ref[there, :], query, preferred_element_type=f32)
            if masked:
                scores = causal(scores)
            new_top = jnp.maximum(top, jnp.max(scores, axis=0, keepdims=True))
            shrink = jnp.exp(top - new_top)
            weights = jnp.exp(scores - new_top)
            total = total * shrink + jnp.sum(weights, axis=0, keepdims=True)
            out = out * shrink + jnp.dot(
                value_ref[:, there], weights.astype(bf16), preferred_element_type=f32
            )
            return new_top, total, out

        state = (
            jnp.full((1, step), masked_value, f32),
            jnp.zeros((1, step), f32),
            jnp.zeros((HEAD_DIM, step), f32),
        )
        state = absorb(q, state, True)
        if q:
            state = lax.fori_loop(0, q, lambda k, s: absorb(k, s, False), state)
        top, total, out = state
        out = out / total
        out_ref[:, here] = out
        total_ref[:, here] = top + jnp.log(total)
        for i in range(step // rows):
            place = q * (step // rows) + i
            sent_ref[place] = out[:, i * rows : (i + 1) * rows].astype(bf16)
            one = slot.outward(sent_ref, landed_ref, out_send, out_recv, place)
            pl.when(slot.me != place)(one.start)

    side.first(side.moving)
    for q in range(span // step):
        pl.when(slot.holds)(functools.partial(query_block, q))
        if q == span // step - 2:
            side.forward_all(side.moving)

    @pl.when(slot.holds)
    def _():
        landed_ref[slot.head] = sent_ref[slot.me]

    for needed, one in slot.outward_landed(landed_ref, out_send, out_recv):
        pl.when(needed)(one.wait_recv)
    side.paired(side.all)
    side.sent()
    for one in side.kept():
        one.wait()
    for needed, one in slot.inward(blocks_ref, qkv_ref, in_send, in_recv):
        pl.when(needed)(one.wait_send)
    for place in range(slot.count):
        one = slot.outward(sent_ref, landed_ref, out_send, out_recv, place)
        pl.when(slot.holds & (slot.me != place))(one.wait_send)


def attend(length, routes, cotangent, tokens, gain, tables, weights, sizes, number):
    rows, width = tokens.shape
    _, ctx_size, expert_size = sizes
    heads, count = width // HEAD_DIM, ctx_size * expert_size
    span = count * rows
    step = min(512, span)
    groups = EXPERTS // expert_size // GROUP
    placed = jax.ShapeDtypeStruct((expert_size, groups, GROUP * PLACES, width), bf16)
    flat = jax.ShapeDtypeStruct((rows, width), bf16)
    kinds, side_shapes, side_scratch = spread_plan([placed, flat], None, sizes)
    blocks = (heads, 3 * HEAD_DIM, rows)
    hits = jax.ShapeDtypeStruct((rows, EXPERTS), f32)
    out = pl.pallas_call(
        functools.partial(attend_kernel, step, heads, kinds),
        out_shape=[
            jax.ShapeDtypeStruct((count,) + blocks[1:], bf16),
            jax.ShapeDtypeStruct((HEAD_DIM, span), f32),
            jax.ShapeDtypeStruct((1, span), f32),
            jax.ShapeDtypeStruct((heads, HEAD_DIM, rows), bf16),
            flat,
            hits,
            hits,
        ]
        + side_shapes,
        in_specs=[SMEM] + [VMEM] * 6 + [ANY] * 3,
        out_specs=[VMEM] * 7 + [ANY] * len(side_shapes),
        scratch_shapes=[pltpu.VMEM(weights[0].shape, bf16)] * 3
        + [
            pltpu.VMEM(blocks, bf16),
            pltpu.VMEM(placed.shape, bf16),
            pltpu.VMEM(flat.shape, bf16),
            pltpu.VMEM((span, 2 * HEAD_DIM), bf16),
            pltpu.VMEM((2 * HEAD_DIM, span), bf16),
            pltpu.VMEM((HEAD_DIM, span), bf16),
            pltpu.VMEM((count, HEAD_DIM, rows), bf16),
        ]
        + [DMA((count,))] * 4
        + [DMA((3,))]
        + side_scratch,
        compiler_params=pltpu.CompilerParams(
            collective_id=number, has_side_effects=True, vmem_limit_bytes=56 << 20
        ),
    )(length, routes, cotangent, tokens, gain, *tables, *weights)
    return out[:4], out[4:7], out[7:]


def unrotate(grad_t, cosine, sine):
    half = HEAD_DIM // 2
    first, second = grad_t[:half], grad_t[half:]
    return jnp.concatenate(
        [first * cosine + second * sine, second * cosine - first * sine], axis=0
    )


def attend_back_kernel(
    step, heads, kinds, masks, shard, length_ref, qkv_ref, out_ref, total_ref, cosine_ref, sine_ref, blocks_ref,
    normed_ref, tokens_ref, gain_ref, d_hidden_ref, attended_ref, d_attn_ref, hidden_ref, hits_ref, earlier_ref, *refs
):
    rest = iter(refs)

    def take(count):
        return [next(rest) for _ in range(count)]

    weights_in, side_ins, carried = take(3), take(len(kinds)), take(len(masks))
    output_ref, input_grad, gain_grad, sums_ref = take(4)
    carried_out = take(len(masks))
    weights, landed_ref, side_outs = take(3), next(rest), take(len(kinds))
    upstream_ref, key_ref, query_ref, value_ref, key_t_ref, key_sum, value_sum, delta_ref, up_ref, sent_ref = take(10)
    in_send, in_recv, out_send, out_recv, weight_sem = take(5)
    carry = Carry(
        masks, by_group(carried, len(masks[0]) if masks else 0), carried_out, take(2) if masks else []
    )
    side = Home(kinds, False, side_ins, None, side_outs, None, list(rest))

    slot = Slot(heads)
    rows = blocks_ref.shape[2]
    span = slot.count * rows
    loads = fetch(weights_in, weights, weight_sem)
    for one in loads:
        one.start()

    @pl.when(slot.holds)
    def _():
        key_sum[...] = jnp.zeros_like(key_sum)
        value_sum[...] = jnp.zeros_like(value_sum)

    greet(slot.partners())
    for needed, one in slot.inward(blocks_ref, upstream_ref, in_send, in_recv):
        pl.when(needed)(one.start)
    side.start(side.all)

    @pl.when(slot.holds)
    def _():
        key_t = head_rows(qkv_ref, HEAD_DIM, HEAD_DIM)
        key_ref[...] = live_keys(key_t, length_ref[0])
        key_t_ref[...] = key_t
        query_ref[...] = scaled_queries(head_rows(qkv_ref, 0, HEAD_DIM))
        value_t = head_rows(qkv_ref, 2 * HEAD_DIM, HEAD_DIM)
        value_ref[...] = jnp.transpose(value_t.astype(f32)).astype(bf16)
        upstream_ref[slot.me] = blocks_ref[slot.head]

    for piece in side.moving:
        side.pair(piece)

    @pl.when(slot.holds)
    def _():
        for one in slot.inward_landed(upstream_ref, in_send, in_recv):
            one.wait_recv()
        upstream = head_rows(upstream_ref, 0, HEAD_DIM)
        up_ref[...] = upstream
        delta_ref[...] = jnp.sum(upstream.astype(f32) * out_ref[...], axis=0, keepdims=True)

    def query_block(q):
        here = pl.ds(q * step, step)
        query, up = query_ref[:, here], up_ref[:, here]
        total, delta = total_ref[:, here], delta_ref[:, here]

        def meet(k, query_sum, masked):
            there = pl.ds(k * step if masked else pl.multiple_of(k * step, step), step)
            scores = jnp.dot(key_ref[there, :], query, preferred_element_type=f32)
            if masked:
                scores = causal(scores)
            probs = jnp.exp(scores - total)
            d_probs = jnp.dot(value_ref[there, :], up, preferred_element_type=f32)
            d_scores = (probs * (d_probs - delta)).astype(bf16)
            key_sum[:, there] += contract(query[:HEAD_DIM], d_scores, NT)
            value_sum[:, there] += contract(up, probs.astype(bf16), NT)
            return query_sum + contract(key_t_ref[:, there], d_scores)

        query_sum = meet(q, jnp.zeros((HEAD_DIM, step), f32), True)
        if q:
            query_sum = lax.fori_loop(0, q, lambda k, s: meet(k, s, False), query_sum)
        cosine, sine = cosine_ref[:, here], sine_ref[:, here]
        grad = jnp.concatenate(
            [
                unrotate(query_sum * score_scale, cosine, sine),
                unrotate(key_sum[:, here], cosine, sine),
                value_sum[:, here],
            ],
            axis=0,
        ).astype(bf16)
        for i in range(step // rows):
            place = q * (step // rows) + i
            sent_ref[place] = grad[:, i * rows : (i + 1) * rows]
            one = slot.outward(sent_ref, landed_ref, out_send, out_recv, place)
            pl.when(slot.me != place)(one.start)

    for piece in side.moving:
        side.step(piece, 0)
    for piece in side.staying:
        side.pair(piece)
    depth = len(bits_of(lax.axis_size("ctx")))
    stages = [
        [functools.partial(side.step, piece, place) for piece in side.staying if place < len(piece.order)]
        for place in range(depth)
    ]
    for q in reversed(range(span // step)):
        pl.when(slot.holds)(functools.partial(query_block, q))
        for one in stages.pop(0) if stages else []:
            one()
        carry.push(3 * len(masks))
    for some in stages:
        for one in some:
            one()
    carry.push(len(masks) * GROUP * carry.CHUNKS)

    @pl.when(slot.holds)
    def _():
        landed_ref[slot.head] = sent_ref[slot.me]

    for needed, one in slot.outward_landed(landed_ref, out_send, out_recv):
        pl.when(needed)(one.wait_recv)
    for one in loads:
        one.wait()

    width = tokens_ref.shape[1]
    lins = []
    d_normed = jnp.zeros((width, rows), f32)
    for kind in range(3):
        at = slice(kind * HEAD_DIM, (kind + 1) * HEAD_DIM)
        lin = jnp.concatenate([landed_ref[head, at, :] for head in range(heads)], axis=0)
        lins.append(lin)
        d_normed = d_normed + contract(weights[kind][...], lin)
    d_normed = jnp.transpose(d_normed)
    inputs = tokens_ref[...].astype(f32)
    scale = rms_scale(inputs)
    normal = inputs * scale
    gain_grad[...] = jnp.sum(d_normed * normal, axis=0, keepdims=True)
    d_inputs = d_hidden_ref[...] + rms_back(normal, scale, gain_ref[...][None], d_normed)
    input_grad[...] = d_inputs.astype(bf16)
    normed_t = jnp.transpose(normed_ref[...].astype(f32)).astype(bf16)
    attended_t = jnp.transpose(attended_ref[...].astype(f32)).astype(bf16)
    grads = [contract(normed_t, lin, NT) for lin in lins] + [contract(attended_t, d_attn_ref[...])]
    weight_sums(shard, grads, sums_ref)

    side.done()
    mixed = collect(hits_ref[...], earlier_ref[...], *side_outs)
    alive = live(length_ref, rows)
    output_ref[...] = (hidden_ref[...] + jnp.where(alive, mixed, 0.0)).astype(bf16)
    carry.done()
    for needed, one in slot.inward(blocks_ref, upstream_ref, in_send, in_recv):
        pl.when(needed)(one.wait_send)
    for place in range(slot.count):
        one = slot.outward(sent_ref, landed_ref, out_send, out_recv, place)
        pl.when(slot.holds & (slot.me != place))(one.wait_send)


def attend_back(qkv, length, out, total, blocks, tables, mine, weights, parts, carried, masks, sizes, number):
    heads, _, rows = blocks.shape
    count = qkv.shape[0]
    span = count * rows
    step = min(512, span)
    dp_size, ctx_size, expert_size = sizes
    width = weights[0].shape[0]
    shard = width // (dp_size * count)
    kinds, side_shapes, side_scratch = home_plan([part.shape for part in parts], sizes)
    carry_shapes = [jax.ShapeDtypeStruct(array.shape, array.dtype) for array in carried]
    carry_sems = [DMA((len(masks), len(masks[0])))] * 2 if masks else []
    sums = (dp_size * ctx_size, expert_size, -(-4 * shard // 16) * 16, width)
    got = pl.pallas_call(
        functools.partial(attend_back_kernel, step, heads, kinds, masks, shard),
        out_shape=[
            jax.ShapeDtypeStruct((rows, width), bf16),
            jax.ShapeDtypeStruct((rows, width), bf16),
            jax.ShapeDtypeStruct((1, width), f32),
            jax.ShapeDtypeStruct(sums, bf16),
        ]
        + carry_shapes,
        in_specs=[SMEM] + [VMEM] * (6 + len(mine)) + [ANY] * (3 + len(parts) + len(carried)),
        out_specs=[VMEM] * 4 + [ANY] * len(carried),
        scratch_shapes=[pltpu.VMEM(weights[0].shape, bf16)] * 3
        + [pltpu.VMEM((heads,) + qkv.shape[1:], bf16)]
        + [pltpu.VMEM(shape.shape, shape.dtype) for shape in side_shapes]
        + [
            pltpu.VMEM((count,) + blocks.shape[1:], bf16),
            pltpu.VMEM((span, 2 * HEAD_DIM), bf16),
            pltpu.VMEM((2 * HEAD_DIM, span), bf16),
            pltpu.VMEM((span, HEAD_DIM), bf16),
            pltpu.VMEM((HEAD_DIM, span), bf16),
            pltpu.VMEM((HEAD_DIM, span), f32),
            pltpu.VMEM((HEAD_DIM, span), f32),
            pltpu.VMEM((1, span), f32),
            pltpu.VMEM((HEAD_DIM, span), bf16),
            pltpu.VMEM(qkv.shape, bf16),
        ]
        + [DMA((count,))] * 4
        + [DMA((3,))]
        + carry_sems
        + side_scratch,
        compiler_params=pltpu.CompilerParams(
            collective_id=number, has_side_effects=True, vmem_limit_bytes=60 << 20
        ),
    )(length, qkv, out, total, *tables, blocks, *mine, *weights, *parts, *carried)
    return got[:4], got[4:]


def local(
    tokens,
    lengths,
    routes,
    norm1_gain,
    query_weight,
    key_weight,
    value_weight,
    output_weight,
    norm2_gain,
    router_weight,
    expert_gate,
    expert_up,
    expert_down,
    shared_gate,
    shared_up,
    shared_down,
    cotangent,
):
    sizes = dp_size, ctx_size, expert_size = sizes_of()
    plane_size, slot_size = dp_size * ctx_size, ctx_size * expert_size
    rows, width = tokens.shape[1:]
    shard = width // (dp_size * slot_size)
    tokens, routes, cotangent = tokens[0], routes[0], cotangent[0]
    weights = (query_weight, key_weight, value_weight)
    tables = rope_tables(jnp.arange(slot_size * rows, dtype=jnp.int32))

    (qkv, out_t, log_total, attended), (normed, *routing), (up_rows, up_flat) = attend(
        lengths, routes.T, cotangent, tokens, norm1_gain, tables, weights, sizes, 1
    )

    bits = bits_of(ctx_size)
    groups = EXPERTS // expert_size // GROUP
    slice_masks = [
        subsets([bit for bit in bits if bit != group_bit(g, ctx_size)]) for g in range(groups)
    ]
    slices = len(slice_masks[0])
    ways = tuple(tuple(masks[k] for masks in slice_masks) for _ in range(3) for k in range(1, slices))
    early = slices - 1

    mine, shared_grads, results, grads = moe(
        lengths, tokens, attended, norm2_gain, router_weight.T, routing, cotangent, output_weight, up_rows, up_flat,
        (expert_gate, expert_up, expert_down), (shared_gate, shared_up, shared_down), sizes, 2,
    )
    hidden, attended, d_hidden, d_attended, d_attn, router_grad, gain_two_grad = mine
    others = [array for kind in grads for array in kind[1:]]
    (output_rows, input_grad, gain_one_grad, sums), early_in = attend_back(
        qkv, lengths, out_t, log_total, d_attended, tables,
        (normed, tokens, norm1_gain, d_hidden, attended, d_attn, hidden, *routing),
        weights, results, others[: 2 * early], ways[: 2 * early], sizes, 3,
    )

    devices = (plane_size, expert_size)
    pad = [(0, 0), (0, 0), (0, 0), (0, 128 - shard)]
    routed = -(-shard * EXPERTS // 128)
    small = jnp.concatenate(
        [
            jnp.pad(
                router_grad.reshape(devices + (shard * EXPERTS,)),
                [(0, 0), (0, 0), (0, routed * 128 - shard * EXPERTS)],
            ).reshape(devices + (routed, 128)),
            jnp.pad(gain_one_grad.reshape(devices + (1, shard)), pad),
            jnp.pad(gain_two_grad.reshape(devices + (1, shard)), pad),
            jnp.zeros(devices + (6 - routed, 128), f32),
        ],
        axis=2,
    )
    landed, small, *last_in = bring_sums(sums, small, others[2 * early :], ways[2 * early :], sizes, 4)
    arrived = [*early_in, *last_in]
    by_slice = [kind[0] for kind in grads]
    for k in range(early):
        by_slice += [arrived[kind * early + k] for kind in range(3)]
    *out, small, output_rows, input_grad, shared_gate_grad, shared_up_grad, shared_down_grad = finish(
        by_slice, landed, small, [output_rows, input_grad, *shared_grads], shard
    )
    return (
        output_rows[None],
        input_grad[None],
        small[routed, :shard],
        *out[3:7],
        small[routed + 1, :shard],
        small[:routed].reshape(-1)[: shard * EXPERTS].reshape(shard, EXPERTS),
        *out[:3],
        shared_gate_grad,
        shared_up_grad,
        shared_down_grad,
    )


def solution(mesh):
    tokens = P("dp", ("ctx", "expert"), None)
    whole = P()
    experts = P("expert", None, None)
    everywhere = ("dp", "ctx", "expert")
    return jax.shard_map(
        local,
        mesh=mesh,
        in_specs=(tokens, P("dp"), tokens)
        + (whole,) * 7
        + (experts,) * 3
        + (whole,) * 3
        + (tokens,),
        out_specs=(tokens, tokens, P(everywhere))
        + (P(everywhere, None),) * 4
        + (P(everywhere), P(everywhere, None))
        + (P("expert", None, PLANE),) * 2
        + (P("expert", PLANE, None),)
        + (P(everywhere, None),) * 3,
        check_vma=False,
    )
```

```python
import functools

import jax
import jax.numpy as jnp
from jax import lax
from jax.experimental import pallas as pl
from jax.experimental.pallas import tpu as pltpu
from jax.sharding import PartitionSpec as P

HEAD_DIM = 64
EXPERTS = 16
TOP = 2
CAP = 22
PLACES = 24

norm_epsilon = 1e-06
rope_base = 10000.0
score_scale = 0.125
masked_value = -1e30
PLANE = ("dp", "ctx")
SLOT = ("ctx", "expert")
bf16 = jnp.bfloat16
f32 = jnp.float32


def rms_scale(values):
    return lax.rsqrt(jnp.mean(values * values, axis=-1, keepdims=True) + norm_epsilon)


def rms_back(normal, scale, gain, upstream):
    lifted = upstream * gain
    return scale * (lifted - normal * jnp.mean(lifted * normal, axis=-1, keepdims=True))


def rope_tables(positions):
    half = HEAD_DIM // 2
    exponent = jnp.arange(half, dtype=f32) * (2.0 / HEAD_DIM)
    inverse_freq = rope_base ** (-exponent)
    angles = inverse_freq[:, None] * positions[None, :].astype(f32)
    return jnp.cos(angles), jnp.sin(angles)


def head_rows(qkv_ref, first, count):
    return jnp.concatenate(
        [qkv_ref[block, first : first + count, :] for block in range(qkv_ref.shape[0])], axis=1
    )


def live_keys(key_t, length):
    span = key_t.shape[1]
    place = lax.broadcasted_iota(jnp.int32, (8, span), 1)
    row = lax.broadcasted_iota(jnp.int32, (8, span), 0)
    bias = jnp.where((place >= length) & (row == 0), masked_value, 0.0)
    padded = jnp.concatenate(
        [key_t.astype(f32), bias, jnp.zeros((HEAD_DIM - 8, span), f32)], axis=0
    )
    return jnp.transpose(padded).astype(bf16)


def scaled_queries(query_t):
    span = query_t.shape[1]
    row = lax.broadcasted_iota(jnp.int32, (HEAD_DIM, span), 0)
    ones = jnp.where(row == 0, 1.0, 0.0)
    return jnp.concatenate([query_t.astype(f32) * score_scale, ones], axis=0).astype(bf16)


def causal(scores):
    key = lax.broadcasted_iota(jnp.int32, scores.shape, 0)
    query = lax.broadcasted_iota(jnp.int32, scores.shape, 1)
    return jnp.where(key <= query, scores, masked_value)


MESH = pl.DeviceIdType.MESH
ANY = pl.BlockSpec(memory_space=pl.ANY)
VMEM = pl.BlockSpec(memory_space=pltpu.VMEM)
SMEM = pl.BlockSpec(memory_space=pltpu.SMEM)
DMA = pltpu.SemaphoreType.DMA


def head_place(head, heads, ctx_size, expert_size):
    per = expert_size - 1
    if ctx_size <= expert_size and ctx_size * per == heads:
        row = head // per
        step = head % per
        return row, step + jnp.where(step >= row, 1, 0)
    return head // expert_size, head % expert_size


def head_of(ctx, expert, heads, ctx_size, expert_size):
    per = expert_size - 1
    if ctx_size <= expert_size and ctx_size * per == heads:
        head = ctx * per + expert - jnp.where(expert > ctx, 1, 0)
        return jnp.where(expert == ctx, heads, head)
    return ctx * expert_size + expert


def sizes_of():
    return tuple(lax.axis_size(a) for a in ("dp", "ctx", "expert"))


def greet(partners, meanwhile=lambda: None):
    barrier = pltpu.get_barrier_semaphore()
    for partner in partners:
        pl.semaphore_signal(barrier, inc=1, device_id=partner, device_id_type=MESH)
    meanwhile()
    pl.semaphore_wait(barrier, len(partners))


def fetch(sources, targets, sems):
    return [
        pltpu.make_async_copy(source, target, sems.at[i]) for i, (source, target) in enumerate(zip(sources, targets))
    ]


GROUP = 2


def flip(index, mask):
    bit = 1
    while bit <= mask:
        if mask & bit:
            index = index + bit * (1 - 2 * ((index // bit) % 2))
        bit *= 2
    return index


def bits_of(ctx_size):
    return [1 << b for b in range(ctx_size.bit_length() - 1)]


def group_bit(group, ctx_size):
    bits = bits_of(ctx_size)
    return bits[group % len(bits)]


def subsets(order):
    masks = [0]
    for bit in order:
        masks = masks + [m | bit for m in masks]
    return masks


class Piece:
    def __init__(self, array, kind, group, step, first, size, order):
        self.array, self.kind, self.group, self.step = array, kind, group, step
        self.first, self.size, self.order = first, size, order
        self.masks = subsets(order)


def pieces(kinds, expert_size, ctx_size):
    bits = bits_of(ctx_size)
    moving, staying = [], []
    for array, (kind, groups, rows) in enumerate(kinds):
        if kind == "flat":
            half = rows // 2
            staying.append(Piece(array, kind, None, None, 0, half, bits))
            staying.append(Piece(array, kind, None, None, half, rows - half, bits[::-1]))
            continue
        for group in range(groups or 1):
            for step in range(expert_size):
                if kind == "group":
                    order = [group_bit(group, ctx_size)]
                else:
                    order = bits if (step + array) % 2 == 0 else bits[::-1]
                (moving if step else staying).append(Piece(array, kind, group, step, 0, rows, order))
    return moving, staying


class Spread:
    def __init__(self, kinds, has_gate, refs, near=False):
        self.near = near
        rest = iter(refs)

        def take(count):
            return [next(rest) for _ in range(count)]

        self.has_gate = has_gate
        self.ins = take(len(kinds))
        self.gate = next(rest) if has_gate else None
        self.outs = take(len(kinds))
        self.gates = next(rest) if has_gate else None
        self.z_send, self.z_recv, self.send, self.recv, self.pair_recv, self.local_sem = take(6)
        if has_gate:
            self.gate_send, self.gate_recv, self.gate_z_send, self.gate_z_recv = take(4)
        self.dp_size, self.ctx_size, self.expert_size = sizes_of()
        self.dp, self.ctx, self.expert = (lax.axis_index(a) for a in ("dp", "ctx", "expert"))
        self.moving, self.staying = pieces(kinds, self.expert_size, self.ctx_size)
        self.all = self.staying + self.moving
        self.number = {id(piece): i for i, piece in enumerate(self.all)}
        self.own = self.dp * self.ctx_size + self.ctx
        self.other = (self.dp + 1) % self.dp_size
        self.bits = bits_of(self.ctx_size)
        self.started = []
        self.plane = [(d, c) for d in range(self.dp_size) for c in range(self.ctx_size) if (d, c) != (0, 0)]

    def z_at(self, step):
        return (self.expert + step) % self.expert_size

    def z_from(self, step):
        return (self.expert + self.expert_size - step) % self.expert_size

    def block(self, core, mask):
        return (self.dp if core == 0 else self.other) * self.ctx_size + flip(self.ctx, mask)

    def landed(self, piece, core, mask, at=0):
        out = self.outs[piece.array]
        if piece.step is None:
            return out.at[self.block(core, mask), pl.ds(piece.first, piece.size)]
        return out.at[piece.group, core * 2 + (1 if mask ^ at else 0), self.z_from(piece.step)]

    def source(self, piece):
        if piece.step is None:
            return self.ins[piece.array].at[pl.ds(piece.first, piece.size)]
        if piece.step == 0:
            return self.ins[piece.array].at[self.expert, piece.group]
        return self.landed(piece, 0, 0)

    def remote(self, source, target, send, recv, there):
        return pltpu.make_async_remote_copy(
            src_ref=source, dst_ref=target, send_sem=send, recv_sem=recv, device_id=there, device_id_type=MESH
        )

    def z_copy(self, piece, landing=False):
        place = self.z_from(piece.step) if landing else self.expert
        at = self.number[id(piece)]
        return self.remote(
            self.ins[piece.array].at[self.z_at(piece.step), piece.group],
            self.outs[piece.array].at[piece.group, 0, place],
            self.z_send.at[at],
            self.z_recv.at[at],
            {"expert": self.z_at(piece.step)},
        )

    def gate_z(self, step, landing=False):
        return self.remote(
            self.gate.at[self.z_at(step)],
            self.gates.at[self.own, self.z_from(step) if landing else self.expert],
            self.gate_z_send.at[step],
            self.gate_z_recv.at[step],
            {"expert": self.z_at(step)},
        )

    def gate_plane(self, d, c, block):
        return self.remote(
            self.gates.at[block],
            self.gates.at[block],
            self.gate_send.at[d, c],
            self.gate_recv.at[d, c],
            {"dp": (self.dp + d) % self.dp_size, "ctx": flip(self.ctx, c)},
        )

    def passing(self, piece, mask, bit):
        at = self.number[id(piece)]
        return self.remote(
            self.landed(piece, 0, mask) if mask else self.source(piece),
            self.landed(piece, 0, mask, bit),
            self.send.at[at, mask, self.bits.index(bit)],
            self.recv.at[at, mask ^ bit],
            {"ctx": flip(self.ctx, bit)},
        )

    def arrived(self, piece, mask):
        here = self.landed(piece, 0, mask)
        recv = self.recv.at[self.number[id(piece)], mask]
        return self.remote(here, here, self.send.at[0, 0, 0], recv, {"ctx": self.ctx})

    def crossing(self, piece, mask, landing=False):
        at = self.number[id(piece)]
        core = 0 if piece.step is None and not landing else 1
        return self.remote(
            self.landed(piece, 0, mask) if mask else self.source(piece),
            self.landed(piece, core, mask),
            self.send.at[at, mask, len(self.bits)],
            self.pair_recv.at[at, mask],
            {"dp": self.other},
        )

    def kept(self):
        if self.near:
            return []
        return [
            pltpu.make_async_copy(self.source(piece), self.landed(piece, 0, 0), self.local_sem.at[i])
            for i, piece in enumerate(self.staying)
        ]

    def begin(self, one):
        one.start()
        self.started.append(one)

    def z_start(self):
        if self.has_gate:
            for step in range(1, self.expert_size):
                self.gate_z(step).start()
        for piece in self.moving:
            self.z_copy(piece).start()

    def first(self, some):
        for piece in some:
            if piece.step:
                self.z_copy(piece, True).wait_recv()
            for bit in piece.order:
                self.begin(self.passing(piece, 0, bit))
            self.begin(self.crossing(piece, 0))

    def keep(self):
        for one in self.kept():
            one.start()
        if self.near:
            for piece in self.staying:
                target = self.landed(piece, 0, 0)
                target[...] = self.source(piece)[...]
        if self.has_gate:
            self.gates[self.own, self.expert] = self.gate[self.expert]

    def forward(self, piece, place):
        if place >= len(piece.order):
            return
        bit = piece.order[place]
        for mask in [m | bit for m in subsets(piece.order[:place])]:
            self.arrived(piece, mask).wait_recv()
            for later in piece.order[place + 1 :]:
                self.begin(self.passing(piece, mask, later))
            self.begin(self.crossing(piece, mask))

    def forward_all(self, some):
        for place in range(len(self.bits)):
            for piece in some:
                self.forward(piece, place)

    def gates_on(self):
        for step in range(1, self.expert_size):
            self.gate_z(step, True).wait_recv()
        for d, c in self.plane:
            self.gate_plane(d, c, self.own).start()

    def gates_landed(self):
        for d, c in self.plane:
            block = ((self.dp + d) % self.dp_size) * self.ctx_size + flip(self.ctx, c)
            self.gate_plane(d, c, block).wait_recv()

    def paired(self, some):
        for piece in some:
            for mask in piece.masks:
                self.crossing(piece, mask, True).wait_recv()

    def sent(self):
        for one in self.started:
            one.wait_send()
        for piece in self.moving:
            self.z_copy(piece).wait_send()
        if self.has_gate:
            for step in range(1, self.expert_size):
                self.gate_z(step).wait_send()
            for d, c in self.plane:
                self.gate_plane(d, c, self.own).wait_send()


def plane_partners():
    dp_size, ctx_size, expert_size = sizes_of()
    dp, ctx, expert = (lax.axis_index(a) for a in ("dp", "ctx", "expert"))
    plane = [(d, c) for d in range(dp_size) for c in range(ctx_size) if (d, c) != (0, 0)]
    return [{"expert": (expert + step) % expert_size} for step in range(1, expert_size)] + [
        {"dp": (dp + d) % dp_size, "ctx": flip(ctx, c)} for d, c in plane
    ]


def spread_plan(arrays, gate, sizes):
    dp_size, ctx_size, expert_size = sizes
    assert dp_size == 2
    plane_size = dp_size * ctx_size
    kinds, out_shape = [], []
    for array in arrays:
        if array.ndim == 4:
            kinds.append(("group", array.shape[1], array.shape[2]))
            shape = (array.shape[1], 4, expert_size) + array.shape[2:]
        else:
            kinds.append(("flat", None, array.shape[0]))
            shape = (plane_size,) + array.shape
        out_shape.append(jax.ShapeDtypeStruct(shape, array.dtype))
    moving, staying = pieces(kinds, expert_size, ctx_size)
    count = len(moving + staying)
    scratch = [
        DMA((count,)),
        DMA((count,)),
        DMA((count, ctx_size, len(bits_of(ctx_size)) + 1)),
        DMA((count, ctx_size)),
        DMA((count, ctx_size)),
        DMA((len(staying),)),
    ]
    if gate is not None:
        out_shape.append(jax.ShapeDtypeStruct((plane_size,) + gate.shape, gate.dtype))
        scratch += [DMA((dp_size, ctx_size))] * 2 + [DMA((expert_size,))] * 2
    return tuple(kinds), out_shape, scratch


def stage(piece, place):
    order = piece.order[::-1]
    done, bit = sum(order[:place]), order[place]
    kept = [m for m in piece.masks if not m & (done | bit)]
    return bit, [(m | bit, m) for m in kept]


def buffer_places(order):
    held, arriving, here, there = {}, {}, 0, 0
    for piece in order:
        for mask in piece.masks:
            held[id(piece), mask] = here
            here += piece.size
        for place in range(len(piece.order)):
            for index in range(len(stage(piece, place)[1])):
                arriving[id(piece), place, index] = there
                there += piece.size
    held["rows"], arriving["rows"] = here, there
    return held, arriving


class Home:
    def __init__(self, kinds, has_dots, parts, dot, outs, dots_out, scratch, near=False):
        self.near = near
        rest = iter(scratch)

        def take(count):
            return [next(rest) for _ in range(count)]

        self.parts, self.dot, self.outs, self.dots_out, self.has_dots = parts, dot, outs, dots_out, has_dots
        self.mine, self.theirs, self.arrivals = take(3)
        self.mine_sem, self.pair_send, self.pair_recv, self.send, self.recv, self.z_send, self.z_recv = take(7)
        if has_dots:
            self.dot_in, self.dot_sum, self.dot_send, self.dot_recv, self.dot_z_send, self.dot_z_recv = take(6)
        self.dp_size, self.ctx_size, self.expert_size = sizes_of()
        self.dp, self.ctx, self.expert = (lax.axis_index(a) for a in ("dp", "ctx", "expert"))
        self.moving, self.staying = pieces(kinds, self.expert_size, self.ctx_size)
        self.all = self.moving + self.staying
        self.number = {id(piece): i for i, piece in enumerate(self.all)}
        self.held, self.arriving = buffer_places(self.all)
        self.own = self.dp * self.ctx_size + self.ctx
        self.other = (self.dp + 1) % self.dp_size
        self.plane = [(d, c) for d in range(self.dp_size) for c in range(self.ctx_size) if (d, c) != (0, 0)]

    def z_at(self, step):
        return (self.expert + step) % self.expert_size

    def z_from(self, step):
        return (self.expert + self.expert_size - step) % self.expert_size

    def plane_at(self, d, c):
        return ((self.dp + d) % self.dp_size) * self.ctx_size + flip(self.ctx, c)

    def partner(self, d, c):
        return {"dp": (self.dp + d) % self.dp_size, "ctx": flip(self.ctx, c)}

    def remote(self, source, target, send, recv, there):
        return pltpu.make_async_remote_copy(
            src_ref=source, dst_ref=target, send_sem=send, recv_sem=recv, device_id=there, device_id_type=MESH
        )

    def whole(self, piece, core, mask):
        part = self.parts[piece.array]
        if piece.kind == "group":
            return part.at[piece.group, core * 2 + (1 if mask else 0), self.z_at(piece.step)]
        block = (self.dp if core == 0 else self.other) * self.ctx_size + flip(self.ctx, mask)
        if piece.kind == "flat":
            return part.at[block, pl.ds(piece.first, piece.size)]
        return part.at[block, self.z_at(piece.step)]

    def at(self, piece, mask):
        return pl.ds(self.held[id(piece), mask], piece.size)

    def load(self, piece, mask):
        return pltpu.make_async_copy(
            self.whole(piece, 0, mask), self.mine.at[self.at(piece, mask)], self.mine_sem.at[self.number[id(piece)], mask]
        )

    def cross(self, piece, mask):
        number = self.number[id(piece)]
        return self.remote(
            self.whole(piece, 1, mask),
            self.theirs.at[self.at(piece, mask)],
            self.pair_send.at[number, mask],
            self.pair_recv.at[number, mask],
            {"dp": self.other},
        )

    def hop(self, piece, place, index):
        bit, moves = stage(piece, place)
        number = self.number[id(piece)]
        return self.remote(
            self.mine.at[self.at(piece, moves[index][0])],
            self.arrivals.at[pl.ds(self.arriving[id(piece), place, index], piece.size)],
            self.send.at[number, moves[index][0]],
            self.recv.at[number, place, index],
            {"ctx": flip(self.ctx, bit)},
        )

    def z_copy(self, piece, landing=False):
        place = self.z_from(piece.step) if landing else self.expert
        out, number = self.outs[piece.array], self.number[id(piece)]
        return self.remote(
            self.mine.at[self.at(piece, 0)],
            out.at[place, piece.group] if piece.kind == "group" else out.at[place],
            self.z_send.at[number],
            self.z_recv.at[number],
            {"expert": self.z_at(piece.step)},
        )

    def start(self, some):
        for piece in some:
            for mask in piece.masks:
                self.cross(piece, mask).start()
                if not self.near:
                    self.load(piece, mask).start()

    def add(self, here, buffer, there):
        total = self.mine[here].astype(f32) + buffer[there].astype(f32)
        self.mine[here] = total.astype(self.mine.dtype)

    def pair(self, piece):
        leaving = [source for source, _ in stage(piece, 0)[1]]
        for mask in leaving + [m for m in piece.masks if m not in leaving]:
            here = self.at(piece, mask)
            if not self.near:
                self.load(piece, mask).wait()
            self.cross(piece, mask).wait_recv()
            if self.near:
                total = self.whole(piece, 0, mask)[...].astype(f32) + self.theirs[here].astype(f32)
                self.mine[here] = total.astype(self.mine.dtype)
            else:
                self.add(here, self.theirs, here)
            if mask in leaving:
                self.hop(piece, 0, leaving.index(mask)).start()

    def step(self, piece, place):
        targets = [target for _, target in stage(piece, place)[1]]
        leaving = []
        if place + 1 < len(piece.order):
            leaving = [source for source, _ in stage(piece, place + 1)[1]]
        for index in range(len(targets)):
            self.hop(piece, place, index).wait_recv()
        for mask in leaving + [m for m in targets if m not in leaving]:
            there = pl.ds(self.arriving[id(piece), place, targets.index(mask)], piece.size)
            self.add(self.at(piece, mask), self.arrivals, there)
            if mask in leaving:
                self.hop(piece, place + 1, leaving.index(mask)).start()
        if place + 1 == len(piece.order):
            self.finish(piece)

    def finish(self, piece):
        result, out = self.mine.at[self.at(piece, 0)], self.outs[piece.array]
        if piece.kind == "flat":
            out[pl.ds(piece.first, piece.size)] = result[...]
        elif piece.step:
            self.z_copy(piece).start()
        elif piece.kind == "group":
            out[self.expert, piece.group] = result[...]
        else:
            out[self.expert] = result[...]

    def ticks(self, some, ahead):
        depth = max(len(piece.order) for piece in some)
        for tick in range(len(some) + ahead + depth):
            for place in range(depth + 1):
                index = tick if place == 0 else tick - ahead - place + 1
                if not 0 <= index < len(some) or place > len(some[index].order):
                    continue
                if place == 0:
                    self.pair(some[index])
                else:
                    self.step(some[index], place - 1)
            yield

    def dot_plane(self, d, c):
        return self.remote(
            self.dot.at[self.plane_at(d, c)],
            self.dot_in.at[d, c],
            self.dot_send.at[d, c],
            self.dot_recv.at[d, c],
            self.partner(d, c),
        )

    def dot_z(self, step, landing=False):
        return self.remote(
            self.dot_sum.at[self.z_at(step)],
            self.dots_out.at[self.z_from(step) if landing else self.expert],
            self.dot_z_send.at[step],
            self.dot_z_recv.at[step],
            {"expert": self.z_at(step)},
        )

    def dots_start(self):
        for d, c in self.plane:
            self.dot_plane(d, c).start()

    def dots_on(self):
        total = self.dot[self.own]
        for d, c in self.plane:
            self.dot_plane(d, c).wait_recv()
            total = total + self.dot_in[d, c]
        self.dot_sum[...] = total
        for step in range(1, self.expert_size):
            self.dot_z(step).start()
        self.dots_out[self.expert] = self.dot_sum[self.expert]

    def dots_landed(self):
        for step in range(1, self.expert_size):
            self.dot_z(step, True).wait_recv()

    def done(self):
        for piece in self.moving:
            self.z_copy(piece, True).wait_recv()
        if self.has_dots:
            for step in range(1, self.expert_size):
                self.dot_z(step).wait_send()
            for d, c in self.plane:
                self.dot_plane(d, c).wait_send()
        for piece in self.moving:
            self.z_copy(piece).wait_send()
        for piece in self.all:
            for mask in piece.masks:
                self.cross(piece, mask).wait_send()
            for place in range(len(piece.order)):
                for index in range(len(stage(piece, place)[1])):
                    self.hop(piece, place, index).wait_send()


def home_plan(shapes, sizes, dots=None):
    dp_size, ctx_size, expert_size = sizes
    assert dp_size == 2
    width = shapes[0][-1]
    kinds, out_shape = [], []
    for given in shapes:
        if len(given) == 5:
            kinds.append(("group", given[0], given[3]))
            shape = (expert_size, given[0]) + given[3:]
        else:
            kinds.append(("plane" if len(given) == 4 else "flat", None, given[-2]))
            shape = given[1:]
        out_shape.append(jax.ShapeDtypeStruct(shape, bf16))
    moving, staying = pieces(kinds, expert_size, ctx_size)
    held, arriving = buffer_places(moving + staying)
    count, depth = len(moving + staying), len(bits_of(ctx_size))
    scratch = [
        pltpu.VMEM((held["rows"], width), bf16),
        pltpu.VMEM((held["rows"], width), bf16),
        pltpu.VMEM((arriving["rows"], width), bf16),
        DMA((count, ctx_size)),
        DMA((count, ctx_size)),
        DMA((count, ctx_size)),
        DMA((count, ctx_size)),
        DMA((count, depth, max(ctx_size // 2, 1))),
        DMA((count,)),
        DMA((count,)),
    ]
    if dots is not None:
        out_shape.append(jax.ShapeDtypeStruct(dots[1:], f32))
        scratch += [
            pltpu.VMEM((dp_size, ctx_size) + dots[1:], f32),
            pltpu.VMEM(dots[1:], f32),
            DMA((dp_size, ctx_size)),
            DMA((dp_size, ctx_size)),
            DMA((expert_size,)),
            DMA((expert_size,)),
        ]
    return tuple(kinds), out_shape, scratch


class Shared:
    def __init__(self, grads, outs, scratch):
        self.grads, self.outs = grads, outs
        self.landing, self.columns = scratch[:3], scratch[3:5]
        self.send, self.recv, self.column_send, self.column_recv = scratch[5:]
        self.dp_size, self.ctx_size, self.expert_size = sizes_of()
        self.dp, self.ctx, self.expert = (lax.axis_index(a) for a in ("dp", "ctx", "expert"))
        self.own = self.dp * self.ctx_size + self.ctx
        self.plane = [(d, c) for d in range(self.dp_size) for c in range(self.ctx_size) if (d, c) != (0, 0)]
        self.part = grads[0].shape[2]

    def z_copy(self, kind, step):
        there = (self.expert + step) % self.expert_size
        return pltpu.make_async_remote_copy(
            src_ref=self.grads[kind].at[there],
            dst_ref=self.landing[kind].at[step],
            send_sem=self.send.at[kind, step],
            recv_sem=self.recv.at[kind, step],
            device_id={"expert": there},
            device_id_type=MESH,
        )

    def column(self, kind, d, c, landing=False):
        there = ((self.dp + d) % self.dp_size) * self.ctx_size + flip(self.ctx, c)
        source = ((self.dp + self.dp_size - d) % self.dp_size) * self.ctx_size + flip(self.ctx, c)
        at = source if landing else self.own
        return pltpu.make_async_remote_copy(
            src_ref=self.columns[kind].at[there],
            dst_ref=self.outs[kind].at[:, pl.ds(pl.multiple_of(at * self.part, 128), self.part)],
            send_sem=self.column_send.at[kind, d, c],
            recv_sem=self.column_recv.at[kind, d, c],
            device_id={"dp": (self.dp + d) % self.dp_size, "ctx": flip(self.ctx, c)},
            device_id_type=MESH,
        )

    def start(self):
        for kind in range(3):
            for step in range(1, self.expert_size):
                self.z_copy(kind, step).start()

    def sum(self):
        for kind in range(3):
            total = self.grads[kind][self.expert].astype(f32)
            for step in range(1, self.expert_size):
                self.z_copy(kind, step).wait_recv()
                total = total + self.landing[kind][step].astype(f32)
            if kind == 2:
                self.outs[2][...] = total
                continue
            shard = self.outs[kind].shape[0]
            for block in range(self.dp_size * self.ctx_size):
                self.columns[kind][block] = total[block * shard : (block + 1) * shard]
            for d, c in self.plane:
                self.column(kind, d, c).start()
            here = pl.ds(pl.multiple_of(self.own * self.part, 128), self.part)
            self.outs[kind][:, here] = self.columns[kind][self.own]

    def done(self):
        for kind in range(3):
            for step in range(1, self.expert_size):
                self.z_copy(kind, step).wait_send()
            if kind < 2:
                for d, c in self.plane:
                    self.column(kind, d, c, True).wait_recv()
                    self.column(kind, d, c).wait_send()


def shared_plan(width, part, sizes):
    dp_size, ctx_size, expert_size = sizes
    plane_size = dp_size * ctx_size
    shard = width // (plane_size * expert_size)
    given = [(expert_size, plane_size * shard, part)] * 2 + [(expert_size, part // expert_size, width)]
    columns = jax.ShapeDtypeStruct((shard, plane_size * part), f32)
    out_shape = [columns, columns, jax.ShapeDtypeStruct(given[2][1:], f32)]
    scratch = [pltpu.VMEM(shape, bf16) for shape in given]
    scratch += [pltpu.VMEM((plane_size, shard, part), f32)] * 2
    scratch += [
        DMA((3, expert_size)),
        DMA((3, expert_size)),
        DMA((2, dp_size, ctx_size)),
        DMA((2, dp_size, ctx_size)),
    ]
    return given, out_shape, scratch


class Carry:
    CHUNKS = 8

    def __init__(self, masks, sources, targets, sems):
        self.masks, self.sources, self.targets, self.sems = masks, sources, targets, sems
        self.ctx = lax.axis_index("ctx")
        groups = len(masks[0]) if masks else 0
        self.queues = [
            [
                (array, g, e, chunk)
                for array in range(len(masks))
                for e in range(GROUP)
                for chunk in range(self.CHUNKS)
            ]
            for g in range(groups)
        ]

    def copy(self, array, g, e, rows):
        return pltpu.make_async_remote_copy(
            src_ref=self.sources[array][g].at[e, rows],
            dst_ref=self.targets[array].at[g * GROUP + e, rows],
            send_sem=self.sems[0].at[array, g],
            recv_sem=self.sems[1].at[array, g],
            device_id={"ctx": flip(self.ctx, self.masks[array][g])},
            device_id_type=MESH,
        )

    def push(self, count, groups=None):
        for g in range(len(self.queues)) if groups is None else groups:
            for array, _, e, chunk in self.queues[g][:count]:
                rows = self.sources[array][g].shape[1] // self.CHUNKS
                self.copy(array, g, e, pl.ds(chunk * rows, rows)).start()
            del self.queues[g][:count]

    def done(self):
        for array, by_group in enumerate(self.masks):
            for g in range(len(by_group)):
                whole = pltpu.make_async_remote_copy(
                    src_ref=self.sources[array][g],
                    dst_ref=self.targets[array].at[pl.ds(g * GROUP, GROUP)],
                    send_sem=self.sems[0].at[array, g],
                    recv_sem=self.sems[1].at[array, g],
                    device_id={"ctx": flip(self.ctx, by_group[g])},
                    device_id_type=MESH,
                )
                whole.wait_recv()
                whole.wait_send()


def by_group(arrays, groups):
    return [[array.at[pl.ds(g * GROUP, GROUP)] for g in range(groups)] for array in arrays]


def sums_kernel(kinds, masks, *refs):
    rest = iter(refs)

    def take(count):
        return [next(rest) for _ in range(count)]

    part, dot, carried, shared_in = next(rest), next(rest), take(len(masks)), take(3)
    landed, dots_landed, carried_out, shared_out = next(rest), next(rest), take(len(masks)), take(3)
    sems = take(2) if masks else []
    shared = Shared(shared_in, shared_out, take(9))
    carry = Carry(masks, by_group(carried, len(masks[0]) if masks else 0), carried_out, sems)
    home = Home(kinds, True, [part], dot, [landed], dots_landed, list(rest))
    greet(plane_partners())
    shared.start()
    home.start(home.all)
    home.dots_start()
    for _ in home.ticks(home.all, 2):
        carry.push(3)
    home.dots_on()
    carry.push(len(masks) * GROUP * carry.CHUNKS)
    shared.sum()
    home.dots_landed()
    home.done()
    shared.done()
    carry.done()


def bring_sums(part, dots, shared_parts, carried, masks, sizes, number):
    kinds, out_shape, scratch = home_plan([part.shape], sizes, dots.shape)
    _, shared_out, shared_scratch = shared_plan(part.shape[-1], shared_parts[0].shape[2], sizes)
    return pl.pallas_call(
        functools.partial(sums_kernel, kinds, masks),
        out_shape=out_shape + [jax.ShapeDtypeStruct(array.shape, array.dtype) for array in carried] + shared_out,
        in_specs=[ANY, VMEM] + [ANY] * len(carried) + [VMEM] * 3,
        out_specs=[VMEM] * 2 + [ANY] * len(carried) + [VMEM] * 3,
        scratch_shapes=([DMA((len(masks), len(masks[0])))] * 2 if masks else []) + shared_scratch + scratch,
        compiler_params=pltpu.CompilerParams(
            collective_id=number, has_side_effects=True, vmem_limit_bytes=58 << 20
        ),
    )(part, dots, *carried, *shared_parts)


def finish_kernel(slices, kept, *refs):
    rest = iter(refs)

    def take(count):
        return [next(rest) for _ in range(count)]

    slices_in, landed, dots_landed, through = take(3 * slices), next(rest), next(rest), take(kept)
    grads, sums, dots, outs = take(3), take(4), next(rest), take(kept)
    for kind, grad in enumerate(grads):
        total = slices_in[kind][...].astype(f32)
        for k in range(1, slices):
            total = total + slices_in[k * 3 + kind][...].astype(f32)
        grad[...] = total

    @pl.when(pl.program_id(0) == 0)
    def _():
        for source, target in zip(through, outs):
            target[...] = source[...]
        expert_size, shard = landed.shape[0], sums[0].shape[0]
        whole, small = landed[0].astype(f32), dots_landed[0]
        for z in range(1, expert_size):
            whole = whole + landed[z].astype(f32)
            small = small + dots_landed[z]
        for i, out in enumerate(sums):
            out[...] = whole[i * shard : (i + 1) * shard]
        dots[...] = small


def finish(slices_in, landed, dots_landed, through, shard):
    width = landed.shape[-1]
    slices = len(slices_in) // 3
    own = slices_in[0].shape[0]

    def each(array):
        return pl.BlockSpec((1,) + array.shape[1:], lambda e: (e, 0, 0))

    def whole(array):
        return pl.BlockSpec(array.shape, lambda e: (0,) * len(array.shape))

    sums = [jax.ShapeDtypeStruct((shard, width), f32)] * 4 + [jax.ShapeDtypeStruct(dots_landed.shape[1:], f32)]
    kept = [jax.ShapeDtypeStruct(array.shape, array.dtype) for array in through]
    return pl.pallas_call(
        functools.partial(finish_kernel, slices, len(through)),
        grid=(own,),
        out_shape=[jax.ShapeDtypeStruct(array.shape, f32) for array in slices_in[:3]] + sums + kept,
        in_specs=[each(array) for array in slices_in]
        + [whole(array) for array in [landed, dots_landed] + list(through)],
        out_specs=[each(array) for array in slices_in[:3]] + [whole(array) for array in sums + kept],
        compiler_params=pltpu.CompilerParams(vmem_limit_bytes=48 << 20),
    )(*slices_in, landed, dots_landed, *through)


NT = (((1,), (1,)), ((), ()))
TN = (((0,), (0,)), ((), ()))


def contract(a, b, dims=(((1,), (0,)), ((), ()))):
    return lax.dot_general(a, b, dims, preferred_element_type=f32)


EXACT = lax.Precision.HIGHEST


def expert_of_place(count, stride, own):
    expert = lax.broadcasted_iota(jnp.int32, (EXPERTS, count), 0)
    column = lax.broadcasted_iota(jnp.int32, (EXPERTS, count), 1)
    place = column - ((expert // own) * stride + (expert % own) * PLACES)
    inside = (place >= 0) & (place < PLACES)
    at = jnp.sum(jnp.where(inside, place, 0), axis=0, keepdims=True)
    return inside.astype(f32), at.astype(f32)


def spots(hits, earlier, count, stride, own):
    expert_at, place_at = expert_of_place(count, stride, own)
    low = expert_at.astype(bf16)
    hit = contract(hits.astype(bf16), low)
    before = contract(earlier.astype(bf16), low)
    return jnp.where((hit > 0.5) & (before == place_at), 1.0, 0.0)


def row_spots(hits, earlier, expert_size):
    own = EXPERTS // expert_size
    return spots(hits, earlier, EXPERTS * PLACES, own * PLACES, own)


def first_place(rows):
    return (lax.axis_index("ctx") * lax.axis_size("expert") + lax.axis_index("expert")) * rows


def live(length_ref, rows):
    return first_place(rows) + lax.broadcasted_iota(jnp.int32, (rows, 1), 0) < length_ref[0]


def route(routes, alive):
    rows = routes.shape[1]
    expert = lax.broadcasted_iota(jnp.int32, (EXPERTS, rows), 0)
    named = (routes[0:1] == expert) | (routes[1:2] == expert)
    hits = jnp.transpose(jnp.where(named, 1.0, 0.0)) * jnp.where(alive, 1.0, 0.0)
    token = lax.broadcasted_iota(jnp.int32, (rows, rows), 0)
    other = lax.broadcasted_iota(jnp.int32, (rows, rows), 1)
    earlier = contract(jnp.where(other < token, 1.0, 0.0).astype(bf16), hits.astype(bf16))
    return hits, earlier


def place_rows(hits, earlier, flat, placed_ref):
    spread_out = jnp.transpose(row_spots(hits, earlier, placed_ref.shape[0])).astype(bf16)
    placed_ref[...] = contract(spread_out, flat).astype(bf16).reshape(placed_ref.shape)


def project(normed, weights, cosine, sine, qkv_ref):
    heads = qkv_ref.shape[0]
    half = HEAD_DIM // 2
    for kind, weight in enumerate(weights):
        lin = jnp.transpose(contract(normed, weight[...]))
        for head in range(heads):
            mine = lin[head * HEAD_DIM : (head + 1) * HEAD_DIM]
            if kind < 2:
                first, second = mine[:half], mine[half:]
                mine = jnp.concatenate(
                    [first * cosine - second * sine, second * cosine + first * sine], axis=0
                )
            qkv_ref[head, kind * HEAD_DIM : (kind + 1) * HEAD_DIM, :] = mine.astype(bf16)


def router_gates(normed, router, hits):
    logits = contract(normed, router, NT)
    top = jnp.max(jnp.where(hits > 0.5, logits, masked_value), axis=1, keepdims=True)
    powers = jnp.where(hits > 0.5, jnp.exp(logits - top), 0.0)
    total = jnp.sum(powers, axis=1, keepdims=True)
    return powers / jnp.where(total > 0.0, total, 1.0)


def gate_tiles(gates, hits, earlier, scale_ref):
    expert_size = scale_ref.shape[0]
    own, lanes = EXPERTS // expert_size, expert_size * 128
    expert_at, _ = expert_of_place(lanes, 128, own)
    by_place = jnp.dot(gates, expert_at, preferred_element_type=f32, precision=EXACT)
    row = jnp.sum(spots(hits, earlier, lanes, 128, own) * by_place, axis=0, keepdims=True)
    for z in range(expert_size):
        scale_ref[z] = jnp.broadcast_to(row[:, z * 128 : (z + 1) * 128], (8, 128))


def gates_back(dots_ref, gates, hits, earlier):
    expert_size = dots_ref.shape[0]
    own, lanes = EXPERTS // expert_size, expert_size * 128
    expert_at, _ = expert_of_place(lanes, 128, own)
    row = jnp.concatenate([dots_ref[z, 0:1, :] for z in range(expert_size)], axis=1)
    at_place = jnp.where(spots(hits, earlier, lanes, 128, own) > 0.5, row, 0.0)
    d_gates = lax.dot_general(at_place, expert_at, NT, preferred_element_type=f32, precision=EXACT)
    mean = jnp.sum(gates * d_gates, axis=1, keepdims=True)
    return (gates * (d_gates - mean)).astype(bf16)


def collect(hits, earlier, back_ref, flat_ref):
    width = flat_ref.shape[1]
    spread_out = row_spots(hits, earlier, back_ref.shape[0]).astype(bf16)
    placed = back_ref[...].reshape(EXPERTS * PLACES, width)
    return contract(spread_out, placed) + flat_ref[...].astype(f32)


def weight_sums(shard, grads, sums_ref):
    plane_size, expert_size, count, width = sums_ref.shape
    for p in range(plane_size):
        for z in range(expert_size):
            first = (p * expert_size + z) * shard
            parts = [grad[first : first + shard] for grad in grads]
            if count > len(grads) * shard:
                parts.append(jnp.zeros((count - len(grads) * shard, width), f32))
            sums_ref[p, z] = jnp.concatenate(parts, axis=0).astype(bf16)


def branch(rows, d_out, gate_w, up_w, down_w):
    gate_lin, up_lin = contract(rows, gate_w), contract(rows, up_w)
    sigmoid = 1.0 / (1.0 + jnp.exp(-gate_lin))
    silu = gate_lin * sigmoid
    hidden = (silu * up_lin).astype(bf16)
    d_hidden = contract(d_out, down_w, NT)
    d_gate = (d_hidden * up_lin * (sigmoid + silu * (1.0 - sigmoid))).astype(bf16)
    d_up = (d_hidden * silu).astype(bf16)
    result = contract(hidden, down_w)
    d_rows = contract(d_gate, gate_w, NT) + contract(d_up, up_w, NT)
    d_lin = contract(rows, jnp.concatenate([d_gate, d_up], axis=1), TN)
    d_down = contract(hidden, d_out, TN)
    return result, d_rows, d_lin, d_down


def moe_kernel(spread_kinds, home_kinds, slices, length_ref, *refs):
    rest = iter(refs)

    def take(count):
        return [next(rest) for _ in range(count)]

    tokens, attended_in, gain, router, hits_ref, earlier_ref, cotangent = take(7)
    output_in = next(rest)
    up_rows_in, up_flat_in = take(2)
    weights_in, shared_in = take(3), take(3)
    hidden, attended_out, d_hidden_out, d_attended_out, d_attn_out, router_grad, gain_grad = take(7)
    result_out, shared_out = take(2)
    shared_grads_out = take(3)
    grads_out = take(3 * slices)
    placed, normed, gate, output_w, output_sem = take(5)
    back, flat, dots_out = take(3)
    in_rows, in_flat, gates = take(3)
    up_rows, up_flat = take(2)
    weights, shared_w = take(3), take(3)
    result, shared_result = take(2)
    d_rows, shared_d = up_rows, up_flat
    lin_out, down_out, rows_f32, up_f32, dot, gates_own = take(6)
    lin_sum, down_sum = take(2)
    shared_parts = take(3)
    load_sem, store_sem = take(2)
    spread = Spread(spread_kinds, True, [placed, normed, gate, in_rows, in_flat, gates] + take(10), True)
    home = Home(home_kinds, True, [d_rows, shared_d], dot, [back, flat], dots_out, list(rest), True)

    dp_size, ctx_size, expert_size = sizes_of()
    ctx, own_block = lax.axis_index("ctx"), spread.own
    groups, blocks, _, size, width = in_rows.shape
    plane_size, rows, _ = in_flat.shape
    part = weights[0].shape[-1]
    sources = blocks * expert_size
    bits = bits_of(ctx_size)

    def column(mask):
        return pl.ds(pl.multiple_of(spread.block(0, mask) * part, 128), part)

    def loads(g):
        masks = subsets([bit for bit in bits if bit != group_bit(g, ctx_size)])
        experts = pl.ds(g * GROUP, GROUP)
        copies = [(up_rows_in.at[g], up_rows.at[g])]
        for k, mask in enumerate(masks):
            copies += [
                (weights_in[0].at[experts, :, column(mask)], weights[0].at[g, k]),
                (weights_in[1].at[experts, :, column(mask)], weights[1].at[g, k]),
                (weights_in[2].at[experts, column(mask)], weights[2].at[g, k]),
            ]
        return [pltpu.make_async_copy(s, t, load_sem.at[g, i]) for i, (s, t) in enumerate(copies)]

    shared_loads = [
        pltpu.make_async_copy(s, t, load_sem.at[groups, i])
        for i, (s, t) in enumerate(
            [
                (shared_in[0].at[:, column(0)], shared_w[0]),
                (shared_in[1].at[:, column(0)], shared_w[1]),
                (shared_in[2].at[column(0)], shared_w[2]),
                (up_flat_in, up_flat),
            ]
        )
    ]
    (output_load,) = fetch([output_in], [output_w], output_sem)
    output_load.start()
    alive = live(length_ref, rows)
    hits, earlier = hits_ref[...], earlier_ref[...]

    def prepare():
        attended = jnp.transpose(attended_in[...].reshape(width, rows).astype(f32)).astype(bf16)
        attended_out[...] = attended
        output_load.wait()
        attn_out = contract(attended, output_w[...])
        into = tokens[...].astype(f32) + jnp.where(alive, attn_out, 0.0)
        hidden[...] = into
        normed[...] = (into * rms_scale(into) * gain[...][None]).astype(bf16)
        gates_own[...] = router_gates(normed[...], router[...], hits)
        place_rows(hits, earlier, normed[...], placed)
        gate_tiles(gates_own[...], hits, earlier, gate)

    greet(plane_partners(), prepare)
    spread.z_start()
    spread.first(spread.staying)
    spread.keep()
    dot[...] = jnp.zeros_like(dot)
    def arriving(g):
        return [piece for piece in spread.moving if piece.group == g]

    for one in shared_loads:
        one.start()
    spread.forward_all(spread.staying)
    for one in loads(0):
        one.start()
    spread.first(arriving(0))
    spread.gates_on()
    spread.paired(spread.staying)
    for one in spread.kept() + shared_loads:
        one.wait()

    def shared_part(first, count):
        here = pl.ds(first, count)
        shape = (count * rows, width)
        some = branch(
            in_flat[here].reshape(shape), up_flat[here].reshape(shape), shared_w[0][...], shared_w[1][...],
            shared_w[2][...],
        )
        shared_result[here] = some[0].reshape((count, rows, width)).astype(bf16)
        shared_d[here] = some[1].reshape((count, rows, width)).astype(bf16)
        if first == 0:
            lin_sum[...] = some[2]
            down_sum[...] = some[3]
        else:
            lin_sum[...] += some[2]
            down_sum[...] += some[3]

    chunk = 4
    flats = home.staying[-2:]
    flat_stores = [
        pltpu.make_async_copy(s, t, store_sem.at[groups, i])
        for i, (s, t) in enumerate(zip([shared_result] + shared_parts, [shared_out] + shared_grads_out))
    ]
    shared_part(0, chunk)
    spread.forward_all(arriving(0))
    for g in range(1, groups):
        spread.first(arriving(g))
        for one in loads(g):
            one.start()
    spread.gates_landed()
    spread.paired(arriving(0))

    def shared_rest():
        for first in range(chunk, plane_size, chunk):
            shared_part(first, chunk)
        home.start(flats)
        shard = shared_parts[0].shape[1] // plane_size
        for z in range(expert_size):
            firsts = [(p * expert_size + z) * shard for p in range(plane_size)]
            mine = jnp.concatenate([lin_sum[first : first + shard] for first in firsts]).astype(bf16)
            shared_parts[0][z] = mine[:, :part]
            shared_parts[1][z] = mine[:, part:]
        shared_parts[2][...] = down_sum[...].astype(bf16).reshape(shared_parts[2].shape)
        for one in flat_stores:
            one.start()

    def expert(g, i):
        bit = group_bit(g, ctx_size)
        lane = (g * GROUP + i) * PLACES
        owners = [spread.block(core, mask) for core in (0, 1) for mask in (0, bit)]
        scale = jnp.concatenate(
            [gates[owner, z, 0:1, lane : lane + PLACES] for owner in owners for z in range(expert_size)]
        )[:, :, None]
        by_source = (sources, PLACES, width)
        up = up_f32[i]
        d_out = (up.reshape(by_source) * scale).reshape(up.shape).astype(bf16)
        some, d_some, d_lin, d_down = branch(
            rows_f32[i].astype(bf16),
            d_out,
            jnp.concatenate([weights[0][g, k, i] for k in range(slices)], axis=1),
            jnp.concatenate([weights[1][g, k, i] for k in range(slices)], axis=1),
            jnp.concatenate([weights[2][g, k, i] for k in range(slices)], axis=0),
        )
        for k in range(slices):
            lin_out[g, 0, k, i] = d_lin[:, k * part : (k + 1) * part].astype(bf16)
            lin_out[g, 1, k, i] = d_lin[:, (slices + k) * part : (slices + k + 1) * part].astype(bf16)
            down_out[g, k, i] = d_down[k * part : (k + 1) * part, :].astype(bf16)
        sums = jnp.sum((some * up).reshape(by_source), axis=-1)
        up_f32[i] = (some.reshape(by_source) * scale).reshape(up.shape)
        rows_f32[i] = d_some
        for at, owner in enumerate(owners):
            for z in range(expert_size):
                line = sums[at * expert_size + z : at * expert_size + z + 1]
                pieces_of = [line]
                if lane:
                    pieces_of.insert(0, jnp.zeros((1, lane), f32))
                if lane + PLACES < 128:
                    pieces_of.append(jnp.zeros((1, 128 - lane - PLACES), f32))
                dot[owner, z, 0:1, :] += jnp.concatenate(pieces_of, axis=1)

    def unpack(g):
        def one(source, carry):
            there = pl.ds(pl.multiple_of(source * PLACES, 8), PLACES)
            at = g, source // expert_size, source % expert_size
            some, up = in_rows[at].astype(f32), up_rows[at].astype(f32)
            for i in range(GROUP):
                rows_f32[i, there] = some[i * PLACES : (i + 1) * PLACES]
                up_f32[i, there] = up[i * PLACES : (i + 1) * PLACES]
            return carry

        lax.fori_loop(0, sources, one, 0)

    def pack(g):
        def one(source, carry):
            there = pl.ds(pl.multiple_of(source * PLACES, 8), PLACES)
            at = g, source // expert_size, source % expert_size
            result[at] = jnp.concatenate([up_f32[i, there] for i in range(GROUP)]).astype(bf16)
            d_rows[at] = jnp.concatenate([rows_f32[i, there] for i in range(GROUP)]).astype(bf16)
            return carry

        lax.fori_loop(0, sources, one, 0)

    def stores_of(g):
        experts = pl.ds(g * GROUP, GROUP)
        copies = [(result.at[g], result_out.at[g])]
        for k in range(slices):
            copies += [
                (lin_out.at[g, 0, k], grads_out[k].at[experts]),
                (lin_out.at[g, 1, k], grads_out[slices + k].at[experts]),
                (down_out.at[g, k], grads_out[2 * slices + k].at[experts]),
            ]
        return [pltpu.make_async_copy(s, t, store_sem.at[g, i]) for i, (s, t) in enumerate(copies)]

    def of_group(g):
        return [piece for piece in home.moving + home.staying if piece.group == g]

    depth = len(bits)
    waiting = []

    def move_on(count):
        for stage_of in waiting[:count]:
            stage_of()
        del waiting[:count]

    for g in range(groups):
        for one in loads(g):
            one.wait()
        if g:
            spread.paired(arriving(g))
        unpack(g)
        for i in range(GROUP):
            expert(g, i)
            if g == 0 and i == 0:
                for later in range(1, groups):
                    spread.forward_all(arriving(later))
            if g < groups - 1 or i < GROUP - 1:
                move_on(-(-len(waiting) // (GROUP - i)))
        if g == groups - 1:
            home.dots_start()
        pack(g)
        home.start(of_group(g))
        if g < groups - 1:
            for one in stores_of(g):
                one.start()
        if g == 0:
            shared_rest()
        waiting += [functools.partial(home.pair, piece) for piece in of_group(g)]
        if g == 0:
            waiting += [functools.partial(home.pair, piece) for piece in flats]
        waiting += [functools.partial(home.step, piece, 0) for piece in of_group(g)]
        if g == 0:
            for place in range(depth):
                waiting += [functools.partial(home.step, piece, place) for piece in flats]
    move_on(len(waiting))
    for one in stores_of(groups - 1):
        one.start()
    home.dots_on()
    home.dots_landed()
    d_logits = gates_back(dots_out, gates_own[...], hits, earlier)
    router_grad[...] = contract(normed[...], d_logits, TN)
    home.done()

    d_normed = collect(hits, earlier, back, flat) + contract(d_logits, router[...])
    into = hidden[...]
    scale = rms_scale(into)
    normal = into * scale
    gain_grad[...] = jnp.sum(d_normed * normal, axis=0, keepdims=True)
    d_hidden = cotangent[...].astype(f32) + rms_back(normal, scale, gain[...][None], d_normed)
    d_hidden_out[...] = d_hidden
    d_attn = jnp.where(alive, d_hidden, 0.0).astype(bf16)
    d_attn_out[...] = d_attn
    d_attended = jnp.transpose(contract(d_attn, output_w[...], NT))
    d_attended_out[...] = d_attended.astype(bf16).reshape(d_attended_out.shape)

    spread.sent()
    for g in range(groups):
        for one in stores_of(g):
            one.wait()
    for one in flat_stores:
        one.wait()


def moe(length, tokens, attended, gain, router, routing, cotangent, output_weight, up_rows, up_flat, weights,
        shared_weights, sizes, number):
    dp_size, ctx_size, expert_size = sizes
    plane_size = dp_size * ctx_size
    rows, width = tokens.shape
    part = shared_weights[0].shape[1] // plane_size
    slices = max(ctx_size // 2, 1)
    own = EXPERTS // expert_size
    groups = own // GROUP
    sources = 4 * expert_size
    placed = jax.ShapeDtypeStruct((expert_size, groups, GROUP * PLACES, width), bf16)
    flat = jax.ShapeDtypeStruct((rows, width), bf16)
    hidden = jax.ShapeDtypeStruct((rows, width), f32)
    gate = jax.ShapeDtypeStruct((expert_size, 8, 128), f32)
    spread_kinds, landing, spread_scratch = spread_plan([placed, flat], gate, sizes)
    dots = (plane_size,) + gate.shape
    home_kinds, home_out, home_scratch = home_plan([up_rows.shape, up_flat.shape], sizes, dots)
    shared_given, _, _ = shared_plan(width, part, sizes)
    lin = jax.ShapeDtypeStruct((own, width, part), bf16)
    down = jax.ShapeDtypeStruct((own, part, width), bf16)
    columns = pltpu.VMEM((groups, slices, GROUP, width, part), bf16)

    def buffers(shapes):
        return [pltpu.VMEM(shape.shape, shape.dtype) for shape in shapes]

    out = pl.pallas_call(
        functools.partial(moe_kernel, spread_kinds, home_kinds, slices),
        out_shape=[
            hidden,
            flat,
            hidden,
            jax.ShapeDtypeStruct(attended.shape, bf16),
            flat,
            jax.ShapeDtypeStruct(router.shape[::-1], f32),
            jax.ShapeDtypeStruct((1, width), f32),
        ]
        + [jax.ShapeDtypeStruct(up_rows.shape, bf16), jax.ShapeDtypeStruct(up_flat.shape, bf16)]
        + [jax.ShapeDtypeStruct(shape, bf16) for shape in shared_given]
        + [lin] * (2 * slices)
        + [down] * slices,
        in_specs=[SMEM] + [VMEM] * 7 + [ANY] * 9,
        out_specs=[VMEM] * 7 + [ANY] * (5 + 3 * slices),
        scratch_shapes=buffers([placed, flat, gate])
        + [pltpu.VMEM(output_weight.shape, bf16), DMA((1,))]
        + buffers(home_out)
        + buffers(landing)
        + [pltpu.VMEM(up_rows.shape, bf16), pltpu.VMEM(up_flat.shape, bf16)]
        + [columns, columns, pltpu.VMEM((groups, slices, GROUP, part, width), bf16)]
        + [pltpu.VMEM((width, part), bf16)] * 2
        + [pltpu.VMEM((part, width), bf16)]
        + [pltpu.VMEM(up_rows.shape, bf16), pltpu.VMEM(up_flat.shape, bf16)]
        + [
            pltpu.VMEM((groups, 2, slices, GROUP, width, part), bf16),
            pltpu.VMEM((groups, slices, GROUP, part, width), bf16),
            pltpu.VMEM((GROUP, sources * PLACES, width), f32),
            pltpu.VMEM((GROUP, sources * PLACES, width), f32),
            pltpu.VMEM(dots, f32),
            pltpu.VMEM((rows, EXPERTS), f32),
            pltpu.VMEM((width, 2 * part), f32),
            pltpu.VMEM((part, width), f32),
        ]
        + [pltpu.VMEM(shape, bf16) for shape in shared_given]
        + [DMA((groups + 1, max(1 + 3 * slices, 4)))] * 2
        + spread_scratch
        + home_scratch,
        compiler_params=pltpu.CompilerParams(
            collective_id=number, has_side_effects=True, vmem_limit_bytes=63 << 20
        ),
    )(length, tokens, attended, gain, router, *routing, cotangent, output_weight, up_rows, up_flat, *weights,
      *shared_weights)
    grads = out[12 : 12 + 3 * slices]
    grads = [grads[kind * slices : (kind + 1) * slices] for kind in range(3)]
    return out[:7], out[9:12], out[7:9], grads


class Slot:
    def __init__(self, heads):
        _, self.ctx_size, self.expert_size = sizes_of()
        self.heads, self.count = heads, self.ctx_size * self.expert_size
        ctx, expert = lax.axis_index("ctx"), lax.axis_index("expert")
        self.me = ctx * self.expert_size + expert
        head = head_of(ctx, expert, heads, self.ctx_size, self.expert_size)
        self.holds = head < heads
        self.head = head % heads

    def device(self, place):
        return {"ctx": place // self.expert_size, "expert": place % self.expert_size}

    def partners(self):
        dp, ctx = lax.axis_index("dp"), lax.axis_index("ctx")
        dp_size = lax.axis_size("dp")
        return [self.device((self.me + i) % self.count) for i in range(1, self.count)] + [
            {"dp": (dp + d) % dp_size, "ctx": flip(ctx, c)} for d in range(1, dp_size) for c in range(self.ctx_size)
        ]

    def copy(self, source, target, send, recv, there):
        return pltpu.make_async_remote_copy(
            src_ref=source, dst_ref=target, send_sem=send, recv_sem=recv, device_id=there, device_id_type=MESH
        )

    def inward(self, blocks, landing, send, recv):
        for i in range(self.heads):
            head = (self.me + i) % self.heads
            row, column = head_place(head, self.heads, self.ctx_size, self.expert_size)
            one = self.copy(
                blocks.at[head], landing.at[self.me], send.at[head], recv.at[self.me],
                {"ctx": row, "expert": column},
            )
            yield jnp.logical_not(self.holds & (head == self.head)), one

    def inward_landed(self, landing, send, recv):
        for i in range(1, self.count):
            source = (self.me + self.count - i) % self.count
            here = landing.at[source]
            yield self.copy(here, here, send.at[0], recv.at[source], self.device(self.me))

    def outward(self, blocks, landing, send, recv, place):
        return self.copy(
            blocks.at[place], landing.at[self.head], send.at[place], recv.at[self.head], self.device(place)
        )

    def outward_landed(self, landing, send, recv):
        for head in range(self.heads):
            here = landing.at[head]
            one = self.copy(here, here, send.at[0], recv.at[head], self.device(self.me))
            yield jnp.logical_not(self.holds & (head == self.head)), one


def attend_kernel(
    step, heads, kinds, length_ref, routes_ref, cotangent_ref, tokens_ref, gain_ref, cosine_ref, sine_ref, *refs
):
    rest = iter(refs)

    def take(count):
        return [next(rest) for _ in range(count)]

    weights_in = take(3)
    qkv_ref, out_ref, total_ref, landed_ref, normed_ref, hits_ref, earlier_ref = take(7)
    side_outs = take(len(kinds))
    weights, blocks_ref, placed_ref, branch_ref = take(3), *take(3)
    key_ref, query_ref, value_ref, sent_ref = take(4)
    in_send, in_recv, out_send, out_recv, weight_sem = take(5)
    side = Spread(kinds, False, [placed_ref, branch_ref] + side_outs + list(rest))

    slot = Slot(heads)
    rows, width = tokens_ref.shape
    span = slot.count * rows
    loads = fetch(weights_in, weights, weight_sem)
    for one in loads:
        one.start()

    def prepare():
        alive = live(length_ref, rows)
        hits, earlier = route(routes_ref[...], alive)
        hits_ref[...] = hits
        earlier_ref[...] = earlier
        branch = jnp.where(alive, cotangent_ref[...].astype(f32), 0.0).astype(bf16)
        branch_ref[...] = branch
        place_rows(hits, earlier, branch, placed_ref)

    greet(slot.partners(), prepare)
    side.z_start()
    inputs = tokens_ref[...].astype(f32)
    normed_ref[...] = (inputs * rms_scale(inputs) * gain_ref[...][None]).astype(bf16)
    for one in loads:
        one.wait()
    here = pl.ds(pl.multiple_of(slot.me * rows, 128), rows)
    project(normed_ref[...], weights, cosine_ref[:, here], sine_ref[:, here], blocks_ref)
    for needed, one in slot.inward(blocks_ref, qkv_ref, in_send, in_recv):
        pl.when(needed)(one.start)
    side.first(side.staying)
    side.keep()
    side.forward_all(side.staying)

    @pl.when(slot.holds)
    def _():
        qkv_ref[slot.me] = blocks_ref[slot.head]
        for one in slot.inward_landed(qkv_ref, in_send, in_recv):
            one.wait_recv()
        key_ref[...] = live_keys(head_rows(qkv_ref, HEAD_DIM, HEAD_DIM), length_ref[0])
        query_ref[...] = scaled_queries(head_rows(qkv_ref, 0, HEAD_DIM))
        value_ref[...] = head_rows(qkv_ref, 2 * HEAD_DIM, HEAD_DIM)

    def query_block(q):
        here = pl.ds(q * step, step)
        query = query_ref[:, here]

        def absorb(k, state, masked):
            top, total, out = state
            there = pl.ds(k * step if masked else pl.multiple_of(k * step, step), step)
            scores = jnp.dot(key_ref[there, :], query, preferred_element_type=f32)
            if masked:
                scores = causal(scores)
            new_top = jnp.maximum(top, jnp.max(scores, axis=0, keepdims=True))
            shrink = jnp.exp(top - new_top)
            weights = jnp.exp(scores - new_top)
            total = total * shrink + jnp.sum(weights, axis=0, keepdims=True)
            out = out * shrink + jnp.dot(
                value_ref[:, there], weights.astype(bf16), preferred_element_type=f32
            )
            return new_top, total, out

        state = (
            jnp.full((1, step), masked_value, f32),
            jnp.zeros((1, step), f32),
            jnp.zeros((HEAD_DIM, step), f32),
        )
        state = absorb(q, state, True)
        if q:
            state = lax.fori_loop(0, q, lambda k, s: absorb(k, s, False), state)
        top, total, out = state
        out = out / total
        out_ref[:, here] = out
        total_ref[:, here] = top + jnp.log(total)
        for i in range(step // rows):
            place = q * (step // rows) + i
            sent_ref[place] = out[:, i * rows : (i + 1) * rows].astype(bf16)
            one = slot.outward(sent_ref, landed_ref, out_send, out_recv, place)
            pl.when(slot.me != place)(one.start)

    side.first(side.moving)
    for q in range(span // step):
        pl.when(slot.holds)(functools.partial(query_block, q))
        if q == span // step - 2:
            side.forward_all(side.moving)

    @pl.when(slot.holds)
    def _():
        landed_ref[slot.head] = sent_ref[slot.me]

    for needed, one in slot.outward_landed(landed_ref, out_send, out_recv):
        pl.when(needed)(one.wait_recv)
    side.paired(side.all)
    side.sent()
    for one in side.kept():
        one.wait()
    for needed, one in slot.inward(blocks_ref, qkv_ref, in_send, in_recv):
        pl.when(needed)(one.wait_send)
    for place in range(slot.count):
        one = slot.outward(sent_ref, landed_ref, out_send, out_recv, place)
        pl.when(slot.holds & (slot.me != place))(one.wait_send)


def attend(length, routes, cotangent, tokens, gain, tables, weights, sizes, number):
    rows, width = tokens.shape
    _, ctx_size, expert_size = sizes
    heads, count = width // HEAD_DIM, ctx_size * expert_size
    span = count * rows
    step = min(512, span)
    groups = EXPERTS // expert_size // GROUP
    placed = jax.ShapeDtypeStruct((expert_size, groups, GROUP * PLACES, width), bf16)
    flat = jax.ShapeDtypeStruct((rows, width), bf16)
    kinds, side_shapes, side_scratch = spread_plan([placed, flat], None, sizes)
    blocks = (heads, 3 * HEAD_DIM, rows)
    hits = jax.ShapeDtypeStruct((rows, EXPERTS), f32)
    out = pl.pallas_call(
        functools.partial(attend_kernel, step, heads, kinds),
        out_shape=[
            jax.ShapeDtypeStruct((count,) + blocks[1:], bf16),
            jax.ShapeDtypeStruct((HEAD_DIM, span), f32),
            jax.ShapeDtypeStruct((1, span), f32),
            jax.ShapeDtypeStruct((heads, HEAD_DIM, rows), bf16),
            flat,
            hits,
            hits,
        ]
        + side_shapes,
        in_specs=[SMEM] + [VMEM] * 6 + [ANY] * 3,
        out_specs=[VMEM] * 7 + [ANY] * len(side_shapes),
        scratch_shapes=[pltpu.VMEM(weights[0].shape, bf16)] * 3
        + [
            pltpu.VMEM(blocks, bf16),
            pltpu.VMEM(placed.shape, bf16),
            pltpu.VMEM(flat.shape, bf16),
            pltpu.VMEM((span, 2 * HEAD_DIM), bf16),
            pltpu.VMEM((2 * HEAD_DIM, span), bf16),
            pltpu.VMEM((HEAD_DIM, span), bf16),
            pltpu.VMEM((count, HEAD_DIM, rows), bf16),
        ]
        + [DMA((count,))] * 4
        + [DMA((3,))]
        + side_scratch,
        compiler_params=pltpu.CompilerParams(
            collective_id=number, has_side_effects=True, vmem_limit_bytes=56 << 20
        ),
    )(length, routes, cotangent, tokens, gain, *tables, *weights)
    return out[:4], out[4:7], out[7:]


def unrotate(grad_t, cosine, sine):
    half = HEAD_DIM // 2
    first, second = grad_t[:half], grad_t[half:]
    return jnp.concatenate(
        [first * cosine + second * sine, second * cosine - first * sine], axis=0
    )


def attend_back_kernel(
    step, heads, kinds, masks, shard, length_ref, gain_ref, hits_ref, earlier_ref, blocks_ref, *refs
):
    rest = iter(refs)

    def take(count):
        return [next(rest) for _ in range(count)]

    soon, later, side_ins, carried = take(5), take(9), take(len(kinds)), take(len(masks))
    output_ref, input_grad, gain_grad, sums_ref = take(4)
    carried_out = take(len(masks))
    soon_here, later_here, landed_ref, side_outs = take(5), take(9), next(rest), take(len(kinds))
    qkv_ref, out_ref, total_ref, cosine_ref, sine_ref = soon_here
    normed_ref, tokens_ref, d_hidden_ref, attended_ref, d_attn_ref, hidden_ref, *weights = later_here
    upstream_ref, key_ref, query_ref, value_ref, key_t_ref, key_sum, value_sum, delta_ref, up_ref, sent_ref = take(10)
    in_send, in_recv, out_send, out_recv, soon_sem, later_sem = take(6)
    carry = Carry(
        masks, by_group(carried, len(masks[0]) if masks else 0), carried_out, take(2) if masks else []
    )
    side = Home(kinds, False, side_ins, None, side_outs, None, list(rest))

    slot = Slot(heads)
    rows = blocks_ref.shape[2]
    span = slot.count * rows
    loads = fetch(soon, soon_here, soon_sem)
    late_loads = fetch(later, later_here, later_sem)

    @pl.when(slot.holds)
    def _():
        key_sum[...] = jnp.zeros_like(key_sum)
        value_sum[...] = jnp.zeros_like(value_sum)

    greet(slot.partners())
    for needed, one in slot.inward(blocks_ref, upstream_ref, in_send, in_recv):
        pl.when(needed)(one.start)
    for one in loads:
        one.start()
    side.start(side.all)
    for one in late_loads:
        one.start()
    carry.push(4)
    for one in loads:
        one.wait()

    @pl.when(slot.holds)
    def _():
        key_t = head_rows(qkv_ref, HEAD_DIM, HEAD_DIM)
        key_ref[...] = live_keys(key_t, length_ref[0])
        key_t_ref[...] = key_t
        query_ref[...] = scaled_queries(head_rows(qkv_ref, 0, HEAD_DIM))
        value_t = head_rows(qkv_ref, 2 * HEAD_DIM, HEAD_DIM)
        value_ref[...] = jnp.transpose(value_t.astype(f32)).astype(bf16)
        upstream_ref[slot.me] = blocks_ref[slot.head]

    for piece in side.moving:
        side.pair(piece)
    carry.push(4)

    @pl.when(slot.holds)
    def _():
        for one in slot.inward_landed(upstream_ref, in_send, in_recv):
            one.wait_recv()
        upstream = head_rows(upstream_ref, 0, HEAD_DIM)
        up_ref[...] = upstream
        delta_ref[...] = jnp.sum(upstream.astype(f32) * out_ref[...], axis=0, keepdims=True)

    def query_block(q):
        here = pl.ds(q * step, step)
        query, up = query_ref[:, here], up_ref[:, here]
        total, delta = total_ref[:, here], delta_ref[:, here]

        def meet(k, query_sum, masked):
            there = pl.ds(k * step if masked else pl.multiple_of(k * step, step), step)
            scores = jnp.dot(key_ref[there, :], query, preferred_element_type=f32)
            if masked:
                scores = causal(scores)
            probs = jnp.exp(scores - total)
            d_probs = jnp.dot(value_ref[there, :], up, preferred_element_type=f32)
            d_scores = (probs * (d_probs - delta)).astype(bf16)
            key_sum[:, there] += contract(query[:HEAD_DIM], d_scores, NT)
            value_sum[:, there] += contract(up, probs.astype(bf16), NT)
            return query_sum + contract(key_t_ref[:, there], d_scores)

        query_sum = meet(q, jnp.zeros((HEAD_DIM, step), f32), True)
        if q:
            query_sum = lax.fori_loop(0, q, lambda k, s: meet(k, s, False), query_sum)
        cosine, sine = cosine_ref[:, here], sine_ref[:, here]
        grad = jnp.concatenate(
            [
                unrotate(query_sum * score_scale, cosine, sine),
                unrotate(key_sum[:, here], cosine, sine),
                value_sum[:, here],
            ],
            axis=0,
        ).astype(bf16)
        for i in range(step // rows):
            place = q * (step // rows) + i
            sent_ref[place] = grad[:, i * rows : (i + 1) * rows]
            one = slot.outward(sent_ref, landed_ref, out_send, out_recv, place)
            pl.when(slot.me != place)(one.start)

    for piece in side.moving:
        side.step(piece, 0)
    for piece in side.staying:
        side.pair(piece)
    depth = len(bits_of(lax.axis_size("ctx")))
    stages = [
        [functools.partial(side.step, piece, place) for piece in side.staying if place < len(piece.order)]
        for place in range(depth)
    ]
    for q in reversed(range(span // step)):
        pl.when(slot.holds)(functools.partial(query_block, q))
        for one in stages.pop(0) if stages else []:
            one()
        carry.push(3 * len(masks))
    for some in stages:
        for one in some:
            one()
    carry.push(len(masks) * GROUP * carry.CHUNKS)

    @pl.when(slot.holds)
    def _():
        landed_ref[slot.head] = sent_ref[slot.me]

    for needed, one in slot.outward_landed(landed_ref, out_send, out_recv):
        pl.when(needed)(one.wait_recv)
    for one in late_loads:
        one.wait()

    width = tokens_ref.shape[1]
    lins = []
    d_normed = jnp.zeros((width, rows), f32)
    for kind in range(3):
        at = slice(kind * HEAD_DIM, (kind + 1) * HEAD_DIM)
        lin = jnp.concatenate([landed_ref[head, at, :] for head in range(heads)], axis=0)
        lins.append(lin)
        d_normed = d_normed + contract(weights[kind][...], lin)
    d_normed = jnp.transpose(d_normed)
    inputs = tokens_ref[...].astype(f32)
    scale = rms_scale(inputs)
    normal = inputs * scale
    gain_grad[...] = jnp.sum(d_normed * normal, axis=0, keepdims=True)
    d_inputs = d_hidden_ref[...] + rms_back(normal, scale, gain_ref[...][None], d_normed)
    input_grad[...] = d_inputs.astype(bf16)
    normed_t = jnp.transpose(normed_ref[...].astype(f32)).astype(bf16)
    attended_t = jnp.transpose(attended_ref[...].astype(f32)).astype(bf16)
    grads = [contract(normed_t, lin, NT) for lin in lins] + [contract(attended_t, d_attn_ref[...])]
    weight_sums(shard, grads, sums_ref)

    side.done()
    mixed = collect(hits_ref[...], earlier_ref[...], *side_outs)
    alive = live(length_ref, rows)
    output_ref[...] = (hidden_ref[...] + jnp.where(alive, mixed, 0.0)).astype(bf16)
    carry.done()
    for needed, one in slot.inward(blocks_ref, upstream_ref, in_send, in_recv):
        pl.when(needed)(one.wait_send)
    for place in range(slot.count):
        one = slot.outward(sent_ref, landed_ref, out_send, out_recv, place)
        pl.when(slot.holds & (slot.me != place))(one.wait_send)


def attend_back(length, gain, routing, blocks, soon, mine, weights, parts, carried, masks, sizes, number):
    qkv, later = soon[0], [*mine, *weights]
    heads, _, rows = blocks.shape
    count = qkv.shape[0]
    span = count * rows
    step = min(512, span)
    dp_size, ctx_size, expert_size = sizes
    width = weights[0].shape[0]
    shard = width // (dp_size * count)
    kinds, side_shapes, side_scratch = home_plan([part.shape for part in parts], sizes)
    carry_shapes = [jax.ShapeDtypeStruct(array.shape, array.dtype) for array in carried]
    carry_sems = [DMA((len(masks), len(masks[0])))] * 2 if masks else []
    sums = (dp_size * ctx_size, expert_size, -(-4 * shard // 16) * 16, width)
    got = pl.pallas_call(
        functools.partial(attend_back_kernel, step, heads, kinds, masks, shard),
        out_shape=[
            jax.ShapeDtypeStruct((rows, width), bf16),
            jax.ShapeDtypeStruct((rows, width), bf16),
            jax.ShapeDtypeStruct((1, width), f32),
            jax.ShapeDtypeStruct(sums, bf16),
        ]
        + carry_shapes,
        in_specs=[SMEM] + [VMEM] * 4 + [ANY] * (14 + len(parts) + len(carried)),
        out_specs=[VMEM] * 4 + [ANY] * len(carried),
        scratch_shapes=[pltpu.VMEM(array.shape, array.dtype) for array in soon + later]
        + [pltpu.VMEM((heads,) + qkv.shape[1:], bf16)]
        + [pltpu.VMEM(shape.shape, shape.dtype) for shape in side_shapes]
        + [
            pltpu.VMEM((count,) + blocks.shape[1:], bf16),
            pltpu.VMEM((span, 2 * HEAD_DIM), bf16),
            pltpu.VMEM((2 * HEAD_DIM, span), bf16),
            pltpu.VMEM((span, HEAD_DIM), bf16),
            pltpu.VMEM((HEAD_DIM, span), bf16),
            pltpu.VMEM((HEAD_DIM, span), f32),
            pltpu.VMEM((HEAD_DIM, span), f32),
            pltpu.VMEM((1, span), f32),
            pltpu.VMEM((HEAD_DIM, span), bf16),
            pltpu.VMEM(qkv.shape, bf16),
        ]
        + [DMA((count,))] * 4
        + [DMA((5,)), DMA((9,))]
        + carry_sems
        + side_scratch,
        compiler_params=pltpu.CompilerParams(
            collective_id=number, has_side_effects=True, vmem_limit_bytes=60 << 20
        ),
    )(length, gain, *routing, blocks, *soon, *later, *parts, *carried)
    return got[:4], got[4:]


def local(
    tokens,
    lengths,
    routes,
    norm1_gain,
    query_weight,
    key_weight,
    value_weight,
    output_weight,
    norm2_gain,
    router_weight,
    expert_gate,
    expert_up,
    expert_down,
    shared_gate,
    shared_up,
    shared_down,
    cotangent,
):
    sizes = dp_size, ctx_size, expert_size = sizes_of()
    plane_size, slot_size = dp_size * ctx_size, ctx_size * expert_size
    rows, width = tokens.shape[1:]
    shard = width // (dp_size * slot_size)
    tokens, routes, cotangent = tokens[0], routes[0], cotangent[0]
    weights = (query_weight, key_weight, value_weight)
    tables = rope_tables(jnp.arange(slot_size * rows, dtype=jnp.int32))

    (qkv, out_t, log_total, attended), (normed, *routing), (up_rows, up_flat) = attend(
        lengths, routes.T, cotangent, tokens, norm1_gain, tables, weights, sizes, 1
    )

    bits = bits_of(ctx_size)
    groups = EXPERTS // expert_size // GROUP
    slice_masks = [
        subsets([bit for bit in bits if bit != group_bit(g, ctx_size)]) for g in range(groups)
    ]
    slices = len(slice_masks[0])
    ways = tuple(tuple(masks[k] for masks in slice_masks) for _ in range(3) for k in range(1, slices))
    early = slices - 1

    mine, shared_parts, results, grads = moe(
        lengths, tokens, attended, norm2_gain, router_weight.T, routing, cotangent, output_weight, up_rows, up_flat,
        (expert_gate, expert_up, expert_down), (shared_gate, shared_up, shared_down), sizes, 2,
    )
    hidden, attended, d_hidden, d_attended, d_attn, router_grad, gain_two_grad = mine
    others = [array for kind in grads for array in kind[1:]]
    (output_rows, input_grad, gain_one_grad, sums), early_in = attend_back(
        lengths, norm1_gain, routing, d_attended, [qkv, out_t, log_total, *tables],
        (normed, tokens, d_hidden, attended, d_attn, hidden),
        weights, results, others[: 2 * early], ways[: 2 * early], sizes, 3,
    )

    devices = (plane_size, expert_size)
    pad = [(0, 0), (0, 0), (0, 0), (0, 128 - shard)]
    routed = -(-shard * EXPERTS // 128)
    small = jnp.concatenate(
        [
            jnp.pad(
                router_grad.reshape(devices + (shard * EXPERTS,)),
                [(0, 0), (0, 0), (0, routed * 128 - shard * EXPERTS)],
            ).reshape(devices + (routed, 128)),
            jnp.pad(gain_one_grad.reshape(devices + (1, shard)), pad),
            jnp.pad(gain_two_grad.reshape(devices + (1, shard)), pad),
            jnp.zeros(devices + (6 - routed, 128), f32),
        ],
        axis=2,
    )
    landed, small, *last_in = bring_sums(
        sums, small, shared_parts, others[2 * early :], ways[2 * early :], sizes, 4
    )
    arrived = [*early_in, *last_in[:early]]
    shared_grads = last_in[early:]
    by_slice = [kind[0] for kind in grads]
    for k in range(early):
        by_slice += [arrived[kind * early + k] for kind in range(3)]
    *out, small, output_rows, input_grad, shared_gate_grad, shared_up_grad, shared_down_grad = finish(
        by_slice, landed, small, [output_rows, input_grad, *shared_grads], shard
    )
    return (
        output_rows[None],
        input_grad[None],
        small[routed, :shard],
        *out[3:7],
        small[routed + 1, :shard],
        small[:routed].reshape(-1)[: shard * EXPERTS].reshape(shard, EXPERTS),
        *out[:3],
        shared_gate_grad,
        shared_up_grad,
        shared_down_grad,
    )


def solution(mesh):
    tokens = P("dp", ("ctx", "expert"), None)
    whole = P()
    experts = P("expert", None, None)
    everywhere = ("dp", "ctx", "expert")
    return jax.shard_map(
        local,
        mesh=mesh,
        in_specs=(tokens, P("dp"), tokens)
        + (whole,) * 7
        + (experts,) * 3
        + (whole,) * 3
        + (tokens,),
        out_specs=(tokens, tokens, P(everywhere))
        + (P(everywhere, None),) * 4
        + (P(everywhere), P(everywhere, None))
        + (P("expert", None, PLANE),) * 2
        + (P("expert", PLANE, None),)
        + (P(everywhere, None),) * 3,
        check_vma=False,
    )
```

```python
import functools

import jax
import jax.numpy as jnp
from jax import lax
from jax.experimental import pallas as pl
from jax.experimental.pallas import tpu as pltpu
from jax.sharding import PartitionSpec as P

HEAD_DIM = 64
EXPERTS = 16
TOP = 2
CAP = 22
PLACES = 24

norm_epsilon = 1e-06
rope_base = 10000.0
score_scale = 0.125
masked_value = -1e30
PLANE = ("dp", "ctx")
SLOT = ("ctx", "expert")
bf16 = jnp.bfloat16
f32 = jnp.float32


def rms_scale(values):
    return lax.rsqrt(jnp.mean(values * values, axis=-1, keepdims=True) + norm_epsilon)


def rms_back(normal, scale, gain, upstream):
    lifted = upstream * gain
    return scale * (lifted - normal * jnp.mean(lifted * normal, axis=-1, keepdims=True))


def rope_tables(positions):
    half = HEAD_DIM // 2
    exponent = jnp.arange(half, dtype=f32) * (2.0 / HEAD_DIM)
    inverse_freq = rope_base ** (-exponent)
    angles = inverse_freq[:, None] * positions[None, :].astype(f32)
    return jnp.cos(angles), jnp.sin(angles)


def head_rows(qkv_ref, first, count):
    return jnp.concatenate(
        [qkv_ref[block, first : first + count, :] for block in range(qkv_ref.shape[0])], axis=1
    )


def live_keys(key_t, length):
    span = key_t.shape[1]
    place = lax.broadcasted_iota(jnp.int32, (8, span), 1)
    row = lax.broadcasted_iota(jnp.int32, (8, span), 0)
    bias = jnp.where((place >= length) & (row == 0), masked_value, 0.0)
    padded = jnp.concatenate(
        [key_t.astype(f32), bias, jnp.zeros((HEAD_DIM - 8, span), f32)], axis=0
    )
    return jnp.transpose(padded).astype(bf16)


def scaled_queries(query_t):
    span = query_t.shape[1]
    row = lax.broadcasted_iota(jnp.int32, (HEAD_DIM, span), 0)
    ones = jnp.where(row == 0, 1.0, 0.0)
    return jnp.concatenate([query_t.astype(f32) * score_scale, ones], axis=0).astype(bf16)


def causal(scores):
    key = lax.broadcasted_iota(jnp.int32, scores.shape, 0)
    query = lax.broadcasted_iota(jnp.int32, scores.shape, 1)
    return jnp.where(key <= query, scores, masked_value)


MESH = pl.DeviceIdType.MESH
ANY = pl.BlockSpec(memory_space=pl.ANY)
VMEM = pl.BlockSpec(memory_space=pltpu.VMEM)
SMEM = pl.BlockSpec(memory_space=pltpu.SMEM)
DMA = pltpu.SemaphoreType.DMA


def head_place(head, heads, ctx_size, expert_size):
    per = expert_size - 1
    if ctx_size <= expert_size and ctx_size * per == heads:
        row = head // per
        step = head % per
        return row, step + jnp.where(step >= row, 1, 0)
    return head // expert_size, head % expert_size


def head_of(ctx, expert, heads, ctx_size, expert_size):
    per = expert_size - 1
    if ctx_size <= expert_size and ctx_size * per == heads:
        head = ctx * per + expert - jnp.where(expert > ctx, 1, 0)
        return jnp.where(expert == ctx, heads, head)
    return ctx * expert_size + expert


def sizes_of():
    return tuple(lax.axis_size(a) for a in ("dp", "ctx", "expert"))


def greet(partners, meanwhile=lambda: None):
    barrier = pltpu.get_barrier_semaphore()
    for partner in partners:
        pl.semaphore_signal(barrier, inc=1, device_id=partner, device_id_type=MESH)
    meanwhile()
    pl.semaphore_wait(barrier, len(partners))


def fetch(sources, targets, sems):
    return [
        pltpu.make_async_copy(source, target, sems.at[i]) for i, (source, target) in enumerate(zip(sources, targets))
    ]


GROUP = 2


def flip(index, mask):
    bit = 1
    while bit <= mask:
        if mask & bit:
            index = index + bit * (1 - 2 * ((index // bit) % 2))
        bit *= 2
    return index


def bits_of(ctx_size):
    return [1 << b for b in range(ctx_size.bit_length() - 1)]


def group_bit(group, ctx_size):
    bits = bits_of(ctx_size)
    return bits[group % len(bits)]


def subsets(order):
    masks = [0]
    for bit in order:
        masks = masks + [m | bit for m in masks]
    return masks


class Piece:
    def __init__(self, array, kind, group, step, first, size, order):
        self.array, self.kind, self.group, self.step = array, kind, group, step
        self.first, self.size, self.order = first, size, order
        self.masks = subsets(order)


def pieces(kinds, expert_size, ctx_size):
    bits = bits_of(ctx_size)
    moving, staying = [], []
    for array, (kind, groups, rows) in enumerate(kinds):
        if kind == "flat":
            half = rows // 2
            staying.append(Piece(array, kind, None, None, 0, half, bits))
            staying.append(Piece(array, kind, None, None, half, rows - half, bits[::-1]))
            continue
        for group in range(groups or 1):
            for step in range(expert_size):
                if kind == "group":
                    order = [group_bit(group, ctx_size)]
                else:
                    order = bits if (step + array) % 2 == 0 else bits[::-1]
                (moving if step else staying).append(Piece(array, kind, group, step, 0, rows, order))
    return moving, staying


class Spread:
    def __init__(self, kinds, has_gate, refs, near=False):
        self.near = near
        rest = iter(refs)

        def take(count):
            return [next(rest) for _ in range(count)]

        self.has_gate = has_gate
        self.ins = take(len(kinds))
        self.gate = next(rest) if has_gate else None
        self.outs = take(len(kinds))
        self.gates = next(rest) if has_gate else None
        self.z_send, self.z_recv, self.send, self.recv, self.pair_recv, self.local_sem = take(6)
        if has_gate:
            self.gate_send, self.gate_recv, self.gate_z_send, self.gate_z_recv = take(4)
        self.dp_size, self.ctx_size, self.expert_size = sizes_of()
        self.dp, self.ctx, self.expert = (lax.axis_index(a) for a in ("dp", "ctx", "expert"))
        self.moving, self.staying = pieces(kinds, self.expert_size, self.ctx_size)
        self.all = self.staying + self.moving
        self.number = {id(piece): i for i, piece in enumerate(self.all)}
        self.own = self.dp * self.ctx_size + self.ctx
        self.other = (self.dp + 1) % self.dp_size
        self.bits = bits_of(self.ctx_size)
        self.started = []
        self.plane = [(d, c) for d in range(self.dp_size) for c in range(self.ctx_size) if (d, c) != (0, 0)]

    def z_at(self, step):
        return (self.expert + step) % self.expert_size

    def z_from(self, step):
        return (self.expert + self.expert_size - step) % self.expert_size

    def block(self, core, mask):
        return (self.dp if core == 0 else self.other) * self.ctx_size + flip(self.ctx, mask)

    def landed(self, piece, core, mask, at=0):
        out = self.outs[piece.array]
        if piece.step is None:
            return out.at[self.block(core, mask), pl.ds(piece.first, piece.size)]
        return out.at[piece.group, core * 2 + (1 if mask ^ at else 0), self.z_from(piece.step)]

    def source(self, piece):
        if piece.step is None:
            return self.ins[piece.array].at[pl.ds(piece.first, piece.size)]
        if piece.step == 0:
            return self.ins[piece.array].at[self.expert, piece.group]
        return self.landed(piece, 0, 0)

    def remote(self, source, target, send, recv, there):
        return pltpu.make_async_remote_copy(
            src_ref=source, dst_ref=target, send_sem=send, recv_sem=recv, device_id=there, device_id_type=MESH
        )

    def z_copy(self, piece, landing=False):
        place = self.z_from(piece.step) if landing else self.expert
        at = self.number[id(piece)]
        return self.remote(
            self.ins[piece.array].at[self.z_at(piece.step), piece.group],
            self.outs[piece.array].at[piece.group, 0, place],
            self.z_send.at[at],
            self.z_recv.at[at],
            {"expert": self.z_at(piece.step)},
        )

    def gate_z(self, step, landing=False):
        return self.remote(
            self.gate.at[self.z_at(step)],
            self.gates.at[self.own, self.z_from(step) if landing else self.expert],
            self.gate_z_send.at[step],
            self.gate_z_recv.at[step],
            {"expert": self.z_at(step)},
        )

    def gate_plane(self, d, c, block):
        return self.remote(
            self.gates.at[block],
            self.gates.at[block],
            self.gate_send.at[d, c],
            self.gate_recv.at[d, c],
            {"dp": (self.dp + d) % self.dp_size, "ctx": flip(self.ctx, c)},
        )

    def passing(self, piece, mask, bit):
        at = self.number[id(piece)]
        return self.remote(
            self.landed(piece, 0, mask) if mask else self.source(piece),
            self.landed(piece, 0, mask, bit),
            self.send.at[at, mask, self.bits.index(bit)],
            self.recv.at[at, mask ^ bit],
            {"ctx": flip(self.ctx, bit)},
        )

    def arrived(self, piece, mask):
        here = self.landed(piece, 0, mask)
        recv = self.recv.at[self.number[id(piece)], mask]
        return self.remote(here, here, self.send.at[0, 0, 0], recv, {"ctx": self.ctx})

    def crossing(self, piece, mask, landing=False):
        at = self.number[id(piece)]
        core = 0 if piece.step is None and not landing else 1
        return self.remote(
            self.landed(piece, 0, mask) if mask else self.source(piece),
            self.landed(piece, core, mask),
            self.send.at[at, mask, len(self.bits)],
            self.pair_recv.at[at, mask],
            {"dp": self.other},
        )

    def kept(self):
        if self.near:
            return []
        return [
            pltpu.make_async_copy(self.source(piece), self.landed(piece, 0, 0), self.local_sem.at[i])
            for i, piece in enumerate(self.staying)
        ]

    def begin(self, one):
        one.start()
        self.started.append(one)

    def z_start(self):
        if self.has_gate:
            for step in range(1, self.expert_size):
                self.gate_z(step).start()
        for piece in self.moving:
            self.z_copy(piece).start()

    def first(self, some):
        for piece in some:
            if piece.step:
                self.z_copy(piece, True).wait_recv()
            for bit in piece.order:
                self.begin(self.passing(piece, 0, bit))
            self.begin(self.crossing(piece, 0))

    def keep(self):
        for one in self.kept():
            one.start()
        if self.near:
            for piece in self.staying:
                target = self.landed(piece, 0, 0)
                target[...] = self.source(piece)[...]
        if self.has_gate:
            self.gates[self.own, self.expert] = self.gate[self.expert]

    def forward(self, piece, place):
        if place >= len(piece.order):
            return
        bit = piece.order[place]
        for mask in [m | bit for m in subsets(piece.order[:place])]:
            self.arrived(piece, mask).wait_recv()
            for later in piece.order[place + 1 :]:
                self.begin(self.passing(piece, mask, later))
            self.begin(self.crossing(piece, mask))

    def forward_all(self, some):
        for place in range(len(self.bits)):
            for piece in some:
                self.forward(piece, place)

    def gates_on(self):
        for step in range(1, self.expert_size):
            self.gate_z(step, True).wait_recv()
        for d, c in self.plane:
            self.gate_plane(d, c, self.own).start()

    def gates_landed(self):
        for d, c in self.plane:
            block = ((self.dp + d) % self.dp_size) * self.ctx_size + flip(self.ctx, c)
            self.gate_plane(d, c, block).wait_recv()

    def paired(self, some):
        for piece in some:
            for mask in piece.masks:
                self.crossing(piece, mask, True).wait_recv()

    def sent(self):
        for one in self.started:
            one.wait_send()
        for piece in self.moving:
            self.z_copy(piece).wait_send()
        if self.has_gate:
            for step in range(1, self.expert_size):
                self.gate_z(step).wait_send()
            for d, c in self.plane:
                self.gate_plane(d, c, self.own).wait_send()


def plane_partners():
    dp_size, ctx_size, expert_size = sizes_of()
    dp, ctx, expert = (lax.axis_index(a) for a in ("dp", "ctx", "expert"))
    plane = [(d, c) for d in range(dp_size) for c in range(ctx_size) if (d, c) != (0, 0)]
    return [{"expert": (expert + step) % expert_size} for step in range(1, expert_size)] + [
        {"dp": (dp + d) % dp_size, "ctx": flip(ctx, c)} for d, c in plane
    ]


def spread_plan(arrays, gate, sizes):
    dp_size, ctx_size, expert_size = sizes
    assert dp_size == 2
    plane_size = dp_size * ctx_size
    kinds, out_shape = [], []
    for array in arrays:
        if array.ndim == 4:
            kinds.append(("group", array.shape[1], array.shape[2]))
            shape = (array.shape[1], 4, expert_size) + array.shape[2:]
        else:
            kinds.append(("flat", None, array.shape[0]))
            shape = (plane_size,) + array.shape
        out_shape.append(jax.ShapeDtypeStruct(shape, array.dtype))
    moving, staying = pieces(kinds, expert_size, ctx_size)
    count = len(moving + staying)
    scratch = [
        DMA((count,)),
        DMA((count,)),
        DMA((count, ctx_size, len(bits_of(ctx_size)) + 1)),
        DMA((count, ctx_size)),
        DMA((count, ctx_size)),
        DMA((len(staying),)),
    ]
    if gate is not None:
        out_shape.append(jax.ShapeDtypeStruct((plane_size,) + gate.shape, gate.dtype))
        scratch += [DMA((dp_size, ctx_size))] * 2 + [DMA((expert_size,))] * 2
    return tuple(kinds), out_shape, scratch


def stage(piece, place):
    order = piece.order[::-1]
    done, bit = sum(order[:place]), order[place]
    kept = [m for m in piece.masks if not m & (done | bit)]
    return bit, [(m | bit, m) for m in kept]


def buffer_places(order):
    held, arriving, here, there = {}, {}, 0, 0
    for piece in order:
        for mask in piece.masks:
            held[id(piece), mask] = here
            here += piece.size
        for place in range(len(piece.order)):
            for index in range(len(stage(piece, place)[1])):
                arriving[id(piece), place, index] = there
                there += piece.size
    held["rows"], arriving["rows"] = here, there
    return held, arriving


class Home:
    def __init__(self, kinds, has_dots, parts, dot, outs, dots_out, scratch, near=False):
        self.near = near
        rest = iter(scratch)

        def take(count):
            return [next(rest) for _ in range(count)]

        self.parts, self.dot, self.outs, self.dots_out, self.has_dots = parts, dot, outs, dots_out, has_dots
        self.mine, self.theirs, self.arrivals = take(3)
        self.mine_sem, self.pair_send, self.pair_recv, self.send, self.recv, self.z_send, self.z_recv = take(7)
        if has_dots:
            self.dot_in, self.dot_sum, self.dot_send, self.dot_recv, self.dot_z_send, self.dot_z_recv = take(6)
        self.dp_size, self.ctx_size, self.expert_size = sizes_of()
        self.dp, self.ctx, self.expert = (lax.axis_index(a) for a in ("dp", "ctx", "expert"))
        self.moving, self.staying = pieces(kinds, self.expert_size, self.ctx_size)
        self.all = self.moving + self.staying
        self.number = {id(piece): i for i, piece in enumerate(self.all)}
        self.held, self.arriving = buffer_places(self.all)
        self.own = self.dp * self.ctx_size + self.ctx
        self.other = (self.dp + 1) % self.dp_size
        self.plane = [(d, c) for d in range(self.dp_size) for c in range(self.ctx_size) if (d, c) != (0, 0)]

    def z_at(self, step):
        return (self.expert + step) % self.expert_size

    def z_from(self, step):
        return (self.expert + self.expert_size - step) % self.expert_size

    def plane_at(self, d, c):
        return ((self.dp + d) % self.dp_size) * self.ctx_size + flip(self.ctx, c)

    def partner(self, d, c):
        return {"dp": (self.dp + d) % self.dp_size, "ctx": flip(self.ctx, c)}

    def remote(self, source, target, send, recv, there):
        return pltpu.make_async_remote_copy(
            src_ref=source, dst_ref=target, send_sem=send, recv_sem=recv, device_id=there, device_id_type=MESH
        )

    def whole(self, piece, core, mask):
        part = self.parts[piece.array]
        if piece.kind == "group":
            return part.at[piece.group, core * 2 + (1 if mask else 0), self.z_at(piece.step)]
        block = (self.dp if core == 0 else self.other) * self.ctx_size + flip(self.ctx, mask)
        if piece.kind == "flat":
            return part.at[block, pl.ds(piece.first, piece.size)]
        return part.at[block, self.z_at(piece.step)]

    def at(self, piece, mask):
        return pl.ds(self.held[id(piece), mask], piece.size)

    def load(self, piece, mask):
        return pltpu.make_async_copy(
            self.whole(piece, 0, mask), self.mine.at[self.at(piece, mask)], self.mine_sem.at[self.number[id(piece)], mask]
        )

    def cross(self, piece, mask):
        number = self.number[id(piece)]
        return self.remote(
            self.whole(piece, 1, mask),
            self.theirs.at[self.at(piece, mask)],
            self.pair_send.at[number, mask],
            self.pair_recv.at[number, mask],
            {"dp": self.other},
        )

    def hop(self, piece, place, index):
        bit, moves = stage(piece, place)
        number = self.number[id(piece)]
        return self.remote(
            self.mine.at[self.at(piece, moves[index][0])],
            self.arrivals.at[pl.ds(self.arriving[id(piece), place, index], piece.size)],
            self.send.at[number, moves[index][0]],
            self.recv.at[number, place, index],
            {"ctx": flip(self.ctx, bit)},
        )

    def z_copy(self, piece, landing=False):
        place = self.z_from(piece.step) if landing else self.expert
        out, number = self.outs[piece.array], self.number[id(piece)]
        return self.remote(
            self.mine.at[self.at(piece, 0)],
            out.at[place, piece.group] if piece.kind == "group" else out.at[place],
            self.z_send.at[number],
            self.z_recv.at[number],
            {"expert": self.z_at(piece.step)},
        )

    def start(self, some):
        for piece in some:
            for mask in piece.masks:
                self.cross(piece, mask).start()
                if not self.near:
                    self.load(piece, mask).start()

    def add(self, here, buffer, there):
        total = self.mine[here].astype(f32) + buffer[there].astype(f32)
        self.mine[here] = total.astype(self.mine.dtype)

    def pair(self, piece):
        leaving = [source for source, _ in stage(piece, 0)[1]]
        for mask in leaving + [m for m in piece.masks if m not in leaving]:
            here = self.at(piece, mask)
            if not self.near:
                self.load(piece, mask).wait()
            self.cross(piece, mask).wait_recv()
            if self.near:
                total = self.whole(piece, 0, mask)[...].astype(f32) + self.theirs[here].astype(f32)
                self.mine[here] = total.astype(self.mine.dtype)
            else:
                self.add(here, self.theirs, here)
            if mask in leaving:
                self.hop(piece, 0, leaving.index(mask)).start()

    def step(self, piece, place):
        targets = [target for _, target in stage(piece, place)[1]]
        leaving = []
        if place + 1 < len(piece.order):
            leaving = [source for source, _ in stage(piece, place + 1)[1]]
        for index in range(len(targets)):
            self.hop(piece, place, index).wait_recv()
        for mask in leaving + [m for m in targets if m not in leaving]:
            there = pl.ds(self.arriving[id(piece), place, targets.index(mask)], piece.size)
            self.add(self.at(piece, mask), self.arrivals, there)
            if mask in leaving:
                self.hop(piece, place + 1, leaving.index(mask)).start()
        if place + 1 == len(piece.order):
            self.finish(piece)

    def finish(self, piece):
        result, out = self.mine.at[self.at(piece, 0)], self.outs[piece.array]
        if piece.kind == "flat":
            out[pl.ds(piece.first, piece.size)] = result[...]
        elif piece.step:
            self.z_copy(piece).start()
        elif piece.kind == "group":
            out[self.expert, piece.group] = result[...]
        else:
            out[self.expert] = result[...]

    def ticks(self, some, ahead):
        depth = max(len(piece.order) for piece in some)
        for tick in range(len(some) + ahead + depth):
            for place in range(depth + 1):
                index = tick if place == 0 else tick - ahead - place + 1
                if not 0 <= index < len(some) or place > len(some[index].order):
                    continue
                if place == 0:
                    self.pair(some[index])
                else:
                    self.step(some[index], place - 1)
            yield

    def dot_plane(self, d, c):
        return self.remote(
            self.dot.at[self.plane_at(d, c)],
            self.dot_in.at[d, c],
            self.dot_send.at[d, c],
            self.dot_recv.at[d, c],
            self.partner(d, c),
        )

    def dot_z(self, step, landing=False):
        return self.remote(
            self.dot_sum.at[self.z_at(step)],
            self.dots_out.at[self.z_from(step) if landing else self.expert],
            self.dot_z_send.at[step],
            self.dot_z_recv.at[step],
            {"expert": self.z_at(step)},
        )

    def dots_start(self):
        for d, c in self.plane:
            self.dot_plane(d, c).start()

    def dots_on(self):
        total = self.dot[self.own]
        for d, c in self.plane:
            self.dot_plane(d, c).wait_recv()
            total = total + self.dot_in[d, c]
        self.dot_sum[...] = total
        for step in range(1, self.expert_size):
            self.dot_z(step).start()
        self.dots_out[self.expert] = self.dot_sum[self.expert]

    def dots_landed(self):
        for step in range(1, self.expert_size):
            self.dot_z(step, True).wait_recv()

    def done(self):
        for piece in self.moving:
            self.z_copy(piece, True).wait_recv()
        if self.has_dots:
            for step in range(1, self.expert_size):
                self.dot_z(step).wait_send()
            for d, c in self.plane:
                self.dot_plane(d, c).wait_send()
        for piece in self.moving:
            self.z_copy(piece).wait_send()
        for piece in self.all:
            for mask in piece.masks:
                self.cross(piece, mask).wait_send()
            for place in range(len(piece.order)):
                for index in range(len(stage(piece, place)[1])):
                    self.hop(piece, place, index).wait_send()


def home_plan(shapes, sizes, dots=None):
    dp_size, ctx_size, expert_size = sizes
    assert dp_size == 2
    width = shapes[0][-1]
    kinds, out_shape = [], []
    for given in shapes:
        if len(given) == 5:
            kinds.append(("group", given[0], given[3]))
            shape = (expert_size, given[0]) + given[3:]
        else:
            kinds.append(("plane" if len(given) == 4 else "flat", None, given[-2]))
            shape = given[1:]
        out_shape.append(jax.ShapeDtypeStruct(shape, bf16))
    moving, staying = pieces(kinds, expert_size, ctx_size)
    held, arriving = buffer_places(moving + staying)
    count, depth = len(moving + staying), len(bits_of(ctx_size))
    scratch = [
        pltpu.VMEM((held["rows"], width), bf16),
        pltpu.VMEM((held["rows"], width), bf16),
        pltpu.VMEM((arriving["rows"], width), bf16),
        DMA((count, ctx_size)),
        DMA((count, ctx_size)),
        DMA((count, ctx_size)),
        DMA((count, ctx_size)),
        DMA((count, depth, max(ctx_size // 2, 1))),
        DMA((count,)),
        DMA((count,)),
    ]
    if dots is not None:
        out_shape.append(jax.ShapeDtypeStruct(dots[1:], f32))
        scratch += [
            pltpu.VMEM((dp_size, ctx_size) + dots[1:], f32),
            pltpu.VMEM(dots[1:], f32),
            DMA((dp_size, ctx_size)),
            DMA((dp_size, ctx_size)),
            DMA((expert_size,)),
            DMA((expert_size,)),
        ]
    return tuple(kinds), out_shape, scratch


class Shared:
    def __init__(self, grads, outs, scratch):
        self.grads, self.outs = grads, outs
        self.landing, self.columns = scratch[:3], scratch[3:5]
        self.send, self.recv, self.column_send, self.column_recv = scratch[5:]
        self.dp_size, self.ctx_size, self.expert_size = sizes_of()
        self.dp, self.ctx, self.expert = (lax.axis_index(a) for a in ("dp", "ctx", "expert"))
        self.own = self.dp * self.ctx_size + self.ctx
        self.plane = [(d, c) for d in range(self.dp_size) for c in range(self.ctx_size) if (d, c) != (0, 0)]
        self.part = grads[0].shape[2]

    def z_copy(self, kind, step):
        there = (self.expert + step) % self.expert_size
        return pltpu.make_async_remote_copy(
            src_ref=self.grads[kind].at[there],
            dst_ref=self.landing[kind].at[step],
            send_sem=self.send.at[kind, step],
            recv_sem=self.recv.at[kind, step],
            device_id={"expert": there},
            device_id_type=MESH,
        )

    def column(self, kind, d, c, landing=False):
        there = ((self.dp + d) % self.dp_size) * self.ctx_size + flip(self.ctx, c)
        source = ((self.dp + self.dp_size - d) % self.dp_size) * self.ctx_size + flip(self.ctx, c)
        at = source if landing else self.own
        return pltpu.make_async_remote_copy(
            src_ref=self.columns[kind].at[there],
            dst_ref=self.outs[kind].at[:, pl.ds(pl.multiple_of(at * self.part, 128), self.part)],
            send_sem=self.column_send.at[kind, d, c],
            recv_sem=self.column_recv.at[kind, d, c],
            device_id={"dp": (self.dp + d) % self.dp_size, "ctx": flip(self.ctx, c)},
            device_id_type=MESH,
        )

    def start(self):
        for kind in range(3):
            for step in range(1, self.expert_size):
                self.z_copy(kind, step).start()

    def sum(self):
        for kind in range(3):
            total = self.grads[kind][self.expert].astype(f32)
            for step in range(1, self.expert_size):
                self.z_copy(kind, step).wait_recv()
                total = total + self.landing[kind][step].astype(f32)
            if kind == 2:
                self.outs[2][...] = total
                continue
            shard = self.outs[kind].shape[0]
            for block in range(self.dp_size * self.ctx_size):
                self.columns[kind][block] = total[block * shard : (block + 1) * shard]
            for d, c in self.plane:
                self.column(kind, d, c).start()
            here = pl.ds(pl.multiple_of(self.own * self.part, 128), self.part)
            self.outs[kind][:, here] = self.columns[kind][self.own]

    def done(self):
        for kind in range(3):
            for step in range(1, self.expert_size):
                self.z_copy(kind, step).wait_send()
            if kind < 2:
                for d, c in self.plane:
                    self.column(kind, d, c, True).wait_recv()
                    self.column(kind, d, c).wait_send()


def shared_plan(width, part, sizes):
    dp_size, ctx_size, expert_size = sizes
    plane_size = dp_size * ctx_size
    shard = width // (plane_size * expert_size)
    given = [(expert_size, plane_size * shard, part)] * 2 + [(expert_size, part // expert_size, width)]
    columns = jax.ShapeDtypeStruct((shard, plane_size * part), f32)
    out_shape = [columns, columns, jax.ShapeDtypeStruct(given[2][1:], f32)]
    scratch = [pltpu.VMEM(shape, bf16) for shape in given]
    scratch += [pltpu.VMEM((plane_size, shard, part), f32)] * 2
    scratch += [
        DMA((3, expert_size)),
        DMA((3, expert_size)),
        DMA((2, dp_size, ctx_size)),
        DMA((2, dp_size, ctx_size)),
    ]
    return given, out_shape, scratch


class Carry:
    CHUNKS = 8

    def __init__(self, masks, sources, targets, sems):
        self.masks, self.sources, self.targets, self.sems = masks, sources, targets, sems
        self.ctx = lax.axis_index("ctx")
        groups = len(masks[0]) if masks else 0
        self.queues = [
            [
                (array, g, e, chunk)
                for array in range(len(masks))
                for e in range(GROUP)
                for chunk in range(self.CHUNKS)
            ]
            for g in range(groups)
        ]

    def copy(self, array, g, e, rows):
        return pltpu.make_async_remote_copy(
            src_ref=self.sources[array][g].at[e, rows],
            dst_ref=self.targets[array].at[g * GROUP + e, rows],
            send_sem=self.sems[0].at[array, g],
            recv_sem=self.sems[1].at[array, g],
            device_id={"ctx": flip(self.ctx, self.masks[array][g])},
            device_id_type=MESH,
        )

    def push(self, count, groups=None):
        for g in range(len(self.queues)) if groups is None else groups:
            for array, _, e, chunk in self.queues[g][:count]:
                rows = self.sources[array][g].shape[1] // self.CHUNKS
                self.copy(array, g, e, pl.ds(chunk * rows, rows)).start()
            del self.queues[g][:count]

    def done(self):
        for array, by_group in enumerate(self.masks):
            for g in range(len(by_group)):
                whole = pltpu.make_async_remote_copy(
                    src_ref=self.sources[array][g],
                    dst_ref=self.targets[array].at[pl.ds(g * GROUP, GROUP)],
                    send_sem=self.sems[0].at[array, g],
                    recv_sem=self.sems[1].at[array, g],
                    device_id={"ctx": flip(self.ctx, by_group[g])},
                    device_id_type=MESH,
                )
                whole.wait_recv()
                whole.wait_send()


def by_group(arrays, groups):
    return [[array.at[pl.ds(g * GROUP, GROUP)] for g in range(groups)] for array in arrays]


def sums_kernel(kinds, masks, *refs):
    rest = iter(refs)

    def take(count):
        return [next(rest) for _ in range(count)]

    part, dot, carried, shared_in = next(rest), next(rest), take(len(masks)), take(3)
    landed, dots_landed, carried_out, shared_out = next(rest), next(rest), take(len(masks)), take(3)
    sems = take(2) if masks else []
    shared = Shared(shared_in, shared_out, take(9))
    carry = Carry(masks, by_group(carried, len(masks[0]) if masks else 0), carried_out, sems)
    home = Home(kinds, True, [part], dot, [landed], dots_landed, list(rest))
    greet(plane_partners())
    shared.start()
    home.start(home.all)
    home.dots_start()
    for _ in home.ticks(home.all, 2):
        carry.push(3)
    home.dots_on()
    carry.push(len(masks) * GROUP * carry.CHUNKS)
    shared.sum()
    home.dots_landed()
    home.done()
    shared.done()
    carry.done()


def bring_sums(part, dots, shared_parts, carried, masks, sizes, number):
    kinds, out_shape, scratch = home_plan([part.shape], sizes, dots.shape)
    _, shared_out, shared_scratch = shared_plan(part.shape[-1], shared_parts[0].shape[2], sizes)
    return pl.pallas_call(
        functools.partial(sums_kernel, kinds, masks),
        out_shape=out_shape + [jax.ShapeDtypeStruct(array.shape, array.dtype) for array in carried] + shared_out,
        in_specs=[ANY, VMEM] + [ANY] * len(carried) + [VMEM] * 3,
        out_specs=[VMEM] * 2 + [ANY] * len(carried) + [VMEM] * 3,
        scratch_shapes=([DMA((len(masks), len(masks[0])))] * 2 if masks else []) + shared_scratch + scratch,
        compiler_params=pltpu.CompilerParams(
            collective_id=number, has_side_effects=True, vmem_limit_bytes=58 << 20
        ),
    )(part, dots, *carried, *shared_parts)


def finish_kernel(slices, kept, *refs):
    rest = iter(refs)

    def take(count):
        return [next(rest) for _ in range(count)]

    slices_in, landed, dots_landed, through = take(3 * slices), next(rest), next(rest), take(kept)
    grads, sums, dots, outs = take(3), take(4), next(rest), take(kept)
    for kind, grad in enumerate(grads):
        total = slices_in[kind][...].astype(f32)
        for k in range(1, slices):
            total = total + slices_in[k * 3 + kind][...].astype(f32)
        grad[...] = total

    @pl.when(pl.program_id(0) == 0)
    def _():
        for source, target in zip(through, outs):
            target[...] = source[...]
        expert_size, shard = landed.shape[0], sums[0].shape[0]
        whole, small = landed[0].astype(f32), dots_landed[0]
        for z in range(1, expert_size):
            whole = whole + landed[z].astype(f32)
            small = small + dots_landed[z]
        for i, out in enumerate(sums):
            out[...] = whole[i * shard : (i + 1) * shard]
        dots[...] = small


def finish(slices_in, landed, dots_landed, through, shard):
    width = landed.shape[-1]
    slices = len(slices_in) // 3
    own = slices_in[0].shape[0]

    def each(array):
        return pl.BlockSpec((1,) + array.shape[1:], lambda e: (e, 0, 0))

    def whole(array):
        return pl.BlockSpec(array.shape, lambda e: (0,) * len(array.shape))

    sums = [jax.ShapeDtypeStruct((shard, width), f32)] * 4 + [jax.ShapeDtypeStruct(dots_landed.shape[1:], f32)]
    kept = [jax.ShapeDtypeStruct(array.shape, array.dtype) for array in through]
    return pl.pallas_call(
        functools.partial(finish_kernel, slices, len(through)),
        grid=(own,),
        out_shape=[jax.ShapeDtypeStruct(array.shape, f32) for array in slices_in[:3]] + sums + kept,
        in_specs=[each(array) for array in slices_in]
        + [whole(array) for array in [landed, dots_landed] + list(through)],
        out_specs=[each(array) for array in slices_in[:3]] + [whole(array) for array in sums + kept],
        compiler_params=pltpu.CompilerParams(vmem_limit_bytes=62 << 20),
    )(*slices_in, landed, dots_landed, *through)


NT = (((1,), (1,)), ((), ()))
TN = (((0,), (0,)), ((), ()))


def contract(a, b, dims=(((1,), (0,)), ((), ()))):
    return lax.dot_general(a, b, dims, preferred_element_type=f32)


EXACT = lax.Precision.HIGHEST


def expert_of_place(count, stride, own):
    expert = lax.broadcasted_iota(jnp.int32, (EXPERTS, count), 0)
    column = lax.broadcasted_iota(jnp.int32, (EXPERTS, count), 1)
    place = column - ((expert // own) * stride + (expert % own) * PLACES)
    inside = (place >= 0) & (place < PLACES)
    at = jnp.sum(jnp.where(inside, place, 0), axis=0, keepdims=True)
    return inside.astype(f32), at.astype(f32)


def spots(hits, earlier, count, stride, own):
    expert_at, place_at = expert_of_place(count, stride, own)
    low = expert_at.astype(bf16)
    hit = contract(hits.astype(bf16), low)
    before = contract(earlier.astype(bf16), low)
    return jnp.where((hit > 0.5) & (before == place_at), 1.0, 0.0)


def row_spots(hits, earlier, expert_size):
    own = EXPERTS // expert_size
    return spots(hits, earlier, EXPERTS * PLACES, own * PLACES, own)


def first_place(rows):
    return (lax.axis_index("ctx") * lax.axis_size("expert") + lax.axis_index("expert")) * rows


def live(length_ref, rows):
    return first_place(rows) + lax.broadcasted_iota(jnp.int32, (rows, 1), 0) < length_ref[0]


def route(routes, alive):
    rows = routes.shape[1]
    expert = lax.broadcasted_iota(jnp.int32, (EXPERTS, rows), 0)
    named = (routes[0:1] == expert) | (routes[1:2] == expert)
    hits = jnp.transpose(jnp.where(named, 1.0, 0.0)) * jnp.where(alive, 1.0, 0.0)
    token = lax.broadcasted_iota(jnp.int32, (rows, rows), 0)
    other = lax.broadcasted_iota(jnp.int32, (rows, rows), 1)
    earlier = contract(jnp.where(other < token, 1.0, 0.0).astype(bf16), hits.astype(bf16))
    return hits, earlier


def place_rows(hits, earlier, flat, placed_ref):
    spread_out = jnp.transpose(row_spots(hits, earlier, placed_ref.shape[0])).astype(bf16)
    placed_ref[...] = contract(spread_out, flat).astype(bf16).reshape(placed_ref.shape)


def project(normed, weights, cosine, sine, qkv_ref):
    heads = qkv_ref.shape[0]
    half = HEAD_DIM // 2
    for kind, weight in enumerate(weights):
        lin = jnp.transpose(contract(normed, weight[...]))
        for head in range(heads):
            mine = lin[head * HEAD_DIM : (head + 1) * HEAD_DIM]
            if kind < 2:
                first, second = mine[:half], mine[half:]
                mine = jnp.concatenate(
                    [first * cosine - second * sine, second * cosine + first * sine], axis=0
                )
            qkv_ref[head, kind * HEAD_DIM : (kind + 1) * HEAD_DIM, :] = mine.astype(bf16)


def router_gates(normed, router, hits):
    logits = contract(normed, router, NT)
    top = jnp.max(jnp.where(hits > 0.5, logits, masked_value), axis=1, keepdims=True)
    powers = jnp.where(hits > 0.5, jnp.exp(logits - top), 0.0)
    total = jnp.sum(powers, axis=1, keepdims=True)
    return powers / jnp.where(total > 0.0, total, 1.0)


def gate_tiles(gates, hits, earlier, scale_ref):
    expert_size = scale_ref.shape[0]
    own, lanes = EXPERTS // expert_size, expert_size * 128
    expert_at, _ = expert_of_place(lanes, 128, own)
    by_place = jnp.dot(gates, expert_at, preferred_element_type=f32, precision=EXACT)
    row = jnp.sum(spots(hits, earlier, lanes, 128, own) * by_place, axis=0, keepdims=True)
    for z in range(expert_size):
        scale_ref[z] = jnp.broadcast_to(row[:, z * 128 : (z + 1) * 128], (8, 128))


def gates_back(dots_ref, gates, hits, earlier):
    expert_size = dots_ref.shape[0]
    own, lanes = EXPERTS // expert_size, expert_size * 128
    expert_at, _ = expert_of_place(lanes, 128, own)
    row = jnp.concatenate([dots_ref[z, 0:1, :] for z in range(expert_size)], axis=1)
    at_place = jnp.where(spots(hits, earlier, lanes, 128, own) > 0.5, row, 0.0)
    d_gates = lax.dot_general(at_place, expert_at, NT, preferred_element_type=f32, precision=EXACT)
    mean = jnp.sum(gates * d_gates, axis=1, keepdims=True)
    return (gates * (d_gates - mean)).astype(bf16)


def collect(hits, earlier, back_ref, flat_ref):
    width = flat_ref.shape[1]
    spread_out = row_spots(hits, earlier, back_ref.shape[0]).astype(bf16)
    placed = back_ref[...].reshape(EXPERTS * PLACES, width)
    return contract(spread_out, placed) + flat_ref[...].astype(f32)


def weight_sums(shard, grads, sums_ref):
    plane_size, expert_size, count, width = sums_ref.shape
    for p in range(plane_size):
        for z in range(expert_size):
            first = (p * expert_size + z) * shard
            parts = [grad[first : first + shard] for grad in grads]
            if count > len(grads) * shard:
                parts.append(jnp.zeros((count - len(grads) * shard, width), f32))
            sums_ref[p, z] = jnp.concatenate(parts, axis=0).astype(bf16)


def branch(rows, d_out, gate_w, up_w, down_w):
    gate_lin, up_lin = contract(rows, gate_w), contract(rows, up_w)
    sigmoid = 1.0 / (1.0 + jnp.exp(-gate_lin))
    silu = gate_lin * sigmoid
    hidden = (silu * up_lin).astype(bf16)
    d_hidden = contract(d_out, down_w, NT)
    d_gate = (d_hidden * up_lin * (sigmoid + silu * (1.0 - sigmoid))).astype(bf16)
    d_up = (d_hidden * silu).astype(bf16)
    result = contract(hidden, down_w)
    d_rows = contract(d_gate, gate_w, NT) + contract(d_up, up_w, NT)
    d_lin = contract(rows, jnp.concatenate([d_gate, d_up], axis=1), TN)
    d_down = contract(hidden, d_out, TN)
    return result, d_rows, d_lin, d_down


def moe_kernel(spread_kinds, home_kinds, slices, length_ref, *refs):
    rest = iter(refs)

    def take(count):
        return [next(rest) for _ in range(count)]

    tokens, attended_in, gain, router, hits_ref, earlier_ref, cotangent = take(7)
    output_in = next(rest)
    up_rows_in, up_flat_in = take(2)
    weights_in, shared_in = take(3), take(3)
    hidden, attended_out, d_hidden_out, d_attended_out, d_attn_out, router_grad, gain_grad = take(7)
    result_out, shared_out = take(2)
    shared_grads_out = take(3)
    grads_out = take(3 * slices)
    placed, normed, gate, output_w, output_sem = take(5)
    back, flat, dots_out = take(3)
    in_rows, in_flat, gates = take(3)
    up_rows, up_flat = take(2)
    weights, shared_w = take(3), take(3)
    result, shared_result = take(2)
    d_rows, shared_d = up_rows, up_flat
    lin_out, down_out, rows_f32, up_f32, dot, gates_own = take(6)
    lin_sum, down_sum = take(2)
    shared_parts = take(3)
    load_sem, store_sem = take(2)
    spread = Spread(spread_kinds, True, [placed, normed, gate, in_rows, in_flat, gates] + take(10), True)
    home = Home(home_kinds, True, [d_rows, shared_d], dot, [back, flat], dots_out, list(rest), True)

    dp_size, ctx_size, expert_size = sizes_of()
    ctx, own_block = lax.axis_index("ctx"), spread.own
    groups, blocks, _, size, width = in_rows.shape
    plane_size, rows, _ = in_flat.shape
    part = weights[0].shape[-1]
    sources = blocks * expert_size
    bits = bits_of(ctx_size)

    def column(mask):
        return pl.ds(pl.multiple_of(spread.block(0, mask) * part, 128), part)

    def loads(g):
        masks = subsets([bit for bit in bits if bit != group_bit(g, ctx_size)])
        experts = pl.ds(g * GROUP, GROUP)
        copies = [(up_rows_in.at[g], up_rows.at[g])]
        for k, mask in enumerate(masks):
            copies += [
                (weights_in[0].at[experts, :, column(mask)], weights[0].at[g, k]),
                (weights_in[1].at[experts, :, column(mask)], weights[1].at[g, k]),
                (weights_in[2].at[experts, column(mask)], weights[2].at[g, k]),
            ]
        return [pltpu.make_async_copy(s, t, load_sem.at[g, i]) for i, (s, t) in enumerate(copies)]

    shared_loads = [
        pltpu.make_async_copy(s, t, load_sem.at[groups, i])
        for i, (s, t) in enumerate(
            [
                (shared_in[0].at[:, column(0)], shared_w[0]),
                (shared_in[1].at[:, column(0)], shared_w[1]),
                (shared_in[2].at[column(0)], shared_w[2]),
                (up_flat_in, up_flat),
            ]
        )
    ]
    (output_load,) = fetch([output_in], [output_w], output_sem)
    output_load.start()
    alive = live(length_ref, rows)
    hits, earlier = hits_ref[...], earlier_ref[...]

    def prepare():
        attended = jnp.transpose(attended_in[...].reshape(width, rows).astype(f32)).astype(bf16)
        attended_out[...] = attended
        output_load.wait()
        attn_out = contract(attended, output_w[...])
        into = tokens[...].astype(f32) + jnp.where(alive, attn_out, 0.0)
        hidden[...] = into
        normed[...] = (into * rms_scale(into) * gain[...][None]).astype(bf16)
        gates_own[...] = router_gates(normed[...], router[...], hits)
        place_rows(hits, earlier, normed[...], placed)
        gate_tiles(gates_own[...], hits, earlier, gate)

    greet(plane_partners(), prepare)
    spread.z_start()
    spread.first(spread.staying)
    spread.keep()
    dot[...] = jnp.zeros_like(dot)
    def arriving(g):
        return [piece for piece in spread.moving if piece.group == g]

    for one in shared_loads:
        one.start()
    spread.forward_all(spread.staying)
    for one in loads(0):
        one.start()
    spread.first(arriving(0))
    spread.gates_on()
    spread.paired(spread.staying)
    for one in spread.kept() + shared_loads:
        one.wait()

    def shared_part(first, count):
        here = pl.ds(first, count)
        shape = (count * rows, width)
        some = branch(
            in_flat[here].reshape(shape), up_flat[here].reshape(shape), shared_w[0][...], shared_w[1][...],
            shared_w[2][...],
        )
        shared_result[here] = some[0].reshape((count, rows, width)).astype(bf16)
        shared_d[here] = some[1].reshape((count, rows, width)).astype(bf16)
        if first == 0:
            lin_sum[...] = some[2]
            down_sum[...] = some[3]
        else:
            lin_sum[...] += some[2]
            down_sum[...] += some[3]

    chunk = 4
    flats = home.staying[-2:]
    flat_stores = [
        pltpu.make_async_copy(s, t, store_sem.at[groups, i])
        for i, (s, t) in enumerate(zip([shared_result] + shared_parts, [shared_out] + shared_grads_out))
    ]
    shared_part(0, chunk)
    spread.forward_all(arriving(0))
    for g in range(1, groups):
        spread.first(arriving(g))
        for one in loads(g):
            one.start()
    spread.gates_landed()
    spread.paired(arriving(0))

    def shared_rest():
        for first in range(chunk, plane_size, chunk):
            shared_part(first, chunk)
        home.start(flats)
        shard = shared_parts[0].shape[1] // plane_size
        for z in range(expert_size):
            firsts = [(p * expert_size + z) * shard for p in range(plane_size)]
            mine = jnp.concatenate([lin_sum[first : first + shard] for first in firsts]).astype(bf16)
            shared_parts[0][z] = mine[:, :part]
            shared_parts[1][z] = mine[:, part:]
        shared_parts[2][...] = down_sum[...].astype(bf16).reshape(shared_parts[2].shape)
        for one in flat_stores:
            one.start()

    def expert(g, i):
        bit = group_bit(g, ctx_size)
        lane = (g * GROUP + i) * PLACES
        owners = [spread.block(core, mask) for core in (0, 1) for mask in (0, bit)]
        scale = jnp.concatenate(
            [gates[owner, z, 0:1, lane : lane + PLACES] for owner in owners for z in range(expert_size)]
        )[:, :, None]
        by_source = (sources, PLACES, width)
        up = up_f32[i]
        d_out = (up.reshape(by_source) * scale).reshape(up.shape).astype(bf16)
        some, d_some, d_lin, d_down = branch(
            rows_f32[i].astype(bf16),
            d_out,
            jnp.concatenate([weights[0][g, k, i] for k in range(slices)], axis=1),
            jnp.concatenate([weights[1][g, k, i] for k in range(slices)], axis=1),
            jnp.concatenate([weights[2][g, k, i] for k in range(slices)], axis=0),
        )
        for k in range(slices):
            lin_out[g, 0, k, i] = d_lin[:, k * part : (k + 1) * part].astype(bf16)
            lin_out[g, 1, k, i] = d_lin[:, (slices + k) * part : (slices + k + 1) * part].astype(bf16)
            down_out[g, k, i] = d_down[k * part : (k + 1) * part, :].astype(bf16)
        sums = jnp.sum((some * up).reshape(by_source), axis=-1)
        up_f32[i] = (some.reshape(by_source) * scale).reshape(up.shape)
        rows_f32[i] = d_some
        for at, owner in enumerate(owners):
            for z in range(expert_size):
                line = sums[at * expert_size + z : at * expert_size + z + 1]
                pieces_of = [line]
                if lane:
                    pieces_of.insert(0, jnp.zeros((1, lane), f32))
                if lane + PLACES < 128:
                    pieces_of.append(jnp.zeros((1, 128 - lane - PLACES), f32))
                dot[owner, z, 0:1, :] += jnp.concatenate(pieces_of, axis=1)

    def unpack(g):
        def one(source, carry):
            there = pl.ds(pl.multiple_of(source * PLACES, 8), PLACES)
            at = g, source // expert_size, source % expert_size
            some, up = in_rows[at].astype(f32), up_rows[at].astype(f32)
            for i in range(GROUP):
                rows_f32[i, there] = some[i * PLACES : (i + 1) * PLACES]
                up_f32[i, there] = up[i * PLACES : (i + 1) * PLACES]
            return carry

        lax.fori_loop(0, sources, one, 0)

    def pack(g):
        def one(source, carry):
            there = pl.ds(pl.multiple_of(source * PLACES, 8), PLACES)
            at = g, source // expert_size, source % expert_size
            result[at] = jnp.concatenate([up_f32[i, there] for i in range(GROUP)]).astype(bf16)
            d_rows[at] = jnp.concatenate([rows_f32[i, there] for i in range(GROUP)]).astype(bf16)
            return carry

        lax.fori_loop(0, sources, one, 0)

    def stores_of(g):
        experts = pl.ds(g * GROUP, GROUP)
        copies = [(result.at[g], result_out.at[g])]
        for k in range(slices):
            copies += [
                (lin_out.at[g, 0, k], grads_out[k].at[experts]),
                (lin_out.at[g, 1, k], grads_out[slices + k].at[experts]),
                (down_out.at[g, k], grads_out[2 * slices + k].at[experts]),
            ]
        return [pltpu.make_async_copy(s, t, store_sem.at[g, i]) for i, (s, t) in enumerate(copies)]

    def of_group(g):
        return [piece for piece in home.moving + home.staying if piece.group == g]

    depth = len(bits)
    waiting = []

    def move_on(count):
        for stage_of in waiting[:count]:
            stage_of()
        del waiting[:count]

    for g in range(groups):
        for one in loads(g):
            one.wait()
        if g:
            spread.paired(arriving(g))
        unpack(g)
        for i in range(GROUP):
            expert(g, i)
            if g == 0 and i == 0:
                for later in range(1, groups):
                    spread.forward_all(arriving(later))
            if g < groups - 1 or i < GROUP - 1:
                move_on(-(-len(waiting) // (GROUP - i)))
        if g == groups - 1:
            home.dots_start()
        pack(g)
        home.start(of_group(g))
        if g < groups - 1:
            for one in stores_of(g):
                one.start()
        if g == 0:
            shared_rest()
        waiting += [functools.partial(home.pair, piece) for piece in of_group(g)]
        if g == 0:
            waiting += [functools.partial(home.pair, piece) for piece in flats]
        waiting += [functools.partial(home.step, piece, 0) for piece in of_group(g)]
        if g == 0:
            for place in range(depth):
                waiting += [functools.partial(home.step, piece, place) for piece in flats]
    move_on(len(waiting))
    for one in stores_of(groups - 1):
        one.start()
    home.dots_on()
    home.dots_landed()
    d_logits = gates_back(dots_out, gates_own[...], hits, earlier)
    router_grad[...] = contract(normed[...], d_logits, TN)
    home.done()

    d_normed = collect(hits, earlier, back, flat) + contract(d_logits, router[...])
    into = hidden[...]
    scale = rms_scale(into)
    normal = into * scale
    gain_grad[...] = jnp.sum(d_normed * normal, axis=0, keepdims=True)
    d_hidden = cotangent[...].astype(f32) + rms_back(normal, scale, gain[...][None], d_normed)
    d_hidden_out[...] = d_hidden
    d_attn = jnp.where(alive, d_hidden, 0.0).astype(bf16)
    d_attn_out[...] = d_attn
    d_attended = jnp.transpose(contract(d_attn, output_w[...], NT))
    d_attended_out[...] = d_attended.astype(bf16).reshape(d_attended_out.shape)

    spread.sent()
    for g in range(groups):
        for one in stores_of(g):
            one.wait()
    for one in flat_stores:
        one.wait()


def moe(length, tokens, attended, gain, router, routing, cotangent, output_weight, up_rows, up_flat, weights,
        shared_weights, sizes, number):
    dp_size, ctx_size, expert_size = sizes
    plane_size = dp_size * ctx_size
    rows, width = tokens.shape
    part = shared_weights[0].shape[1] // plane_size
    slices = max(ctx_size // 2, 1)
    own = EXPERTS // expert_size
    groups = own // GROUP
    sources = 4 * expert_size
    placed = jax.ShapeDtypeStruct((expert_size, groups, GROUP * PLACES, width), bf16)
    flat = jax.ShapeDtypeStruct((rows, width), bf16)
    hidden = jax.ShapeDtypeStruct((rows, width), f32)
    gate = jax.ShapeDtypeStruct((expert_size, 8, 128), f32)
    spread_kinds, landing, spread_scratch = spread_plan([placed, flat], gate, sizes)
    dots = (plane_size,) + gate.shape
    home_kinds, home_out, home_scratch = home_plan([up_rows.shape, up_flat.shape], sizes, dots)
    shared_given, _, _ = shared_plan(width, part, sizes)
    lin = jax.ShapeDtypeStruct((own, width, part), bf16)
    down = jax.ShapeDtypeStruct((own, part, width), bf16)
    columns = pltpu.VMEM((groups, slices, GROUP, width, part), bf16)

    def buffers(shapes):
        return [pltpu.VMEM(shape.shape, shape.dtype) for shape in shapes]

    out = pl.pallas_call(
        functools.partial(moe_kernel, spread_kinds, home_kinds, slices),
        out_shape=[
            hidden,
            flat,
            hidden,
            jax.ShapeDtypeStruct(attended.shape, bf16),
            flat,
            jax.ShapeDtypeStruct(router.shape[::-1], f32),
            jax.ShapeDtypeStruct((1, width), f32),
        ]
        + [jax.ShapeDtypeStruct(up_rows.shape, bf16), jax.ShapeDtypeStruct(up_flat.shape, bf16)]
        + [jax.ShapeDtypeStruct(shape, bf16) for shape in shared_given]
        + [lin] * (2 * slices)
        + [down] * slices,
        in_specs=[SMEM] + [VMEM] * 7 + [ANY] * 9,
        out_specs=[VMEM] * 7 + [ANY] * (5 + 3 * slices),
        scratch_shapes=buffers([placed, flat, gate])
        + [pltpu.VMEM(output_weight.shape, bf16), DMA((1,))]
        + buffers(home_out)
        + buffers(landing)
        + [pltpu.VMEM(up_rows.shape, bf16), pltpu.VMEM(up_flat.shape, bf16)]
        + [columns, columns, pltpu.VMEM((groups, slices, GROUP, part, width), bf16)]
        + [pltpu.VMEM((width, part), bf16)] * 2
        + [pltpu.VMEM((part, width), bf16)]
        + [pltpu.VMEM(up_rows.shape, bf16), pltpu.VMEM(up_flat.shape, bf16)]
        + [
            pltpu.VMEM((groups, 2, slices, GROUP, width, part), bf16),
            pltpu.VMEM((groups, slices, GROUP, part, width), bf16),
            pltpu.VMEM((GROUP, sources * PLACES, width), f32),
            pltpu.VMEM((GROUP, sources * PLACES, width), f32),
            pltpu.VMEM(dots, f32),
            pltpu.VMEM((rows, EXPERTS), f32),
            pltpu.VMEM((width, 2 * part), f32),
            pltpu.VMEM((part, width), f32),
        ]
        + [pltpu.VMEM(shape, bf16) for shape in shared_given]
        + [DMA((groups + 1, max(1 + 3 * slices, 4)))] * 2
        + spread_scratch
        + home_scratch,
        compiler_params=pltpu.CompilerParams(
            collective_id=number, has_side_effects=True, vmem_limit_bytes=63 << 20
        ),
    )(length, tokens, attended, gain, router, *routing, cotangent, output_weight, up_rows, up_flat, *weights,
      *shared_weights)
    grads = out[12 : 12 + 3 * slices]
    grads = [grads[kind * slices : (kind + 1) * slices] for kind in range(3)]
    return out[:7], out[9:12], out[7:9], grads


class Slot:
    def __init__(self, heads):
        _, self.ctx_size, self.expert_size = sizes_of()
        self.heads, self.count = heads, self.ctx_size * self.expert_size
        ctx, expert = lax.axis_index("ctx"), lax.axis_index("expert")
        self.me = ctx * self.expert_size + expert
        head = head_of(ctx, expert, heads, self.ctx_size, self.expert_size)
        self.holds = head < heads
        self.head = head % heads

    def device(self, place):
        return {"ctx": place // self.expert_size, "expert": place % self.expert_size}

    def partners(self):
        dp, ctx = lax.axis_index("dp"), lax.axis_index("ctx")
        dp_size = lax.axis_size("dp")
        return [self.device((self.me + i) % self.count) for i in range(1, self.count)] + [
            {"dp": (dp + d) % dp_size, "ctx": flip(ctx, c)} for d in range(1, dp_size) for c in range(self.ctx_size)
        ]

    def copy(self, source, target, send, recv, there):
        return pltpu.make_async_remote_copy(
            src_ref=source, dst_ref=target, send_sem=send, recv_sem=recv, device_id=there, device_id_type=MESH
        )

    def inward(self, blocks, landing, send, recv):
        for i in range(self.heads):
            head = (self.me + i) % self.heads
            row, column = head_place(head, self.heads, self.ctx_size, self.expert_size)
            one = self.copy(
                blocks.at[head], landing.at[self.me], send.at[head], recv.at[self.me],
                {"ctx": row, "expert": column},
            )
            yield jnp.logical_not(self.holds & (head == self.head)), one

    def inward_landed(self, landing, send, recv):
        for i in range(1, self.count):
            source = (self.me + self.count - i) % self.count
            here = landing.at[source]
            yield self.copy(here, here, send.at[0], recv.at[source], self.device(self.me))

    def outward(self, blocks, landing, send, recv, place):
        return self.copy(
            blocks.at[place], landing.at[self.head], send.at[place], recv.at[self.head], self.device(place)
        )

    def outward_landed(self, landing, send, recv):
        for head in range(self.heads):
            here = landing.at[head]
            one = self.copy(here, here, send.at[0], recv.at[head], self.device(self.me))
            yield jnp.logical_not(self.holds & (head == self.head)), one


def attend_kernel(
    step, heads, kinds, length_ref, routes_ref, cotangent_ref, tokens_ref, gain_ref, cosine_ref, sine_ref, *refs
):
    rest = iter(refs)

    def take(count):
        return [next(rest) for _ in range(count)]

    weights_in = take(3)
    qkv_ref, out_ref, total_ref, landed_ref, normed_ref, hits_ref, earlier_ref = take(7)
    side_outs = take(len(kinds))
    weights, blocks_ref, placed_ref, branch_ref = take(3), *take(3)
    key_ref, query_ref, value_ref, sent_ref = take(4)
    in_send, in_recv, out_send, out_recv, weight_sem = take(5)
    side = Spread(kinds, False, [placed_ref, branch_ref] + side_outs + list(rest))

    slot = Slot(heads)
    rows, width = tokens_ref.shape
    span = slot.count * rows
    loads = fetch(weights_in, weights, weight_sem)
    for one in loads:
        one.start()

    def prepare():
        alive = live(length_ref, rows)
        hits, earlier = route(routes_ref[...], alive)
        hits_ref[...] = hits
        earlier_ref[...] = earlier
        branch = jnp.where(alive, cotangent_ref[...].astype(f32), 0.0).astype(bf16)
        branch_ref[...] = branch
        place_rows(hits, earlier, branch, placed_ref)

    greet(slot.partners(), prepare)
    inputs = tokens_ref[...].astype(f32)
    normed_ref[...] = (inputs * rms_scale(inputs) * gain_ref[...][None]).astype(bf16)
    for one in loads:
        one.wait()
    here = pl.ds(pl.multiple_of(slot.me * rows, 128), rows)
    project(normed_ref[...], weights, cosine_ref[:, here], sine_ref[:, here], blocks_ref)
    for needed, one in slot.inward(blocks_ref, qkv_ref, in_send, in_recv):
        pl.when(needed)(one.start)
    side.first(side.staying)
    side.keep()
    side.z_start()
    side.forward_all(side.staying)

    @pl.when(slot.holds)
    def _():
        qkv_ref[slot.me] = blocks_ref[slot.head]
        for one in slot.inward_landed(qkv_ref, in_send, in_recv):
            one.wait_recv()
        key_ref[...] = live_keys(head_rows(qkv_ref, HEAD_DIM, HEAD_DIM), length_ref[0])
        query_ref[...] = scaled_queries(head_rows(qkv_ref, 0, HEAD_DIM))
        value_ref[...] = head_rows(qkv_ref, 2 * HEAD_DIM, HEAD_DIM)

    def query_block(q):
        here = pl.ds(q * step, step)
        query = query_ref[:, here]

        def absorb(k, state, masked):
            top, total, out = state
            there = pl.ds(k * step if masked else pl.multiple_of(k * step, step), step)
            scores = jnp.dot(key_ref[there, :], query, preferred_element_type=f32)
            if masked:
                scores = causal(scores)
            new_top = jnp.maximum(top, jnp.max(scores, axis=0, keepdims=True))
            shrink = jnp.exp(top - new_top)
            weights = jnp.exp(scores - new_top)
            total = total * shrink + jnp.sum(weights, axis=0, keepdims=True)
            out = out * shrink + jnp.dot(
                value_ref[:, there], weights.astype(bf16), preferred_element_type=f32
            )
            return new_top, total, out

        state = (
            jnp.full((1, step), masked_value, f32),
            jnp.zeros((1, step), f32),
            jnp.zeros((HEAD_DIM, step), f32),
        )
        state = absorb(q, state, True)
        if q:
            state = lax.fori_loop(0, q, lambda k, s: absorb(k, s, False), state)
        top, total, out = state
        out = out / total
        out_ref[:, here] = out
        total_ref[:, here] = top + jnp.log(total)
        for i in range(step // rows):
            place = q * (step // rows) + i
            sent_ref[place] = out[:, i * rows : (i + 1) * rows].astype(bf16)
            one = slot.outward(sent_ref, landed_ref, out_send, out_recv, place)
            pl.when(slot.me != place)(one.start)

    for q in range(span // step):
        pl.when(slot.holds)(functools.partial(query_block, q))
        if q == span // step - 2:
            side.first(side.moving)
    side.forward_all(side.moving)

    @pl.when(slot.holds)
    def _():
        landed_ref[slot.head] = sent_ref[slot.me]

    for needed, one in slot.outward_landed(landed_ref, out_send, out_recv):
        pl.when(needed)(one.wait_recv)
    side.paired(side.all)
    side.sent()
    for one in side.kept():
        one.wait()
    for needed, one in slot.inward(blocks_ref, qkv_ref, in_send, in_recv):
        pl.when(needed)(one.wait_send)
    for place in range(slot.count):
        one = slot.outward(sent_ref, landed_ref, out_send, out_recv, place)
        pl.when(slot.holds & (slot.me != place))(one.wait_send)


def attend(length, routes, cotangent, tokens, gain, tables, weights, sizes, number):
    rows, width = tokens.shape
    _, ctx_size, expert_size = sizes
    heads, count = width // HEAD_DIM, ctx_size * expert_size
    span = count * rows
    step = min(512, span)
    groups = EXPERTS // expert_size // GROUP
    placed = jax.ShapeDtypeStruct((expert_size, groups, GROUP * PLACES, width), bf16)
    flat = jax.ShapeDtypeStruct((rows, width), bf16)
    kinds, side_shapes, side_scratch = spread_plan([placed, flat], None, sizes)
    blocks = (heads, 3 * HEAD_DIM, rows)
    hits = jax.ShapeDtypeStruct((rows, EXPERTS), f32)
    out = pl.pallas_call(
        functools.partial(attend_kernel, step, heads, kinds),
        out_shape=[
            jax.ShapeDtypeStruct((count,) + blocks[1:], bf16),
            jax.ShapeDtypeStruct((HEAD_DIM, span), f32),
            jax.ShapeDtypeStruct((1, span), f32),
            jax.ShapeDtypeStruct((heads, HEAD_DIM, rows), bf16),
            flat,
            hits,
            hits,
        ]
        + side_shapes,
        in_specs=[SMEM] + [VMEM] * 6 + [ANY] * 3,
        out_specs=[VMEM] * 7 + [ANY] * len(side_shapes),
        scratch_shapes=[pltpu.VMEM(weights[0].shape, bf16)] * 3
        + [
            pltpu.VMEM(blocks, bf16),
            pltpu.VMEM(placed.shape, bf16),
            pltpu.VMEM(flat.shape, bf16),
            pltpu.VMEM((span, 2 * HEAD_DIM), bf16),
            pltpu.VMEM((2 * HEAD_DIM, span), bf16),
            pltpu.VMEM((HEAD_DIM, span), bf16),
            pltpu.VMEM((count, HEAD_DIM, rows), bf16),
        ]
        + [DMA((count,))] * 4
        + [DMA((3,))]
        + side_scratch,
        compiler_params=pltpu.CompilerParams(
            collective_id=number, has_side_effects=True, vmem_limit_bytes=56 << 20
        ),
    )(length, routes, cotangent, tokens, gain, *tables, *weights)
    return out[:4], out[4:7], out[7:]


def unrotate(grad_t, cosine, sine):
    half = HEAD_DIM // 2
    first, second = grad_t[:half], grad_t[half:]
    return jnp.concatenate(
        [first * cosine + second * sine, second * cosine - first * sine], axis=0
    )


def attend_back_kernel(
    step, heads, kinds, masks, shard, length_ref, gain_ref, hits_ref, earlier_ref, blocks_ref, *refs
):
    rest = iter(refs)

    def take(count):
        return [next(rest) for _ in range(count)]

    soon, later, side_ins, carried = take(5), take(9), take(len(kinds)), take(len(masks))
    output_ref, input_grad, gain_grad, sums_out = take(4)
    carried_out = take(len(masks))
    soon_here, later_here, landed_ref, sums_ref, side_outs = take(5), take(9), next(rest), next(rest), take(len(kinds))
    qkv_ref, out_ref, total_ref, cosine_ref, sine_ref = soon_here
    normed_ref, tokens_ref, d_hidden_ref, attended_ref, d_attn_ref, hidden_ref, *weights = later_here
    upstream_ref, key_ref, query_ref, value_ref, key_t_ref, key_sum, value_sum, delta_ref, up_ref, sent_ref = take(10)
    in_send, in_recv, out_send, out_recv, soon_sem, later_sem, sums_sem = take(7)
    carry = Carry(
        masks, by_group(carried, len(masks[0]) if masks else 0), carried_out, take(2) if masks else []
    )
    side = Home(kinds, False, side_ins, None, side_outs, None, list(rest))

    slot = Slot(heads)
    rows = blocks_ref.shape[2]
    span = slot.count * rows
    loads = fetch(soon, soon_here, soon_sem)
    late_loads = fetch(later, later_here, later_sem)

    @pl.when(slot.holds)
    def _():
        key_sum[...] = jnp.zeros_like(key_sum)
        value_sum[...] = jnp.zeros_like(value_sum)

    greet(slot.partners())
    for needed, one in slot.inward(blocks_ref, upstream_ref, in_send, in_recv):
        pl.when(needed)(one.start)
    for one in loads:
        one.start()
    side.start(side.all)
    for one in late_loads:
        one.start()
    carry.push(4)
    for one in loads:
        one.wait()

    @pl.when(slot.holds)
    def _():
        key_t = head_rows(qkv_ref, HEAD_DIM, HEAD_DIM)
        key_ref[...] = live_keys(key_t, length_ref[0])
        key_t_ref[...] = key_t
        query_ref[...] = scaled_queries(head_rows(qkv_ref, 0, HEAD_DIM))
        value_t = head_rows(qkv_ref, 2 * HEAD_DIM, HEAD_DIM)
        value_ref[...] = jnp.transpose(value_t.astype(f32)).astype(bf16)
        upstream_ref[slot.me] = blocks_ref[slot.head]

    for piece in side.moving:
        side.pair(piece)
    carry.push(4)

    @pl.when(slot.holds)
    def _():
        for one in slot.inward_landed(upstream_ref, in_send, in_recv):
            one.wait_recv()
        upstream = head_rows(upstream_ref, 0, HEAD_DIM)
        up_ref[...] = upstream
        delta_ref[...] = jnp.sum(upstream.astype(f32) * out_ref[...], axis=0, keepdims=True)

    def query_block(q):
        here = pl.ds(q * step, step)
        query, up = query_ref[:, here], up_ref[:, here]
        total, delta = total_ref[:, here], delta_ref[:, here]

        def meet(k, query_sum, masked):
            there = pl.ds(k * step if masked else pl.multiple_of(k * step, step), step)
            scores = jnp.dot(key_ref[there, :], query, preferred_element_type=f32)
            if masked:
                scores = causal(scores)
            probs = jnp.exp(scores - total)
            d_probs = jnp.dot(value_ref[there, :], up, preferred_element_type=f32)
            d_scores = (probs * (d_probs - delta)).astype(bf16)
            key_sum[:, there] += contract(query[:HEAD_DIM], d_scores, NT)
            value_sum[:, there] += contract(up, probs.astype(bf16), NT)
            return query_sum + contract(key_t_ref[:, there], d_scores)

        query_sum = meet(q, jnp.zeros((HEAD_DIM, step), f32), True)
        if q:
            query_sum = lax.fori_loop(0, q, lambda k, s: meet(k, s, False), query_sum)
        cosine, sine = cosine_ref[:, here], sine_ref[:, here]
        grad = jnp.concatenate(
            [
                unrotate(query_sum * score_scale, cosine, sine),
                unrotate(key_sum[:, here], cosine, sine),
                value_sum[:, here],
            ],
            axis=0,
        ).astype(bf16)
        for i in range(step // rows):
            place = q * (step // rows) + i
            sent_ref[place] = grad[:, i * rows : (i + 1) * rows]
            one = slot.outward(sent_ref, landed_ref, out_send, out_recv, place)
            pl.when(slot.me != place)(one.start)

    for piece in side.moving:
        side.step(piece, 0)
    for piece in side.staying:
        side.pair(piece)
    depth = len(bits_of(lax.axis_size("ctx")))
    stages = [
        [functools.partial(side.step, piece, place) for piece in side.staying if place < len(piece.order)]
        for place in range(depth)
    ]
    for q in reversed(range(span // step)):
        pl.when(slot.holds)(functools.partial(query_block, q))
        for one in stages.pop(0) if stages else []:
            one()
        carry.push(4)
    for some in stages:
        for one in some:
            one()
    carry.push(len(masks) * GROUP * carry.CHUNKS)

    @pl.when(slot.holds)
    def _():
        landed_ref[slot.head] = sent_ref[slot.me]

    for needed, one in slot.outward_landed(landed_ref, out_send, out_recv):
        pl.when(needed)(one.wait_recv)
    for one in late_loads:
        one.wait()

    width = tokens_ref.shape[1]
    lins = []
    d_normed = jnp.zeros((width, rows), f32)
    for kind in range(3):
        at = slice(kind * HEAD_DIM, (kind + 1) * HEAD_DIM)
        lin = jnp.concatenate([landed_ref[head, at, :] for head in range(heads)], axis=0)
        lins.append(lin)
        d_normed = d_normed + contract(weights[kind][...], lin)
    d_normed = jnp.transpose(d_normed)
    inputs = tokens_ref[...].astype(f32)
    scale = rms_scale(inputs)
    normal = inputs * scale
    gain_grad[...] = jnp.sum(d_normed * normal, axis=0, keepdims=True)
    d_inputs = d_hidden_ref[...] + rms_back(normal, scale, gain_ref[...][None], d_normed)
    input_grad[...] = d_inputs.astype(bf16)
    normed_t = jnp.transpose(normed_ref[...].astype(f32)).astype(bf16)
    attended_t = jnp.transpose(attended_ref[...].astype(f32)).astype(bf16)
    grads = [contract(normed_t, lin, NT) for lin in lins] + [contract(attended_t, d_attn_ref[...])]
    weight_sums(shard, grads, sums_ref)
    (sums_store,) = fetch([sums_ref], [sums_out], sums_sem)
    sums_store.start()

    side.done()
    mixed = collect(hits_ref[...], earlier_ref[...], *side_outs)
    alive = live(length_ref, rows)
    output_ref[...] = (hidden_ref[...] + jnp.where(alive, mixed, 0.0)).astype(bf16)
    carry.done()
    sums_store.wait()
    for needed, one in slot.inward(blocks_ref, upstream_ref, in_send, in_recv):
        pl.when(needed)(one.wait_send)
    for place in range(slot.count):
        one = slot.outward(sent_ref, landed_ref, out_send, out_recv, place)
        pl.when(slot.holds & (slot.me != place))(one.wait_send)


def attend_back(length, gain, routing, blocks, soon, mine, weights, parts, carried, masks, sizes, number):
    qkv, later = soon[0], [*mine, *weights]
    heads, _, rows = blocks.shape
    count = qkv.shape[0]
    span = count * rows
    step = min(512, span)
    dp_size, ctx_size, expert_size = sizes
    width = weights[0].shape[0]
    shard = width // (dp_size * count)
    kinds, side_shapes, side_scratch = home_plan([part.shape for part in parts], sizes)
    carry_shapes = [jax.ShapeDtypeStruct(array.shape, array.dtype) for array in carried]
    carry_sems = [DMA((len(masks), len(masks[0])))] * 2 if masks else []
    sums = (dp_size * ctx_size, expert_size, -(-4 * shard // 16) * 16, width)
    got = pl.pallas_call(
        functools.partial(attend_back_kernel, step, heads, kinds, masks, shard),
        out_shape=[
            jax.ShapeDtypeStruct((rows, width), bf16),
            jax.ShapeDtypeStruct((rows, width), bf16),
            jax.ShapeDtypeStruct((1, width), f32),
            jax.ShapeDtypeStruct(sums, bf16),
        ]
        + carry_shapes,
        in_specs=[SMEM] + [VMEM] * 4 + [ANY] * (14 + len(parts) + len(carried)),
        out_specs=[VMEM] * 3 + [ANY] * (1 + len(carried)),
        scratch_shapes=[pltpu.VMEM(array.shape, array.dtype) for array in soon + later]
        + [pltpu.VMEM((heads,) + qkv.shape[1:], bf16), pltpu.VMEM(sums, bf16)]
        + [pltpu.VMEM(shape.shape, shape.dtype) for shape in side_shapes]
        + [
            pltpu.VMEM((count,) + blocks.shape[1:], bf16),
            pltpu.VMEM((span, 2 * HEAD_DIM), bf16),
            pltpu.VMEM((2 * HEAD_DIM, span), bf16),
            pltpu.VMEM((span, HEAD_DIM), bf16),
            pltpu.VMEM((HEAD_DIM, span), bf16),
            pltpu.VMEM((HEAD_DIM, span), f32),
            pltpu.VMEM((HEAD_DIM, span), f32),
            pltpu.VMEM((1, span), f32),
            pltpu.VMEM((HEAD_DIM, span), bf16),
            pltpu.VMEM(qkv.shape, bf16),
        ]
        + [DMA((count,))] * 4
        + [DMA((5,)), DMA((9,)), DMA((1,))]
        + carry_sems
        + side_scratch,
        compiler_params=pltpu.CompilerParams(
            collective_id=number, has_side_effects=True, vmem_limit_bytes=60 << 20
        ),
    )(length, gain, *routing, blocks, *soon, *later, *parts, *carried)
    return got[:4], got[4:]


def local(
    tokens,
    lengths,
    routes,
    norm1_gain,
    query_weight,
    key_weight,
    value_weight,
    output_weight,
    norm2_gain,
    router_weight,
    expert_gate,
    expert_up,
    expert_down,
    shared_gate,
    shared_up,
    shared_down,
    cotangent,
):
    sizes = dp_size, ctx_size, expert_size = sizes_of()
    plane_size, slot_size = dp_size * ctx_size, ctx_size * expert_size
    rows, width = tokens.shape[1:]
    shard = width // (dp_size * slot_size)
    tokens, routes, cotangent = tokens[0], routes[0], cotangent[0]
    weights = (query_weight, key_weight, value_weight)
    tables = rope_tables(jnp.arange(slot_size * rows, dtype=jnp.int32))

    (qkv, out_t, log_total, attended), (normed, *routing), (up_rows, up_flat) = attend(
        lengths, routes.T, cotangent, tokens, norm1_gain, tables, weights, sizes, 1
    )

    bits = bits_of(ctx_size)
    groups = EXPERTS // expert_size // GROUP
    slice_masks = [
        subsets([bit for bit in bits if bit != group_bit(g, ctx_size)]) for g in range(groups)
    ]
    slices = len(slice_masks[0])
    ways = tuple(tuple(masks[k] for masks in slice_masks) for _ in range(3) for k in range(1, slices))
    early = slices - 1

    mine, shared_parts, results, grads = moe(
        lengths, tokens, attended, norm2_gain, router_weight.T, routing, cotangent, output_weight, up_rows, up_flat,
        (expert_gate, expert_up, expert_down), (shared_gate, shared_up, shared_down), sizes, 2,
    )
    hidden, attended, d_hidden, d_attended, d_attn, router_grad, gain_two_grad = mine
    others = [array for kind in grads for array in kind[1:]]
    (output_rows, input_grad, gain_one_grad, sums), early_in = attend_back(
        lengths, norm1_gain, routing, d_attended, [qkv, out_t, log_total, *tables],
        (normed, tokens, d_hidden, attended, d_attn, hidden),
        weights, results, others[: 2 * early], ways[: 2 * early], sizes, 3,
    )

    devices = (plane_size, expert_size)
    pad = [(0, 0), (0, 0), (0, 0), (0, 128 - shard)]
    routed = -(-shard * EXPERTS // 128)
    small = jnp.concatenate(
        [
            jnp.pad(
                router_grad.reshape(devices + (shard * EXPERTS,)),
                [(0, 0), (0, 0), (0, routed * 128 - shard * EXPERTS)],
            ).reshape(devices + (routed, 128)),
            jnp.pad(gain_one_grad.reshape(devices + (1, shard)), pad),
            jnp.pad(gain_two_grad.reshape(devices + (1, shard)), pad),
            jnp.zeros(devices + (6 - routed, 128), f32),
        ],
        axis=2,
    )
    landed, small, *last_in = bring_sums(
        sums, small, shared_parts, others[2 * early :], ways[2 * early :], sizes, 4
    )
    arrived = [*early_in, *last_in[:early]]
    shared_grads = last_in[early:]
    by_slice = [kind[0] for kind in grads]
    for k in range(early):
        by_slice += [arrived[kind * early + k] for kind in range(3)]
    *out, small, output_rows, input_grad, shared_gate_grad, shared_up_grad, shared_down_grad = finish(
        by_slice, landed, small, [output_rows, input_grad, *shared_grads], shard
    )
    return (
        output_rows[None],
        input_grad[None],
        small[routed, :shard],
        *out[3:7],
        small[routed + 1, :shard],
        small[:routed].reshape(-1)[: shard * EXPERTS].reshape(shard, EXPERTS),
        *out[:3],
        shared_gate_grad,
        shared_up_grad,
        shared_down_grad,
    )


def solution(mesh):
    tokens = P("dp", ("ctx", "expert"), None)
    whole = P()
    experts = P("expert", None, None)
    everywhere = ("dp", "ctx", "expert")
    return jax.shard_map(
        local,
        mesh=mesh,
        in_specs=(tokens, P("dp"), tokens)
        + (whole,) * 7
        + (experts,) * 3
        + (whole,) * 3
        + (tokens,),
        out_specs=(tokens, tokens, P(everywhere))
        + (P(everywhere, None),) * 4
        + (P(everywhere), P(everywhere, None))
        + (P("expert", None, PLANE),) * 2
        + (P("expert", PLANE, None),)
        + (P(everywhere, None),) * 3,
        check_vma=False,
    )
```

```python
import functools

import jax
import jax.numpy as jnp
from jax import lax
from jax.experimental import pallas as pl
from jax.experimental.pallas import tpu as pltpu
from jax.sharding import PartitionSpec as P

HEAD_DIM = 64
EXPERTS = 16
TOP = 2
CAP = 22
PLACES = 24

norm_epsilon = 1e-06
rope_base = 10000.0
score_scale = 0.125
masked_value = -1e30
PLANE = ("dp", "ctx")
SLOT = ("ctx", "expert")
bf16 = jnp.bfloat16
f32 = jnp.float32


def rms_scale(values):
    return lax.rsqrt(jnp.mean(values * values, axis=-1, keepdims=True) + norm_epsilon)


def rms_back(normal, scale, gain, upstream):
    lifted = upstream * gain
    return scale * (lifted - normal * jnp.mean(lifted * normal, axis=-1, keepdims=True))


def rope_tables(positions):
    half = HEAD_DIM // 2
    exponent = jnp.arange(half, dtype=f32) * (2.0 / HEAD_DIM)
    inverse_freq = rope_base ** (-exponent)
    angles = inverse_freq[:, None] * positions[None, :].astype(f32)
    return jnp.cos(angles), jnp.sin(angles)


def head_rows(qkv_ref, first, count):
    return jnp.concatenate(
        [qkv_ref[block, first : first + count, :] for block in range(qkv_ref.shape[0])], axis=1
    )


def live_keys(key_t, length):
    span = key_t.shape[1]
    place = lax.broadcasted_iota(jnp.int32, (8, span), 1)
    row = lax.broadcasted_iota(jnp.int32, (8, span), 0)
    bias = jnp.where((place >= length) & (row == 0), masked_value, 0.0)
    padded = jnp.concatenate(
        [key_t.astype(f32), bias, jnp.zeros((HEAD_DIM - 8, span), f32)], axis=0
    )
    return jnp.transpose(padded).astype(bf16)


def scaled_queries(query_t):
    span = query_t.shape[1]
    row = lax.broadcasted_iota(jnp.int32, (HEAD_DIM, span), 0)
    ones = jnp.where(row == 0, 1.0, 0.0)
    return jnp.concatenate([query_t.astype(f32) * score_scale, ones], axis=0).astype(bf16)


def causal(scores):
    key = lax.broadcasted_iota(jnp.int32, scores.shape, 0)
    query = lax.broadcasted_iota(jnp.int32, scores.shape, 1)
    return jnp.where(key <= query, scores, masked_value)


MESH = pl.DeviceIdType.MESH
ANY = pl.BlockSpec(memory_space=pl.ANY)
VMEM = pl.BlockSpec(memory_space=pltpu.VMEM)
SMEM = pl.BlockSpec(memory_space=pltpu.SMEM)
DMA = pltpu.SemaphoreType.DMA


def head_place(head, heads, ctx_size, expert_size):
    per = expert_size - 1
    if ctx_size <= expert_size and ctx_size * per == heads:
        row = head // per
        step = head % per
        return row, step + jnp.where(step >= row, 1, 0)
    return head // expert_size, head % expert_size


def head_of(ctx, expert, heads, ctx_size, expert_size):
    per = expert_size - 1
    if ctx_size <= expert_size and ctx_size * per == heads:
        head = ctx * per + expert - jnp.where(expert > ctx, 1, 0)
        return jnp.where(expert == ctx, heads, head)
    return ctx * expert_size + expert


def sizes_of():
    return tuple(lax.axis_size(a) for a in ("dp", "ctx", "expert"))


def greet(partners, meanwhile=lambda: None):
    barrier = pltpu.get_barrier_semaphore()
    for partner in partners:
        pl.semaphore_signal(barrier, inc=1, device_id=partner, device_id_type=MESH)
    meanwhile()
    pl.semaphore_wait(barrier, len(partners))


def fetch(sources, targets, sems):
    return [
        pltpu.make_async_copy(source, target, sems.at[i]) for i, (source, target) in enumerate(zip(sources, targets))
    ]


GROUP = 2


def flip(index, mask):
    bit = 1
    while bit <= mask:
        if mask & bit:
            index = index + bit * (1 - 2 * ((index // bit) % 2))
        bit *= 2
    return index


def bits_of(ctx_size):
    return [1 << b for b in range(ctx_size.bit_length() - 1)]


def group_bit(group, ctx_size):
    bits = bits_of(ctx_size)
    return bits[group % len(bits)]


def subsets(order):
    masks = [0]
    for bit in order:
        masks = masks + [m | bit for m in masks]
    return masks


class Piece:
    def __init__(self, array, kind, group, step, first, size, order):
        self.array, self.kind, self.group, self.step = array, kind, group, step
        self.first, self.size, self.order = first, size, order
        self.masks = subsets(order)


def pieces(kinds, expert_size, ctx_size):
    bits = bits_of(ctx_size)
    moving, staying = [], []
    for array, (kind, groups, rows) in enumerate(kinds):
        if kind == "flat":
            half = rows // 2
            staying.append(Piece(array, kind, None, None, 0, half, bits))
            staying.append(Piece(array, kind, None, None, half, rows - half, bits[::-1]))
            continue
        for group in range(groups or 1):
            for step in range(expert_size):
                if kind == "group":
                    order = [group_bit(group, ctx_size)]
                else:
                    order = bits if (step + array) % 2 == 0 else bits[::-1]
                (moving if step else staying).append(Piece(array, kind, group, step, 0, rows, order))
    return moving, staying


class Spread:
    def __init__(self, kinds, has_gate, refs, near=False):
        self.near = near
        rest = iter(refs)

        def take(count):
            return [next(rest) for _ in range(count)]

        self.has_gate = has_gate
        self.ins = take(len(kinds))
        self.gate = next(rest) if has_gate else None
        self.outs = take(len(kinds))
        self.gates = next(rest) if has_gate else None
        self.z_send, self.z_recv, self.send, self.recv, self.pair_recv, self.local_sem = take(6)
        if has_gate:
            self.gate_send, self.gate_recv, self.gate_z_send, self.gate_z_recv = take(4)
        self.dp_size, self.ctx_size, self.expert_size = sizes_of()
        self.dp, self.ctx, self.expert = (lax.axis_index(a) for a in ("dp", "ctx", "expert"))
        self.moving, self.staying = pieces(kinds, self.expert_size, self.ctx_size)
        self.all = self.staying + self.moving
        self.number = {id(piece): i for i, piece in enumerate(self.all)}
        self.own = self.dp * self.ctx_size + self.ctx
        self.other = (self.dp + 1) % self.dp_size
        self.bits = bits_of(self.ctx_size)
        self.started = []
        self.plane = [(d, c) for d in range(self.dp_size) for c in range(self.ctx_size) if (d, c) != (0, 0)]

    def z_at(self, step):
        return (self.expert + step) % self.expert_size

    def z_from(self, step):
        return (self.expert + self.expert_size - step) % self.expert_size

    def block(self, core, mask):
        return (self.dp if core == 0 else self.other) * self.ctx_size + flip(self.ctx, mask)

    def landed(self, piece, core, mask, at=0):
        out = self.outs[piece.array]
        if piece.step is None:
            return out.at[self.block(core, mask), pl.ds(piece.first, piece.size)]
        return out.at[piece.group, core * 2 + (1 if mask ^ at else 0), self.z_from(piece.step)]

    def source(self, piece):
        if piece.step is None:
            return self.ins[piece.array].at[pl.ds(piece.first, piece.size)]
        if piece.step == 0:
            return self.ins[piece.array].at[self.expert, piece.group]
        return self.landed(piece, 0, 0)

    def remote(self, source, target, send, recv, there):
        return pltpu.make_async_remote_copy(
            src_ref=source, dst_ref=target, send_sem=send, recv_sem=recv, device_id=there, device_id_type=MESH
        )

    def z_copy(self, piece, landing=False):
        place = self.z_from(piece.step) if landing else self.expert
        at = self.number[id(piece)]
        return self.remote(
            self.ins[piece.array].at[self.z_at(piece.step), piece.group],
            self.outs[piece.array].at[piece.group, 0, place],
            self.z_send.at[at],
            self.z_recv.at[at],
            {"expert": self.z_at(piece.step)},
        )

    def gate_z(self, step, landing=False):
        return self.remote(
            self.gate.at[self.z_at(step)],
            self.gates.at[self.own, self.z_from(step) if landing else self.expert],
            self.gate_z_send.at[step],
            self.gate_z_recv.at[step],
            {"expert": self.z_at(step)},
        )

    def gate_plane(self, d, c, block):
        return self.remote(
            self.gates.at[block],
            self.gates.at[block],
            self.gate_send.at[d, c],
            self.gate_recv.at[d, c],
            {"dp": (self.dp + d) % self.dp_size, "ctx": flip(self.ctx, c)},
        )

    def passing(self, piece, mask, bit):
        at = self.number[id(piece)]
        return self.remote(
            self.landed(piece, 0, mask) if mask else self.source(piece),
            self.landed(piece, 0, mask, bit),
            self.send.at[at, mask, self.bits.index(bit)],
            self.recv.at[at, mask ^ bit],
            {"ctx": flip(self.ctx, bit)},
        )

    def arrived(self, piece, mask):
        here = self.landed(piece, 0, mask)
        recv = self.recv.at[self.number[id(piece)], mask]
        return self.remote(here, here, self.send.at[0, 0, 0], recv, {"ctx": self.ctx})

    def crossing(self, piece, mask, landing=False):
        at = self.number[id(piece)]
        core = 0 if piece.step is None and not landing else 1
        return self.remote(
            self.landed(piece, 0, mask) if mask else self.source(piece),
            self.landed(piece, core, mask),
            self.send.at[at, mask, len(self.bits)],
            self.pair_recv.at[at, mask],
            {"dp": self.other},
        )

    def kept(self):
        if self.near:
            return []
        return [
            pltpu.make_async_copy(self.source(piece), self.landed(piece, 0, 0), self.local_sem.at[i])
            for i, piece in enumerate(self.staying)
        ]

    def begin(self, one):
        one.start()
        self.started.append(one)

    def z_start(self):
        if self.has_gate:
            for step in range(1, self.expert_size):
                self.gate_z(step).start()
        for piece in self.moving:
            self.z_copy(piece).start()

    def first(self, some):
        for piece in some:
            if piece.step:
                self.z_copy(piece, True).wait_recv()
            for bit in piece.order:
                self.begin(self.passing(piece, 0, bit))
            self.begin(self.crossing(piece, 0))

    def keep(self):
        for one in self.kept():
            one.start()
        if self.near:
            for piece in self.staying:
                target = self.landed(piece, 0, 0)
                target[...] = self.source(piece)[...]
        if self.has_gate:
            self.gates[self.own, self.expert] = self.gate[self.expert]

    def forward(self, piece, place):
        if place >= len(piece.order):
            return
        bit = piece.order[place]
        for mask in [m | bit for m in subsets(piece.order[:place])]:
            self.arrived(piece, mask).wait_recv()
            for later in piece.order[place + 1 :]:
                self.begin(self.passing(piece, mask, later))
            self.begin(self.crossing(piece, mask))

    def forward_all(self, some):
        for place in range(len(self.bits)):
            for piece in some:
                self.forward(piece, place)

    def gates_on(self):
        for step in range(1, self.expert_size):
            self.gate_z(step, True).wait_recv()
        for d, c in self.plane:
            self.gate_plane(d, c, self.own).start()

    def gates_landed(self):
        for d, c in self.plane:
            block = ((self.dp + d) % self.dp_size) * self.ctx_size + flip(self.ctx, c)
            self.gate_plane(d, c, block).wait_recv()

    def paired(self, some):
        for piece in some:
            for mask in piece.masks:
                self.crossing(piece, mask, True).wait_recv()

    def sent(self):
        for one in self.started:
            one.wait_send()
        for piece in self.moving:
            self.z_copy(piece).wait_send()
        if self.has_gate:
            for step in range(1, self.expert_size):
                self.gate_z(step).wait_send()
            for d, c in self.plane:
                self.gate_plane(d, c, self.own).wait_send()


def plane_partners():
    dp_size, ctx_size, expert_size = sizes_of()
    dp, ctx, expert = (lax.axis_index(a) for a in ("dp", "ctx", "expert"))
    plane = [(d, c) for d in range(dp_size) for c in range(ctx_size) if (d, c) != (0, 0)]
    return [{"expert": (expert + step) % expert_size} for step in range(1, expert_size)] + [
        {"dp": (dp + d) % dp_size, "ctx": flip(ctx, c)} for d, c in plane
    ]


def spread_plan(arrays, gate, sizes):
    dp_size, ctx_size, expert_size = sizes
    assert dp_size == 2
    plane_size = dp_size * ctx_size
    kinds, out_shape = [], []
    for array in arrays:
        if array.ndim == 4:
            kinds.append(("group", array.shape[1], array.shape[2]))
            shape = (array.shape[1], 4, expert_size) + array.shape[2:]
        else:
            kinds.append(("flat", None, array.shape[0]))
            shape = (plane_size,) + array.shape
        out_shape.append(jax.ShapeDtypeStruct(shape, array.dtype))
    moving, staying = pieces(kinds, expert_size, ctx_size)
    count = len(moving + staying)
    scratch = [
        DMA((count,)),
        DMA((count,)),
        DMA((count, ctx_size, len(bits_of(ctx_size)) + 1)),
        DMA((count, ctx_size)),
        DMA((count, ctx_size)),
        DMA((len(staying),)),
    ]
    if gate is not None:
        out_shape.append(jax.ShapeDtypeStruct((plane_size,) + gate.shape, gate.dtype))
        scratch += [DMA((dp_size, ctx_size))] * 2 + [DMA((expert_size,))] * 2
    return tuple(kinds), out_shape, scratch


def stage(piece, place):
    order = piece.order[::-1]
    done, bit = sum(order[:place]), order[place]
    kept = [m for m in piece.masks if not m & (done | bit)]
    return bit, [(m | bit, m) for m in kept]


def buffer_places(order):
    held, arriving, here, there = {}, {}, 0, 0
    for piece in order:
        for mask in piece.masks:
            held[id(piece), mask] = here
            here += piece.size
        for place in range(len(piece.order)):
            for index in range(len(stage(piece, place)[1])):
                arriving[id(piece), place, index] = there
                there += piece.size
    held["rows"], arriving["rows"] = here, there
    return held, arriving


class Home:
    def __init__(self, kinds, has_dots, parts, dot, outs, dots_out, scratch, near=False):
        self.near = near
        rest = iter(scratch)

        def take(count):
            return [next(rest) for _ in range(count)]

        self.parts, self.dot, self.outs, self.dots_out, self.has_dots = parts, dot, outs, dots_out, has_dots
        self.mine, self.theirs, self.arrivals = take(3)
        self.mine_sem, self.pair_send, self.pair_recv, self.send, self.recv, self.z_send, self.z_recv = take(7)
        if has_dots:
            self.dot_in, self.dot_sum, self.dot_send, self.dot_recv, self.dot_z_send, self.dot_z_recv = take(6)
        self.dp_size, self.ctx_size, self.expert_size = sizes_of()
        self.dp, self.ctx, self.expert = (lax.axis_index(a) for a in ("dp", "ctx", "expert"))
        self.moving, self.staying = pieces(kinds, self.expert_size, self.ctx_size)
        self.all = self.moving + self.staying
        self.number = {id(piece): i for i, piece in enumerate(self.all)}
        self.held, self.arriving = buffer_places(self.all)
        self.own = self.dp * self.ctx_size + self.ctx
        self.other = (self.dp + 1) % self.dp_size
        self.plane = [(d, c) for d in range(self.dp_size) for c in range(self.ctx_size) if (d, c) != (0, 0)]

    def z_at(self, step):
        return (self.expert + step) % self.expert_size

    def z_from(self, step):
        return (self.expert + self.expert_size - step) % self.expert_size

    def plane_at(self, d, c):
        return ((self.dp + d) % self.dp_size) * self.ctx_size + flip(self.ctx, c)

    def partner(self, d, c):
        return {"dp": (self.dp + d) % self.dp_size, "ctx": flip(self.ctx, c)}

    def remote(self, source, target, send, recv, there):
        return pltpu.make_async_remote_copy(
            src_ref=source, dst_ref=target, send_sem=send, recv_sem=recv, device_id=there, device_id_type=MESH
        )

    def whole(self, piece, core, mask):
        part = self.parts[piece.array]
        if piece.kind == "group":
            return part.at[piece.group, core * 2 + (1 if mask else 0), self.z_at(piece.step)]
        block = (self.dp if core == 0 else self.other) * self.ctx_size + flip(self.ctx, mask)
        if piece.kind == "flat":
            return part.at[block, pl.ds(piece.first, piece.size)]
        return part.at[block, self.z_at(piece.step)]

    def at(self, piece, mask):
        return pl.ds(self.held[id(piece), mask], piece.size)

    def load(self, piece, mask):
        return pltpu.make_async_copy(
            self.whole(piece, 0, mask), self.mine.at[self.at(piece, mask)], self.mine_sem.at[self.number[id(piece)], mask]
        )

    def cross(self, piece, mask):
        number = self.number[id(piece)]
        return self.remote(
            self.whole(piece, 1, mask),
            self.theirs.at[self.at(piece, mask)],
            self.pair_send.at[number, mask],
            self.pair_recv.at[number, mask],
            {"dp": self.other},
        )

    def hop(self, piece, place, index):
        bit, moves = stage(piece, place)
        number = self.number[id(piece)]
        return self.remote(
            self.mine.at[self.at(piece, moves[index][0])],
            self.arrivals.at[pl.ds(self.arriving[id(piece), place, index], piece.size)],
            self.send.at[number, moves[index][0]],
            self.recv.at[number, place, index],
            {"ctx": flip(self.ctx, bit)},
        )

    def z_copy(self, piece, landing=False):
        place = self.z_from(piece.step) if landing else self.expert
        out, number = self.outs[piece.array], self.number[id(piece)]
        return self.remote(
            self.mine.at[self.at(piece, 0)],
            out.at[place, piece.group] if piece.kind == "group" else out.at[place],
            self.z_send.at[number],
            self.z_recv.at[number],
            {"expert": self.z_at(piece.step)},
        )

    def start(self, some):
        for piece in some:
            for mask in piece.masks:
                self.cross(piece, mask).start()
                if not self.near:
                    self.load(piece, mask).start()

    def add(self, here, buffer, there):
        total = self.mine[here].astype(f32) + buffer[there].astype(f32)
        self.mine[here] = total.astype(self.mine.dtype)

    def pair(self, piece):
        leaving = [source for source, _ in stage(piece, 0)[1]]
        for mask in leaving + [m for m in piece.masks if m not in leaving]:
            here = self.at(piece, mask)
            if not self.near:
                self.load(piece, mask).wait()
            self.cross(piece, mask).wait_recv()
            if self.near:
                total = self.whole(piece, 0, mask)[...].astype(f32) + self.theirs[here].astype(f32)
                self.mine[here] = total.astype(self.mine.dtype)
            else:
                self.add(here, self.theirs, here)
            if mask in leaving:
                self.hop(piece, 0, leaving.index(mask)).start()

    def step(self, piece, place):
        targets = [target for _, target in stage(piece, place)[1]]
        leaving = []
        if place + 1 < len(piece.order):
            leaving = [source for source, _ in stage(piece, place + 1)[1]]
        for index in range(len(targets)):
            self.hop(piece, place, index).wait_recv()
        for mask in leaving + [m for m in targets if m not in leaving]:
            there = pl.ds(self.arriving[id(piece), place, targets.index(mask)], piece.size)
            self.add(self.at(piece, mask), self.arrivals, there)
            if mask in leaving:
                self.hop(piece, place + 1, leaving.index(mask)).start()
        if place + 1 == len(piece.order):
            self.finish(piece)

    def finish(self, piece):
        result, out = self.mine.at[self.at(piece, 0)], self.outs[piece.array]
        if piece.kind == "flat":
            out[pl.ds(piece.first, piece.size)] = result[...]
        elif piece.step:
            self.z_copy(piece).start()
        elif piece.kind == "group":
            out[self.expert, piece.group] = result[...]
        else:
            out[self.expert] = result[...]

    def ticks(self, some, ahead):
        depth = max(len(piece.order) for piece in some)
        for tick in range(len(some) + ahead + depth):
            for place in range(depth + 1):
                index = tick if place == 0 else tick - ahead - place + 1
                if not 0 <= index < len(some) or place > len(some[index].order):
                    continue
                if place == 0:
                    self.pair(some[index])
                else:
                    self.step(some[index], place - 1)
            yield

    def dot_plane(self, d, c):
        return self.remote(
            self.dot.at[self.plane_at(d, c)],
            self.dot_in.at[d, c],
            self.dot_send.at[d, c],
            self.dot_recv.at[d, c],
            self.partner(d, c),
        )

    def dot_z(self, step, landing=False):
        return self.remote(
            self.dot_sum.at[self.z_at(step)],
            self.dots_out.at[self.z_from(step) if landing else self.expert],
            self.dot_z_send.at[step],
            self.dot_z_recv.at[step],
            {"expert": self.z_at(step)},
        )

    def dots_start(self):
        for d, c in self.plane:
            self.dot_plane(d, c).start()

    def dots_on(self):
        total = self.dot[self.own]
        for d, c in self.plane:
            self.dot_plane(d, c).wait_recv()
            total = total + self.dot_in[d, c]
        self.dot_sum[...] = total
        for step in range(1, self.expert_size):
            self.dot_z(step).start()
        self.dots_out[self.expert] = self.dot_sum[self.expert]

    def dots_landed(self):
        for step in range(1, self.expert_size):
            self.dot_z(step, True).wait_recv()

    def done(self):
        for piece in self.moving:
            self.z_copy(piece, True).wait_recv()
        if self.has_dots:
            for step in range(1, self.expert_size):
                self.dot_z(step).wait_send()
            for d, c in self.plane:
                self.dot_plane(d, c).wait_send()
        for piece in self.moving:
            self.z_copy(piece).wait_send()
        for piece in self.all:
            for mask in piece.masks:
                self.cross(piece, mask).wait_send()
            for place in range(len(piece.order)):
                for index in range(len(stage(piece, place)[1])):
                    self.hop(piece, place, index).wait_send()


def home_plan(shapes, sizes, dots=None):
    dp_size, ctx_size, expert_size = sizes
    assert dp_size == 2
    width = shapes[0][-1]
    kinds, out_shape = [], []
    for given in shapes:
        if len(given) == 5:
            kinds.append(("group", given[0], given[3]))
            shape = (expert_size, given[0]) + given[3:]
        else:
            kinds.append(("plane" if len(given) == 4 else "flat", None, given[-2]))
            shape = given[1:]
        out_shape.append(jax.ShapeDtypeStruct(shape, bf16))
    moving, staying = pieces(kinds, expert_size, ctx_size)
    held, arriving = buffer_places(moving + staying)
    count, depth = len(moving + staying), len(bits_of(ctx_size))
    scratch = [
        pltpu.VMEM((held["rows"], width), bf16),
        pltpu.VMEM((held["rows"], width), bf16),
        pltpu.VMEM((arriving["rows"], width), bf16),
        DMA((count, ctx_size)),
        DMA((count, ctx_size)),
        DMA((count, ctx_size)),
        DMA((count, ctx_size)),
        DMA((count, depth, max(ctx_size // 2, 1))),
        DMA((count,)),
        DMA((count,)),
    ]
    if dots is not None:
        out_shape.append(jax.ShapeDtypeStruct(dots[1:], f32))
        scratch += [
            pltpu.VMEM((dp_size, ctx_size) + dots[1:], f32),
            pltpu.VMEM(dots[1:], f32),
            DMA((dp_size, ctx_size)),
            DMA((dp_size, ctx_size)),
            DMA((expert_size,)),
            DMA((expert_size,)),
        ]
    return tuple(kinds), out_shape, scratch


class Shared:
    def __init__(self, grads, outs, scratch):
        self.grads, self.outs = grads, outs
        self.landing, self.columns = scratch[:3], scratch[3:5]
        self.send, self.recv, self.column_send, self.column_recv = scratch[5:]
        self.dp_size, self.ctx_size, self.expert_size = sizes_of()
        self.dp, self.ctx, self.expert = (lax.axis_index(a) for a in ("dp", "ctx", "expert"))
        self.own = self.dp * self.ctx_size + self.ctx
        self.plane = [(d, c) for d in range(self.dp_size) for c in range(self.ctx_size) if (d, c) != (0, 0)]
        self.part = grads[0].shape[2]

    def z_copy(self, kind, step):
        there = (self.expert + step) % self.expert_size
        return pltpu.make_async_remote_copy(
            src_ref=self.grads[kind].at[there],
            dst_ref=self.landing[kind].at[step],
            send_sem=self.send.at[kind, step],
            recv_sem=self.recv.at[kind, step],
            device_id={"expert": there},
            device_id_type=MESH,
        )

    def column(self, kind, d, c, landing=False):
        there = ((self.dp + d) % self.dp_size) * self.ctx_size + flip(self.ctx, c)
        source = ((self.dp + self.dp_size - d) % self.dp_size) * self.ctx_size + flip(self.ctx, c)
        at = source if landing else self.own
        return pltpu.make_async_remote_copy(
            src_ref=self.columns[kind].at[there],
            dst_ref=self.outs[kind].at[:, pl.ds(pl.multiple_of(at * self.part, 128), self.part)],
            send_sem=self.column_send.at[kind, d, c],
            recv_sem=self.column_recv.at[kind, d, c],
            device_id={"dp": (self.dp + d) % self.dp_size, "ctx": flip(self.ctx, c)},
            device_id_type=MESH,
        )

    def start(self):
        for kind in range(3):
            for step in range(1, self.expert_size):
                self.z_copy(kind, step).start()

    def sum(self):
        for kind in range(3):
            total = self.grads[kind][self.expert].astype(f32)
            for step in range(1, self.expert_size):
                self.z_copy(kind, step).wait_recv()
                total = total + self.landing[kind][step].astype(f32)
            if kind == 2:
                self.outs[2][...] = total
                continue
            shard = self.outs[kind].shape[0]
            for block in range(self.dp_size * self.ctx_size):
                self.columns[kind][block] = total[block * shard : (block + 1) * shard]
            for d, c in self.plane:
                self.column(kind, d, c).start()
            here = pl.ds(pl.multiple_of(self.own * self.part, 128), self.part)
            self.outs[kind][:, here] = self.columns[kind][self.own]

    def done(self):
        for kind in range(3):
            for step in range(1, self.expert_size):
                self.z_copy(kind, step).wait_send()
            if kind < 2:
                for d, c in self.plane:
                    self.column(kind, d, c, True).wait_recv()
                    self.column(kind, d, c).wait_send()


def shared_plan(width, part, sizes):
    dp_size, ctx_size, expert_size = sizes
    plane_size = dp_size * ctx_size
    shard = width // (plane_size * expert_size)
    given = [(expert_size, plane_size * shard, part)] * 2 + [(expert_size, part // expert_size, width)]
    columns = jax.ShapeDtypeStruct((shard, plane_size * part), f32)
    out_shape = [columns, columns, jax.ShapeDtypeStruct(given[2][1:], f32)]
    scratch = [pltpu.VMEM(shape, bf16) for shape in given]
    scratch += [pltpu.VMEM((plane_size, shard, part), f32)] * 2
    scratch += [
        DMA((3, expert_size)),
        DMA((3, expert_size)),
        DMA((2, dp_size, ctx_size)),
        DMA((2, dp_size, ctx_size)),
    ]
    return given, out_shape, scratch


class Carry:
    CHUNKS = 8

    def __init__(self, masks, sources, targets, sems):
        self.masks, self.sources, self.targets, self.sems = masks, sources, targets, sems
        self.ctx = lax.axis_index("ctx")
        groups = len(masks[0]) if masks else 0
        self.queues = [
            [
                (array, g, e, chunk)
                for array in range(len(masks))
                for e in range(GROUP)
                for chunk in range(self.CHUNKS)
            ]
            for g in range(groups)
        ]

    def copy(self, array, g, e, rows):
        return pltpu.make_async_remote_copy(
            src_ref=self.sources[array][g].at[e, rows],
            dst_ref=self.targets[array].at[g * GROUP + e, rows],
            send_sem=self.sems[0].at[array, g],
            recv_sem=self.sems[1].at[array, g],
            device_id={"ctx": flip(self.ctx, self.masks[array][g])},
            device_id_type=MESH,
        )

    def push(self, count, groups=None):
        for g in range(len(self.queues)) if groups is None else groups:
            for array, _, e, chunk in self.queues[g][:count]:
                rows = self.sources[array][g].shape[1] // self.CHUNKS
                self.copy(array, g, e, pl.ds(chunk * rows, rows)).start()
            del self.queues[g][:count]

    def done(self):
        for array, by_group in enumerate(self.masks):
            for g in range(len(by_group)):
                whole = pltpu.make_async_remote_copy(
                    src_ref=self.sources[array][g],
                    dst_ref=self.targets[array].at[pl.ds(g * GROUP, GROUP)],
                    send_sem=self.sems[0].at[array, g],
                    recv_sem=self.sems[1].at[array, g],
                    device_id={"ctx": flip(self.ctx, by_group[g])},
                    device_id_type=MESH,
                )
                whole.wait_recv()
                whole.wait_send()


def by_group(arrays, groups):
    return [[array.at[pl.ds(g * GROUP, GROUP)] for g in range(groups)] for array in arrays]


def sums_kernel(kinds, masks, *refs):
    rest = iter(refs)

    def take(count):
        return [next(rest) for _ in range(count)]

    part, dot, carried, shared_in = next(rest), next(rest), take(len(masks)), take(3)
    landed, dots_landed, carried_out, shared_out = next(rest), next(rest), take(len(masks)), take(3)
    sems = take(2) if masks else []
    shared = Shared(shared_in, shared_out, take(9))
    carry = Carry(masks, by_group(carried, len(masks[0]) if masks else 0), carried_out, sems)
    home = Home(kinds, True, [part], dot, [landed], dots_landed, list(rest))
    greet(plane_partners())
    shared.start()
    home.start(home.all)
    home.dots_start()
    for _ in home.ticks(home.all, 2):
        carry.push(3)
    home.dots_on()
    carry.push(len(masks) * GROUP * carry.CHUNKS)
    shared.sum()
    home.dots_landed()
    home.done()
    shared.done()
    carry.done()


def bring_sums(part, dots, shared_parts, carried, masks, sizes, number):
    kinds, out_shape, scratch = home_plan([part.shape], sizes, dots.shape)
    _, shared_out, shared_scratch = shared_plan(part.shape[-1], shared_parts[0].shape[2], sizes)
    return pl.pallas_call(
        functools.partial(sums_kernel, kinds, masks),
        out_shape=out_shape + [jax.ShapeDtypeStruct(array.shape, array.dtype) for array in carried] + shared_out,
        in_specs=[ANY, VMEM] + [ANY] * len(carried) + [VMEM] * 3,
        out_specs=[VMEM] * 2 + [ANY] * len(carried) + [VMEM] * 3,
        scratch_shapes=([DMA((len(masks), len(masks[0])))] * 2 if masks else []) + shared_scratch + scratch,
        compiler_params=pltpu.CompilerParams(
            collective_id=number, has_side_effects=True, vmem_limit_bytes=58 << 20
        ),
    )(part, dots, *carried, *shared_parts)


def finish_kernel(slices, kept, *refs):
    rest = iter(refs)

    def take(count):
        return [next(rest) for _ in range(count)]

    slices_in, landed, dots_landed, through = take(3 * slices), next(rest), next(rest), take(kept)
    grads, sums, dots, outs = take(3), take(4), next(rest), take(kept)
    for kind, grad in enumerate(grads):
        total = slices_in[kind][...].astype(f32)
        for k in range(1, slices):
            total = total + slices_in[k * 3 + kind][...].astype(f32)
        grad[...] = total

    @pl.when(pl.program_id(0) == 0)
    def _():
        for source, target in zip(through, outs):
            target[...] = source[...]
        expert_size, shard = landed.shape[0], sums[0].shape[0]
        whole, small = landed[0].astype(f32), dots_landed[0]
        for z in range(1, expert_size):
            whole = whole + landed[z].astype(f32)
            small = small + dots_landed[z]
        for i, out in enumerate(sums):
            out[...] = whole[i * shard : (i + 1) * shard]
        dots[...] = small


def finish(slices_in, landed, dots_landed, through, shard):
    width = landed.shape[-1]
    slices = len(slices_in) // 3
    own = slices_in[0].shape[0]

    def each(array):
        return pl.BlockSpec((1,) + array.shape[1:], lambda e: (e, 0, 0))

    def whole(array):
        return pl.BlockSpec(array.shape, lambda e: (0,) * len(array.shape))

    sums = [jax.ShapeDtypeStruct((shard, width), f32)] * 4 + [jax.ShapeDtypeStruct(dots_landed.shape[1:], f32)]
    kept = [jax.ShapeDtypeStruct(array.shape, array.dtype) for array in through]
    return pl.pallas_call(
        functools.partial(finish_kernel, slices, len(through)),
        grid=(own,),
        out_shape=[jax.ShapeDtypeStruct(array.shape, f32) for array in slices_in[:3]] + sums + kept,
        in_specs=[each(array) for array in slices_in]
        + [whole(array) for array in [landed, dots_landed] + list(through)],
        out_specs=[each(array) for array in slices_in[:3]] + [whole(array) for array in sums + kept],
        compiler_params=pltpu.CompilerParams(vmem_limit_bytes=62 << 20),
    )(*slices_in, landed, dots_landed, *through)


NT = (((1,), (1,)), ((), ()))
TN = (((0,), (0,)), ((), ()))


def contract(a, b, dims=(((1,), (0,)), ((), ()))):
    return lax.dot_general(a, b, dims, preferred_element_type=f32)


EXACT = lax.Precision.HIGHEST


def expert_of_place(count, stride, own):
    expert = lax.broadcasted_iota(jnp.int32, (EXPERTS, count), 0)
    column = lax.broadcasted_iota(jnp.int32, (EXPERTS, count), 1)
    place = column - ((expert // own) * stride + (expert % own) * PLACES)
    inside = (place >= 0) & (place < PLACES)
    at = jnp.sum(jnp.where(inside, place, 0), axis=0, keepdims=True)
    return inside.astype(f32), at.astype(f32)


def spots(hits, earlier, count, stride, own):
    expert_at, place_at = expert_of_place(count, stride, own)
    low = expert_at.astype(bf16)
    hit = contract(hits.astype(bf16), low)
    before = contract(earlier.astype(bf16), low)
    return jnp.where((hit > 0.5) & (before == place_at), 1.0, 0.0)


def row_spots(hits, earlier, expert_size):
    own = EXPERTS // expert_size
    return spots(hits, earlier, EXPERTS * PLACES, own * PLACES, own)


def first_place(rows):
    return (lax.axis_index("ctx") * lax.axis_size("expert") + lax.axis_index("expert")) * rows


def live(length_ref, rows):
    return first_place(rows) + lax.broadcasted_iota(jnp.int32, (rows, 1), 0) < length_ref[0]


def route(routes, alive):
    rows = routes.shape[1]
    expert = lax.broadcasted_iota(jnp.int32, (EXPERTS, rows), 0)
    named = (routes[0:1] == expert) | (routes[1:2] == expert)
    hits = jnp.transpose(jnp.where(named, 1.0, 0.0)) * jnp.where(alive, 1.0, 0.0)
    token = lax.broadcasted_iota(jnp.int32, (rows, rows), 0)
    other = lax.broadcasted_iota(jnp.int32, (rows, rows), 1)
    earlier = contract(jnp.where(other < token, 1.0, 0.0).astype(bf16), hits.astype(bf16))
    return hits, earlier


def place_rows(hits, earlier, flat, placed_ref):
    spread_out = jnp.transpose(row_spots(hits, earlier, placed_ref.shape[0])).astype(bf16)
    placed_ref[...] = contract(spread_out, flat).astype(bf16).reshape(placed_ref.shape)


def project(normed, weights, cosine, sine, qkv_ref):
    heads = qkv_ref.shape[0]
    half = HEAD_DIM // 2
    for kind, weight in enumerate(weights):
        lin = jnp.transpose(contract(normed, weight[...]))
        for head in range(heads):
            mine = lin[head * HEAD_DIM : (head + 1) * HEAD_DIM]
            if kind < 2:
                first, second = mine[:half], mine[half:]
                mine = jnp.concatenate(
                    [first * cosine - second * sine, second * cosine + first * sine], axis=0
                )
            qkv_ref[head, kind * HEAD_DIM : (kind + 1) * HEAD_DIM, :] = mine.astype(bf16)


def router_gates(normed, router, hits):
    logits = contract(normed, router, NT)
    top = jnp.max(jnp.where(hits > 0.5, logits, masked_value), axis=1, keepdims=True)
    powers = jnp.where(hits > 0.5, jnp.exp(logits - top), 0.0)
    total = jnp.sum(powers, axis=1, keepdims=True)
    return powers / jnp.where(total > 0.0, total, 1.0)


def gate_tiles(gates, hits, earlier, scale_ref):
    expert_size = scale_ref.shape[0]
    own, lanes = EXPERTS // expert_size, expert_size * 128
    expert_at, _ = expert_of_place(lanes, 128, own)
    by_place = jnp.dot(gates, expert_at, preferred_element_type=f32, precision=EXACT)
    row = jnp.sum(spots(hits, earlier, lanes, 128, own) * by_place, axis=0, keepdims=True)
    for z in range(expert_size):
        scale_ref[z] = jnp.broadcast_to(row[:, z * 128 : (z + 1) * 128], (8, 128))


def gates_back(dots_ref, gates, hits, earlier):
    expert_size = dots_ref.shape[0]
    own, lanes = EXPERTS // expert_size, expert_size * 128
    expert_at, _ = expert_of_place(lanes, 128, own)
    row = jnp.concatenate([dots_ref[z, 0:1, :] for z in range(expert_size)], axis=1)
    at_place = jnp.where(spots(hits, earlier, lanes, 128, own) > 0.5, row, 0.0)
    d_gates = lax.dot_general(at_place, expert_at, NT, preferred_element_type=f32, precision=EXACT)
    mean = jnp.sum(gates * d_gates, axis=1, keepdims=True)
    return (gates * (d_gates - mean)).astype(bf16)


def collect(hits, earlier, back_ref, flat_ref):
    width = flat_ref.shape[1]
    spread_out = row_spots(hits, earlier, back_ref.shape[0]).astype(bf16)
    placed = back_ref[...].reshape(EXPERTS * PLACES, width)
    return contract(spread_out, placed) + flat_ref[...].astype(f32)


def weight_sums(shard, grads, sums_ref):
    plane_size, expert_size, count, width = sums_ref.shape
    for p in range(plane_size):
        for z in range(expert_size):
            first = (p * expert_size + z) * shard
            parts = [grad[first : first + shard] for grad in grads]
            if count > len(grads) * shard:
                parts.append(jnp.zeros((count - len(grads) * shard, width), f32))
            sums_ref[p, z] = jnp.concatenate(parts, axis=0).astype(bf16)


def branch(rows, d_out, gate_w, up_w, down_w):
    gate_lin, up_lin = contract(rows, gate_w), contract(rows, up_w)
    sigmoid = 1.0 / (1.0 + jnp.exp(-gate_lin))
    silu = gate_lin * sigmoid
    hidden = (silu * up_lin).astype(bf16)
    d_hidden = contract(d_out, down_w, NT)
    d_gate = (d_hidden * up_lin * (sigmoid + silu * (1.0 - sigmoid))).astype(bf16)
    d_up = (d_hidden * silu).astype(bf16)
    result = contract(hidden, down_w)
    d_rows = contract(d_gate, gate_w, NT) + contract(d_up, up_w, NT)
    d_lin = contract(rows, jnp.concatenate([d_gate, d_up], axis=1), TN)
    d_down = contract(hidden, d_out, TN)
    return result, d_rows, d_lin, d_down


def moe_kernel(spread_kinds, home_kinds, slices, length_ref, *refs):
    rest = iter(refs)

    def take(count):
        return [next(rest) for _ in range(count)]

    tokens, attended_in, gain, router, hits_ref, earlier_ref, cotangent = take(7)
    output_in = next(rest)
    up_rows_in, up_flat_in = take(2)
    weights_in, shared_in = take(3), take(3)
    hidden, attended_out, d_hidden_out, d_attended_out, d_attn_out, router_grad, gain_grad = take(7)
    result_out, shared_out = take(2)
    shared_grads_out = take(3)
    grads_out = take(3 * slices)
    placed, normed, gate, output_w, output_sem = take(5)
    back, flat, dots_out = take(3)
    in_rows, in_flat, gates = take(3)
    up_rows, up_flat = take(2)
    weights, shared_w = take(3), take(3)
    result, shared_result = take(2)
    d_rows, shared_d = up_rows, up_flat
    lin_out, down_out, rows_f32, up_f32, dot, gates_own = take(6)
    lin_sum, down_sum = take(2)
    shared_parts = take(3)
    load_sem, store_sem = take(2)
    spread = Spread(spread_kinds, True, [placed, normed, gate, in_rows, in_flat, gates] + take(10), True)
    home = Home(home_kinds, True, [d_rows, shared_d], dot, [back, flat], dots_out, list(rest), True)

    dp_size, ctx_size, expert_size = sizes_of()
    ctx, own_block = lax.axis_index("ctx"), spread.own
    groups, blocks, _, size, width = in_rows.shape
    plane_size, rows, _ = in_flat.shape
    part = weights[0].shape[-1]
    sources = blocks * expert_size
    bits = bits_of(ctx_size)

    def column(mask):
        return pl.ds(pl.multiple_of(spread.block(0, mask) * part, 128), part)

    def loads(g):
        masks = subsets([bit for bit in bits if bit != group_bit(g, ctx_size)])
        experts = pl.ds(g * GROUP, GROUP)
        copies = [(up_rows_in.at[g], up_rows.at[g])]
        for k, mask in enumerate(masks):
            copies += [
                (weights_in[0].at[experts, :, column(mask)], weights[0].at[g, k]),
                (weights_in[1].at[experts, :, column(mask)], weights[1].at[g, k]),
                (weights_in[2].at[experts, column(mask)], weights[2].at[g, k]),
            ]
        return [pltpu.make_async_copy(s, t, load_sem.at[g, i]) for i, (s, t) in enumerate(copies)]

    shared_loads = [
        pltpu.make_async_copy(s, t, load_sem.at[groups, i])
        for i, (s, t) in enumerate(
            [
                (shared_in[0].at[:, column(0)], shared_w[0]),
                (shared_in[1].at[:, column(0)], shared_w[1]),
                (shared_in[2].at[column(0)], shared_w[2]),
                (up_flat_in, up_flat),
            ]
        )
    ]
    (output_load,) = fetch([output_in], [output_w], output_sem)
    output_load.start()
    alive = live(length_ref, rows)
    hits, earlier = hits_ref[...], earlier_ref[...]

    def prepare():
        attended = jnp.transpose(attended_in[...].reshape(width, rows).astype(f32)).astype(bf16)
        attended_out[...] = attended
        output_load.wait()
        attn_out = contract(attended, output_w[...])
        into = tokens[...].astype(f32) + jnp.where(alive, attn_out, 0.0)
        hidden[...] = into
        normed[...] = (into * rms_scale(into) * gain[...][None]).astype(bf16)
        gates_own[...] = router_gates(normed[...], router[...], hits)
        place_rows(hits, earlier, normed[...], placed)
        gate_tiles(gates_own[...], hits, earlier, gate)

    greet(plane_partners(), prepare)
    spread.z_start()
    spread.first(spread.staying)
    spread.keep()
    dot[...] = jnp.zeros_like(dot)
    def arriving(g):
        return [piece for piece in spread.moving if piece.group == g]

    for one in shared_loads:
        one.start()
    spread.forward_all(spread.staying)
    for one in loads(0):
        one.start()
    spread.first(arriving(0))
    spread.gates_on()
    spread.paired(spread.staying)
    for one in spread.kept() + shared_loads:
        one.wait()

    def shared_part(first, count):
        here = pl.ds(first, count)
        shape = (count * rows, width)
        some = branch(
            in_flat[here].reshape(shape), up_flat[here].reshape(shape), shared_w[0][...], shared_w[1][...],
            shared_w[2][...],
        )
        shared_result[here] = some[0].reshape((count, rows, width)).astype(bf16)
        shared_d[here] = some[1].reshape((count, rows, width)).astype(bf16)
        if first == 0:
            lin_sum[...] = some[2]
            down_sum[...] = some[3]
        else:
            lin_sum[...] += some[2]
            down_sum[...] += some[3]

    chunk = 4
    flats = home.staying[-2:]
    flat_stores = [
        pltpu.make_async_copy(s, t, store_sem.at[groups, i])
        for i, (s, t) in enumerate(zip([shared_result] + shared_parts, [shared_out] + shared_grads_out))
    ]
    shared_part(0, chunk)
    spread.forward_all(arriving(0))
    for g in range(1, groups):
        spread.first(arriving(g))
        for one in loads(g):
            one.start()
    spread.gates_landed()
    spread.paired(arriving(0))

    def shared_rest():
        for first in range(chunk, plane_size, chunk):
            shared_part(first, chunk)
        home.start(flats)
        shard = shared_parts[0].shape[1] // plane_size
        for z in range(expert_size):
            firsts = [(p * expert_size + z) * shard for p in range(plane_size)]
            mine = jnp.concatenate([lin_sum[first : first + shard] for first in firsts]).astype(bf16)
            shared_parts[0][z] = mine[:, :part]
            shared_parts[1][z] = mine[:, part:]
        shared_parts[2][...] = down_sum[...].astype(bf16).reshape(shared_parts[2].shape)
        for one in flat_stores:
            one.start()

    def expert(g, i):
        bit = group_bit(g, ctx_size)
        lane = (g * GROUP + i) * PLACES
        owners = [spread.block(core, mask) for core in (0, 1) for mask in (0, bit)]
        scale = jnp.concatenate(
            [gates[owner, z, 0:1, lane : lane + PLACES] for owner in owners for z in range(expert_size)]
        )[:, :, None]
        by_source = (sources, PLACES, width)
        up = up_f32[i]
        d_out = (up.reshape(by_source) * scale).reshape(up.shape).astype(bf16)
        some, d_some, d_lin, d_down = branch(
            rows_f32[i].astype(bf16),
            d_out,
            jnp.concatenate([weights[0][g, k, i] for k in range(slices)], axis=1),
            jnp.concatenate([weights[1][g, k, i] for k in range(slices)], axis=1),
            jnp.concatenate([weights[2][g, k, i] for k in range(slices)], axis=0),
        )
        for k in range(slices):
            lin_out[g, 0, k, i] = d_lin[:, k * part : (k + 1) * part].astype(bf16)
            lin_out[g, 1, k, i] = d_lin[:, (slices + k) * part : (slices + k + 1) * part].astype(bf16)
            down_out[g, k, i] = d_down[k * part : (k + 1) * part, :].astype(bf16)
        sums = jnp.sum((some * up).reshape(by_source), axis=-1)
        up_f32[i] = (some.reshape(by_source) * scale).reshape(up.shape)
        rows_f32[i] = d_some
        for at, owner in enumerate(owners):
            for z in range(expert_size):
                line = sums[at * expert_size + z : at * expert_size + z + 1]
                pieces_of = [line]
                if lane:
                    pieces_of.insert(0, jnp.zeros((1, lane), f32))
                if lane + PLACES < 128:
                    pieces_of.append(jnp.zeros((1, 128 - lane - PLACES), f32))
                dot[owner, z, 0:1, :] += jnp.concatenate(pieces_of, axis=1)

    def unpack(g):
        def one(source, carry):
            there = pl.ds(source * PLACES, PLACES)
            at = g, source // expert_size, source % expert_size
            some, up = in_rows[at].astype(f32), up_rows[at].astype(f32)
            for i in range(GROUP):
                rows_f32[i, there] = some[i * PLACES : (i + 1) * PLACES]
                up_f32[i, there] = up[i * PLACES : (i + 1) * PLACES]
            return carry

        for source in range(sources):
            one(source, 0)

    def pack(g):
        def one(source, carry):
            there = pl.ds(source * PLACES, PLACES)
            at = g, source // expert_size, source % expert_size
            result[at] = jnp.concatenate([up_f32[i, there] for i in range(GROUP)]).astype(bf16)
            d_rows[at] = jnp.concatenate([rows_f32[i, there] for i in range(GROUP)]).astype(bf16)
            return carry

        for source in range(sources):
            one(source, 0)

    def stores_of(g):
        experts = pl.ds(g * GROUP, GROUP)
        copies = [(result.at[g], result_out.at[g])]
        for k in range(slices):
            copies += [
                (lin_out.at[g, 0, k], grads_out[k].at[experts]),
                (lin_out.at[g, 1, k], grads_out[slices + k].at[experts]),
                (down_out.at[g, k], grads_out[2 * slices + k].at[experts]),
            ]
        return [pltpu.make_async_copy(s, t, store_sem.at[g, i]) for i, (s, t) in enumerate(copies)]

    def of_group(g):
        return [piece for piece in home.moving + home.staying if piece.group == g]

    depth = len(bits)
    waiting = []

    def move_on(count):
        for stage_of in waiting[:count]:
            stage_of()
        del waiting[:count]

    for g in range(groups):
        for one in loads(g):
            one.wait()
        if g:
            spread.paired(arriving(g))
        unpack(g)
        if g:
            move_on(len(waiting) * 3 // 7)
        for i in range(GROUP):
            expert(g, i)
            if g == 0 and i == 0:
                for later in range(1, groups):
                    spread.forward_all(arriving(later))
            if g < groups - 1 or i < GROUP - 1:
                move_on(len(waiting) * 3 // 4)
        if g == groups - 1:
            home.dots_start()
        pack(g)
        home.start(of_group(g))
        if g < groups - 1:
            for one in stores_of(g):
                one.start()
        if g == 0:
            shared_rest()
        waiting += [functools.partial(home.pair, piece) for piece in of_group(g)]
        if g == 0:
            waiting += [functools.partial(home.pair, piece) for piece in flats]
        waiting += [functools.partial(home.step, piece, 0) for piece in of_group(g)]
        if g == 0:
            for place in range(depth):
                waiting += [functools.partial(home.step, piece, place) for piece in flats]
    move_on(len(waiting))
    for one in stores_of(groups - 1):
        one.start()
    home.dots_on()
    home.dots_landed()
    d_logits = gates_back(dots_out, gates_own[...], hits, earlier)
    router_grad[...] = contract(normed[...], d_logits, TN)
    home.done()

    d_normed = collect(hits, earlier, back, flat) + contract(d_logits, router[...])
    into = hidden[...]
    scale = rms_scale(into)
    normal = into * scale
    gain_grad[...] = jnp.sum(d_normed * normal, axis=0, keepdims=True)
    d_hidden = cotangent[...].astype(f32) + rms_back(normal, scale, gain[...][None], d_normed)
    d_hidden_out[...] = d_hidden
    d_attn = jnp.where(alive, d_hidden, 0.0).astype(bf16)
    d_attn_out[...] = d_attn
    d_attended = jnp.transpose(contract(d_attn, output_w[...], NT))
    d_attended_out[...] = d_attended.astype(bf16).reshape(d_attended_out.shape)

    spread.sent()
    for g in range(groups):
        for one in stores_of(g):
            one.wait()
    for one in flat_stores:
        one.wait()


def moe(length, tokens, attended, gain, router, routing, cotangent, output_weight, up_rows, up_flat, weights,
        shared_weights, sizes, number):
    dp_size, ctx_size, expert_size = sizes
    plane_size = dp_size * ctx_size
    rows, width = tokens.shape
    part = shared_weights[0].shape[1] // plane_size
    slices = max(ctx_size // 2, 1)
    own = EXPERTS // expert_size
    groups = own // GROUP
    sources = 4 * expert_size
    placed = jax.ShapeDtypeStruct((expert_size, groups, GROUP * PLACES, width), bf16)
    flat = jax.ShapeDtypeStruct((rows, width), bf16)
    hidden = jax.ShapeDtypeStruct((rows, width), f32)
    gate = jax.ShapeDtypeStruct((expert_size, 8, 128), f32)
    spread_kinds, landing, spread_scratch = spread_plan([placed, flat], gate, sizes)
    dots = (plane_size,) + gate.shape
    home_kinds, home_out, home_scratch = home_plan([up_rows.shape, up_flat.shape], sizes, dots)
    shared_given, _, _ = shared_plan(width, part, sizes)
    lin = jax.ShapeDtypeStruct((own, width, part), bf16)
    down = jax.ShapeDtypeStruct((own, part, width), bf16)
    columns = pltpu.VMEM((groups, slices, GROUP, width, part), bf16)

    def buffers(shapes):
        return [pltpu.VMEM(shape.shape, shape.dtype) for shape in shapes]

    out = pl.pallas_call(
        functools.partial(moe_kernel, spread_kinds, home_kinds, slices),
        out_shape=[
            hidden,
            flat,
            hidden,
            jax.ShapeDtypeStruct(attended.shape, bf16),
            flat,
            jax.ShapeDtypeStruct(router.shape[::-1], f32),
            jax.ShapeDtypeStruct((1, width), f32),
        ]
        + [jax.ShapeDtypeStruct(up_rows.shape, bf16), jax.ShapeDtypeStruct(up_flat.shape, bf16)]
        + [jax.ShapeDtypeStruct(shape, bf16) for shape in shared_given]
        + [lin] * (2 * slices)
        + [down] * slices,
        in_specs=[SMEM] + [VMEM] * 7 + [ANY] * 9,
        out_specs=[VMEM] * 7 + [ANY] * (5 + 3 * slices),
        scratch_shapes=buffers([placed, flat, gate])
        + [pltpu.VMEM(output_weight.shape, bf16), DMA((1,))]
        + buffers(home_out)
        + buffers(landing)
        + [pltpu.VMEM(up_rows.shape, bf16), pltpu.VMEM(up_flat.shape, bf16)]
        + [columns, columns, pltpu.VMEM((groups, slices, GROUP, part, width), bf16)]
        + [pltpu.VMEM((width, part), bf16)] * 2
        + [pltpu.VMEM((part, width), bf16)]
        + [pltpu.VMEM(up_rows.shape, bf16), pltpu.VMEM(up_flat.shape, bf16)]
        + [
            pltpu.VMEM((groups, 2, slices, GROUP, width, part), bf16),
            pltpu.VMEM((groups, slices, GROUP, part, width), bf16),
            pltpu.VMEM((GROUP, sources * PLACES, width), f32),
            pltpu.VMEM((GROUP, sources * PLACES, width), f32),
            pltpu.VMEM(dots, f32),
            pltpu.VMEM((rows, EXPERTS), f32),
            pltpu.VMEM((width, 2 * part), f32),
            pltpu.VMEM((part, width), f32),
        ]
        + [pltpu.VMEM(shape, bf16) for shape in shared_given]
        + [DMA((groups + 1, max(1 + 3 * slices, 4)))] * 2
        + spread_scratch
        + home_scratch,
        compiler_params=pltpu.CompilerParams(
            collective_id=number, has_side_effects=True, vmem_limit_bytes=63 << 20
        ),
    )(length, tokens, attended, gain, router, *routing, cotangent, output_weight, up_rows, up_flat, *weights,
      *shared_weights)
    grads = out[12 : 12 + 3 * slices]
    grads = [grads[kind * slices : (kind + 1) * slices] for kind in range(3)]
    return out[:7], out[9:12], out[7:9], grads


class Slot:
    def __init__(self, heads):
        _, self.ctx_size, self.expert_size = sizes_of()
        self.heads, self.count = heads, self.ctx_size * self.expert_size
        ctx, expert = lax.axis_index("ctx"), lax.axis_index("expert")
        self.me = ctx * self.expert_size + expert
        head = head_of(ctx, expert, heads, self.ctx_size, self.expert_size)
        self.holds = head < heads
        self.head = head % heads

    def device(self, place):
        return {"ctx": place // self.expert_size, "expert": place % self.expert_size}

    def partners(self):
        dp, ctx = lax.axis_index("dp"), lax.axis_index("ctx")
        dp_size = lax.axis_size("dp")
        return [self.device((self.me + i) % self.count) for i in range(1, self.count)] + [
            {"dp": (dp + d) % dp_size, "ctx": flip(ctx, c)} for d in range(1, dp_size) for c in range(self.ctx_size)
        ]

    def copy(self, source, target, send, recv, there):
        return pltpu.make_async_remote_copy(
            src_ref=source, dst_ref=target, send_sem=send, recv_sem=recv, device_id=there, device_id_type=MESH
        )

    def inward(self, blocks, landing, send, recv):
        for i in range(self.heads):
            head = (self.me + i) % self.heads
            row, column = head_place(head, self.heads, self.ctx_size, self.expert_size)
            one = self.copy(
                blocks.at[head], landing.at[self.me], send.at[head], recv.at[self.me],
                {"ctx": row, "expert": column},
            )
            yield jnp.logical_not(self.holds & (head == self.head)), one

    def inward_landed(self, landing, send, recv):
        for i in range(1, self.count):
            source = (self.me + self.count - i) % self.count
            here = landing.at[source]
            yield self.copy(here, here, send.at[0], recv.at[source], self.device(self.me))

    def outward(self, blocks, landing, send, recv, place):
        return self.copy(
            blocks.at[place], landing.at[self.head], send.at[place], recv.at[self.head], self.device(place)
        )

    def outward_landed(self, landing, send, recv):
        for head in range(self.heads):
            here = landing.at[head]
            one = self.copy(here, here, send.at[0], recv.at[head], self.device(self.me))
            yield jnp.logical_not(self.holds & (head == self.head)), one


def attend_kernel(
    step, heads, kinds, length_ref, routes_ref, cotangent_ref, tokens_ref, gain_ref, cosine_ref, sine_ref, *refs
):
    rest = iter(refs)

    def take(count):
        return [next(rest) for _ in range(count)]

    weights_in = take(3)
    qkv_ref, out_ref, total_ref, landed_ref, normed_ref, hits_ref, earlier_ref = take(7)
    side_outs = take(len(kinds))
    weights, blocks_ref, placed_ref, branch_ref = take(3), *take(3)
    key_ref, query_ref, value_ref, sent_ref = take(4)
    in_send, in_recv, out_send, out_recv, weight_sem = take(5)
    side = Spread(kinds, False, [placed_ref, branch_ref] + side_outs + list(rest))

    slot = Slot(heads)
    rows, width = tokens_ref.shape
    span = slot.count * rows
    loads = fetch(weights_in, weights, weight_sem)
    for one in loads:
        one.start()

    def prepare():
        alive = live(length_ref, rows)
        hits, earlier = route(routes_ref[...], alive)
        hits_ref[...] = hits
        earlier_ref[...] = earlier
        branch = jnp.where(alive, cotangent_ref[...].astype(f32), 0.0).astype(bf16)
        branch_ref[...] = branch
        place_rows(hits, earlier, branch, placed_ref)

    greet(slot.partners(), prepare)
    inputs = tokens_ref[...].astype(f32)
    normed_ref[...] = (inputs * rms_scale(inputs) * gain_ref[...][None]).astype(bf16)
    for one in loads:
        one.wait()
    here = pl.ds(pl.multiple_of(slot.me * rows, 128), rows)
    project(normed_ref[...], weights, cosine_ref[:, here], sine_ref[:, here], blocks_ref)
    for needed, one in slot.inward(blocks_ref, qkv_ref, in_send, in_recv):
        pl.when(needed)(one.start)
    side.first(side.staying)
    side.keep()
    side.z_start()
    side.forward_all(side.staying)

    @pl.when(slot.holds)
    def _():
        qkv_ref[slot.me] = blocks_ref[slot.head]
        for one in slot.inward_landed(qkv_ref, in_send, in_recv):
            one.wait_recv()
        key_ref[...] = live_keys(head_rows(qkv_ref, HEAD_DIM, HEAD_DIM), length_ref[0])
        query_ref[...] = scaled_queries(head_rows(qkv_ref, 0, HEAD_DIM))
        value_ref[...] = head_rows(qkv_ref, 2 * HEAD_DIM, HEAD_DIM)

    def query_block(q):
        here = pl.ds(q * step, step)
        query = query_ref[:, here]

        def absorb(k, state, masked):
            top, total, out = state
            there = pl.ds(k * step if masked else pl.multiple_of(k * step, step), step)
            scores = jnp.dot(key_ref[there, :], query, preferred_element_type=f32)
            if masked:
                scores = causal(scores)
            new_top = jnp.maximum(top, jnp.max(scores, axis=0, keepdims=True))
            shrink = jnp.exp(top - new_top)
            weights = jnp.exp(scores - new_top)
            total = total * shrink + jnp.sum(weights, axis=0, keepdims=True)
            out = out * shrink + jnp.dot(
                value_ref[:, there], weights.astype(bf16), preferred_element_type=f32
            )
            return new_top, total, out

        state = (
            jnp.full((1, step), masked_value, f32),
            jnp.zeros((1, step), f32),
            jnp.zeros((HEAD_DIM, step), f32),
        )
        state = absorb(q, state, True)
        if q:
            state = lax.fori_loop(0, q, lambda k, s: absorb(k, s, False), state)
        top, total, out = state
        out = out / total
        out_ref[:, here] = out
        total_ref[:, here] = top + jnp.log(total)
        for i in range(step // rows):
            place = q * (step // rows) + i
            sent_ref[place] = out[:, i * rows : (i + 1) * rows].astype(bf16)
            one = slot.outward(sent_ref, landed_ref, out_send, out_recv, place)
            pl.when(slot.me != place)(one.start)

    for q in range(span // step):
        pl.when(slot.holds)(functools.partial(query_block, q))
        if q == span // step - 2:
            side.first(side.moving)
    side.forward_all(side.moving)

    @pl.when(slot.holds)
    def _():
        landed_ref[slot.head] = sent_ref[slot.me]

    for needed, one in slot.outward_landed(landed_ref, out_send, out_recv):
        pl.when(needed)(one.wait_recv)
    side.paired(side.all)
    side.sent()
    for one in side.kept():
        one.wait()
    for needed, one in slot.inward(blocks_ref, qkv_ref, in_send, in_recv):
        pl.when(needed)(one.wait_send)
    for place in range(slot.count):
        one = slot.outward(sent_ref, landed_ref, out_send, out_recv, place)
        pl.when(slot.holds & (slot.me != place))(one.wait_send)


def attend(length, routes, cotangent, tokens, gain, tables, weights, sizes, number):
    rows, width = tokens.shape
    _, ctx_size, expert_size = sizes
    heads, count = width // HEAD_DIM, ctx_size * expert_size
    span = count * rows
    step = min(512, span)
    groups = EXPERTS // expert_size // GROUP
    placed = jax.ShapeDtypeStruct((expert_size, groups, GROUP * PLACES, width), bf16)
    flat = jax.ShapeDtypeStruct((rows, width), bf16)
    kinds, side_shapes, side_scratch = spread_plan([placed, flat], None, sizes)
    blocks = (heads, 3 * HEAD_DIM, rows)
    hits = jax.ShapeDtypeStruct((rows, EXPERTS), f32)
    out = pl.pallas_call(
        functools.partial(attend_kernel, step, heads, kinds),
        out_shape=[
            jax.ShapeDtypeStruct((count,) + blocks[1:], bf16),
            jax.ShapeDtypeStruct((HEAD_DIM, span), f32),
            jax.ShapeDtypeStruct((1, span), f32),
            jax.ShapeDtypeStruct((heads, HEAD_DIM, rows), bf16),
            flat,
            hits,
            hits,
        ]
        + side_shapes,
        in_specs=[SMEM] + [VMEM] * 6 + [ANY] * 3,
        out_specs=[VMEM] * 7 + [ANY] * len(side_shapes),
        scratch_shapes=[pltpu.VMEM(weights[0].shape, bf16)] * 3
        + [
            pltpu.VMEM(blocks, bf16),
            pltpu.VMEM(placed.shape, bf16),
            pltpu.VMEM(flat.shape, bf16),
            pltpu.VMEM((span, 2 * HEAD_DIM), bf16),
            pltpu.VMEM((2 * HEAD_DIM, span), bf16),
            pltpu.VMEM((HEAD_DIM, span), bf16),
            pltpu.VMEM((count, HEAD_DIM, rows), bf16),
        ]
        + [DMA((count,))] * 4
        + [DMA((3,))]
        + side_scratch,
        compiler_params=pltpu.CompilerParams(
            collective_id=number, has_side_effects=True, vmem_limit_bytes=56 << 20
        ),
    )(length, routes, cotangent, tokens, gain, *tables, *weights)
    return out[:4], out[4:7], out[7:]


def unrotate(grad_t, cosine, sine):
    half = HEAD_DIM // 2
    first, second = grad_t[:half], grad_t[half:]
    return jnp.concatenate(
        [first * cosine + second * sine, second * cosine - first * sine], axis=0
    )


def attend_back_kernel(
    step, heads, kinds, masks, shard, length_ref, gain_ref, hits_ref, earlier_ref, blocks_ref, *refs
):
    rest = iter(refs)

    def take(count):
        return [next(rest) for _ in range(count)]

    soon, later, side_ins, carried = take(5), take(9), take(len(kinds)), take(len(masks))
    output_ref, input_grad, gain_grad, sums_out = take(4)
    carried_out = take(len(masks))
    soon_here, later_here, landed_ref, sums_ref, side_outs = take(5), take(9), next(rest), next(rest), take(len(kinds))
    qkv_ref, out_ref, total_ref, cosine_ref, sine_ref = soon_here
    normed_ref, tokens_ref, d_hidden_ref, attended_ref, d_attn_ref, hidden_ref, *weights = later_here
    upstream_ref, key_ref, query_ref, value_ref, key_t_ref, key_sum, value_sum, delta_ref, up_ref, sent_ref = take(10)
    in_send, in_recv, out_send, out_recv, soon_sem, later_sem, sums_sem = take(7)
    carry = Carry(
        masks, by_group(carried, len(masks[0]) if masks else 0), carried_out, take(2) if masks else []
    )
    side = Home(kinds, False, side_ins, None, side_outs, None, list(rest))

    slot = Slot(heads)
    rows = blocks_ref.shape[2]
    span = slot.count * rows
    loads = fetch(soon, soon_here, soon_sem)
    late_loads = fetch(later, later_here, later_sem)

    @pl.when(slot.holds)
    def _():
        key_sum[...] = jnp.zeros_like(key_sum)
        value_sum[...] = jnp.zeros_like(value_sum)

    greet(slot.partners())
    for needed, one in slot.inward(blocks_ref, upstream_ref, in_send, in_recv):
        pl.when(needed)(one.start)
    for one in loads:
        one.start()
    side.start(side.all)
    for one in late_loads:
        one.start()
    carry.push(4)
    for one in loads:
        one.wait()

    @pl.when(slot.holds)
    def _():
        key_t = head_rows(qkv_ref, HEAD_DIM, HEAD_DIM)
        key_ref[...] = live_keys(key_t, length_ref[0])
        key_t_ref[...] = key_t
        query_ref[...] = scaled_queries(head_rows(qkv_ref, 0, HEAD_DIM))
        value_t = head_rows(qkv_ref, 2 * HEAD_DIM, HEAD_DIM)
        value_ref[...] = jnp.transpose(value_t.astype(f32)).astype(bf16)
        upstream_ref[slot.me] = blocks_ref[slot.head]

    for piece in side.moving:
        side.pair(piece)
    carry.push(4)

    @pl.when(slot.holds)
    def _():
        for one in slot.inward_landed(upstream_ref, in_send, in_recv):
            one.wait_recv()
        upstream = head_rows(upstream_ref, 0, HEAD_DIM)
        up_ref[...] = upstream
        delta_ref[...] = jnp.sum(upstream.astype(f32) * out_ref[...], axis=0, keepdims=True)

    def query_block(q):
        here = pl.ds(q * step, step)
        query, up = query_ref[:, here], up_ref[:, here]
        total, delta = total_ref[:, here], delta_ref[:, here]

        def meet(k, query_sum, masked):
            there = pl.ds(k * step if masked else pl.multiple_of(k * step, step), step)
            scores = jnp.dot(key_ref[there, :], query, preferred_element_type=f32)
            if masked:
                scores = causal(scores)
            probs = jnp.exp(scores - total)
            d_probs = jnp.dot(value_ref[there, :], up, preferred_element_type=f32)
            d_scores = (probs * (d_probs - delta)).astype(bf16)
            key_sum[:, there] += contract(query[:HEAD_DIM], d_scores, NT)
            value_sum[:, there] += contract(up, probs.astype(bf16), NT)
            return query_sum + contract(key_t_ref[:, there], d_scores)

        query_sum = meet(q, jnp.zeros((HEAD_DIM, step), f32), True)
        if q:
            query_sum = lax.fori_loop(0, q, lambda k, s: meet(k, s, False), query_sum)
        cosine, sine = cosine_ref[:, here], sine_ref[:, here]
        grad = jnp.concatenate(
            [
                unrotate(query_sum * score_scale, cosine, sine),
                unrotate(key_sum[:, here], cosine, sine),
                value_sum[:, here],
            ],
            axis=0,
        ).astype(bf16)
        for i in range(step // rows):
            place = q * (step // rows) + i
            sent_ref[place] = grad[:, i * rows : (i + 1) * rows]
            one = slot.outward(sent_ref, landed_ref, out_send, out_recv, place)
            pl.when(slot.me != place)(one.start)

    for piece in side.moving:
        side.step(piece, 0)
    for piece in side.staying:
        side.pair(piece)
    depth = len(bits_of(lax.axis_size("ctx")))
    stages = [
        [functools.partial(side.step, piece, place) for piece in side.staying if place < len(piece.order)]
        for place in range(depth)
    ]
    for q in reversed(range(span // step)):
        pl.when(slot.holds)(functools.partial(query_block, q))
        for one in stages.pop(0) if stages else []:
            one()
        carry.push(4)
    for some in stages:
        for one in some:
            one()
    carry.push(len(masks) * GROUP * carry.CHUNKS)

    @pl.when(slot.holds)
    def _():
        landed_ref[slot.head] = sent_ref[slot.me]

    for needed, one in slot.outward_landed(landed_ref, out_send, out_recv):
        pl.when(needed)(one.wait_recv)
    for one in late_loads:
        one.wait()

    width = tokens_ref.shape[1]
    lins = []
    d_normed = jnp.zeros((width, rows), f32)
    for kind in range(3):
        at = slice(kind * HEAD_DIM, (kind + 1) * HEAD_DIM)
        lin = jnp.concatenate([landed_ref[head, at, :] for head in range(heads)], axis=0)
        lins.append(lin)
        d_normed = d_normed + contract(weights[kind][...], lin)
    d_normed = jnp.transpose(d_normed)
    inputs = tokens_ref[...].astype(f32)
    scale = rms_scale(inputs)
    normal = inputs * scale
    gain_grad[...] = jnp.sum(d_normed * normal, axis=0, keepdims=True)
    d_inputs = d_hidden_ref[...] + rms_back(normal, scale, gain_ref[...][None], d_normed)
    input_grad[...] = d_inputs.astype(bf16)
    normed_t = jnp.transpose(normed_ref[...].astype(f32)).astype(bf16)
    attended_t = jnp.transpose(attended_ref[...].astype(f32)).astype(bf16)
    grads = [contract(normed_t, lin, NT) for lin in lins] + [contract(attended_t, d_attn_ref[...])]
    weight_sums(shard, grads, sums_ref)
    (sums_store,) = fetch([sums_ref], [sums_out], sums_sem)
    sums_store.start()

    side.done()
    mixed = collect(hits_ref[...], earlier_ref[...], *side_outs)
    alive = live(length_ref, rows)
    output_ref[...] = (hidden_ref[...] + jnp.where(alive, mixed, 0.0)).astype(bf16)
    carry.done()
    sums_store.wait()
    for needed, one in slot.inward(blocks_ref, upstream_ref, in_send, in_recv):
        pl.when(needed)(one.wait_send)
    for place in range(slot.count):
        one = slot.outward(sent_ref, landed_ref, out_send, out_recv, place)
        pl.when(slot.holds & (slot.me != place))(one.wait_send)


def attend_back(length, gain, routing, blocks, soon, mine, weights, parts, carried, masks, sizes, number):
    qkv, later = soon[0], [*mine, *weights]
    heads, _, rows = blocks.shape
    count = qkv.shape[0]
    span = count * rows
    step = min(512, span)
    dp_size, ctx_size, expert_size = sizes
    width = weights[0].shape[0]
    shard = width // (dp_size * count)
    kinds, side_shapes, side_scratch = home_plan([part.shape for part in parts], sizes)
    carry_shapes = [jax.ShapeDtypeStruct(array.shape, array.dtype) for array in carried]
    carry_sems = [DMA((len(masks), len(masks[0])))] * 2 if masks else []
    sums = (dp_size * ctx_size, expert_size, -(-4 * shard // 16) * 16, width)
    got = pl.pallas_call(
        functools.partial(attend_back_kernel, step, heads, kinds, masks, shard),
        out_shape=[
            jax.ShapeDtypeStruct((rows, width), bf16),
            jax.ShapeDtypeStruct((rows, width), bf16),
            jax.ShapeDtypeStruct((1, width), f32),
            jax.ShapeDtypeStruct(sums, bf16),
        ]
        + carry_shapes,
        in_specs=[SMEM] + [VMEM] * 4 + [ANY] * (14 + len(parts) + len(carried)),
        out_specs=[VMEM] * 3 + [ANY] * (1 + len(carried)),
        scratch_shapes=[pltpu.VMEM(array.shape, array.dtype) for array in soon + later]
        + [pltpu.VMEM((heads,) + qkv.shape[1:], bf16), pltpu.VMEM(sums, bf16)]
        + [pltpu.VMEM(shape.shape, shape.dtype) for shape in side_shapes]
        + [
            pltpu.VMEM((count,) + blocks.shape[1:], bf16),
            pltpu.VMEM((span, 2 * HEAD_DIM), bf16),
            pltpu.VMEM((2 * HEAD_DIM, span), bf16),
            pltpu.VMEM((span, HEAD_DIM), bf16),
            pltpu.VMEM((HEAD_DIM, span), bf16),
            pltpu.VMEM((HEAD_DIM, span), f32),
            pltpu.VMEM((HEAD_DIM, span), f32),
            pltpu.VMEM((1, span), f32),
            pltpu.VMEM((HEAD_DIM, span), bf16),
            pltpu.VMEM(qkv.shape, bf16),
        ]
        + [DMA((count,))] * 4
        + [DMA((5,)), DMA((9,)), DMA((1,))]
        + carry_sems
        + side_scratch,
        compiler_params=pltpu.CompilerParams(
            collective_id=number, has_side_effects=True, vmem_limit_bytes=60 << 20
        ),
    )(length, gain, *routing, blocks, *soon, *later, *parts, *carried)
    return got[:4], got[4:]


def local(
    tokens,
    lengths,
    routes,
    norm1_gain,
    query_weight,
    key_weight,
    value_weight,
    output_weight,
    norm2_gain,
    router_weight,
    expert_gate,
    expert_up,
    expert_down,
    shared_gate,
    shared_up,
    shared_down,
    cotangent,
):
    sizes = dp_size, ctx_size, expert_size = sizes_of()
    plane_size, slot_size = dp_size * ctx_size, ctx_size * expert_size
    rows, width = tokens.shape[1:]
    shard = width // (dp_size * slot_size)
    tokens, routes, cotangent = tokens[0], routes[0], cotangent[0]
    weights = (query_weight, key_weight, value_weight)
    tables = rope_tables(jnp.arange(slot_size * rows, dtype=jnp.int32))

    (qkv, out_t, log_total, attended), (normed, *routing), (up_rows, up_flat) = attend(
        lengths, routes.T, cotangent, tokens, norm1_gain, tables, weights, sizes, 1
    )

    bits = bits_of(ctx_size)
    groups = EXPERTS // expert_size // GROUP
    slice_masks = [
        subsets([bit for bit in bits if bit != group_bit(g, ctx_size)]) for g in range(groups)
    ]
    slices = len(slice_masks[0])
    ways = tuple(tuple(masks[k] for masks in slice_masks) for _ in range(3) for k in range(1, slices))
    early = slices - 1

    mine, shared_parts, results, grads = moe(
        lengths, tokens, attended, norm2_gain, router_weight.T, routing, cotangent, output_weight, up_rows, up_flat,
        (expert_gate, expert_up, expert_down), (shared_gate, shared_up, shared_down), sizes, 2,
    )
    hidden, attended, d_hidden, d_attended, d_attn, router_grad, gain_two_grad = mine
    others = [array for kind in grads for array in kind[1:]]
    (output_rows, input_grad, gain_one_grad, sums), early_in = attend_back(
        lengths, norm1_gain, routing, d_attended, [qkv, out_t, log_total, *tables],
        (normed, tokens, d_hidden, attended, d_attn, hidden),
        weights, results, others[: 2 * early], ways[: 2 * early], sizes, 3,
    )

    devices = (plane_size, expert_size)
    pad = [(0, 0), (0, 0), (0, 0), (0, 128 - shard)]
    routed = -(-shard * EXPERTS // 128)
    small = jnp.concatenate(
        [
            jnp.pad(
                router_grad.reshape(devices + (shard * EXPERTS,)),
                [(0, 0), (0, 0), (0, routed * 128 - shard * EXPERTS)],
            ).reshape(devices + (routed, 128)),
            jnp.pad(gain_one_grad.reshape(devices + (1, shard)), pad),
            jnp.pad(gain_two_grad.reshape(devices + (1, shard)), pad),
            jnp.zeros(devices + (6 - routed, 128), f32),
        ],
        axis=2,
    )
    landed, small, *last_in = bring_sums(
        sums, small, shared_parts, others[2 * early :], ways[2 * early :], sizes, 4
    )
    arrived = [*early_in, *last_in[:early]]
    shared_grads = last_in[early:]
    by_slice = [kind[0] for kind in grads]
    for k in range(early):
        by_slice += [arrived[kind * early + k] for kind in range(3)]
    *out, small, output_rows, input_grad, shared_gate_grad, shared_up_grad, shared_down_grad = finish(
        by_slice, landed, small, [output_rows, input_grad, *shared_grads], shard
    )
    return (
        output_rows[None],
        input_grad[None],
        small[routed, :shard],
        *out[3:7],
        small[routed + 1, :shard],
        small[:routed].reshape(-1)[: shard * EXPERTS].reshape(shard, EXPERTS),
        *out[:3],
        shared_gate_grad,
        shared_up_grad,
        shared_down_grad,
    )


def solution(mesh):
    tokens = P("dp", ("ctx", "expert"), None)
    whole = P()
    experts = P("expert", None, None)
    everywhere = ("dp", "ctx", "expert")
    return jax.shard_map(
        local,
        mesh=mesh,
        in_specs=(tokens, P("dp"), tokens)
        + (whole,) * 7
        + (experts,) * 3
        + (whole,) * 3
        + (tokens,),
        out_specs=(tokens, tokens, P(everywhere))
        + (P(everywhere, None),) * 4
        + (P(everywhere), P(everywhere, None))
        + (P("expert", None, PLANE),) * 2
        + (P("expert", PLANE, None),)
        + (P(everywhere, None),) * 3,
        check_vma=False,
    )
```
